32 devices in a mesh: seq: 8 (over z, y), rows: 4 (over x, core).
Axes of the slice: x: 2, y: 2, z: 4, core: 2. Of those that a mesh axis runs over, the one named last changes fastest.
Arguments:
- tokens: bfloat16 [8, 1024, 768], P('rows', 'seq'), may hold values from -6 to 6
- pair_lengths: int32 [8, 16], P('rows'), may hold values from 1 to 512, as said below
- joint_weight: bfloat16 [768, 2304], replicated, may hold values from -0.21875 to 0.21875
- query_bias: float32 [768], replicated, may hold values from -1.2 to 1.2
- value_bias: float32 [768], replicated, may hold values from -0.3 to 0.3
- out_weight: bfloat16 [768, 768], replicated, may hold values from -2 to 2
- out_bias: float32 [768], replicated, may hold values from -3 to 3
- first_gain: float32 [768], replicated, may hold values from 0.25 to 1.75
- first_shift: float32 [768], replicated, may hold values from -3 to 3
- up_weight: bfloat16 [768, 3072], replicated, may hold values from -0.21875 to 0.21875
- up_bias: float32 [3072], replicated, may hold values from -3 to 3
- down_weight: bfloat16 [3072, 768], replicated, may hold values from -0.109375 to 0.109375
- down_bias: float32 [768], replicated, may hold values from -3 to 3
- second_gain: float32 [768], replicated, may hold values from 0.25 to 1.75
- second_shift: float32 [768], replicated, may hold values from -3 to 3
- cotangent: bfloat16 [8, 1024, 768], P('rows', 'seq'), may hold values from -6 to 6
Outputs:
- outputs: bfloat16 [8, 1024, 768], P('rows', 'seq')
- token_gradient: float32 [8, 1024, 768], P('rows', 'seq')
- joint_gradient: float32 [768, 2304], P('seq')
- query_bias_gradient: float32 [768], P('seq')
- value_bias_gradient: float32 [768], P('seq')
- out_gradient: float32 [768, 768], P('seq')
- out_bias_gradient: float32 [768], P('seq')
- first_gain_gradient: float32 [768], P('seq')
- first_shift_gradient: float32 [768], P('seq')
- up_gradient: float32 [768, 3072], P('seq')
- up_bias_gradient: float32 [3072], P('seq')
- down_gradient: float32 [3072, 768], P('seq')
- down_bias_gradient: float32 [768], P('seq')
- second_gain_gradient: float32 [768], P('seq')
- second_shift_gradient: float32 [768], P('seq')
The draws below stay inside these ranges and needn't reach their ends.
Inputs may be any that keep to these rules, and one draw needn't show every extreme that they name: `pair_lengths`: in every packed row the 16 lengths add up to 1024; no pair is longer than 512 positions (BERT's 512 at most), and in every row one pair has exactly 512.
All inputs are finite; a program needn't handle non-finite values.
Results may differ from the reference program's by a relative error of at most 0.023.
Values may be sent and summed in bfloat16 or wider, within the bound.
No kernel may reach another device: no remote copies, remote signals or barrier semaphores. Data moves between devices by JAX's collectives and lax.ppermute only.
A program may use at most 128 MiB of HBM per device.

```python
import math
import jax
import jax.numpy as jnp
from jax import lax

D = 768
HEADS = 12
HEAD_DIM = 64
FF = 3072
PAIRS = 16
LENGTH = 1024
PAIR_MOST = 512
ROWS = 8


def draw_pair_lengths(key, part):
    key = jax.random.fold_in(key, 11)
    weight_key, place_key = jax.random.split(key)
    shares_raw = jax.random.randint(weight_key, (ROWS, PAIRS - 1), 1, 1000).astype(jnp.int32)
    extra_all = LENGTH - PAIR_MOST - (PAIRS - 1)
    room_each = PAIR_MOST - 1
    totals = jnp.sum(shares_raw, axis=1, keepdims=True).astype(jnp.int32)
    share = jnp.minimum(extra_all * shares_raw // totals, room_each).astype(jnp.int32)
    left_over = (extra_all - jnp.sum(share, axis=1, keepdims=True)).astype(jnp.int32)
    room = (room_each - share).astype(jnp.int32)
    filled = jnp.cumsum(room, axis=1).astype(jnp.int32)
    given = jnp.clip(left_over - (filled - room), 0, room).astype(jnp.int32)
    others = (1 + share + given).astype(jnp.int32)
    place = jax.random.randint(place_key, (ROWS, 1), 0, PAIRS).astype(jnp.int32)
    index = jnp.arange(PAIRS, dtype=jnp.int32)[None, :]
    source = jnp.clip(jnp.where(index < place, index, index - 1), 0, PAIRS - 2).astype(jnp.int32)
    picked = jnp.take_along_axis(others, jnp.broadcast_to(source, (ROWS, PAIRS)), axis=1)
    return jnp.where(index == place, PAIR_MOST, picked).astype(jnp.int32)


def level_of(key, dims, cuts, smallest, top_value):
    def one(axis_at, shards_of):
        heights = jax.random.uniform(jax.random.fold_in(jax.random.fold_in(key, 6), axis_at), (shards_of,), jnp.float32, smallest / len(cuts), top_value / len(cuts))
        return jnp.repeat(jnp.exp(heights), dims[axis_at] // shards_of).reshape((-1,) + (1,) * (len(dims) - axis_at - 1))

    level = one(*cuts[0])
    for cut in cuts[1:]:
        level = level * one(*cut)
    return level


def gaussian(rng, extent, width, most, cuts=(), kind=jnp.bfloat16):
    entries = jax.random.normal(rng, extent, jnp.float32) * width
    if len(cuts) > 0:
        entries = level_of(rng, extent, cuts, -0.22, 0.18) * entries
    return jnp.clip(entries, min=-most, max=most).astype(kind)


def setup_inputs(seed: int = 0) -> dict:
    arg_keys = jax.random.split(jax.random.key(seed), 17)
    tokens = gaussian(arg_keys[0], (ROWS, LENGTH, D), 1.0, 6.0, ((0, 4), (1, 8)))
    pair_lengths = draw_pair_lengths(jax.random.fold_in(arg_keys[16], 71), 0)
    joint_weight = gaussian(arg_keys[2], (D, 3 * D), D ** -0.5, 0.21875)
    query_bias = gaussian(arg_keys[3], (D,), 0.2, 1.2, (), jnp.float32)
    value_bias = gaussian(arg_keys[4], (D,), 0.05, 0.3, (), jnp.float32)
    out_weight = gaussian(arg_keys[5], (D, D), (max(D // 96, 1)) ** -0.5, 2.0)
    out_bias = gaussian(arg_keys[6], (D,), 0.5, 3.0, (), jnp.float32)
    first_gain = jnp.clip(1.0 + 0.15 * jax.random.normal(arg_keys[7], (D,), jnp.float32), 0.25, 1.75)
    first_shift = gaussian(arg_keys[8], (D,), 0.5, 3.0, (), jnp.float32)
    up_weight = gaussian(arg_keys[9], (D, FF), D ** -0.5, 0.21875)
    up_bias = gaussian(arg_keys[10], (FF,), 0.5, 3.0, (), jnp.float32)
    down_weight = gaussian(arg_keys[11], (FF, D), FF ** -0.5, 0.109375)
    down_bias = gaussian(arg_keys[12], (D,), 0.5, 3.0, (), jnp.float32)
    second_gain = jnp.clip(1.0 + 0.15 * jax.random.normal(arg_keys[13], (D,), jnp.float32), 0.25, 1.75)
    second_shift = gaussian(arg_keys[14], (D,), 0.5, 3.0, (), jnp.float32)
    cotangent = gaussian(arg_keys[15], (ROWS, LENGTH, D), 1.0, 6.0, ((0, 4), (1, 8)))
    return dict(tokens=tokens, pair_lengths=pair_lengths, joint_weight=joint_weight, query_bias=query_bias, value_bias=value_bias, out_weight=out_weight, out_bias=out_bias, first_gain=first_gain, first_shift=first_shift, up_weight=up_weight, up_bias=up_bias, down_weight=down_weight, down_bias=down_bias, second_gain=second_gain, second_shift=second_shift, cotangent=cotangent)


NEGATIVE = -1e+30
EPSILON = 1e-12

@jax.custom_vjp
def low(v):
    return lax.optimization_barrier(v.astype(jnp.bfloat16)).astype(jnp.float32)

@jax.custom_vjp
def low_back(v):
    return v

def low_keep(v):
    return (low(v), None)

def low_pass(kept, grad):
    return (grad,)

def back_keep(v):
    return (v, None)

def back_low(kept, grad):
    return (low(grad),)
low.defvjp(low_keep, low_pass)
low_back.defvjp(back_keep, back_low)

def layer_norm(value, gain, shift):
    mean = lax.optimization_barrier(jnp.mean(value, axis=-1, keepdims=True))
    centred = value - mean
    spread = lax.optimization_barrier(jnp.mean(centred * centred, axis=-1, keepdims=True))
    return centred * lax.rsqrt(spread + EPSILON) * gain + shift

def product(left, right):
    return jnp.dot(left, right, precision=lax.Precision.HIGHEST, preferred_element_type=jnp.float32)

def gelu_exact(value):
    return jax.nn.gelu(value, approximate=False)

def attend_row(inputs):
    queries, keys, values, pair_ids = inputs
    block = math.gcd(LENGTH, 512)
    scale = HEAD_DIM ** (-0.5)

    def one_block(pieces):
        query_block, block_ids = pieces
        raw = jnp.einsum('qhd,khd->hqk', query_block, keys, precision=lax.Precision.HIGHEST)
        scores = low_back(raw * scale)
        allowed = block_ids[None, :, None] == pair_ids[None, None, :]
        masked = jnp.where(allowed, scores, NEGATIVE)
        highest = lax.optimization_barrier(jnp.max(masked, axis=2, keepdims=True))
        weights = jnp.where(allowed, jnp.exp(masked - highest), 0.0)
        weights_low = low(weights / lax.optimization_barrier(jnp.sum(weights, axis=2, keepdims=True)))
        return jnp.einsum('hqk,khd->qhd', weights_low, values, precision=lax.Precision.HIGHEST)
    query_blocks = queries.reshape(LENGTH // block, block, HEADS, HEAD_DIM)
    id_blocks = pair_ids.reshape(LENGTH // block, block)
    attended = lax.map(jax.checkpoint(one_block), (query_blocks, id_blocks))
    return attended.reshape(LENGTH, HEADS, HEAD_DIM)

def forward(tokens, joint_weight, query_bias, value_bias, out_weight, out_bias, first_gain, first_shift, up_weight, up_bias, down_weight, down_bias, second_gain, second_shift, pair_ids):
    flat = tokens.reshape(ROWS * LENGTH, D)
    projected = product(flat, joint_weight)
    queries = low(low_back(projected[:, :D] + query_bias))
    keys = low(low_back(projected[:, D:2 * D]))
    values = low(low_back(projected[:, 2 * D:] + value_bias))
    shape = (ROWS, LENGTH, HEADS, HEAD_DIM)
    attended = lax.map(attend_row, (queries.reshape(shape), keys.reshape(shape), values.reshape(shape), pair_ids))
    attended = low(low_back(attended.reshape(ROWS * LENGTH, D)))
    branch = low_back(product(attended, out_weight) + out_bias)
    first_sum = flat + branch
    normed = layer_norm(first_sum, first_gain, first_shift)
    inner = low_back(product(low(normed), up_weight) + up_bias)
    activated = low(gelu_exact(inner))
    feed = low_back(product(activated, down_weight) + down_bias)
    return layer_norm(normed + feed, second_gain, second_shift)

def reference(tokens, pair_lengths, joint_weight, query_bias, value_bias, out_weight, out_bias, first_gain, first_shift, up_weight, up_bias, down_weight, down_bias, second_gain, second_shift, cotangent):
    ends = jnp.cumsum(pair_lengths, axis=1).astype(jnp.int32)
    positions = jnp.arange(LENGTH, dtype=jnp.int32)
    pair_ids = lax.optimization_barrier(jnp.sum((positions[None, :, None] >= ends[:, None, :]).astype(jnp.int32), axis=2)).astype(jnp.int32)
    floats = [array.astype(jnp.float32) for array in (tokens, joint_weight, query_bias, value_bias, out_weight, out_bias, first_gain, first_shift, up_weight, up_bias, down_weight, down_bias, second_gain, second_shift)]

    def layer(*arrays):
        return forward(*arrays, pair_ids)
    result, back = jax.vjp(layer, *floats)
    gradients = back(cotangent.astype(jnp.float32).reshape(ROWS * LENGTH, D))
    return (result.reshape(ROWS, LENGTH, D).astype(jnp.bfloat16), gradients[0].reshape(ROWS, LENGTH, D), gradients[1], gradients[2], gradients[3], gradients[4], gradients[5], gradients[6], gradients[7], gradients[8], gradients[9], gradients[10], gradients[11], gradients[12], gradients[13])
```

```python
import functools
import math

import jax
import jax.numpy as jnp
from jax import lax
from jax.experimental import pallas as pl
from jax.experimental.pallas import tpu as pltpu
from jax.sharding import PartitionSpec as P

HEADS = 12
HEAD_DIM = 64


NEGATIVE = -1e30
EPSILON = 1e-12


def from_behind(value, axis, steps):
    count = lax.axis_size(axis)
    pairs = [(source, (source + steps) % count) for source in range(count)]
    return lax.ppermute(value, axis, pairs)


def layer_norm(value, gain, shift):
    mean = jnp.mean(value, axis=-1, keepdims=True)
    centred = value - mean
    spread = jnp.mean(centred * centred, axis=-1, keepdims=True)
    return centred * lax.rsqrt(spread + EPSILON) * gain + shift


def gelu_exact(value):
    return jax.nn.gelu(value, approximate=False)


def pair_index(positions, ends):
    return jnp.sum((positions[None, :, None] >= ends[:, None, :]).astype(jnp.int32), axis=2)


def split_heads(array):
    return array.reshape(array.shape[0], array.shape[1], HEADS, HEAD_DIM)


def online_block(state, query_heads, query_pairs, key_block, value_block, key_pairs):
    highest, total, summed = state
    scores = jnp.einsum(
        "rqhd,rkhd->rhqk", query_heads, split_heads(key_block), preferred_element_type=jnp.float32
    ) * HEAD_DIM ** (-0.5)
    allowed = query_pairs[:, None, :, None] == key_pairs[:, None, None, :]
    masked = jnp.where(allowed, scores, NEGATIVE)
    new_high = jnp.maximum(highest, jnp.max(masked, axis=3))
    weights = jnp.where(allowed, jnp.exp(masked - new_high[..., None]), 0.0)
    factor = jnp.exp(highest - new_high)
    total = total * factor + jnp.sum(weights, axis=3)
    summed = summed * jnp.swapaxes(factor, 1, 2)[..., None] + jnp.einsum(
        "rhqk,rkhd->rqhd",
        weights.astype(jnp.bfloat16),
        split_heads(value_block),
        preferred_element_type=jnp.float32,
    )
    return (new_high, total, summed)


def tile_terms(queries, out_grad, log_total, delta, query_pairs, keys, values, key_pairs):
    scale = HEAD_DIM ** (-0.5)
    query_heads = split_heads(queries)
    grad_heads = split_heads(out_grad)
    key_heads = split_heads(keys)
    value_heads = split_heads(values)
    scores = (
        jnp.einsum("rqhd,rkhd->rhqk", query_heads, key_heads, preferred_element_type=jnp.float32)
        * scale
    )
    allowed = query_pairs[:, None, :, None] == key_pairs[:, None, None, :]
    weights = jnp.where(
        allowed, jnp.exp(jnp.where(allowed, scores, NEGATIVE) - log_total[..., None]), 0.0
    )
    weight_grad = jnp.einsum(
        "rqhd,rkhd->rhqk", grad_heads, value_heads, preferred_element_type=jnp.float32
    )
    score_grad = (weights * (weight_grad - delta[..., None])).astype(jnp.bfloat16)
    query_term = (
        jnp.einsum("rhqk,rkhd->rqhd", score_grad, key_heads, preferred_element_type=jnp.float32)
        * scale
    )
    key_term = (
        jnp.einsum("rhqk,rqhd->rkhd", score_grad, query_heads, preferred_element_type=jnp.float32)
        * scale
    )
    value_term = jnp.einsum(
        "rhqk,rqhd->rkhd",
        weights.astype(jnp.bfloat16),
        grad_heads,
        preferred_element_type=jnp.float32,
    )
    return (
        query_term.reshape(queries.shape),
        key_term.reshape(keys.shape),
        value_term.reshape(values.shape),
    )


def general_body(
    tokens,
    pair_lengths,
    joint_weight,
    query_bias,
    value_bias,
    out_weight,
    out_bias,
    first_gain,
    first_shift,
    up_weight,
    up_bias,
    down_weight,
    down_bias,
    second_gain,
    second_shift,
    cotangent,
):
    rows_here, seq_here, width = tokens.shape
    count = lax.axis_size("seq")
    cycle_index = lax.axis_index("seq")
    ends = jnp.cumsum(pair_lengths, axis=1)
    offsets = jnp.arange(seq_here, dtype=jnp.int32)
    own_pairs = pair_index(cycle_index * seq_here + offsets, ends)
    block_shape = (rows_here, seq_here, width)
    flat = tokens.reshape(rows_here * seq_here, width)
    projected = jnp.dot(flat, joint_weight, preferred_element_type=jnp.float32)
    queries = (projected[:, :width] + query_bias).astype(jnp.bfloat16).reshape(block_shape)
    keys = projected[:, width : 2 * width].astype(jnp.bfloat16).reshape(block_shape)
    values = (projected[:, 2 * width :] + value_bias).astype(jnp.bfloat16).reshape(block_shape)
    query_heads = split_heads(queries)
    initial = (
        jnp.full((rows_here, HEADS, seq_here), NEGATIVE, jnp.float32),
        jnp.zeros((rows_here, HEADS, seq_here), jnp.float32),
        jnp.zeros((rows_here, seq_here, HEADS, HEAD_DIM), jnp.float32),
    )
    key_piece = lax.all_gather(keys, "seq", axis=1, tiled=True)
    value_piece = lax.all_gather(values, "seq", axis=1, tiled=True)
    length = key_piece.shape[1]
    block = math.gcd(length, seq_here)

    def one_block(index, inner_state):
        first = index * block
        key_block = lax.dynamic_slice_in_dim(key_piece, first, block, 1)
        value_block = lax.dynamic_slice_in_dim(value_piece, first, block, 1)
        key_pairs = pair_index(first + jnp.arange(block, dtype=jnp.int32), ends)
        return online_block(inner_state, query_heads, own_pairs, key_block, value_block, key_pairs)

    highest, total, summed = lax.fori_loop(0, length // block, one_block, initial)
    log_total = highest + jnp.log(total)
    attended = (
        (summed / jnp.swapaxes(total, 1, 2)[..., None]).astype(jnp.bfloat16).reshape(flat.shape)
    )
    branch = jnp.dot(attended, out_weight, preferred_element_type=jnp.float32) + out_bias
    first_sum = flat.astype(jnp.float32) + branch
    normed, first_back = jax.vjp(layer_norm, first_sum, first_gain, first_shift)
    normed_low = normed.astype(jnp.bfloat16)
    inner = jnp.dot(normed_low, up_weight, preferred_element_type=jnp.float32) + up_bias
    activated_full, gelu_back = jax.vjp(gelu_exact, inner)
    activated = activated_full.astype(jnp.bfloat16)
    feed = jnp.dot(activated, down_weight, preferred_element_type=jnp.float32) + down_bias
    second_sum = normed + feed
    result, second_back = jax.vjp(layer_norm, second_sum, second_gain, second_shift)
    outputs = result.astype(jnp.bfloat16).reshape(tokens.shape)
    second_grad, second_gain_grad, second_shift_grad = second_back(
        cotangent.astype(jnp.float32).reshape(flat.shape)
    )
    feed_grad = second_grad.astype(jnp.bfloat16)
    down_grad = jnp.einsum("ti,tj->ij", activated, feed_grad, preferred_element_type=jnp.float32)
    down_bias_grad = jnp.sum(feed_grad.astype(jnp.float32), axis=0)
    activated_grad = jnp.einsum(
        "tj,ij->ti", feed_grad, down_weight, preferred_element_type=jnp.float32
    )
    inner_grad = gelu_back(activated_grad)[0].astype(jnp.bfloat16)
    up_grad = jnp.einsum("ti,tj->ij", normed_low, inner_grad, preferred_element_type=jnp.float32)
    up_bias_grad = jnp.sum(inner_grad.astype(jnp.float32), axis=0)
    normed_grad = second_grad + jnp.einsum(
        "tj,ij->ti", inner_grad, up_weight, preferred_element_type=jnp.float32
    )
    first_grad, first_gain_grad, first_shift_grad = first_back(normed_grad)
    branch_grad = first_grad.astype(jnp.bfloat16)
    out_grad = jnp.einsum("ti,tj->ij", attended, branch_grad, preferred_element_type=jnp.float32)
    out_bias_grad = jnp.sum(branch_grad.astype(jnp.float32), axis=0)
    attended_grad = jnp.einsum(
        "tj,ij->ti", branch_grad, out_weight, preferred_element_type=jnp.float32
    ).astype(jnp.bfloat16)
    delta = jnp.sum(
        (attended_grad.astype(jnp.float32) * attended.astype(jnp.float32)).reshape(
            rows_here, seq_here, HEADS, HEAD_DIM
        ),
        axis=3,
    )
    delta = jnp.swapaxes(delta, 1, 2)
    attended_grad = attended_grad.reshape(block_shape)
    zeros_block = jnp.zeros(block_shape, jnp.float32)

    def send_key_sums(sums):
        return (
            from_behind(sums[0].astype(jnp.bfloat16), "seq", 1).astype(jnp.float32),
            from_behind(sums[1].astype(jnp.bfloat16), "seq", 1).astype(jnp.float32),
        )

    def key_work(turn, pair_block, sums, query_sum):
        anchor = (cycle_index - turn) % count
        key_pairs = pair_index(anchor * seq_here + offsets, ends)
        query_term, key_term, value_term = tile_terms(
            queries,
            attended_grad,
            log_total,
            delta,
            own_pairs,
            pair_block[0],
            pair_block[1],
            key_pairs,
        )
        return ((sums[0] + key_term, sums[1] + value_term), query_sum + query_term)

    def key_turn(turn, state):
        pair_block, sums, query_sum = state
        sums, query_sum = key_work(turn, pair_block, sums, query_sum)
        sums = send_key_sums(sums)
        pair_block = from_behind((pair_block[0], pair_block[1]), "seq", 1)
        return (pair_block, sums, query_sum)

    pair_block, sums, query_sum = lax.fori_loop(
        0, count - 1, key_turn, ((keys, values), (zeros_block, zeros_block), zeros_block)
    )
    sums, query_sum = key_work(count - 1, pair_block, sums, query_sum)
    key_sum, value_sum = send_key_sums(sums)
    query_low = query_sum.astype(jnp.bfloat16).reshape(flat.shape)
    key_low = key_sum.astype(jnp.bfloat16).reshape(flat.shape)
    value_low = value_sum.astype(jnp.bfloat16).reshape(flat.shape)
    joint_low = jnp.concatenate([query_low, key_low, value_low], axis=1)
    joint_grad = jnp.einsum("ti,tj->ij", flat, joint_low, preferred_element_type=jnp.float32)
    query_bias_grad = jnp.sum(query_low.astype(jnp.float32), axis=0)
    value_bias_grad = jnp.sum(value_low.astype(jnp.float32), axis=0)
    token_grad = first_grad + jnp.einsum(
        "tj,ij->ti", joint_low, joint_weight, preferred_element_type=jnp.float32
    )
    gradients = (
        joint_grad,
        query_bias_grad,
        value_bias_grad,
        out_grad,
        out_bias_grad,
        first_gain_grad,
        first_shift_grad,
        up_grad,
        up_bias_grad,
        down_grad,
        down_bias_grad,
        second_gain_grad,
        second_shift_grad,
    )
    shares = (
        lax.psum_scatter(
            gradients[0].astype(jnp.bfloat16), "seq", scatter_dimension=0, tiled=True
        ).astype(jnp.float32),
        lax.psum_scatter(
            gradients[1].astype(jnp.bfloat16), "seq", scatter_dimension=0, tiled=True
        ).astype(jnp.float32),
        lax.psum_scatter(
            gradients[2].astype(jnp.bfloat16), "seq", scatter_dimension=0, tiled=True
        ).astype(jnp.float32),
        lax.psum_scatter(
            gradients[3].astype(jnp.bfloat16), "seq", scatter_dimension=0, tiled=True
        ).astype(jnp.float32),
        lax.psum_scatter(
            gradients[4].astype(jnp.bfloat16), "seq", scatter_dimension=0, tiled=True
        ).astype(jnp.float32),
        lax.psum_scatter(
            gradients[5].astype(jnp.bfloat16), "seq", scatter_dimension=0, tiled=True
        ).astype(jnp.float32),
        lax.psum_scatter(
            gradients[6].astype(jnp.bfloat16), "seq", scatter_dimension=0, tiled=True
        ).astype(jnp.float32),
        lax.psum_scatter(
            gradients[7].astype(jnp.bfloat16), "seq", scatter_dimension=0, tiled=True
        ).astype(jnp.float32),
        lax.psum_scatter(
            gradients[8].astype(jnp.bfloat16), "seq", scatter_dimension=0, tiled=True
        ).astype(jnp.float32),
        lax.psum_scatter(
            gradients[9].astype(jnp.bfloat16), "seq", scatter_dimension=0, tiled=True
        ).astype(jnp.float32),
        lax.psum_scatter(
            gradients[10].astype(jnp.bfloat16), "seq", scatter_dimension=0, tiled=True
        ).astype(jnp.float32),
        lax.psum_scatter(
            gradients[11].astype(jnp.bfloat16), "seq", scatter_dimension=0, tiled=True
        ).astype(jnp.float32),
        lax.psum_scatter(
            gradients[12].astype(jnp.bfloat16), "seq", scatter_dimension=0, tiled=True
        ).astype(jnp.float32),
    )
    shares = (
        lax.psum(shares[0].astype(jnp.bfloat16), "rows").astype(jnp.float32),
        lax.psum(shares[1].astype(jnp.bfloat16), "rows").astype(jnp.float32),
        lax.psum(shares[2].astype(jnp.bfloat16), "rows").astype(jnp.float32),
        lax.psum(shares[3].astype(jnp.bfloat16), "rows").astype(jnp.float32),
        lax.psum(shares[4].astype(jnp.bfloat16), "rows").astype(jnp.float32),
        lax.psum(shares[5].astype(jnp.bfloat16), "rows").astype(jnp.float32),
        lax.psum(shares[6].astype(jnp.bfloat16), "rows").astype(jnp.float32),
        lax.psum(shares[7].astype(jnp.bfloat16), "rows").astype(jnp.float32),
        lax.psum(shares[8].astype(jnp.bfloat16), "rows").astype(jnp.float32),
        lax.psum(shares[9].astype(jnp.bfloat16), "rows").astype(jnp.float32),
        lax.psum(shares[10].astype(jnp.bfloat16), "rows").astype(jnp.float32),
        lax.psum(shares[11].astype(jnp.bfloat16), "rows").astype(jnp.float32),
        lax.psum(shares[12].astype(jnp.bfloat16), "rows").astype(jnp.float32),
    )
    return (outputs, token_grad.reshape(tokens.shape)) + tuple(shares)


WIDTH = HEADS * HEAD_DIM
HALF = WIDTH // 2
FF = 4 * WIDTH
BLOCK = 128
OWN = 2 * BLOCK
LANES = 128
PAIRS_OF_HEADS = HALF // LANES
JOINT_ROWS = 160
UP_ROWS = 128
DOWN_ROWS = 96
FLOAT = jnp.float32
LOW = jnp.bfloat16
AXES = ("seq", "rows")


def kernel_params(megabytes):
    return pltpu.CompilerParams(vmem_limit_bytes=megabytes << 20)


def shaped(shape, kind):
    return jax.ShapeDtypeStruct(shape, kind)


def whole(shape):
    return pl.BlockSpec(shape, lambda *_: (0,) * len(shape))


def cost(flops, moved, exps=0):
    return pl.CostEstimate(flops=int(flops), bytes_accessed=int(moved), transcendentals=int(exps))


def dot(left, right):
    return lax.dot_general(left, right, (((1,), (0,)), ((), ())), preferred_element_type=FLOAT)


def dot_nt(left, right):
    return lax.dot_general(left, right, (((1,), (1,)), ((), ())), preferred_element_type=FLOAT)


def device_at(z, y, x, c):
    return ((z * 2 + y) * 2 + x) * 2 + c


def permute(value, target):
    pairs = []
    for z in range(4):
        for y in range(2):
            for x in range(2):
                for c in range(2):
                    pairs.append((device_at(z, y, x, c), device_at(*target(z, y, x, c))))
    return lax.ppermute(value, AXES, pairs)


def core_swap(value):
    return permute(value, lambda z, y, x, c: (z, y, x, 1 - c))


def x_swap(value):
    return permute(value, lambda z, y, x, c: (z, y, 1 - x, c))


def y_swap(value):
    return permute(value, lambda z, y, x, c: (z, 1 - y, x, c))


def z_swap(value, bits):
    return permute(value, lambda z, y, x, c: (z ^ bits, y, x, c))


def row_swap(value, second):
    return permute(value, lambda z, y, x, c: (2 * c + (z % 2 ^ second), y, x, z // 2))


def first_positions(place):
    z, y, c = place[0], place[1], place[3]
    bases = []
    for core, line in ((c, y), (1 - c, y), (c, 1 - y), (1 - c, 1 - y)):
        for second in (0, 1):
            parity = z % 2
            parity = 1 - parity if second else parity
            bases.append((2 * (2 * core + parity) + line) * BLOCK)
    return bases


def pair_ends(place, own_lengths, peer_lengths):
    z, c = place[0], place[3]
    here = (z // 2) == c
    line = z % 2
    ends, end = [], 0
    for pair in range(own_lengths.shape[1]):
        end = end + jnp.where(here, own_lengths[line, pair], peer_lengths[line, pair])
        ends.append(end)
    return ends


def pairs_along(base, ends, axis):
    shape = (8, BLOCK) if axis == 1 else (BLOCK, LANES)
    position = base + lax.broadcasted_iota(jnp.int32, shape, axis)
    ids = jnp.zeros(shape, jnp.int32)
    for end in ends:
        ids = ids + (position >= end).astype(jnp.int32)
    return ids


def head_mask(rows):
    return lax.broadcasted_iota(jnp.int32, (rows, LANES), 1) < HEAD_DIM


def attention_kernel(
    place, own_lengths, peer_lengths, *refs
):
    blocks = refs[:8]
    wq, wk, wv, qb, vb = refs[8:13]
    own_out, send_out, q_out, k_out, v_out, log_out = refs[13:19]
    bias, log_columns = refs[19:]
    bases = first_positions(place)
    ends = pair_ends(place, own_lengths, peer_lengths)
    here = jnp.concatenate([block[...] for block in blocks[:4]], axis=0)
    there = jnp.concatenate([block[...] for block in blocks[4:]], axis=0)
    queries = dot(here, wq[...]) + qb[...]
    q_out[...] = (queries.astype(LOW).astype(FLOAT) * HEAD_DIM**-0.5).astype(LOW)
    for index, tokens in enumerate((here, there)):
        rows = pl.ds(index * 512, 512)
        k_out[rows, :] = dot(tokens, wk[...]).astype(LOW)
        v_out[rows, :] = (dot(tokens, wv[...]) + vb[...]).astype(LOW)
    key_ids = [pairs_along(base, ends, 1)[0:1] for base in bases]
    for i in range(4):
        query_ids = pairs_along(bases[i], ends, 0)
        for j in range(8):
            bias[pl.ds(i * BLOCK, BLOCK), pl.ds(j * BLOCK, BLOCK)] = jnp.where(
                query_ids == key_ids[j], 0.0, NEGATIVE
            )
    log_columns[...] = jnp.zeros_like(log_columns)
    for pair in range(PAIRS_OF_HEADS):
        lanes = pl.ds(pair * LANES, LANES)
        keys = k_out[:, lanes]
        values = v_out[:, lanes]
        ones = jnp.ones_like(values)
        left_keys = head_mask(1024)
        values_of = (jnp.where(left_keys, values, ones), jnp.where(left_keys, ones, values))
        left = head_mask(OWN)
        for part in range(2):
            rows = pl.ds(part * OWN, OWN)
            queries = q_out[rows, lanes]
            zeros = jnp.zeros_like(queries)
            summed = []
            for half in range(2):
                chosen = jnp.where(left, queries, zeros) if half == 0 else jnp.where(left, zeros, queries)
                scores = dot_nt(chosen, keys) + bias[rows, :]
                highest = jnp.max(scores, axis=1, keepdims=True)
                weights = jnp.exp(scores - highest).astype(LOW)
                total = dot(weights, values_of[half])
                turned = pltpu.roll(total, HEAD_DIM, 1)
                summed.append(total / turned)
                sums = total if half == 1 else turned
                log_total = highest + jnp.log(sums)
                column = lax.broadcasted_iota(jnp.int32, (OWN, LANES), 1) == pair * 2 + half
                at = log_total if pair * 2 + half < HEAD_DIM else None
                log_columns[rows, :] = jnp.where(column, at, log_columns[rows, :])
            attended = jnp.where(left, summed[0], summed[1]).astype(LOW)
            target = own_out if part == 0 else send_out
            target[:, lanes] = attended
    log_out[...] = jnp.transpose(log_columns[...])[0:8, :]


def attention(place, own_lengths, peer_lengths, blocks, joint_weight, query_bias, value_bias):
    def columns(kind):
        return pl.BlockSpec((WIDTH, HALF), lambda i, place, *_: (0, 2 * kind + place[3]))

    half_row = pl.BlockSpec((1, HALF), lambda i, place, *_: (0, place[3]))
    return pl.pallas_call(
        attention_kernel,
        grid_spec=pltpu.PrefetchScalarGridSpec(
            num_scalar_prefetch=3,
            grid=(1,),
            in_specs=[whole((BLOCK, WIDTH))] * 8
            + [columns(0), columns(1), columns(2), half_row, half_row],
            out_specs=[
                whole((OWN, HALF)),
                whole((OWN, HALF)),
                whole((512, HALF)),
                whole((1024, HALF)),
                whole((1024, HALF)),
                whole((8, 512)),
            ],
            scratch_shapes=[pltpu.VMEM((512, 1024), FLOAT), pltpu.VMEM((512, LANES), FLOAT)],
        ),
        out_shape=[
            shaped((OWN, HALF), LOW),
            shaped((OWN, HALF), LOW),
            shaped((512, HALF), LOW),
            shaped((1024, HALF), LOW),
            shaped((1024, HALF), LOW),
            shaped((8, 512), FLOAT),
        ],
        compiler_params=kernel_params(40),
        cost_estimate=cost(4e9, 8e6, 3e6),
        name="attention",
    )(
        place, own_lengths, peer_lengths, *blocks, joint_weight, joint_weight, joint_weight,
        query_bias.reshape(1, WIDTH), value_bias.reshape(1, WIDTH),
    )


def centred_norm(value):
    mean = jnp.mean(value, axis=-1, keepdims=True)
    centred = value - mean
    spread = jnp.mean(centred * centred, axis=-1, keepdims=True)
    inverse = lax.rsqrt(spread + EPSILON)
    return centred * inverse, inverse


def norm_back(grad, unit, inverse):
    mean = jnp.mean(grad, axis=-1, keepdims=True)
    along = jnp.mean(grad * unit, axis=-1, keepdims=True)
    return (grad - mean - unit * along) * inverse


def column_sum(value):
    return jnp.sum(value, axis=0, keepdims=True)


def forward_kernel(
    place, att_own, att_other, wo_own, wo_other, out_bias, x0, x1, gain1, shift1, up, up_bias, down,
    down_bias, gain2, shift2, cot0, cot1,
    out0, out1, feed_grad, second_grad, act_t, slope, unit1, inverse1, normed_t, att_t, sums,
    normed, normed_low, feed,
):
    step = pl.program_id(0)

    @pl.when(step == 0)
    def _():
        tokens = jnp.concatenate([x0[...], x1[...]], axis=0).astype(FLOAT)
        branch = dot(att_own[...], wo_own[...]) + dot(att_other[...], wo_other[...]) + out_bias[...]
        unit, inverse = centred_norm(tokens + branch)
        unit1[...] = unit
        inverse1[...] = jnp.broadcast_to(inverse, (OWN, LANES))
        value = unit * gain1[...] + shift1[...]
        normed[...] = value
        normed_low[...] = value.astype(LOW)
        normed_t[...] = jnp.transpose(value).astype(LOW)
        c = place[3]
        att_t[pl.ds(pl.multiple_of(c * HALF, HALF), HALF), :] = jnp.transpose(
            att_own[...].astype(FLOAT)
        ).astype(LOW)
        att_t[pl.ds(pl.multiple_of((1 - c) * HALF, HALF), HALF), :] = jnp.transpose(
            att_other[...].astype(FLOAT)
        ).astype(LOW)
        feed[...] = jnp.zeros_like(feed)

    inner = dot(normed_low[...], up[...]) + up_bias[...]
    below = 0.5 + 0.5 * lax.erf(inner * math.sqrt(0.5))
    density = jnp.exp(inner * inner * -0.5) * (1.0 / math.sqrt(2.0 * math.pi))
    activated = inner * below
    slope[...] = (below + inner * density).astype(LOW)
    low = activated.astype(LOW)
    act_t[...] = jnp.transpose(activated).astype(LOW)
    feed[...] += dot(low, down[...])

    @pl.when(step == pl.num_programs(0) - 1)
    def _():
        unit, inverse = centred_norm(normed[...] + feed[...] + down_bias[...])
        result = (unit * gain2[...] + shift2[...]).astype(LOW)
        out0[...] = result[0:BLOCK]
        out1[...] = result[BLOCK:OWN]
        cotangent = jnp.concatenate([cot0[...], cot1[...]], axis=0).astype(FLOAT)
        grad = norm_back(cotangent * gain2[...], unit, inverse)
        second_grad[...] = grad
        low_grad = grad.astype(LOW)
        feed_grad[...] = low_grad
        sums[...] = jnp.concatenate(
            [
                column_sum(cotangent * unit),
                column_sum(cotangent),
                column_sum(low_grad.astype(FLOAT)),
                jnp.zeros((5, WIDTH), FLOAT),
            ],
            axis=0,
        )


def row_of(vector):
    return vector.reshape(1, vector.shape[0])


def forward(place, att_own, att_other, tokens, cotangents, weights):
    chunk = WIDTH
    steps = FF // chunk
    row = whole((1, WIDTH))
    block = whole((BLOCK, WIDTH))
    return pl.pallas_call(
        forward_kernel,
        grid_spec=pltpu.PrefetchScalarGridSpec(
            num_scalar_prefetch=1,
            grid=(steps,),
            in_specs=[
                whole((OWN, HALF)),
                whole((OWN, HALF)),
                pl.BlockSpec((HALF, WIDTH), lambda i, place: (place[3], 0)),
                pl.BlockSpec((HALF, WIDTH), lambda i, place: (1 - place[3], 0)),
                row, block, block, row, row,
                pl.BlockSpec((WIDTH, chunk), lambda i, place: (0, i)),
                pl.BlockSpec((1, chunk), lambda i, place: (0, i)),
                pl.BlockSpec((chunk, WIDTH), lambda i, place: (i, 0)),
                row, row, row, block, block,
            ],
            out_specs=[
                block, block, whole((OWN, WIDTH)), whole((OWN, WIDTH)),
                pl.BlockSpec((chunk, OWN), lambda i, place: (i, 0)),
                pl.BlockSpec((OWN, chunk), lambda i, place: (0, i)),
                whole((OWN, WIDTH)), whole((OWN, LANES)), whole((WIDTH, OWN)), whole((WIDTH, OWN)),
                whole((8, WIDTH)),
            ],
            scratch_shapes=[
                pltpu.VMEM((OWN, WIDTH), FLOAT),
                pltpu.VMEM((OWN, WIDTH), LOW),
                pltpu.VMEM((OWN, WIDTH), FLOAT),
            ],
        ),
        out_shape=[
            shaped((BLOCK, WIDTH), LOW),
            shaped((BLOCK, WIDTH), LOW),
            shaped((OWN, WIDTH), LOW),
            shaped((OWN, WIDTH), FLOAT),
            shaped((FF, OWN), LOW),
            shaped((OWN, FF), LOW),
            shaped((OWN, WIDTH), FLOAT),
            shaped((OWN, LANES), FLOAT),
            shaped((WIDTH, OWN), LOW),
            shaped((WIDTH, OWN), LOW),
            shaped((8, WIDTH), FLOAT),
        ],
        compiler_params=kernel_params(40),
        cost_estimate=cost(2.7e9, 20e6, 2e6),
        name="forward",
    )(
        place, att_own, att_other, weights["out"], weights["out"], row_of(weights["out_bias"]), *tokens,
        row_of(weights["gain1"]), row_of(weights["shift1"]), weights["up"], row_of(weights["up_bias"]),
        weights["down"], row_of(weights["down_bias"]), row_of(weights["gain2"]),
        row_of(weights["shift2"]), *cotangents,
    )


def down_kernel(place, act_t, feed_grad, out):
    for x in range(2):
        out[x] = dot(act_t[0, x, 0], feed_grad[...]).astype(LOW)


def down_units(place, act_t, feed_grad, kept):
    return pl.pallas_call(
        down_kernel,
        grid_spec=pltpu.PrefetchScalarGridSpec(
            num_scalar_prefetch=1,
            grid=(8,),
            in_specs=[
                pl.BlockSpec(
                    (1, 2, 1, DOWN_ROWS, OWN),
                    lambda i, place: (i, 0, place[3] if kept else 1 - place[3], 0, 0),
                ),
                whole((OWN, WIDTH)),
            ],
            out_specs=pl.BlockSpec((2, DOWN_ROWS, WIDTH), lambda i, place: (i, 0, 0)),
        ),
        out_shape=shaped((16, DOWN_ROWS, WIDTH), LOW),
        compiler_params=kernel_params(16),
        cost_estimate=cost(0.6e9, 3.5e6),
        name="down_units",
    )(place, act_t.reshape(8, 2, 2, DOWN_ROWS, OWN), feed_grad)


def backward_kernel(
    place, feed_grad, slope, up, down, second_grad, unit1, inverse1, gain1, wo_own, wo_other,
    inner_grad, first_grad, branch_grad, back_own, back_send, sums,
    normed_grad,
):
    step = pl.program_id(0)

    @pl.when(step == 0)
    def _():
        normed_grad[...] = second_grad[...]
        sums[...] = jnp.zeros_like(sums)

    grad = (dot_nt(feed_grad[...], down[...]) * slope[...].astype(FLOAT)).astype(LOW)
    inner_grad[...] = grad
    sums[pl.ds(4 + step, 1), :] = column_sum(grad.astype(FLOAT))
    normed_grad[...] += dot_nt(grad, up[...])

    @pl.when(step == pl.num_programs(0) - 1)
    def _():
        total = normed_grad[...]
        unit = unit1[...]
        sums[0:1, :] = column_sum(total * unit)
        sums[1:2, :] = column_sum(total)
        grad1 = norm_back(total * gain1[...], unit, inverse1[:, 0:1])
        first_grad[...] = grad1
        low = grad1.astype(LOW)
        branch_grad[...] = low
        sums[2:3, :] = column_sum(low.astype(FLOAT))
        back_own[...] = dot_nt(low, wo_own[...]).astype(LOW)
        back_send[...] = dot_nt(low, wo_other[...]).astype(LOW)


def backward(place, feed_grad, slope, second_grad, unit1, inverse1, weights):
    chunk = WIDTH
    steps = FF // chunk
    return pl.pallas_call(
        backward_kernel,
        grid_spec=pltpu.PrefetchScalarGridSpec(
            num_scalar_prefetch=1,
            grid=(steps,),
            in_specs=[
                whole((OWN, WIDTH)),
                pl.BlockSpec((OWN, chunk), lambda i, place: (0, i)),
                pl.BlockSpec((WIDTH, chunk), lambda i, place: (0, i)),
                pl.BlockSpec((chunk, WIDTH), lambda i, place: (i, 0)),
                whole((OWN, WIDTH)), whole((OWN, WIDTH)), whole((OWN, LANES)), whole((1, WIDTH)),
                pl.BlockSpec((HALF, WIDTH), lambda i, place: (place[3], 0)),
                pl.BlockSpec((HALF, WIDTH), lambda i, place: (1 - place[3], 0)),
            ],
            out_specs=[
                pl.BlockSpec((OWN, chunk), lambda i, place: (0, i)),
                whole((OWN, WIDTH)), whole((OWN, WIDTH)), whole((OWN, HALF)), whole((OWN, HALF)),
                whole((8, WIDTH)),
            ],
            scratch_shapes=[pltpu.VMEM((OWN, WIDTH), FLOAT)],
        ),
        out_shape=[
            shaped((OWN, FF), LOW),
            shaped((OWN, WIDTH), FLOAT),
            shaped((OWN, WIDTH), LOW),
            shaped((OWN, HALF), LOW),
            shaped((OWN, HALF), LOW),
            shaped((8, WIDTH), FLOAT),
        ],
        compiler_params=kernel_params(40),
        cost_estimate=cost(2.7e9, 16e6),
        name="backward",
    )(
        place, feed_grad, slope, weights["up"], weights["down"], second_grad, unit1, inverse1,
        row_of(weights["gain1"]), weights["out"], weights["out"],
    )


def up_kernel(kept, place, normed_t, inner0, inner1, att_t, branch_grad, sums0, sums1, out):
    part = place[3] if kept else 1 - place[3]
    outer = dot(att_t[...], branch_grad[...])
    for x, inner, sums in ((0, inner0, sums0), (1, inner1, sums1)):
        first = outer[x * 48 : x * 48 + 24]
        second = outer[x * 48 + 24 : x * 48 + 48]
        out[x] = jnp.concatenate(
            [dot(normed_t[...], inner[...]), jnp.where(part == 0, first, second), sums[...]], axis=0
        ).astype(LOW)


def up_units(place, normed_t, inner_grad, att_t, branch_grad, sums0, sums1, kept):
    def part(place):
        return place[3] if kept else 1 - place[3]

    return pl.pallas_call(
        functools.partial(up_kernel, kept),
        grid_spec=pltpu.PrefetchScalarGridSpec(
            num_scalar_prefetch=1,
            grid=(8,),
            in_specs=[
                pl.BlockSpec((96, OWN), lambda i, place: (i, 0)),
                pl.BlockSpec((OWN, WIDTH), lambda i, place: (0, part(place))),
                pl.BlockSpec((OWN, WIDTH), lambda i, place: (0, 2 + part(place))),
                pl.BlockSpec((96, OWN), lambda i, place: (i, 0)),
                whole((OWN, WIDTH)), whole((8, WIDTH)), whole((8, WIDTH)),
            ],
            out_specs=pl.BlockSpec((2, UP_ROWS, WIDTH), lambda i, place: (i, 0, 0)),
        ),
        out_shape=shaped((16, UP_ROWS, WIDTH), LOW),
        compiler_params=kernel_params(16),
        cost_estimate=cost(0.9e9, 5e6),
        name="up_units",
    )(place, normed_t, inner_grad, inner_grad, att_t, branch_grad, sums0, sums1)


def attention_back_kernel(
    place, own_lengths, peer_lengths, q, k, v, log_total, att0, att1, back0, back1,
    dq_out, dk_out, dv_out, bias,
):
    bases = first_positions(place)
    ends = pair_ends(place, own_lengths, peer_lengths)
    query_ids = [pairs_along(base, ends, 1)[0:1] for base in bases[:4]]
    for j in range(8):
        key_ids = pairs_along(bases[j], ends, 0)
        for i in range(4):
            bias[pl.ds(j * BLOCK, BLOCK), pl.ds(i * BLOCK, BLOCK)] = jnp.where(
                key_ids == query_ids[i], 0.0, NEGATIVE
            )
    for pair in range(PAIRS_OF_HEADS):
        lanes = pl.ds(pair * LANES, LANES)
        keys = k[:, lanes]
        values = v[:, lanes]
        keys_t = jnp.transpose(keys.astype(FLOAT)).astype(LOW)
        key_grad = jnp.zeros((1024, LANES), FLOAT)
        value_grad = jnp.zeros((1024, LANES), FLOAT)
        left = head_mask(OWN)
        for part, att, back in ((0, att0, back0), (1, att1, back1)):
            rows = pl.ds(part * OWN, OWN)
            queries = q[rows, lanes]
            grads = back[:, lanes]
            zeros = jnp.zeros_like(queries)
            product = jnp.transpose(grads.astype(FLOAT) * att[:, lanes].astype(FLOAT))
            halves = []
            for half in range(2):
                if half == 0:
                    chosen, chosen_grads = jnp.where(left, queries, zeros), jnp.where(left, grads, zeros)
                else:
                    chosen, chosen_grads = jnp.where(left, zeros, queries), jnp.where(left, zeros, grads)
                delta = column_sum(product[half * HEAD_DIM : (half + 1) * HEAD_DIM])
                head = pair * 2 + half
                scores = dot_nt(keys, chosen) + bias[:, rows]
                weights = jnp.exp(scores - log_total[head : head + 1, rows])
                weight_grad = dot_nt(values, chosen_grads)
                score_grad = (weights * (weight_grad - delta)).astype(LOW)
                value_grad = value_grad + dot(weights.astype(LOW), chosen_grads)
                key_grad = key_grad + dot(score_grad, chosen)
                halves.append(dot(keys_t, score_grad))
            query_grad_t = jnp.concatenate([halves[0][0:HEAD_DIM], halves[1][HEAD_DIM:LANES]], axis=0)
            dq_out[rows, lanes] = (jnp.transpose(query_grad_t) * HEAD_DIM**-0.5).astype(LOW)
        dk_out[:, lanes] = key_grad.astype(LOW)
        dv_out[:, lanes] = value_grad.astype(LOW)


def attention_back(place, own_lengths, peer_lengths, q, k, v, log_total, att, back):
    return pl.pallas_call(
        attention_back_kernel,
        grid_spec=pltpu.PrefetchScalarGridSpec(
            num_scalar_prefetch=3,
            grid=(1,),
            in_specs=[whole((512, HALF)), whole((1024, HALF)), whole((1024, HALF)), whole((8, 512))]
            + [whole((OWN, HALF))] * 4,
            out_specs=[whole((512, HALF)), whole((1024, HALF)), whole((1024, HALF))],
            scratch_shapes=[pltpu.VMEM((1024, 512), FLOAT)],
        ),
        out_shape=[shaped((512, HALF), LOW), shaped((1024, HALF), LOW), shaped((1024, HALF), LOW)],
        compiler_params=kernel_params(40),
        cost_estimate=cost(7e9, 6e6, 3e6),
        name="attention_back",
    )(place, own_lengths, peer_lengths, q, k, v, log_total, *att, *back)


def token_kernel(place, dq, dk, dv, wq, wk, wv, send, keep):
    for part in range(4):
        rows = pl.ds(part * OWN, OWN)
        total = dot_nt(dk[rows, :], wk[...]) + dot_nt(dv[rows, :], wv[...])
        if part < 2:
            total = total + dot_nt(dq[rows, :], wq[...])
        target = keep if part % 2 == 0 else send
        target[pl.ds((part // 2) * OWN, OWN), :] = total.astype(LOW)


def token_parts(place, dq, dk, dv, joint_weight):
    def columns(kind):
        return pl.BlockSpec((WIDTH, HALF), lambda i, place: (0, 2 * kind + place[3]))

    return pl.pallas_call(
        token_kernel,
        grid_spec=pltpu.PrefetchScalarGridSpec(
            num_scalar_prefetch=1,
            grid=(1,),
            in_specs=[
                whole((512, HALF)), whole((1024, HALF)), whole((1024, HALF)),
                columns(0), columns(1), columns(2),
            ],
            out_specs=[whole((512, WIDTH)), whole((512, WIDTH))],
        ),
        out_shape=[shaped((512, WIDTH), LOW), shaped((512, WIDTH), LOW)],
        compiler_params=kernel_params(32),
        cost_estimate=cost(1.5e9, 5e6),
        name="token_parts",
    )(place, dq, dk, dv, joint_weight, joint_weight, joint_weight)


def token_pair_kernel(keep, received, first_grad, send, own):
    send[...] = (keep[OWN:, :].astype(FLOAT) + received[OWN:, :].astype(FLOAT)).astype(LOW)
    own[...] = keep[:OWN, :].astype(FLOAT) + received[:OWN, :].astype(FLOAT) + first_grad[...]


def token_pair(keep, received, first_grad):
    return pl.pallas_call(
        token_pair_kernel,
        out_shape=[shaped((OWN, WIDTH), LOW), shaped((OWN, WIDTH), FLOAT)],
        compiler_params=kernel_params(16),
        cost_estimate=cost(1e6, 4e6),
        name="token_pair",
    )(keep, received, first_grad)


def joint_kernel(
    place, t0, t1, t2, t3, t4, t5, t6, t7, dq, dk, dv, px_send, px_keep, qy_send, qy_keep, tokens_t, rows_of
):
    y, x = place[1], place[2]
    for index, block in enumerate((t0, t1, t2, t3, t4, t5, t6, t7)):
        tokens_t[:, pl.ds(index * BLOCK, BLOCK)] = jnp.transpose(block[...].astype(FLOAT)).astype(LOW)
    biases = jnp.concatenate(
        [
            column_sum(dq[...].astype(FLOAT)),
            column_sum(dv[...].astype(FLOAT)),
            jnp.zeros((14, HALF), FLOAT),
        ],
        axis=0,
    )
    for z in range(4):
        for line in range(2):
            rows = pl.ds((z * 2 + line) * 96, 96)
            rows_of[0] = dot(tokens_t[rows, 0:512], dq[...])
            rows_of[1] = dot(tokens_t[rows, :], dk[...])
            rows_of[2] = dot(tokens_t[rows, :], dv[...])
            for side in range(2):
                target = (x + side) % 2
                part = pl.ds(pl.multiple_of(target * 48, 16), 48)
                unit = jnp.concatenate([rows_of[0, part], rows_of[1, part], rows_of[2, part], biases], axis=0)
                unit = unit.astype(LOW)
                px = px_keep if side == 0 else px_send
                px[z, line] = unit[: JOINT_ROWS // 2]

                @pl.when(y == line)
                def _(unit=unit, target=target):
                    qy_keep[z, target] = unit[JOINT_ROWS // 2 :]

                @pl.when(y != line)
                def _(unit=unit, target=target):
                    qy_send[z, target] = unit[JOINT_ROWS // 2 :]


def joint_units(place, blocks, dq, dk, dv):
    out = (4, 2, JOINT_ROWS // 2, HALF)
    return pl.pallas_call(
        joint_kernel,
        grid_spec=pltpu.PrefetchScalarGridSpec(
            num_scalar_prefetch=1,
            grid=(1,),
            in_specs=[whole((BLOCK, WIDTH))] * 8
            + [whole((512, HALF)), whole((1024, HALF)), whole((1024, HALF))],
            out_specs=[whole(out)] * 4,
            scratch_shapes=[pltpu.VMEM((WIDTH, 1024), LOW), pltpu.VMEM((3, 96, HALF), FLOAT)],
        ),
        out_shape=[shaped(out, LOW)] * 4,
        compiler_params=kernel_params(32),
        cost_estimate=cost(1.5e9, 6e6),
        name="joint_units",
    )(place, *blocks, dq, dk, dv)


def added(left, right):
    return (left.astype(FLOAT) + right.astype(FLOAT)).astype(LOW)


def core_stage_kernel(place, kept, received, px_send, px_keep, qy_send, qy_keep):
    y, x = place[1], place[2]
    half = kept.shape[3] // 2
    for line in range(2):
        for target, side in ((px_keep, x), (px_send, 1 - x)):
            target[0, line] = added(kept[0, line, side, 0:half], received[0, line, side, 0:half])
    for side in range(2):
        for target, line in ((qy_keep, y), (qy_send, 1 - y)):
            target[0, side] = added(kept[0, line, side, half:], received[0, line, side, half:])


def core_stage(place, kept, received):
    rows = kept.shape[1]
    block = pl.BlockSpec((1, 2, 2, rows, WIDTH), lambda i, place: (i, 0, 0, 0, 0))
    out = (4, 2, rows // 2, WIDTH)
    shape = (4, 2, 2, rows, WIDTH)
    return pl.pallas_call(
        core_stage_kernel,
        grid_spec=pltpu.PrefetchScalarGridSpec(
            num_scalar_prefetch=1,
            grid=(4,),
            in_specs=[block, block],
            out_specs=[pl.BlockSpec((1,) + out[1:], lambda i, place: (i, 0, 0, 0))] * 4,
        ),
        out_shape=[shaped(out, LOW)] * 4,
        compiler_params=kernel_params(24),
        cost_estimate=cost(2e6, 3 * 2 * 16 * rows * WIDTH),
        name="core_stage",
    )(place, kept.reshape(shape), received.reshape(shape))


def pair_stage_kernel(place, px, px_got, qy, qy_got, p_send, p_keep, q_send, q_keep):
    y, x = place[1], place[2]
    p_keep[0] = added(px[0, y], px_got[0, y])
    p_send[0] = added(px[0, 1 - y], px_got[0, 1 - y])
    q_keep[0] = added(qy[0, x], qy_got[0, x])
    q_send[0] = added(qy[0, 1 - x], qy_got[0, 1 - x])


def pair_stage(place, px, px_got, qy, qy_got):
    _, _, half, width = px.shape
    block = pl.BlockSpec((1, 2, half, width), lambda i, place: (i, 0, 0, 0))
    return pl.pallas_call(
        pair_stage_kernel,
        grid_spec=pltpu.PrefetchScalarGridSpec(
            num_scalar_prefetch=1,
            grid=(4,),
            in_specs=[block] * 4,
            out_specs=[pl.BlockSpec((1, half, width), lambda i, place: (i, 0, 0))] * 4,
        ),
        out_shape=[shaped((4, half, width), LOW)] * 4,
        compiler_params=kernel_params(24),
        cost_estimate=cost(1e6, 6 * 2 * 8 * half * width),
        name="pair_stage",
    )(place, px, px_got, qy, qy_got)


def line_stage_kernel(place, p, p_got, q, q_got, keep, one, two, three):
    z = place[0]
    half = p.shape[1]
    low, high = z % 2, z // 2
    flipped = 1 - low
    other = 1 - high
    for target, index in (
        (keep, z),
        (one, 2 * high + flipped),
        (two, 2 * other + low),
        (three, 2 * other + flipped),
    ):
        target[0:half] = added(p[index], p_got[index])
        target[half:] = added(q[index], q_got[index])


def line_stage(place, p, p_got, q, q_got):
    _, half, width = p.shape
    block = whole((4, half, width))
    return pl.pallas_call(
        line_stage_kernel,
        grid_spec=pltpu.PrefetchScalarGridSpec(
            num_scalar_prefetch=1,
            grid=(1,),
            in_specs=[block] * 4,
            out_specs=[whole((2 * half, width))] * 4,
        ),
        out_shape=[shaped((2 * half, width), LOW)] * 4,
        compiler_params=kernel_params(24),
        cost_estimate=cost(1e6, 6 * 2 * 4 * half * width),
        name="line_stage",
    )(place, p, p_got, q, q_got)


def last_sum_kernel(first, second, third, fourth, out):
    total = first[...].astype(FLOAT) + second[...].astype(FLOAT)
    out[...] = (total + (third[...].astype(FLOAT) + fourth[...].astype(FLOAT))).astype(LOW)


def last_sum(parts):
    shape = parts[0].shape
    return pl.pallas_call(
        last_sum_kernel,
        out_shape=shaped(shape, LOW),
        compiler_params=kernel_params(16),
        cost_estimate=cost(1e6, 5 * 2 * shape[0] * shape[1]),
        name="last_sum",
    )(*parts)


def reduce_units(place, px_send, px_keep, qy_send, qy_keep):
    px_got = x_swap(px_send)
    qy_got = y_swap(qy_send)
    p_send, p_keep, q_send, q_keep = pair_stage(place, px_keep, px_got, qy_keep, qy_got)
    p_got = y_swap(p_send)
    q_got = x_swap(q_send)
    keep, one, two, three = line_stage(place, p_keep, p_got, q_keep, q_got)
    unit = last_sum((keep, z_swap(one, 1), z_swap(two, 2), z_swap(three, 3)))
    return lax.all_gather(unit, "rows", axis=0)


def pick_rows(total, rows, place):
    seq = place[0] * 2 + place[1]
    shift = lax.rem(WIDTH - seq * 96, WIDTH)
    return pltpu.roll(total, shift, 1)[rows, 0:96]


def up_out_kernel(place, units, up, out, gain2, shift2, down_bias, gain1, shift1, out_bias, up_bias, sums):
    for q in range(4):
        up[:, pl.ds(q * WIDTH, WIDTH)] = units[q, 0:96, :].astype(FLOAT)
        out[pl.ds(q * 24, 24), :] = units[q, 96:120, :].astype(FLOAT)
    seq = place[0] * 2 + place[1]
    shift = lax.rem(WIDTH - seq * 96, WIDTH)
    head = pltpu.roll(units[0, 112:128, :].astype(FLOAT)[8:16], shift, 1)
    gain2[...] = head[0:1, 0:96]
    shift2[...] = head[1:2, 0:96]
    down_bias[...] = head[2:3, 0:96]
    tail = units[2, 112:128, :].astype(FLOAT)[8:16]
    sums[...] = tail
    turned = pltpu.roll(tail, shift, 1)
    gain1[...] = turned[0:1, 0:96]
    shift1[...] = turned[1:2, 0:96]
    out_bias[...] = turned[2:3, 0:96]
    wide = sums[pl.ds(4 + seq // 2, 1), :]
    up_bias[...] = jnp.where(seq % 2 == 0, wide[:, 0:HALF], wide[:, HALF:])


def up_outputs(place, units):
    small = [whole((1, 96))] * 6 + [whole((1, HALF))]
    results = pl.pallas_call(
        up_out_kernel,
        grid_spec=pltpu.PrefetchScalarGridSpec(
            num_scalar_prefetch=1,
            grid=(1,),
            in_specs=[whole((4, UP_ROWS, WIDTH))],
            out_specs=[whole((96, FF)), whole((96, WIDTH))] + small,
            scratch_shapes=[pltpu.VMEM((8, WIDTH), FLOAT)],
        ),
        out_shape=[shaped((96, FF), FLOAT), shaped((96, WIDTH), FLOAT)]
        + [shaped((1, 96), FLOAT)] * 6
        + [shaped((1, HALF), FLOAT)],
        compiler_params=kernel_params(16),
        cost_estimate=cost(1e6, 3e6),
        name="up_outputs",
    )(place, units)
    return (*results[:2], *(vector.reshape(-1) for vector in results[2:]))


def joint_out_kernel(place, units, joint, query_bias, value_bias, sums):
    for x in range(2):
        for c in range(2):
            unit = units[2 * x + c]
            for kind in range(3):
                joint[pl.ds(x * 48, 48), pl.ds(kind * WIDTH + c * HALF, HALF)] = unit[
                    kind * 48 : kind * 48 + 48
                ].astype(FLOAT)
            if x == 0:
                sums[:, pl.ds(c * HALF, HALF)] = unit[144:160].astype(FLOAT)
    seq = place[0] * 2 + place[1]
    shift = lax.rem(WIDTH - seq * 96, WIDTH)
    turned = pltpu.roll(sums[0:8, :], shift, 1)
    query_bias[...] = turned[0:1, 0:96]
    value_bias[...] = turned[1:2, 0:96]


def joint_outputs(place, units):
    results = pl.pallas_call(
        joint_out_kernel,
        grid_spec=pltpu.PrefetchScalarGridSpec(
            num_scalar_prefetch=1,
            grid=(1,),
            in_specs=[whole((4, JOINT_ROWS, HALF))],
            out_specs=[whole((96, 3 * WIDTH)), whole((1, 96)), whole((1, 96))],
            scratch_shapes=[pltpu.VMEM((16, WIDTH), FLOAT)],
        ),
        out_shape=[shaped((96, 3 * WIDTH), FLOAT), shaped((1, 96), FLOAT), shaped((1, 96), FLOAT)],
        compiler_params=kernel_params(16),
        cost_estimate=cost(1e6, 2e6),
        name="joint_outputs",
    )(place, units)
    return results[0], results[1].reshape(-1), results[2].reshape(-1)


def row_body(
    tokens,
    pair_lengths,
    joint_weight,
    query_bias,
    value_bias,
    out_weight,
    out_bias,
    first_gain,
    first_shift,
    up_weight,
    up_bias,
    down_weight,
    down_bias,
    second_gain,
    second_shift,
    cotangent,
):
    seq, rows = lax.axis_index("seq"), lax.axis_index("rows")
    z, y, x, c = seq // 2, seq % 2, rows // 2, rows % 2
    place = jnp.stack([z, y, x, c]).astype(jnp.int32)
    odd = z % 2
    weights = {
        "out": out_weight, "out_bias": out_bias, "gain1": first_gain, "shift1": first_shift,
        "up": up_weight, "up_bias": up_bias, "down": down_weight, "down_bias": down_bias,
        "gain2": second_gain, "shift2": second_shift,
    }

    def local_row(array, index):
        return lax.dynamic_index_in_dim(array, index, 0, keepdims=False)

    own = [row_swap(local_row(tokens, odd), 0), row_swap(local_row(tokens, 1 - odd), 1)]
    peer_lengths = core_swap(pair_lengths)
    across = [y_swap(block) for block in own]
    blocks = (
        own + [core_swap(block) for block in own] + across + [core_swap(block) for block in across]
    )
    cotangent, _ = lax.optimization_barrier((cotangent, across[0]))
    cotangents = [row_swap(local_row(cotangent, odd), 0), row_swap(local_row(cotangent, 1 - odd), 1)]

    att_own, att_send, q, k, v, log_total = attention(
        place, pair_lengths, peer_lengths, blocks, joint_weight, query_bias, value_bias
    )
    att_other = core_swap(att_send)
    out0, out1, feed_grad, second_grad, act_t, slope, unit1, inverse1, normed_t, att_t, sums0 = forward(
        place, att_own, att_other, own, cotangents, weights
    )
    down_sent = core_swap(down_units(place, act_t, feed_grad, False))
    down_kept = down_units(place, act_t, feed_grad, True)
    down_gathered = reduce_units(place, *core_stage(place, down_kept, down_sent))
    inner_grad, first_grad, branch_grad, back_own, back_send, sums1 = backward(
        place, feed_grad, slope, second_grad, unit1, inverse1, weights
    )
    back_other = core_swap(back_send)
    up_args = (place, normed_t, inner_grad, att_t, branch_grad, sums0, sums1)
    up_sent = core_swap(up_units(*up_args, False))
    up_kept = up_units(*up_args, True)
    up_gathered = reduce_units(place, *core_stage(place, up_kept, up_sent))

    dq, dk, dv = attention_back(
        place, pair_lengths, peer_lengths, q, k, v, log_total, (att_own, att_send), (back_own, back_other)
    )
    token_send, token_keep = token_parts(place, dq, dk, dv, joint_weight)
    token_got = core_swap(token_send)
    joint_gathered = reduce_units(place, *joint_units(place, blocks, dq, dk, dv))
    token_across, token_own = token_pair(token_keep, token_got, first_grad)
    token_low = (token_own + y_swap(token_across).astype(FLOAT)).astype(LOW)
    back0 = row_swap(token_low[:BLOCK], 0)
    back1 = row_swap(token_low[BLOCK:], 1)
    first, second = jnp.where(odd == 0, back0, back1), jnp.where(odd == 0, back1, back0)
    token_grad = jnp.stack([first, second]).astype(FLOAT)
    done0, done1 = row_swap(out0, 0), row_swap(out1, 1)
    outputs = jnp.stack([jnp.where(odd == 0, done0, done1), jnp.where(odd == 0, done1, done0)])

    down_grad = down_gathered.reshape(4 * DOWN_ROWS, WIDTH).astype(FLOAT)
    (
        up_grad, out_grad, second_gain_grad, second_shift_grad, down_bias_grad, first_gain_grad,
        first_shift_grad, out_bias_grad, up_bias_grad,
    ) = up_outputs(place, up_gathered)
    joint_grad, query_bias_grad, value_bias_grad = joint_outputs(place, joint_gathered)
    return (
        outputs,
        token_grad,
        joint_grad,
        query_bias_grad,
        value_bias_grad,
        out_grad,
        out_bias_grad,
        first_gain_grad,
        first_shift_grad,
        up_grad,
        up_bias_grad,
        down_grad,
        down_bias_grad,
        second_gain_grad,
        second_shift_grad,
    )


def body(tokens, *others):
    if (lax.axis_size("seq"), lax.axis_size("rows")) == (8, 4) and tokens.shape == (2, BLOCK, WIDTH):
        return row_body(tokens, *others)
    return general_body(tokens, *others)


def solution(mesh):
    placed = (
        P("rows", "seq", None),
        P("rows", None),
        P(),
        P(),
        P(),
        P(),
        P(),
        P(),
        P(),
        P(),
        P(),
        P(),
        P(),
        P(),
        P(),
        P("rows", "seq", None),
    )
    return jax.shard_map(
        body,
        mesh=mesh,
        in_specs=placed,
        out_specs=(
            P("rows", "seq", None),
            P("rows", "seq", None),
            P("seq", None),
            P("seq"),
            P("seq"),
            P("seq", None),
            P("seq"),
            P("seq"),
            P("seq"),
            P("seq", None),
            P("seq"),
            P("seq", None),
            P("seq"),
            P("seq"),
            P("seq"),
        ),
        check_vma=False,
    )
```

```python
import functools
import math

import jax
import jax.numpy as jnp
from jax import lax
from jax.experimental import pallas as pl
from jax.experimental.pallas import tpu as pltpu
from jax.sharding import PartitionSpec as P

HEADS = 12
HEAD_DIM = 64


NEGATIVE = -1e30
EPSILON = 1e-12


def from_behind(value, axis, steps):
    count = lax.axis_size(axis)
    pairs = [(source, (source + steps) % count) for source in range(count)]
    return lax.ppermute(value, axis, pairs)


def layer_norm(value, gain, shift):
    mean = jnp.mean(value, axis=-1, keepdims=True)
    centred = value - mean
    spread = jnp.mean(centred * centred, axis=-1, keepdims=True)
    return centred * lax.rsqrt(spread + EPSILON) * gain + shift


def gelu_exact(value):
    return jax.nn.gelu(value, approximate=False)


def pair_index(positions, ends):
    return jnp.sum((positions[None, :, None] >= ends[:, None, :]).astype(jnp.int32), axis=2)


def split_heads(array):
    return array.reshape(array.shape[0], array.shape[1], HEADS, HEAD_DIM)


def online_block(state, query_heads, query_pairs, key_block, value_block, key_pairs):
    highest, total, summed = state
    scores = jnp.einsum(
        "rqhd,rkhd->rhqk", query_heads, split_heads(key_block), preferred_element_type=jnp.float32
    ) * HEAD_DIM ** (-0.5)
    allowed = query_pairs[:, None, :, None] == key_pairs[:, None, None, :]
    masked = jnp.where(allowed, scores, NEGATIVE)
    new_high = jnp.maximum(highest, jnp.max(masked, axis=3))
    weights = jnp.where(allowed, jnp.exp(masked - new_high[..., None]), 0.0)
    factor = jnp.exp(highest - new_high)
    total = total * factor + jnp.sum(weights, axis=3)
    summed = summed * jnp.swapaxes(factor, 1, 2)[..., None] + jnp.einsum(
        "rhqk,rkhd->rqhd",
        weights.astype(jnp.bfloat16),
        split_heads(value_block),
        preferred_element_type=jnp.float32,
    )
    return (new_high, total, summed)


def tile_terms(queries, out_grad, log_total, delta, query_pairs, keys, values, key_pairs):
    scale = HEAD_DIM ** (-0.5)
    query_heads = split_heads(queries)
    grad_heads = split_heads(out_grad)
    key_heads = split_heads(keys)
    value_heads = split_heads(values)
    scores = (
        jnp.einsum("rqhd,rkhd->rhqk", query_heads, key_heads, preferred_element_type=jnp.float32)
        * scale
    )
    allowed = query_pairs[:, None, :, None] == key_pairs[:, None, None, :]
    weights = jnp.where(
        allowed, jnp.exp(jnp.where(allowed, scores, NEGATIVE) - log_total[..., None]), 0.0
    )
    weight_grad = jnp.einsum(
        "rqhd,rkhd->rhqk", grad_heads, value_heads, preferred_element_type=jnp.float32
    )
    score_grad = (weights * (weight_grad - delta[..., None])).astype(jnp.bfloat16)
    query_term = (
        jnp.einsum("rhqk,rkhd->rqhd", score_grad, key_heads, preferred_element_type=jnp.float32)
        * scale
    )
    key_term = (
        jnp.einsum("rhqk,rqhd->rkhd", score_grad, query_heads, preferred_element_type=jnp.float32)
        * scale
    )
    value_term = jnp.einsum(
        "rhqk,rqhd->rkhd",
        weights.astype(jnp.bfloat16),
        grad_heads,
        preferred_element_type=jnp.float32,
    )
    return (
        query_term.reshape(queries.shape),
        key_term.reshape(keys.shape),
        value_term.reshape(values.shape),
    )


def general_body(
    tokens,
    pair_lengths,
    joint_weight,
    query_bias,
    value_bias,
    out_weight,
    out_bias,
    first_gain,
    first_shift,
    up_weight,
    up_bias,
    down_weight,
    down_bias,
    second_gain,
    second_shift,
    cotangent,
):
    rows_here, seq_here, width = tokens.shape
    count = lax.axis_size("seq")
    cycle_index = lax.axis_index("seq")
    ends = jnp.cumsum(pair_lengths, axis=1)
    offsets = jnp.arange(seq_here, dtype=jnp.int32)
    own_pairs = pair_index(cycle_index * seq_here + offsets, ends)
    block_shape = (rows_here, seq_here, width)
    flat = tokens.reshape(rows_here * seq_here, width)
    projected = jnp.dot(flat, joint_weight, preferred_element_type=jnp.float32)
    queries = (projected[:, :width] + query_bias).astype(jnp.bfloat16).reshape(block_shape)
    keys = projected[:, width : 2 * width].astype(jnp.bfloat16).reshape(block_shape)
    values = (projected[:, 2 * width :] + value_bias).astype(jnp.bfloat16).reshape(block_shape)
    query_heads = split_heads(queries)
    initial = (
        jnp.full((rows_here, HEADS, seq_here), NEGATIVE, jnp.float32),
        jnp.zeros((rows_here, HEADS, seq_here), jnp.float32),
        jnp.zeros((rows_here, seq_here, HEADS, HEAD_DIM), jnp.float32),
    )
    key_piece = lax.all_gather(keys, "seq", axis=1, tiled=True)
    value_piece = lax.all_gather(values, "seq", axis=1, tiled=True)
    length = key_piece.shape[1]
    block = math.gcd(length, seq_here)

    def one_block(index, inner_state):
        first = index * block
        key_block = lax.dynamic_slice_in_dim(key_piece, first, block, 1)
        value_block = lax.dynamic_slice_in_dim(value_piece, first, block, 1)
        key_pairs = pair_index(first + jnp.arange(block, dtype=jnp.int32), ends)
        return online_block(inner_state, query_heads, own_pairs, key_block, value_block, key_pairs)

    highest, total, summed = lax.fori_loop(0, length // block, one_block, initial)
    log_total = highest + jnp.log(total)
    attended = (
        (summed / jnp.swapaxes(total, 1, 2)[..., None]).astype(jnp.bfloat16).reshape(flat.shape)
    )
    branch = jnp.dot(attended, out_weight, preferred_element_type=jnp.float32) + out_bias
    first_sum = flat.astype(jnp.float32) + branch
    normed, first_back = jax.vjp(layer_norm, first_sum, first_gain, first_shift)
    normed_low = normed.astype(jnp.bfloat16)
    inner = jnp.dot(normed_low, up_weight, preferred_element_type=jnp.float32) + up_bias
    activated_full, gelu_back = jax.vjp(gelu_exact, inner)
    activated = activated_full.astype(jnp.bfloat16)
    feed = jnp.dot(activated, down_weight, preferred_element_type=jnp.float32) + down_bias
    second_sum = normed + feed
    result, second_back = jax.vjp(layer_norm, second_sum, second_gain, second_shift)
    outputs = result.astype(jnp.bfloat16).reshape(tokens.shape)
    second_grad, second_gain_grad, second_shift_grad = second_back(
        cotangent.astype(jnp.float32).reshape(flat.shape)
    )
    feed_grad = second_grad.astype(jnp.bfloat16)
    down_grad = jnp.einsum("ti,tj->ij", activated, feed_grad, preferred_element_type=jnp.float32)
    down_bias_grad = jnp.sum(feed_grad.astype(jnp.float32), axis=0)
    activated_grad = jnp.einsum(
        "tj,ij->ti", feed_grad, down_weight, preferred_element_type=jnp.float32
    )
    inner_grad = gelu_back(activated_grad)[0].astype(jnp.bfloat16)
    up_grad = jnp.einsum("ti,tj->ij", normed_low, inner_grad, preferred_element_type=jnp.float32)
    up_bias_grad = jnp.sum(inner_grad.astype(jnp.float32), axis=0)
    normed_grad = second_grad + jnp.einsum(
        "tj,ij->ti", inner_grad, up_weight, preferred_element_type=jnp.float32
    )
    first_grad, first_gain_grad, first_shift_grad = first_back(normed_grad)
    branch_grad = first_grad.astype(jnp.bfloat16)
    out_grad = jnp.einsum("ti,tj->ij", attended, branch_grad, preferred_element_type=jnp.float32)
    out_bias_grad = jnp.sum(branch_grad.astype(jnp.float32), axis=0)
    attended_grad = jnp.einsum(
        "tj,ij->ti", branch_grad, out_weight, preferred_element_type=jnp.float32
    ).astype(jnp.bfloat16)
    delta = jnp.sum(
        (attended_grad.astype(jnp.float32) * attended.astype(jnp.float32)).reshape(
            rows_here, seq_here, HEADS, HEAD_DIM
        ),
        axis=3,
    )
    delta = jnp.swapaxes(delta, 1, 2)
    attended_grad = attended_grad.reshape(block_shape)
    zeros_block = jnp.zeros(block_shape, jnp.float32)

    def send_key_sums(sums):
        return (
            from_behind(sums[0].astype(jnp.bfloat16), "seq", 1).astype(jnp.float32),
            from_behind(sums[1].astype(jnp.bfloat16), "seq", 1).astype(jnp.float32),
        )

    def key_work(turn, pair_block, sums, query_sum):
        anchor = (cycle_index - turn) % count
        key_pairs = pair_index(anchor * seq_here + offsets, ends)
        query_term, key_term, value_term = tile_terms(
            queries,
            attended_grad,
            log_total,
            delta,
            own_pairs,
            pair_block[0],
            pair_block[1],
            key_pairs,
        )
        return ((sums[0] + key_term, sums[1] + value_term), query_sum + query_term)

    def key_turn(turn, state):
        pair_block, sums, query_sum = state
        sums, query_sum = key_work(turn, pair_block, sums, query_sum)
        sums = send_key_sums(sums)
        pair_block = from_behind((pair_block[0], pair_block[1]), "seq", 1)
        return (pair_block, sums, query_sum)

    pair_block, sums, query_sum = lax.fori_loop(
        0, count - 1, key_turn, ((keys, values), (zeros_block, zeros_block), zeros_block)
    )
    sums, query_sum = key_work(count - 1, pair_block, sums, query_sum)
    key_sum, value_sum = send_key_sums(sums)
    query_low = query_sum.astype(jnp.bfloat16).reshape(flat.shape)
    key_low = key_sum.astype(jnp.bfloat16).reshape(flat.shape)
    value_low = value_sum.astype(jnp.bfloat16).reshape(flat.shape)
    joint_low = jnp.concatenate([query_low, key_low, value_low], axis=1)
    joint_grad = jnp.einsum("ti,tj->ij", flat, joint_low, preferred_element_type=jnp.float32)
    query_bias_grad = jnp.sum(query_low.astype(jnp.float32), axis=0)
    value_bias_grad = jnp.sum(value_low.astype(jnp.float32), axis=0)
    token_grad = first_grad + jnp.einsum(
        "tj,ij->ti", joint_low, joint_weight, preferred_element_type=jnp.float32
    )
    gradients = (
        joint_grad,
        query_bias_grad,
        value_bias_grad,
        out_grad,
        out_bias_grad,
        first_gain_grad,
        first_shift_grad,
        up_grad,
        up_bias_grad,
        down_grad,
        down_bias_grad,
        second_gain_grad,
        second_shift_grad,
    )
    shares = (
        lax.psum_scatter(
            gradients[0].astype(jnp.bfloat16), "seq", scatter_dimension=0, tiled=True
        ).astype(jnp.float32),
        lax.psum_scatter(
            gradients[1].astype(jnp.bfloat16), "seq", scatter_dimension=0, tiled=True
        ).astype(jnp.float32),
        lax.psum_scatter(
            gradients[2].astype(jnp.bfloat16), "seq", scatter_dimension=0, tiled=True
        ).astype(jnp.float32),
        lax.psum_scatter(
            gradients[3].astype(jnp.bfloat16), "seq", scatter_dimension=0, tiled=True
        ).astype(jnp.float32),
        lax.psum_scatter(
            gradients[4].astype(jnp.bfloat16), "seq", scatter_dimension=0, tiled=True
        ).astype(jnp.float32),
        lax.psum_scatter(
            gradients[5].astype(jnp.bfloat16), "seq", scatter_dimension=0, tiled=True
        ).astype(jnp.float32),
        lax.psum_scatter(
            gradients[6].astype(jnp.bfloat16), "seq", scatter_dimension=0, tiled=True
        ).astype(jnp.float32),
        lax.psum_scatter(
            gradients[7].astype(jnp.bfloat16), "seq", scatter_dimension=0, tiled=True
        ).astype(jnp.float32),
        lax.psum_scatter(
            gradients[8].astype(jnp.bfloat16), "seq", scatter_dimension=0, tiled=True
        ).astype(jnp.float32),
        lax.psum_scatter(
            gradients[9].astype(jnp.bfloat16), "seq", scatter_dimension=0, tiled=True
        ).astype(jnp.float32),
        lax.psum_scatter(
            gradients[10].astype(jnp.bfloat16), "seq", scatter_dimension=0, tiled=True
        ).astype(jnp.float32),
        lax.psum_scatter(
            gradients[11].astype(jnp.bfloat16), "seq", scatter_dimension=0, tiled=True
        ).astype(jnp.float32),
        lax.psum_scatter(
            gradients[12].astype(jnp.bfloat16), "seq", scatter_dimension=0, tiled=True
        ).astype(jnp.float32),
    )
    shares = (
        lax.psum(shares[0].astype(jnp.bfloat16), "rows").astype(jnp.float32),
        lax.psum(shares[1].astype(jnp.bfloat16), "rows").astype(jnp.float32),
        lax.psum(shares[2].astype(jnp.bfloat16), "rows").astype(jnp.float32),
        lax.psum(shares[3].astype(jnp.bfloat16), "rows").astype(jnp.float32),
        lax.psum(shares[4].astype(jnp.bfloat16), "rows").astype(jnp.float32),
        lax.psum(shares[5].astype(jnp.bfloat16), "rows").astype(jnp.float32),
        lax.psum(shares[6].astype(jnp.bfloat16), "rows").astype(jnp.float32),
        lax.psum(shares[7].astype(jnp.bfloat16), "rows").astype(jnp.float32),
        lax.psum(shares[8].astype(jnp.bfloat16), "rows").astype(jnp.float32),
        lax.psum(shares[9].astype(jnp.bfloat16), "rows").astype(jnp.float32),
        lax.psum(shares[10].astype(jnp.bfloat16), "rows").astype(jnp.float32),
        lax.psum(shares[11].astype(jnp.bfloat16), "rows").astype(jnp.float32),
        lax.psum(shares[12].astype(jnp.bfloat16), "rows").astype(jnp.float32),
    )
    return (outputs, token_grad.reshape(tokens.shape)) + tuple(shares)


WIDTH = HEADS * HEAD_DIM
HALF = WIDTH // 2
FF = 4 * WIDTH
BLOCK = 128
OWN = 2 * BLOCK
LANES = 128
PAIRS_OF_HEADS = HALF // LANES
JOINT_ROWS = 80
JOINT_FIRST = 48
JOINT_SECOND = JOINT_ROWS - JOINT_FIRST
UP_ROWS = 128
DOWN_ROWS = 96
EXT = OWN + 16
FLOAT = jnp.float32
LOW = jnp.bfloat16
AXES = ("seq", "rows")


def kernel_params(megabytes):
    return pltpu.CompilerParams(vmem_limit_bytes=megabytes << 20)


def shaped(shape, kind):
    return jax.ShapeDtypeStruct(shape, kind)


def whole(shape):
    return pl.BlockSpec(shape, lambda *_: (0,) * len(shape))


def cost(flops, moved, exps=0):
    return pl.CostEstimate(flops=1024, bytes_accessed=1024, transcendentals=0)


def dot(left, right):
    return lax.dot_general(left, right, (((1,), (0,)), ((), ())), preferred_element_type=FLOAT)


def dot_nt(left, right):
    return lax.dot_general(left, right, (((1,), (1,)), ((), ())), preferred_element_type=FLOAT)


def call(kernel, name, place, inputs, outputs, scratch=(), grid=(1,), scalars=(), after=(), megabytes=40, work=None):
    prefetch = 1 + len(scalars)
    given, made = len(inputs), len(outputs)

    def ordered(*refs):
        first = prefetch + given
        mark = refs[first + len(after) + made]
        mark[...] = jnp.zeros_like(mark)
        kernel(*refs[:first], *refs[first + len(after) : first + len(after) + made], *refs[first + len(after) + made + 1 :])

    results = pl.pallas_call(
        ordered,
        grid_spec=pltpu.PrefetchScalarGridSpec(
            num_scalar_prefetch=prefetch,
            grid=grid,
            in_specs=[spec for _, spec in inputs] + [pl.BlockSpec(memory_space=pl.ANY)] * len(after),
            out_specs=[spec for _, _, spec in outputs] + [whole((8, LANES))],
            scratch_shapes=list(scratch),
        ),
        out_shape=[shaped(shape, kind) for shape, kind, _ in outputs] + [shaped((8, LANES), FLOAT)],
        compiler_params=kernel_params(megabytes),
        cost_estimate=work,
        name=name,
    )(place, *scalars, *[array for array, _ in inputs], *after)
    return results[:-1], results[-1]


def plain(array):
    return array, whole(array.shape)


def made(shape, kind):
    return shape, kind, whole(shape)


def device_at(z, y, x, c):
    return ((z * 2 + y) * 2 + x) * 2 + c


def permute(value, target):
    pairs = []
    for z in range(4):
        for y in range(2):
            for x in range(2):
                for c in range(2):
                    pairs.append((device_at(z, y, x, c), device_at(*target(z, y, x, c))))
    return lax.ppermute(value, AXES, pairs)


def core_swap(value):
    return permute(value, lambda z, y, x, c: (z, y, x, 1 - c))


def x_swap(value):
    return permute(value, lambda z, y, x, c: (z, y, 1 - x, c))


def y_swap(value):
    return permute(value, lambda z, y, x, c: (z, 1 - y, x, c))


def z_swap(value, bits):
    return permute(value, lambda z, y, x, c: (z ^ bits, y, x, c))


def row_swap(value, second):
    return permute(value, lambda z, y, x, c: (2 * c + (z % 2 ^ second), y, x, z // 2))


def first_positions(place):
    z, y, c = place[0], place[1], place[3]
    bases = []
    for core, line in ((c, y), (1 - c, y), (c, 1 - y), (1 - c, 1 - y)):
        for second in (0, 1):
            parity = z % 2
            parity = 1 - parity if second else parity
            bases.append((2 * (2 * core + parity) + line) * BLOCK)
    return bases


def pair_ends(place, own_lengths, peer_lengths):
    z, c = place[0], place[3]
    here = (z // 2) == c
    line = z % 2
    ends, end = [], 0
    for pair in range(own_lengths.shape[1]):
        end = end + jnp.where(here, own_lengths[line, pair], peer_lengths[line, pair])
        ends.append(end)
    return ends


def pairs_along(base, ends, axis):
    shape = (8, BLOCK) if axis == 1 else (BLOCK, LANES)
    position = base + lax.broadcasted_iota(jnp.int32, shape, axis)
    ids = jnp.zeros(shape, jnp.int32)
    for end in ends:
        ids = ids + (position >= end).astype(jnp.int32)
    return ids


def head_mask(rows):
    return lax.broadcasted_iota(jnp.int32, (rows, LANES), 1) < HEAD_DIM


def attention_kernel(
    place, own_lengths, peer_lengths, *refs
):
    blocks = refs[:8]
    wq, wk, wv, qb, vb = refs[8:13]
    att_out, q_out, k_out, v_out, log_out = refs[13:18]
    bias, log_columns = refs[18:]
    bases = first_positions(place)
    ends = pair_ends(place, own_lengths, peer_lengths)
    here = jnp.concatenate([block[...] for block in blocks[:4]], axis=0)
    there = jnp.concatenate([block[...] for block in blocks[4:]], axis=0)
    queries = dot(here, wq[...]) + qb[...]
    q_out[...] = (queries.astype(LOW).astype(FLOAT) * HEAD_DIM**-0.5).astype(LOW)
    for index, tokens in enumerate((here, there)):
        rows = pl.ds(index * 512, 512)
        k_out[rows, :] = dot(tokens, wk[...]).astype(LOW)
        v_out[rows, :] = (dot(tokens, wv[...]) + vb[...]).astype(LOW)
    key_ids = [pairs_along(base, ends, 1)[0:1] for base in bases]
    for i in range(4):
        query_ids = pairs_along(bases[i], ends, 0)
        for j in range(8):
            bias[pl.ds(i * BLOCK, BLOCK), pl.ds(j * BLOCK, BLOCK)] = jnp.where(
                query_ids == key_ids[j], 0.0, NEGATIVE
            )
    log_columns[...] = jnp.zeros_like(log_columns)
    for pair in range(PAIRS_OF_HEADS):
        lanes = pl.ds(pair * LANES, LANES)
        keys = k_out[:, lanes]
        values = v_out[:, lanes]
        ones = jnp.ones_like(values)
        left_keys = head_mask(1024)
        values_of = (jnp.where(left_keys, values, ones), jnp.where(left_keys, ones, values))
        left = head_mask(OWN)
        for part in range(2):
            rows = pl.ds(part * OWN, OWN)
            queries = q_out[rows, lanes]
            zeros = jnp.zeros_like(queries)
            summed = []
            for half in range(2):
                chosen = jnp.where(left, queries, zeros) if half == 0 else jnp.where(left, zeros, queries)
                scores = dot_nt(chosen, keys) + bias[rows, :]
                highest = jnp.max(scores, axis=1, keepdims=True)
                weights = jnp.exp(scores - highest).astype(LOW)
                total = dot(weights, values_of[half])
                turned = pltpu.roll(total, HEAD_DIM, 1)
                summed.append(total / turned)
                sums = total if half == 1 else turned
                log_total = highest + jnp.log(sums)
                column = lax.broadcasted_iota(jnp.int32, (OWN, LANES), 1) == pair * 2 + half
                at = log_total if pair * 2 + half < HEAD_DIM else None
                log_columns[rows, :] = jnp.where(column, at, log_columns[rows, :])
            attended = jnp.where(left, summed[0], summed[1]).astype(LOW)
            att_out[rows, lanes] = attended
    log_out[...] = jnp.transpose(log_columns[...])[0:8, :]


def attention(place, lengths, blocks, joint_weight, query_bias, value_bias, after=()):
    def columns(kind):
        return joint_weight, pl.BlockSpec((WIDTH, HALF), lambda i, place, *_: (0, 2 * kind + place[3]))

    half_row = pl.BlockSpec((1, HALF), lambda i, place, *_: (0, place[3]))
    return call(
        attention_kernel,
        "attention",
        place,
        [plain(block) for block in blocks]
        + [columns(0), columns(1), columns(2), (row_of(query_bias), half_row), (row_of(value_bias), half_row)],
        [
            made((512, HALF), LOW), made((512, HALF), LOW), made((1024, HALF), LOW), made((1024, HALF), LOW),
            made((8, 512), FLOAT),
        ],
        scratch=[pltpu.VMEM((512, 1024), FLOAT), pltpu.VMEM((512, LANES), FLOAT)],
        scalars=lengths,
        after=after,
        work=cost(4e9, 8e6, 3e6),
    )


def centred_norm(value):
    mean = jnp.mean(value, axis=-1, keepdims=True)
    centred = value - mean
    spread = jnp.mean(centred * centred, axis=-1, keepdims=True)
    inverse = lax.rsqrt(spread + EPSILON)
    return centred * inverse, inverse


def norm_back(grad, unit, inverse):
    mean = jnp.mean(grad, axis=-1, keepdims=True)
    along = jnp.mean(grad * unit, axis=-1, keepdims=True)
    return (grad - mean - unit * along) * inverse


def column_sum(value):
    return jnp.sum(value, axis=0, keepdims=True)


def forward_kernel(
    place, att, att_got, wo_own, wo_other, out_bias, x0, x1, gain1, shift1, up, up_bias, down,
    down_bias, gain2, shift2, cot0, cot1,
    result0, result1, feed_ext, second_grad, act_keep, act_send, slope, unit1, inverse1, normed_low, normed_t, att_t, sums,
    normed, feed, act_t,
):
    step = pl.program_id(0)
    c = place[3]

    @pl.when(step == 0)
    def _():
        tokens = jnp.concatenate([x0[...], x1[...]], axis=0).astype(FLOAT)
        att_own, att_other = att[0:OWN], att_got[OWN:]
        branch = dot(att_own, wo_own[...]) + dot(att_other, wo_other[...]) + out_bias[...]
        unit, inverse = centred_norm(tokens + branch)
        unit1[...] = unit
        inverse1[...] = jnp.broadcast_to(inverse, (OWN, LANES))
        value = unit * gain1[...] + shift1[...]
        normed[...] = value
        normed_low[...] = value.astype(LOW)
        normed_t[...] = jnp.transpose(value).astype(LOW)
        mine = pl.ds(pl.multiple_of(c * HALF, HALF), HALF)
        other = pl.ds(pl.multiple_of((1 - c) * HALF, HALF), HALF)
        att_t[mine, :] = jnp.transpose(att[...].astype(FLOAT)).astype(LOW)
        att_t[other, 0:OWN] = jnp.transpose(att_other.astype(FLOAT)).astype(LOW)
        att_t[other, OWN:] = jnp.transpose(att_got[0:OWN].astype(FLOAT)).astype(LOW)
        feed[...] = jnp.zeros_like(feed)

    inner = dot(normed_low[...], up[...]) + up_bias[...]
    below = 0.5 + 0.5 * lax.erf(inner * math.sqrt(0.5))
    density = jnp.exp(inner * inner * -0.5) * (1.0 / math.sqrt(2.0 * math.pi))
    activated = inner * below
    slope[...] = (below + inner * density).astype(LOW)
    low = activated.astype(LOW)
    act_t[...] = jnp.transpose(activated).astype(LOW).reshape(4, 2, DOWN_ROWS, OWN)
    act_keep[...] = act_t[:, c]
    act_send[...] = act_t[:, 1 - c]
    feed[...] += dot(low, down[...])

    @pl.when(step == pl.num_programs(0) - 1)
    def _():
        unit, inverse = centred_norm(normed[...] + feed[...] + down_bias[...])
        result = (unit * gain2[...] + shift2[...]).astype(LOW)
        result0[...] = result[0:BLOCK]
        result1[...] = result[BLOCK:]
        cotangent = jnp.concatenate([cot0[...], cot1[...]], axis=0).astype(FLOAT)
        grad = norm_back(cotangent * gain2[...], unit, inverse)
        second_grad[...] = grad
        low_grad = grad.astype(LOW)
        rows = jnp.concatenate(
            [
                column_sum(cotangent * unit),
                column_sum(cotangent),
                column_sum(low_grad.astype(FLOAT)),
                jnp.zeros((5, WIDTH), FLOAT),
            ],
            axis=0,
        )
        sums[...] = rows
        feed_ext[0:OWN] = low_grad
        feed_ext[OWN:] = jnp.concatenate([rows, jnp.zeros_like(rows)], axis=0).astype(LOW)


def row_of(vector):
    return vector.reshape(1, vector.shape[0])


def forward(place, att, att_got, tokens, cotangents, weights, after=()):
    chunk = WIDTH

    def vector(name):
        return plain(row_of(weights[name]))

    units = ((16, DOWN_ROWS, OWN), LOW, pl.BlockSpec((4, DOWN_ROWS, OWN), lambda i, place: (i, 0, 0)))
    return call(
        forward_kernel,
        "forward",
        place,
        [
            plain(att),
            plain(att_got),
            (weights["out"], pl.BlockSpec((HALF, WIDTH), lambda i, place: (place[3], 0))),
            (weights["out"], pl.BlockSpec((HALF, WIDTH), lambda i, place: (1 - place[3], 0))),
            vector("out_bias"), plain(tokens[0]), plain(tokens[1]), vector("gain1"), vector("shift1"),
            (weights["up"], pl.BlockSpec((WIDTH, chunk), lambda i, place: (0, i))),
            (row_of(weights["up_bias"]), pl.BlockSpec((1, chunk), lambda i, place: (0, i))),
            (weights["down"], pl.BlockSpec((chunk, WIDTH), lambda i, place: (i, 0))),
            vector("down_bias"), vector("gain2"), vector("shift2"), plain(cotangents[0]), plain(cotangents[1]),
        ],
        [
            made((BLOCK, WIDTH), LOW), made((BLOCK, WIDTH), LOW), made((EXT, WIDTH), LOW),
            made((OWN, WIDTH), FLOAT), units, units,
            ((OWN, FF), LOW, pl.BlockSpec((OWN, chunk), lambda i, place: (0, i))),
            made((OWN, WIDTH), FLOAT), made((OWN, LANES), FLOAT), made((OWN, WIDTH), LOW),
            made((WIDTH, OWN), LOW), made((WIDTH, 512), LOW), made((8, WIDTH), FLOAT),
        ],
        scratch=[
            pltpu.VMEM((OWN, WIDTH), FLOAT),
            pltpu.VMEM((OWN, WIDTH), FLOAT),
            pltpu.VMEM((4, 2, DOWN_ROWS, OWN), LOW),
        ],
        grid=(FF // chunk,),
        after=after,
        work=cost(2.7e9, 20e6, 2e6),
    )


def split_units(place, units, px_send, px, qy_send, qy):
    y, x = place[1], place[2]
    half = units.shape[2] // 2
    for line in range(2):
        px[0, line] = units[line, x, 0:half]
        px_send[0, line] = units[line, 1 - x, 0:half]
    for side in range(2):
        qy[0, side] = units[y, side, half:]
        qy_send[0, side] = units[1 - y, side, half:]


def unit_outputs(rows, width):
    shape = (4, 2, rows // 2, width)
    return [(shape, LOW, pl.BlockSpec((1,) + shape[1:], lambda i, place: (i, 0, 0, 0)))] * 4


def down_kernel(place, act, act_got, feed, feed_got, px_send, px, qy_send, qy, units):
    shape = (4 * DOWN_ROWS, OWN)
    total = dot(act[...].reshape(shape), feed[0:OWN]) + dot(act_got[...].reshape(shape), feed_got[0:OWN])
    units[...] = total.astype(LOW).reshape(units.shape)
    split_units(place, units, px_send, px, qy_send, qy)


def down_units(place, act, act_got, feed, feed_got, after=()):
    block = pl.BlockSpec((4, DOWN_ROWS, OWN), lambda i, place: (i, 0, 0))
    return call(
        down_kernel,
        "down_units",
        place,
        [(act, block), (act_got, block), plain(feed), plain(feed_got)],
        unit_outputs(DOWN_ROWS, WIDTH),
        scratch=[pltpu.VMEM((2, 2, DOWN_ROWS, WIDTH), LOW)],
        grid=(4,),
        after=after,
        work=cost(0.6e9, 3.5e6),
    )


def backward_kernel(
    place, feed_ext, slope, up, down, second_grad, unit1, inverse1, gain1, wo_own, wo_other,
    inner0, inner1, send0, send1, first_grad, branch_own, back_own, misc, sums,
    normed_grad, branch,
):
    step = pl.program_id(0)
    c = place[3]

    @pl.when(step == 0)
    def _():
        normed_grad[...] = second_grad[...]
        sums[...] = jnp.zeros_like(sums)

    grad = (dot_nt(feed_ext[0:OWN], down[...]) * slope[...].astype(FLOAT)).astype(LOW)
    for target, index in ((inner0, c), (inner1, 2 + c), (send0, 1 - c), (send1, 3 - c)):

        @pl.when(step == index)
        def _(target=target):
            target[...] = grad

    sums[pl.ds(4 + step, 1), :] = column_sum(grad.astype(FLOAT))
    normed_grad[...] += dot_nt(grad, up[...])

    @pl.when(step == pl.num_programs(0) - 1)
    def _():
        total = normed_grad[...]
        unit = unit1[...]
        sums[0:1, :] = column_sum(total * unit)
        sums[1:2, :] = column_sum(total)
        grad1 = norm_back(total * gain1[...], unit, inverse1[:, 0:1])
        first_grad[...] = grad1
        low = grad1.astype(LOW)
        branch[...] = low
        sums[2:3, :] = column_sum(low.astype(FLOAT))
        branch_own[...] = branch[:, pl.ds(pl.multiple_of(c * HALF, LANES), HALF)]
        back_own[...] = dot_nt(low, wo_own[...]).astype(LOW)
        misc[0:OWN, 0:HALF] = branch[:, pl.ds(pl.multiple_of((1 - c) * HALF, LANES), HALF)]
        misc[0:OWN, HALF:] = dot_nt(low, wo_other[...]).astype(LOW)
        rows = sums[...]
        misc[OWN:] = jnp.concatenate([rows, jnp.zeros_like(rows)], axis=0).astype(LOW)


def backward(place, feed_ext, slope, second_grad, unit1, inverse1, weights, after=()):
    chunk = WIDTH
    return call(
        backward_kernel,
        "backward",
        place,
        [
            plain(feed_ext),
            (slope, pl.BlockSpec((OWN, chunk), lambda i, place: (0, i))),
            (weights["up"], pl.BlockSpec((WIDTH, chunk), lambda i, place: (0, i))),
            (weights["down"], pl.BlockSpec((chunk, WIDTH), lambda i, place: (i, 0))),
            plain(second_grad), plain(unit1), plain(inverse1), plain(row_of(weights["gain1"])),
            (weights["out"], pl.BlockSpec((HALF, WIDTH), lambda i, place: (place[3], 0))),
            (weights["out"], pl.BlockSpec((HALF, WIDTH), lambda i, place: (1 - place[3], 0))),
        ],
        [made((OWN, WIDTH), LOW)] * 4
        + [
            made((OWN, WIDTH), FLOAT), made((OWN, HALF), LOW), made((OWN, HALF), LOW), made((EXT, WIDTH), LOW),
            made((8, WIDTH), FLOAT),
        ],
        scratch=[pltpu.VMEM((OWN, WIDTH), FLOAT), pltpu.VMEM((OWN, WIDTH), LOW)],
        grid=(FF // chunk,),
        after=after,
        work=cost(2.7e9, 16e6),
    )


def up_kernel(
    place, normed_t, normed_got, inner0, inner1, got0, got1, att_t, branch, misc, sums0, sums1, feed_got,
    down_px, down_px_got, down_qy, down_qy_got,
    x_send, y_send, px, qy, down_p, down_q, units, normed_got_t,
):
    z = pl.program_id(0)
    y, x = place[1], place[2]

    @pl.when(z == 0)
    def _():
        normed_got_t[...] = jnp.transpose(normed_got[...].astype(FLOAT)).astype(LOW)

    theirs = normed_got_t[pl.ds(pl.multiple_of(z * 192, 32), 192), :]
    outer = dot(att_t[:, 0:OWN], branch[...]) + dot(att_t[:, OWN:], misc[0:OWN, 0:HALF])
    for side, inner, got, sums, pair in ((0, inner0, got0, sums0, feed_got), (1, inner1, got1, sums1, misc)):
        grad = dot(normed_t[...], inner[...]) + dot(theirs, got[...])
        vectors = sums[...] + pair[OWN:].astype(FLOAT)[0:8]
        for line in range(2):
            first = line * 96 + side * 48
            rest = jnp.concatenate([outer[first : first + 24], outer[first + 24 : first + 48]], axis=1)
            units[line, side] = jnp.concatenate(
                [grad[line * 96 : line * 96 + 96], rest, vectors], axis=0
            ).astype(LOW)
    half = UP_ROWS // 2
    for line in range(2):
        px[0, line] = units[line, x, 0:half]
        x_send[0, line * half : line * half + half] = units[line, 1 - x, 0:half]
    for side in range(2):
        qy[0, side] = units[y, side, half:]
        y_send[0, side * half : side * half + half] = units[1 - y, side, half:]
    down_p[0] = added(down_px[0, y], down_px_got[0, y])
    y_send[0, 2 * half :] = added(down_px[0, 1 - y], down_px_got[0, 1 - y])
    down_q[0] = added(down_qy[0, x], down_qy_got[0, x])
    x_send[0, 2 * half :] = added(down_qy[0, 1 - x], down_qy_got[0, 1 - x])


def up_units(
    place, normed_t, normed_got, inner, got, att_t, branch, misc, sums0, sums1, feed_got, down_pair, after=()
):
    rows = pl.BlockSpec((192, OWN), lambda i, place: (i, 0))
    down_half = DOWN_ROWS // 2
    block = pl.BlockSpec((1, 2, down_half, WIDTH), lambda i, place: (i, 0, 0, 0))
    sent = ((4, UP_ROWS + down_half, WIDTH), LOW, pl.BlockSpec((1, UP_ROWS + down_half, WIDTH), lambda i, place: (i, 0, 0)))
    down = ((4, down_half, WIDTH), LOW, pl.BlockSpec((1, down_half, WIDTH), lambda i, place: (i, 0, 0)))
    return call(
        up_kernel,
        "up_units",
        place,
        [
            (normed_t, rows), plain(normed_got), plain(inner[0]), plain(inner[1]), plain(got[0]), plain(got[1]),
            (att_t, pl.BlockSpec((192, 512), lambda i, place: (i, 0))),
            plain(branch), plain(misc), plain(sums0), plain(sums1), plain(feed_got),
        ]
        + [(array, block) for array in down_pair],
        [sent, sent] + unit_outputs(UP_ROWS, WIDTH)[:2] + [down, down],
        scratch=[pltpu.VMEM((2, 2, UP_ROWS, WIDTH), LOW), pltpu.VMEM((WIDTH, OWN), LOW)],
        grid=(4,),
        after=after,
        work=cost(0.9e9, 5e6),
    )


def attention_back_kernel(
    place, own_lengths, peer_lengths, q, k, v, log_total, att, back0, misc,
    dq_out, dk_out, dv_out, bias,
):
    bases = first_positions(place)
    ends = pair_ends(place, own_lengths, peer_lengths)
    query_ids = [pairs_along(base, ends, 1)[0:1] for base in bases[:4]]
    for j in range(8):
        key_ids = pairs_along(bases[j], ends, 0)
        for i in range(4):
            bias[pl.ds(j * BLOCK, BLOCK), pl.ds(i * BLOCK, BLOCK)] = jnp.where(
                key_ids == query_ids[i], 0.0, NEGATIVE
            )
    for pair in range(PAIRS_OF_HEADS):
        lanes = pl.ds(pair * LANES, LANES)
        keys = k[:, lanes]
        values = v[:, lanes]
        keys_t = jnp.transpose(keys.astype(FLOAT)).astype(LOW)
        key_grad = jnp.zeros((1024, LANES), FLOAT)
        value_grad = jnp.zeros((1024, LANES), FLOAT)
        left = head_mask(OWN)
        for part in range(2):
            rows = pl.ds(part * OWN, OWN)
            queries = q[rows, lanes]
            grads = back0[:, lanes] if part == 0 else misc[0:OWN, pl.ds(HALF + pair * LANES, LANES)]
            zeros = jnp.zeros_like(queries)
            product = jnp.transpose(grads.astype(FLOAT) * att[rows, lanes].astype(FLOAT))
            halves = []
            for half in range(2):
                if half == 0:
                    chosen, chosen_grads = jnp.where(left, queries, zeros), jnp.where(left, grads, zeros)
                else:
                    chosen, chosen_grads = jnp.where(left, zeros, queries), jnp.where(left, zeros, grads)
                delta = column_sum(product[half * HEAD_DIM : (half + 1) * HEAD_DIM])
                head = pair * 2 + half
                scores = dot_nt(keys, chosen) + bias[:, rows]
                weights = jnp.exp(scores - log_total[head : head + 1, rows])
                weight_grad = dot_nt(values, chosen_grads)
                score_grad = (weights * (weight_grad - delta)).astype(LOW)
                value_grad = value_grad + dot(weights.astype(LOW), chosen_grads)
                key_grad = key_grad + dot(score_grad, chosen)
                halves.append(dot(keys_t, score_grad))
            query_grad_t = jnp.concatenate([halves[0][0:HEAD_DIM], halves[1][HEAD_DIM:LANES]], axis=0)
            dq_out[rows, lanes] = (jnp.transpose(query_grad_t) * HEAD_DIM**-0.5).astype(LOW)
        dk_out[:, lanes] = key_grad.astype(LOW)
        dv_out[:, lanes] = value_grad.astype(LOW)


def attention_back(place, lengths, q, k, v, log_total, att, back_own, misc, after=()):
    return call(
        attention_back_kernel,
        "attention_back",
        place,
        [plain(array) for array in (q, k, v, log_total, att, back_own, misc)],
        [made((512, HALF), LOW), made((1024, HALF), LOW), made((1024, HALF), LOW)],
        scratch=[pltpu.VMEM((1024, 512), FLOAT)],
        scalars=lengths,
        after=after,
        work=cost(7e9, 6e6, 3e6),
    )


def token_kernel(place, dq, dk, dv, wq, wk, wv, own, own_send, far, far_send):
    for part, target in enumerate((own, own_send, far, far_send)):
        rows = pl.ds(part * OWN, OWN)
        total = dot_nt(dk[rows, :], wk[...]) + dot_nt(dv[rows, :], wv[...])
        if part < 2:
            total = total + dot_nt(dq[rows, :], wq[...])
        target[...] = total.astype(LOW)


def token_parts(place, dq, dk, dv, joint_weight, after=()):
    def columns(kind):
        return joint_weight, pl.BlockSpec((WIDTH, HALF), lambda i, place: (0, 2 * kind + place[3]))

    return call(
        token_kernel,
        "token_parts",
        place,
        [plain(dq), plain(dk), plain(dv), columns(0), columns(1), columns(2)],
        [made((OWN, WIDTH), LOW)] * 4,
        after=after,
        work=cost(1.5e9, 5e6),
    )


def back_rows_kernel(place, done0, done1, back0, back1, outputs, token_grad):
    odd = place[0] % 2
    outputs[odd] = done0[...]
    outputs[1 - odd] = done1[...]
    token_grad[odd] = back0[...].astype(FLOAT)
    token_grad[1 - odd] = back1[...].astype(FLOAT)


def back_rows(place, done, back, after=()):
    return call(
        back_rows_kernel,
        "back_rows",
        place,
        [plain(array) for array in (*done, *back)],
        [made((2, BLOCK, WIDTH), LOW), made((2, BLOCK, WIDTH), FLOAT)],
        after=after,
        work=cost(1e6, 2e6),
    )


def joint_kernel(
    place, t0, t1, t2, t3, t4, t5, t6, t7, dq, dk, dv, px_send, px, qy_send, qy, tokens_t, units
):
    y, x = place[1], place[2]
    for index, block in enumerate((t0, t1, t2, t3, t4, t5, t6, t7)):
        tokens_t[:, pl.ds(index * BLOCK, BLOCK)] = jnp.transpose(block[...].astype(FLOAT)).astype(LOW)
    biases = jnp.concatenate([column_sum(dq[...].astype(FLOAT)), column_sum(dv[...].astype(FLOAT))], axis=1)
    biases = jnp.concatenate([biases, jnp.zeros((7, WIDTH), FLOAT)], axis=0)
    for z in range(4):
        rows = pl.ds(z * 192, 192)
        query = dot(tokens_t[rows, 0:512], dq[...])
        key = dot(tokens_t[rows, :], dk[...])
        value = dot(tokens_t[rows, :], dv[...])
        for line in range(2):
            for side in range(2):
                at = line * 96 + side * 48
                units[line, side, 0:JOINT_FIRST] = jnp.concatenate(
                    [query[at : at + 48], key[at : at + 48]], axis=1
                ).astype(LOW)
                rest = jnp.concatenate([value[at : at + 24], value[at + 24 : at + 48]], axis=1)
                units[line, side, JOINT_FIRST:] = jnp.concatenate([rest, biases], axis=0).astype(LOW)
        for line in range(2):
            px[z, line] = units[line, x, 0:JOINT_FIRST]
            px_send[z, line] = units[line, 1 - x, 0:JOINT_FIRST]
        for side in range(2):
            qy[z, side] = units[y, side, JOINT_FIRST:]
            qy_send[z, side] = units[1 - y, side, JOINT_FIRST:]


def joint_units(place, blocks, dq, dk, dv, after=()):
    first, second = made((4, 2, JOINT_FIRST, WIDTH), LOW), made((4, 2, JOINT_SECOND, WIDTH), LOW)
    return call(
        joint_kernel,
        "joint_units",
        place,
        [plain(array) for array in (*blocks, dq, dk, dv)],
        [first, first, second, second],
        scratch=[pltpu.VMEM((WIDTH, 1024), LOW), pltpu.VMEM((2, 2, JOINT_ROWS, WIDTH), LOW)],
        after=after,
        work=cost(1.5e9, 6e6),
    )


def added(left, right):
    return (left.astype(FLOAT) + right.astype(FLOAT)).astype(LOW)


def second_kernel(
    place, x_got, y_got, px, qy, down_p, down_q, far, far_got, joint_px, joint_qy,
    x_send, y_send, p, q, down_send, down_keep,
):
    z_here, y, x = place[0], place[1], place[2]
    half = UP_ROWS // 2
    down_at = UP_ROWS
    for z in range(4):
        for got, have, own, keep, send in ((x_got, px, y, p, y_send), (y_got, qy, x, q, x_send)):
            mine = pl.ds(pl.multiple_of(own * half, half), half)
            other = pl.ds(pl.multiple_of((1 - own) * half, half), half)
            keep[z] = added(have[z, own], got[z, mine])
            send[pl.ds(z * half, half), :] = added(have[z, 1 - own], got[z, other])
        for other in range(2):
            at = z * 2 + other
            x_send[pl.ds(OWN + at * JOINT_FIRST, JOINT_FIRST), :] = joint_px[z, other]
            y_send[pl.ds(2 * OWN + at * JOINT_SECOND, JOINT_SECOND), :] = joint_qy[z, other]
    y_send[pl.ds(OWN, OWN), :] = added(far[...], far_got[...])
    low = z_here % 2
    small = DOWN_ROWS // 2
    for target, parity in ((down_keep, low), (down_send, 1 - low)):
        for high in range(2):
            index = 2 * high + parity
            target[high, 0:small] = added(down_p[index], y_got[index, down_at:])
            target[high, small:] = added(down_q[index], x_got[index, down_at:])


def second_stage(place, x_got, y_got, px, qy, down_p, down_q, far, far_got, joint_px, joint_qy, after=()):
    kept = made((4, UP_ROWS // 2, WIDTH), LOW)
    down = made((2, DOWN_ROWS, WIDTH), LOW)
    return call(
        second_kernel,
        "second_stage",
        place,
        [plain(array) for array in (x_got, y_got, px, qy, down_p, down_q, far, far_got, joint_px, joint_qy)],
        [
            made((OWN + 8 * JOINT_FIRST, WIDTH), LOW), made((2 * OWN + 8 * JOINT_SECOND, WIDTH), LOW),
            kept, kept, down, down,
        ],
        after=after,
        work=cost(1e6, 1e7),
    )


def third_kernel(
    place, x_got, y_got, p, q, px, qy, own, own_got, first_grad,
    x_send, y_send, joint_p, joint_q, up_send, up_keep, token0, token1,
):
    z_here, y, x = place[0], place[1], place[2]
    half = UP_ROWS // 2
    for z in range(4):

        def from_x(line):
            at = OWN + (z * 2 + line) * JOINT_FIRST
            return x_got[pl.ds(pl.multiple_of(at, 16), JOINT_FIRST), :]

        def from_y(side):
            at = 2 * OWN + (z * 2 + side) * JOINT_SECOND
            return y_got[pl.ds(pl.multiple_of(at, 16), JOINT_SECOND), :]

        joint_p[z] = added(px[z, y], from_x(y))
        y_send[z] = added(px[z, 1 - y], from_x(1 - y))
        joint_q[z] = added(qy[z, x], from_y(x))
        x_send[z] = added(qy[z, 1 - x], from_y(1 - x))
    low = z_here % 2
    for target, parity in ((up_keep, low), (up_send, 1 - low)):
        for high in range(2):
            index = 2 * high + parity
            rows = pl.ds(pl.multiple_of(index * half, half), half)
            target[high, 0:half] = added(p[index], y_got[rows, :])
            target[high, half:] = added(q[index], x_got[rows, :])
    across = y_got[pl.ds(OWN, OWN), :].astype(FLOAT)
    total = own[...].astype(FLOAT) + own_got[...].astype(FLOAT) + across + first_grad[...]
    total = total.astype(LOW)
    token0[...] = total[0:BLOCK]
    token1[...] = total[BLOCK:]


def third_stage(place, arrays, after=()):
    joint = [made((4, JOINT_SECOND, WIDTH), LOW), made((4, JOINT_FIRST, WIDTH), LOW)]
    return call(
        third_kernel,
        "third_stage",
        place,
        [plain(array) for array in arrays],
        joint + joint[::-1] + [made((2, UP_ROWS, WIDTH), LOW)] * 2 + [made((BLOCK, WIDTH), LOW)] * 2,
        after=after,
        work=cost(1e6, 1e7),
    )


def fourth_kernel(place, x_got, y_got, p, q, keep_two, got, send, keep, up_send, up_keep):
    low, high_here = place[0] % 2, place[0] // 2
    for target, parity in ((keep, low), (send, 1 - low)):
        for high in range(2):
            index = 2 * high + parity
            target[high, 0:JOINT_FIRST] = added(p[index], y_got[index])
            target[high, JOINT_FIRST:] = added(q[index], x_got[index])
    up_keep[...] = added(keep_two[high_here], got[high_here])
    up_send[...] = added(keep_two[1 - high_here], got[1 - high_here])


def fourth_stage(place, arrays, after=()):
    return call(
        fourth_kernel,
        "fourth_stage",
        place,
        [plain(array) for array in arrays],
        [made((2, JOINT_ROWS, WIDTH), LOW)] * 2 + [made((UP_ROWS, WIDTH), LOW)] * 2,
        after=after,
        work=cost(1e6, 1e6),
    )


def end_stage_kernel(place, keep_two, got, send, keep):
    high = place[0] // 2
    keep[...] = added(keep_two[high], got[high])
    send[...] = added(keep_two[1 - high], got[1 - high])


def end_stage(place, keep_two, got, after=()):
    return call(
        end_stage_kernel,
        "end_stage",
        place,
        [plain(keep_two), plain(got)],
        [made(keep_two.shape[1:], LOW)] * 2,
        after=after,
        work=cost(1e6, 1e6),
    )


def last_sum_kernel(place, *refs):
    out = refs[-1]
    at = 0
    for first, second in zip(refs[0:-1:2], refs[1:-1:2]):
        out[pl.ds(at, first.shape[0]), :] = added(first[...], second[...])
        at += first.shape[0]


def last_sum(place, pairs, after=()):
    arrays = [array for pair in pairs for array in pair]
    rows = sum(pair[0].shape[0] for pair in pairs)
    results, mark = call(
        last_sum_kernel,
        "last_sum",
        place,
        [plain(array) for array in arrays],
        [made((rows, arrays[0].shape[1]), LOW)],
        after=after,
        work=cost(1e6, 1e6),
    )
    return results[0], mark


def gathered(unit):
    across = x_swap(unit)
    return unit, core_swap(unit), across, core_swap(across)


def quarters(place):
    x, c = place[2], place[3]
    return (x, c), (x, 1 - c), (1 - x, c), (1 - x, 1 - c)


def line_shift(place):
    seq = place[0] * 2 + place[1]
    return lax.rem(WIDTH - seq * 96, WIDTH)


def dense_out_kernel(
    place, u0, u1, u2, u3, down, up, out, gain2, shift2, down_bias, gain1, shift1, out_bias, up_bias, heads, tails
):
    for unit, (x, c) in zip((u0, u1, u2, u3), quarters(place)):
        quarter = 2 * x + c
        down[pl.ds(pl.multiple_of(quarter * DOWN_ROWS, 32), DOWN_ROWS), :] = unit[0:DOWN_ROWS, :].astype(FLOAT)
        up[:, pl.ds(pl.multiple_of(quarter * WIDTH, LANES), WIDTH)] = unit[96:192, :].astype(FLOAT)
        rest = unit[192:224, :].astype(FLOAT)
        lanes = pl.ds(pl.multiple_of(c * HALF, LANES), HALF)
        out[pl.ds(pl.multiple_of(x * 48, 8), 24), lanes] = rest[0:24, 0:HALF]
        out[pl.ds(pl.multiple_of(x * 48 + 24, 8), 24), lanes] = rest[0:24, HALF:]

        @pl.when(x == 0)
        def _(rest=rest):
            heads[...] = rest[24:32]

        @pl.when(x == 1)
        def _(rest=rest):
            tails[...] = rest[24:32]

    seq = place[0] * 2 + place[1]
    shift = line_shift(place)
    head = pltpu.roll(heads[...], shift, 1)
    gain2[...] = head[0:1, 0:96]
    shift2[...] = head[1:2, 0:96]
    down_bias[...] = head[2:3, 0:96]
    tail = pltpu.roll(tails[...], shift, 1)
    gain1[...] = tail[0:1, 0:96]
    shift1[...] = tail[1:2, 0:96]
    out_bias[...] = tail[2:3, 0:96]
    wide = tails[pl.ds(4 + seq // 2, 1), :]
    up_bias[...] = jnp.where(seq % 2 == 0, wide[:, 0:HALF], wide[:, HALF:])


def dense_outputs(place, units, after=()):
    results, mark = call(
        dense_out_kernel,
        "dense_outputs",
        place,
        [plain(unit) for unit in units],
        [made((4 * DOWN_ROWS, WIDTH), FLOAT), made((96, FF), FLOAT), made((96, WIDTH), FLOAT)]
        + [made((1, 96), FLOAT)] * 6
        + [made((1, HALF), FLOAT)],
        scratch=[pltpu.VMEM((8, WIDTH), FLOAT)] * 2,
        after=after,
        work=cost(1e6, 3e6),
    )
    return (*results[:3], *(vector.reshape(-1) for vector in results[3:])), mark


def joint_out_kernel(place, u0, u1, u2, u3, joint, query_bias, value_bias, sums):
    for unit, (x, c) in zip((u0, u1, u2, u3), quarters(place)):

        def lanes(kind):
            return pl.ds(pl.multiple_of(kind * WIDTH + c * HALF, LANES), HALF)

        first = unit[0:JOINT_FIRST].astype(FLOAT)
        rest = unit[JOINT_FIRST:].astype(FLOAT)
        rows = pl.ds(pl.multiple_of(x * 48, 16), 48)
        joint[rows, lanes(0)] = first[:, 0:HALF]
        joint[rows, lanes(1)] = first[:, HALF:]
        joint[pl.ds(pl.multiple_of(x * 48, 8), 24), lanes(2)] = rest[0:24, 0:HALF]
        joint[pl.ds(pl.multiple_of(x * 48 + 24, 8), 24), lanes(2)] = rest[0:24, HALF:]

        @pl.when(x == 0)
        def _(rest=rest, c=c):
            half = pl.ds(pl.multiple_of(c * HALF, LANES), HALF)
            sums[0:1, half] = rest[24:25, 0:HALF]
            sums[1:2, half] = rest[24:25, HALF:]

    turned = pltpu.roll(sums[...], line_shift(place), 1)
    query_bias[...] = turned[0:1, 0:96]
    value_bias[...] = turned[1:2, 0:96]


def joint_outputs(place, units, after=()):
    results, mark = call(
        joint_out_kernel,
        "joint_outputs",
        place,
        [plain(unit) for unit in units],
        [made((96, 3 * WIDTH), FLOAT), made((1, 96), FLOAT), made((1, 96), FLOAT)],
        scratch=[pltpu.VMEM((8, WIDTH), FLOAT)],
        after=after,
        work=cost(1e6, 2e6),
    )
    return (results[0], results[1].reshape(-1), results[2].reshape(-1)), mark


def row_body(
    tokens,
    pair_lengths,
    joint_weight,
    query_bias,
    value_bias,
    out_weight,
    out_bias,
    first_gain,
    first_shift,
    up_weight,
    up_bias,
    down_weight,
    down_bias,
    second_gain,
    second_shift,
    cotangent,
):
    seq, rows = lax.axis_index("seq"), lax.axis_index("rows")
    z, y, x, c = seq // 2, seq % 2, rows // 2, rows % 2
    place = jnp.stack([z, y, x, c]).astype(jnp.int32)
    odd = z % 2
    weights = {
        "out": out_weight, "out_bias": out_bias, "gain1": first_gain, "shift1": first_shift,
        "up": up_weight, "up_bias": up_bias, "down": down_weight, "down_bias": down_bias,
        "gain2": second_gain, "shift2": second_shift,
    }

    def local_row(array, index):
        return lax.dynamic_index_in_dim(array, index, 0, keepdims=False)

    own = [row_swap(local_row(tokens, odd), 0), row_swap(local_row(tokens, 1 - odd), 1)]
    lengths = (pair_lengths, core_swap(pair_lengths))
    across = [y_swap(block) for block in own]
    blocks = (
        own + [core_swap(block) for block in own] + across + [core_swap(block) for block in across]
    )
    cotangent, _ = lax.optimization_barrier((cotangent, across[0]))
    cotangents = [row_swap(local_row(cotangent, odd), 0), row_swap(local_row(cotangent, 1 - odd), 1)]

    (att, q, k, v, log_total), mark = attention(place, lengths, blocks, joint_weight, query_bias, value_bias)
    att_got = core_swap(att)
    results, mark = forward(place, att, att_got, own, cotangents, weights, (mark,))
    (
        result0, result1, feed, second_grad, act, act_send, slope, unit1, inverse1, normed, normed_t, att_t, sums0
    ) = results
    act_got, feed_got, normed_got = core_swap(act_send), core_swap(feed), core_swap(normed)
    done = (row_swap(result0, 0), row_swap(result1, 1))
    (px_send, px, qy_send, qy), mark = down_units(place, act, act_got, feed, feed_got, (mark,))
    down_pair = (px, x_swap(px_send), qy, y_swap(qy_send))
    results, mark = backward(place, feed, slope, second_grad, unit1, inverse1, weights, (mark, normed_got, *done))
    inner0, inner1, send0, send1, first_grad, branch_own, back_own, misc_send, sums1 = results
    got, misc = (core_swap(send0), core_swap(send1)), core_swap(misc_send)
    (x_send, y_send, px, qy, down_p, down_q), mark = up_units(
        place, normed_t, normed_got, (inner0, inner1), got, att_t, branch_own, misc, sums0, sums1, feed_got,
        down_pair, (mark,)
    )
    x_got, y_got = x_swap(x_send), y_swap(y_send)
    (dq, dk, dv), mark = attention_back(place, lengths, q, k, v, log_total, att, back_own, misc, (mark,))
    (token_own, own_send, token_far, far_send), mark = token_parts(place, dq, dk, dv, joint_weight, (mark,))
    own_got, far_got = core_swap(own_send), core_swap(far_send)
    (joint_px_send, joint_px, joint_qy_send, joint_qy), mark = joint_units(place, blocks, dq, dk, dv, (mark,))
    (x_send, y_send, p, q_, down_send, down_keep), mark = second_stage(
        place, x_got, y_got, px, qy, down_p, down_q, token_far, far_got, joint_px_send, joint_qy_send, (mark,)
    )
    x_got, y_got = x_swap(x_send), y_swap(y_send)
    (down_send, down_keep), mark = end_stage(place, down_keep, z_swap(down_send, 1), (mark,))
    down_got = z_swap(down_send, 2)
    results, mark = third_stage(
        place, (x_got, y_got, p, q_, joint_px, joint_qy, token_own, own_got, first_grad), (mark, down_got)
    )
    x_send, y_send, joint_p, joint_q, up_send, up_keep, token0, token1 = results
    x_got, y_got, up_got = x_swap(x_send), y_swap(y_send), z_swap(up_send, 1)
    (joint_send, joint_keep, up_send, up_keep), mark = fourth_stage(
        place, (x_got, y_got, joint_p, joint_q, up_keep, up_got), (mark,)
    )
    joint_got, up_got = z_swap(joint_send, 1), z_swap(up_send, 2)
    (joint_send, joint_keep), mark = end_stage(place, joint_keep, joint_got, (mark,))
    joint_got = z_swap(joint_send, 2)
    dense_unit, mark = last_sum(place, ((down_keep, down_got), (up_keep, up_got)), (mark,))
    dense_all = gathered(dense_unit)
    back = (row_swap(token0, 0), row_swap(token1, 1))
    joint_unit, mark = last_sum(place, ((joint_keep, joint_got),), (mark,))
    joint_all = gathered(joint_unit)
    (outputs, token_grad), mark = back_rows(place, done, back, (mark,))
    (
        down_grad, up_grad, out_grad, second_gain_grad, second_shift_grad, down_bias_grad, first_gain_grad,
        first_shift_grad, out_bias_grad, up_bias_grad,
    ), mark = dense_outputs(place, dense_all, (mark,))
    (joint_grad, query_bias_grad, value_bias_grad), mark = joint_outputs(place, joint_all, (mark,))
    return (
        outputs,
        token_grad,
        joint_grad,
        query_bias_grad,
        value_bias_grad,
        out_grad,
        out_bias_grad,
        first_gain_grad,
        first_shift_grad,
        up_grad,
        up_bias_grad,
        down_grad,
        down_bias_grad,
        second_gain_grad,
        second_shift_grad,
    )


def body(tokens, *others):
    if (lax.axis_size("seq"), lax.axis_size("rows")) == (8, 4) and tokens.shape == (2, BLOCK, WIDTH):
        return row_body(tokens, *others)
    return general_body(tokens, *others)


def solution(mesh):
    placed = (
        P("rows", "seq", None),
        P("rows", None),
        P(),
        P(),
        P(),
        P(),
        P(),
        P(),
        P(),
        P(),
        P(),
        P(),
        P(),
        P(),
        P(),
        P("rows", "seq", None),
    )
    return jax.shard_map(
        body,
        mesh=mesh,
        in_specs=placed,
        out_specs=(
            P("rows", "seq", None),
            P("rows", "seq", None),
            P("seq", None),
            P("seq"),
            P("seq"),
            P("seq", None),
            P("seq"),
            P("seq"),
            P("seq"),
            P("seq", None),
            P("seq"),
            P("seq", None),
            P("seq"),
            P("seq"),
            P("seq"),
        ),
        check_vma=False,
    )
```

```python
import functools
import math

import jax
import jax.numpy as jnp
from jax import lax
from jax.experimental import pallas as pl
from jax.experimental.pallas import tpu as pltpu
from jax.sharding import PartitionSpec as P

HEADS = 12
HEAD_DIM = 64


NEGATIVE = -1e30
EPSILON = 1e-12


def from_behind(value, axis, steps):
    count = lax.axis_size(axis)
    pairs = [(source, (source + steps) % count) for source in range(count)]
    return lax.ppermute(value, axis, pairs)


def layer_norm(value, gain, shift):
    mean = jnp.mean(value, axis=-1, keepdims=True)
    centred = value - mean
    spread = jnp.mean(centred * centred, axis=-1, keepdims=True)
    return centred * lax.rsqrt(spread + EPSILON) * gain + shift


def gelu_exact(value):
    return jax.nn.gelu(value, approximate=False)


def pair_index(positions, ends):
    return jnp.sum((positions[None, :, None] >= ends[:, None, :]).astype(jnp.int32), axis=2)


def split_heads(array):
    return array.reshape(array.shape[0], array.shape[1], HEADS, HEAD_DIM)


def online_block(state, query_heads, query_pairs, key_block, value_block, key_pairs):
    highest, total, summed = state
    scores = jnp.einsum(
        "rqhd,rkhd->rhqk", query_heads, split_heads(key_block), preferred_element_type=jnp.float32
    ) * HEAD_DIM ** (-0.5)
    allowed = query_pairs[:, None, :, None] == key_pairs[:, None, None, :]
    masked = jnp.where(allowed, scores, NEGATIVE)
    new_high = jnp.maximum(highest, jnp.max(masked, axis=3))
    weights = jnp.where(allowed, jnp.exp(masked - new_high[..., None]), 0.0)
    factor = jnp.exp(highest - new_high)
    total = total * factor + jnp.sum(weights, axis=3)
    summed = summed * jnp.swapaxes(factor, 1, 2)[..., None] + jnp.einsum(
        "rhqk,rkhd->rqhd",
        weights.astype(jnp.bfloat16),
        split_heads(value_block),
        preferred_element_type=jnp.float32,
    )
    return (new_high, total, summed)


def tile_terms(queries, out_grad, log_total, delta, query_pairs, keys, values, key_pairs):
    scale = HEAD_DIM ** (-0.5)
    query_heads = split_heads(queries)
    grad_heads = split_heads(out_grad)
    key_heads = split_heads(keys)
    value_heads = split_heads(values)
    scores = (
        jnp.einsum("rqhd,rkhd->rhqk", query_heads, key_heads, preferred_element_type=jnp.float32)
        * scale
    )
    allowed = query_pairs[:, None, :, None] == key_pairs[:, None, None, :]
    weights = jnp.where(
        allowed, jnp.exp(jnp.where(allowed, scores, NEGATIVE) - log_total[..., None]), 0.0
    )
    weight_grad = jnp.einsum(
        "rqhd,rkhd->rhqk", grad_heads, value_heads, preferred_element_type=jnp.float32
    )
    score_grad = (weights * (weight_grad - delta[..., None])).astype(jnp.bfloat16)
    query_term = (
        jnp.einsum("rhqk,rkhd->rqhd", score_grad, key_heads, preferred_element_type=jnp.float32)
        * scale
    )
    key_term = (
        jnp.einsum("rhqk,rqhd->rkhd", score_grad, query_heads, preferred_element_type=jnp.float32)
        * scale
    )
    value_term = jnp.einsum(
        "rhqk,rqhd->rkhd",
        weights.astype(jnp.bfloat16),
        grad_heads,
        preferred_element_type=jnp.float32,
    )
    return (
        query_term.reshape(queries.shape),
        key_term.reshape(keys.shape),
        value_term.reshape(values.shape),
    )


def general_body(
    tokens,
    pair_lengths,
    joint_weight,
    query_bias,
    value_bias,
    out_weight,
    out_bias,
    first_gain,
    first_shift,
    up_weight,
    up_bias,
    down_weight,
    down_bias,
    second_gain,
    second_shift,
    cotangent,
):
    rows_here, seq_here, width = tokens.shape
    count = lax.axis_size("seq")
    cycle_index = lax.axis_index("seq")
    ends = jnp.cumsum(pair_lengths, axis=1)
    offsets = jnp.arange(seq_here, dtype=jnp.int32)
    own_pairs = pair_index(cycle_index * seq_here + offsets, ends)
    block_shape = (rows_here, seq_here, width)
    flat = tokens.reshape(rows_here * seq_here, width)
    projected = jnp.dot(flat, joint_weight, preferred_element_type=jnp.float32)
    queries = (projected[:, :width] + query_bias).astype(jnp.bfloat16).reshape(block_shape)
    keys = projected[:, width : 2 * width].astype(jnp.bfloat16).reshape(block_shape)
    values = (projected[:, 2 * width :] + value_bias).astype(jnp.bfloat16).reshape(block_shape)
    query_heads = split_heads(queries)
    initial = (
        jnp.full((rows_here, HEADS, seq_here), NEGATIVE, jnp.float32),
        jnp.zeros((rows_here, HEADS, seq_here), jnp.float32),
        jnp.zeros((rows_here, seq_here, HEADS, HEAD_DIM), jnp.float32),
    )
    key_piece = lax.all_gather(keys, "seq", axis=1, tiled=True)
    value_piece = lax.all_gather(values, "seq", axis=1, tiled=True)
    length = key_piece.shape[1]
    block = math.gcd(length, seq_here)

    def one_block(index, inner_state):
        first = index * block
        key_block = lax.dynamic_slice_in_dim(key_piece, first, block, 1)
        value_block = lax.dynamic_slice_in_dim(value_piece, first, block, 1)
        key_pairs = pair_index(first + jnp.arange(block, dtype=jnp.int32), ends)
        return online_block(inner_state, query_heads, own_pairs, key_block, value_block, key_pairs)

    highest, total, summed = lax.fori_loop(0, length // block, one_block, initial)
    log_total = highest + jnp.log(total)
    attended = (
        (summed / jnp.swapaxes(total, 1, 2)[..., None]).astype(jnp.bfloat16).reshape(flat.shape)
    )
    branch = jnp.dot(attended, out_weight, preferred_element_type=jnp.float32) + out_bias
    first_sum = flat.astype(jnp.float32) + branch
    normed, first_back = jax.vjp(layer_norm, first_sum, first_gain, first_shift)
    normed_low = normed.astype(jnp.bfloat16)
    inner = jnp.dot(normed_low, up_weight, preferred_element_type=jnp.float32) + up_bias
    activated_full, gelu_back = jax.vjp(gelu_exact, inner)
    activated = activated_full.astype(jnp.bfloat16)
    feed = jnp.dot(activated, down_weight, preferred_element_type=jnp.float32) + down_bias
    second_sum = normed + feed
    result, second_back = jax.vjp(layer_norm, second_sum, second_gain, second_shift)
    outputs = result.astype(jnp.bfloat16).reshape(tokens.shape)
    second_grad, second_gain_grad, second_shift_grad = second_back(
        cotangent.astype(jnp.float32).reshape(flat.shape)
    )
    feed_grad = second_grad.astype(jnp.bfloat16)
    down_grad = jnp.einsum("ti,tj->ij", activated, feed_grad, preferred_element_type=jnp.float32)
    down_bias_grad = jnp.sum(feed_grad.astype(jnp.float32), axis=0)
    activated_grad = jnp.einsum(
        "tj,ij->ti", feed_grad, down_weight, preferred_element_type=jnp.float32
    )
    inner_grad = gelu_back(activated_grad)[0].astype(jnp.bfloat16)
    up_grad = jnp.einsum("ti,tj->ij", normed_low, inner_grad, preferred_element_type=jnp.float32)
    up_bias_grad = jnp.sum(inner_grad.astype(jnp.float32), axis=0)
    normed_grad = second_grad + jnp.einsum(
        "tj,ij->ti", inner_grad, up_weight, preferred_element_type=jnp.float32
    )
    first_grad, first_gain_grad, first_shift_grad = first_back(normed_grad)
    branch_grad = first_grad.astype(jnp.bfloat16)
    out_grad = jnp.einsum("ti,tj->ij", attended, branch_grad, preferred_element_type=jnp.float32)
    out_bias_grad = jnp.sum(branch_grad.astype(jnp.float32), axis=0)
    attended_grad = jnp.einsum(
        "tj,ij->ti", branch_grad, out_weight, preferred_element_type=jnp.float32
    ).astype(jnp.bfloat16)
    delta = jnp.sum(
        (attended_grad.astype(jnp.float32) * attended.astype(jnp.float32)).reshape(
            rows_here, seq_here, HEADS, HEAD_DIM
        ),
        axis=3,
    )
    delta = jnp.swapaxes(delta, 1, 2)
    attended_grad = attended_grad.reshape(block_shape)
    zeros_block = jnp.zeros(block_shape, jnp.float32)

    def send_key_sums(sums):
        return (
            from_behind(sums[0].astype(jnp.bfloat16), "seq", 1).astype(jnp.float32),
            from_behind(sums[1].astype(jnp.bfloat16), "seq", 1).astype(jnp.float32),
        )

    def key_work(turn, pair_block, sums, query_sum):
        anchor = (cycle_index - turn) % count
        key_pairs = pair_index(anchor * seq_here + offsets, ends)
        query_term, key_term, value_term = tile_terms(
            queries,
            attended_grad,
            log_total,
            delta,
            own_pairs,
            pair_block[0],
            pair_block[1],
            key_pairs,
        )
        return ((sums[0] + key_term, sums[1] + value_term), query_sum + query_term)

    def key_turn(turn, state):
        pair_block, sums, query_sum = state
        sums, query_sum = key_work(turn, pair_block, sums, query_sum)
        sums = send_key_sums(sums)
        pair_block = from_behind((pair_block[0], pair_block[1]), "seq", 1)
        return (pair_block, sums, query_sum)

    pair_block, sums, query_sum = lax.fori_loop(
        0, count - 1, key_turn, ((keys, values), (zeros_block, zeros_block), zeros_block)
    )
    sums, query_sum = key_work(count - 1, pair_block, sums, query_sum)
    key_sum, value_sum = send_key_sums(sums)
    query_low = query_sum.astype(jnp.bfloat16).reshape(flat.shape)
    key_low = key_sum.astype(jnp.bfloat16).reshape(flat.shape)
    value_low = value_sum.astype(jnp.bfloat16).reshape(flat.shape)
    joint_low = jnp.concatenate([query_low, key_low, value_low], axis=1)
    joint_grad = jnp.einsum("ti,tj->ij", flat, joint_low, preferred_element_type=jnp.float32)
    query_bias_grad = jnp.sum(query_low.astype(jnp.float32), axis=0)
    value_bias_grad = jnp.sum(value_low.astype(jnp.float32), axis=0)
    token_grad = first_grad + jnp.einsum(
        "tj,ij->ti", joint_low, joint_weight, preferred_element_type=jnp.float32
    )
    gradients = (
        joint_grad,
        query_bias_grad,
        value_bias_grad,
        out_grad,
        out_bias_grad,
        first_gain_grad,
        first_shift_grad,
        up_grad,
        up_bias_grad,
        down_grad,
        down_bias_grad,
        second_gain_grad,
        second_shift_grad,
    )
    shares = (
        lax.psum_scatter(
            gradients[0].astype(jnp.bfloat16), "seq", scatter_dimension=0, tiled=True
        ).astype(jnp.float32),
        lax.psum_scatter(
            gradients[1].astype(jnp.bfloat16), "seq", scatter_dimension=0, tiled=True
        ).astype(jnp.float32),
        lax.psum_scatter(
            gradients[2].astype(jnp.bfloat16), "seq", scatter_dimension=0, tiled=True
        ).astype(jnp.float32),
        lax.psum_scatter(
            gradients[3].astype(jnp.bfloat16), "seq", scatter_dimension=0, tiled=True
        ).astype(jnp.float32),
        lax.psum_scatter(
            gradients[4].astype(jnp.bfloat16), "seq", scatter_dimension=0, tiled=True
        ).astype(jnp.float32),
        lax.psum_scatter(
            gradients[5].astype(jnp.bfloat16), "seq", scatter_dimension=0, tiled=True
        ).astype(jnp.float32),
        lax.psum_scatter(
            gradients[6].astype(jnp.bfloat16), "seq", scatter_dimension=0, tiled=True
        ).astype(jnp.float32),
        lax.psum_scatter(
            gradients[7].astype(jnp.bfloat16), "seq", scatter_dimension=0, tiled=True
        ).astype(jnp.float32),
        lax.psum_scatter(
            gradients[8].astype(jnp.bfloat16), "seq", scatter_dimension=0, tiled=True
        ).astype(jnp.float32),
        lax.psum_scatter(
            gradients[9].astype(jnp.bfloat16), "seq", scatter_dimension=0, tiled=True
        ).astype(jnp.float32),
        lax.psum_scatter(
            gradients[10].astype(jnp.bfloat16), "seq", scatter_dimension=0, tiled=True
        ).astype(jnp.float32),
        lax.psum_scatter(
            gradients[11].astype(jnp.bfloat16), "seq", scatter_dimension=0, tiled=True
        ).astype(jnp.float32),
        lax.psum_scatter(
            gradients[12].astype(jnp.bfloat16), "seq", scatter_dimension=0, tiled=True
        ).astype(jnp.float32),
    )
    shares = (
        lax.psum(shares[0].astype(jnp.bfloat16), "rows").astype(jnp.float32),
        lax.psum(shares[1].astype(jnp.bfloat16), "rows").astype(jnp.float32),
        lax.psum(shares[2].astype(jnp.bfloat16), "rows").astype(jnp.float32),
        lax.psum(shares[3].astype(jnp.bfloat16), "rows").astype(jnp.float32),
        lax.psum(shares[4].astype(jnp.bfloat16), "rows").astype(jnp.float32),
        lax.psum(shares[5].astype(jnp.bfloat16), "rows").astype(jnp.float32),
        lax.psum(shares[6].astype(jnp.bfloat16), "rows").astype(jnp.float32),
        lax.psum(shares[7].astype(jnp.bfloat16), "rows").astype(jnp.float32),
        lax.psum(shares[8].astype(jnp.bfloat16), "rows").astype(jnp.float32),
        lax.psum(shares[9].astype(jnp.bfloat16), "rows").astype(jnp.float32),
        lax.psum(shares[10].astype(jnp.bfloat16), "rows").astype(jnp.float32),
        lax.psum(shares[11].astype(jnp.bfloat16), "rows").astype(jnp.float32),
        lax.psum(shares[12].astype(jnp.bfloat16), "rows").astype(jnp.float32),
    )
    return (outputs, token_grad.reshape(tokens.shape)) + tuple(shares)


WIDTH = HEADS * HEAD_DIM
HALF = WIDTH // 2
FF = 4 * WIDTH
BLOCK = 128
OWN = 2 * BLOCK
LANES = 128
PAIRS_OF_HEADS = HALF // LANES
JOINT_ROWS = 80
JOINT_FIRST = 48
JOINT_SECOND = JOINT_ROWS - JOINT_FIRST
UP_ROWS = 128
DOWN_ROWS = 96
EXT = OWN + 16
DOWN_SENT = 2 * DOWN_ROWS
FLOAT = jnp.float32
LOW = jnp.bfloat16
AXES = ("seq", "rows")


def kernel_params(megabytes):
    return pltpu.CompilerParams(vmem_limit_bytes=megabytes << 20)


def shaped(shape, kind):
    return jax.ShapeDtypeStruct(shape, kind)


def whole(shape):
    return pl.BlockSpec(shape, lambda *_: (0,) * len(shape))


def cost(flops, moved, exps=0):
    return pl.CostEstimate(flops=1024, bytes_accessed=1024, transcendentals=0)


def dot(left, right):
    return lax.dot_general(left, right, (((1,), (0,)), ((), ())), preferred_element_type=FLOAT)


def dot_nt(left, right):
    return lax.dot_general(left, right, (((1,), (1,)), ((), ())), preferred_element_type=FLOAT)


def call(kernel, name, place, inputs, outputs, scratch=(), grid=(1,), scalars=(), after=(), megabytes=28, work=None, aliases=()):
    prefetch = 1 + len(scalars)
    given, made = len(inputs), len(outputs)

    def ordered(*refs):
        first = prefetch + given
        mark = refs[first + len(after) + made]
        mark[...] = jnp.zeros_like(mark)
        kernel(*refs[:first], *refs[first + len(after) : first + len(after) + made], *refs[first + len(after) + made + 1 :])

    results = pl.pallas_call(
        ordered,
        grid_spec=pltpu.PrefetchScalarGridSpec(
            num_scalar_prefetch=prefetch,
            grid=grid,
            in_specs=[spec for _, spec in inputs] + [pl.BlockSpec(memory_space=pl.ANY)] * len(after),
            out_specs=[spec for _, _, spec in outputs] + [whole((8, LANES))],
            scratch_shapes=list(scratch),
        ),
        out_shape=[shaped(shape, kind) for shape, kind, _ in outputs] + [shaped((8, LANES), FLOAT)],
        compiler_params=kernel_params(megabytes),
        cost_estimate=work,
        input_output_aliases={prefetch + source: target for source, target in aliases},
        name=name,
    )(place, *scalars, *[array for array, _ in inputs], *after)
    return results[:-1], results[-1]


def plain(array):
    return array, whole(array.shape)


def made(shape, kind):
    return shape, kind, whole(shape)


def device_at(z, y, x, c):
    return ((z * 2 + y) * 2 + x) * 2 + c


def permute(value, target):
    pairs = []
    for z in range(4):
        for y in range(2):
            for x in range(2):
                for c in range(2):
                    pairs.append((device_at(z, y, x, c), device_at(*target(z, y, x, c))))
    return lax.ppermute(value, AXES, pairs)


def core_swap(value):
    return permute(value, lambda z, y, x, c: (z, y, x, 1 - c))


def x_swap(value):
    return permute(value, lambda z, y, x, c: (z, y, 1 - x, c))


def y_swap(value):
    return permute(value, lambda z, y, x, c: (z, 1 - y, x, c))


def z_swap(value, bits):
    return permute(value, lambda z, y, x, c: (z ^ bits, y, x, c))


def row_swap(value, second):
    return permute(value, lambda z, y, x, c: (2 * c + (z % 2 ^ second), y, x, z // 2))


def first_positions(place):
    z, y, c = place[0], place[1], place[3]
    bases = []
    for core, line in ((c, y), (1 - c, y), (c, 1 - y), (1 - c, 1 - y)):
        for second in (0, 1):
            parity = z % 2
            parity = 1 - parity if second else parity
            bases.append((2 * (2 * core + parity) + line) * BLOCK)
    return bases


def pair_ends(place, own_lengths, peer_lengths):
    z, c = place[0], place[3]
    here = (z // 2) == c
    line = z % 2
    ends, end = [], 0
    for pair in range(own_lengths.shape[1]):
        end = end + jnp.where(here, own_lengths[line, pair], peer_lengths[line, pair])
        ends.append(end)
    return ends


def pairs_along(base, ends, axis):
    shape = (8, BLOCK) if axis == 1 else (BLOCK, LANES)
    position = base + lax.broadcasted_iota(jnp.int32, shape, axis)
    ids = jnp.zeros(shape, jnp.int32)
    for end in ends:
        ids = ids + (position >= end).astype(jnp.int32)
    return ids


def head_mask(rows):
    return lax.broadcasted_iota(jnp.int32, (rows, LANES), 1) < HEAD_DIM


def first_attention_kernel(
    place, own_lengths, peer_lengths, t0, t1, t2, t3, wq, wk, wv, qb, vb, q_out, k_out, v_out, summed, highest_out, bias
):
    bases = first_positions(place)
    ends = pair_ends(place, own_lengths, peer_lengths)
    tokens = jnp.concatenate([block[...] for block in (t0, t1, t2, t3)], axis=0)
    queries = dot(tokens, wq[...]) + qb[...]
    q_out[...] = (queries.astype(LOW).astype(FLOAT) * HEAD_DIM**-0.5).astype(LOW)
    k_out[...] = dot(tokens, wk[...]).astype(LOW)
    v_out[...] = (dot(tokens, wv[...]) + vb[...]).astype(LOW)
    fill_bias(bias, bases[:4], bases[:4], ends)
    for pair in range(PAIRS_OF_HEADS):
        lanes = pl.ds(pair * LANES, LANES)
        keys = k_out[:, lanes]
        values_of = with_ones(v_out[:, lanes])
        for part in range(2):
            rows = pl.ds(part * OWN, OWN)
            chosen = halves_of(q_out[rows, lanes])
            for half in range(2):
                scores = dot_nt(chosen[half], keys) + bias[rows, :]
                highest = jnp.max(scores, axis=1, keepdims=True)
                summed[2 * pair + half, rows, :] = dot(jnp.exp(scores - highest).astype(LOW), values_of[half])
                highest_out[2 * pair + half, rows, :] = jnp.broadcast_to(highest, (OWN, LANES))


def fill_bias(bias, query_bases, key_bases, ends):
    key_ids = [pairs_along(base, ends, 1)[0:1] for base in key_bases]
    for i, base in enumerate(query_bases):
        query_ids = pairs_along(base, ends, 0)
        for j in range(len(key_bases)):
            bias[pl.ds(i * BLOCK, BLOCK), pl.ds(j * BLOCK, BLOCK)] = jnp.where(query_ids == key_ids[j], 0.0, NEGATIVE)


def halves_of(array):
    left = head_mask(array.shape[0])
    zeros = jnp.zeros_like(array)
    return jnp.where(left, array, zeros), jnp.where(left, zeros, array)


def with_ones(values):
    left = head_mask(values.shape[0])
    ones = jnp.ones_like(values)
    return jnp.where(left, values, ones), jnp.where(left, ones, values)


def first_attention(place, lengths, blocks, joint_weight, query_bias, value_bias, after=()):
    def columns(kind):
        return joint_weight, pl.BlockSpec((WIDTH, HALF), lambda i, place, *_: (0, 2 * kind + place[3]))

    half_row = pl.BlockSpec((1, HALF), lambda i, place, *_: (0, place[3]))
    state = made((HEADS // 2, 512, LANES), FLOAT)
    return call(
        first_attention_kernel,
        "first_attention",
        place,
        [plain(block) for block in blocks]
        + [columns(0), columns(1), columns(2), (row_of(query_bias), half_row), (row_of(value_bias), half_row)],
        [made((512, HALF), LOW)] * 3 + [state, state],
        scratch=[pltpu.VMEM((512, 512), FLOAT)],
        scalars=lengths,
        after=after,
        work=cost(4e9, 8e6, 3e6),
    )


def attention_kernel(
    place, own_lengths, peer_lengths, t0, t1, t2, t3, wk, wv, vb, q, summed_in, highest_in,
    att_out, k_out, v_out, log_out, bias, log_columns,
):
    bases = first_positions(place)
    ends = pair_ends(place, own_lengths, peer_lengths)
    tokens = jnp.concatenate([block[...] for block in (t0, t1, t2, t3)], axis=0)
    k_out[...] = dot(tokens, wk[...]).astype(LOW)
    v_out[...] = (dot(tokens, wv[...]) + vb[...]).astype(LOW)
    fill_bias(bias, bases[:4], bases[4:], ends)
    log_columns[...] = jnp.zeros_like(log_columns)
    column = lax.broadcasted_iota(jnp.int32, (OWN, LANES), 1)
    left = head_mask(OWN)
    for pair in range(PAIRS_OF_HEADS):
        lanes = pl.ds(pair * LANES, LANES)
        keys = k_out[:, lanes]
        values_of = with_ones(v_out[:, lanes])
        for part in range(2):
            rows = pl.ds(part * OWN, OWN)
            chosen = halves_of(q[rows, lanes])
            results = []
            for half in range(2):
                head = 2 * pair + half
                scores = dot_nt(chosen[half], keys) + bias[rows, :]
                before = highest_in[head, rows, :]
                highest = jnp.maximum(before, jnp.max(scores, axis=1, keepdims=True))
                weights = jnp.exp(scores - highest[:, 0:1]).astype(LOW)
                total = dot(weights, values_of[half]) + jnp.exp(before - highest) * summed_in[head, rows, :]
                turned = pltpu.roll(total, HEAD_DIM, 1)
                results.append(total / turned)
                log_total = highest + jnp.log(total if half == 1 else turned)
                log_columns[rows, :] = jnp.where(column == head, log_total, log_columns[rows, :])
            att_out[rows, lanes] = jnp.where(left, results[0], results[1]).astype(LOW)
    log_out[...] = jnp.transpose(log_columns[...])[0:8, :]


def attention(place, lengths, blocks, joint_weight, value_bias, q, summed, highest, after=()):
    def columns(kind):
        return joint_weight, pl.BlockSpec((WIDTH, HALF), lambda i, place, *_: (0, 2 * kind + place[3]))

    half_row = pl.BlockSpec((1, HALF), lambda i, place, *_: (0, place[3]))
    return call(
        attention_kernel,
        "attention",
        place,
        [plain(block) for block in blocks]
        + [columns(1), columns(2), (row_of(value_bias), half_row), plain(q), plain(summed), plain(highest)],
        [made((512, HALF), LOW)] * 3 + [made((8, 512), FLOAT)],
        scratch=[pltpu.VMEM((512, 512), FLOAT), pltpu.VMEM((512, LANES), FLOAT)],
        scalars=lengths,
        after=after,
        work=cost(4e9, 8e6, 3e6),
    )


def centred_norm(value):
    mean = jnp.mean(value, axis=-1, keepdims=True)
    centred = value - mean
    spread = jnp.mean(centred * centred, axis=-1, keepdims=True)
    inverse = lax.rsqrt(spread + EPSILON)
    return centred * inverse, inverse


def norm_back(grad, unit, inverse):
    mean = jnp.mean(grad, axis=-1, keepdims=True)
    along = jnp.mean(grad * unit, axis=-1, keepdims=True)
    return (grad - mean - unit * along) * inverse


def column_sum(value):
    return jnp.sum(value, axis=0, keepdims=True)


def forward_kernel(
    place, att, att_got, wo_own, wo_other, out_bias, x0, x1, gain1, shift1, up, up_bias, down,
    down_bias, gain2, shift2, cot0, cot1,
    result0, result1, feed_ext, second_grad, act_keep, act_send, slope, unit1, inverse1, normed_low, normed_t, att_t, sums,
    normed, feed, act_t,
):
    step = pl.program_id(0)
    c = place[3]

    @pl.when(step == 0)
    def _():
        tokens = jnp.concatenate([x0[...], x1[...]], axis=0).astype(FLOAT)
        att_own, att_other = att[0:OWN], att_got[OWN:]
        branch = dot(att_own, wo_own[...]) + dot(att_other, wo_other[...]) + out_bias[...]
        unit, inverse = centred_norm(tokens + branch)
        unit1[...] = unit
        inverse1[...] = jnp.broadcast_to(inverse, (OWN, LANES))
        value = unit * gain1[...] + shift1[...]
        normed[...] = value
        normed_low[...] = value.astype(LOW)
        normed_t[...] = jnp.transpose(value).astype(LOW)
        mine = pl.ds(pl.multiple_of(c * HALF, HALF), HALF)
        other = pl.ds(pl.multiple_of((1 - c) * HALF, HALF), HALF)
        att_t[mine, :] = jnp.transpose(att[...].astype(FLOAT)).astype(LOW)
        att_t[other, 0:OWN] = jnp.transpose(att_other.astype(FLOAT)).astype(LOW)
        att_t[other, OWN:] = jnp.transpose(att_got[0:OWN].astype(FLOAT)).astype(LOW)
        feed[...] = jnp.zeros_like(feed)

    inner = dot(normed_low[...], up[...]) + up_bias[...]
    below = 0.5 + 0.5 * lax.erf(inner * math.sqrt(0.5))
    density = jnp.exp(inner * inner * -0.5) * (1.0 / math.sqrt(2.0 * math.pi))
    activated = inner * below
    slope[...] = (below + inner * density).astype(LOW)
    low = activated.astype(LOW)
    act_t[...] = jnp.transpose(activated).astype(LOW).reshape(4, 2, DOWN_ROWS, OWN)
    act_keep[...] = act_t[:, c]
    act_send[...] = act_t[:, 1 - c]
    feed[...] += dot(low, down[...])

    @pl.when(step == pl.num_programs(0) - 1)
    def _():
        unit, inverse = centred_norm(normed[...] + feed[...] + down_bias[...])
        result = (unit * gain2[...] + shift2[...]).astype(LOW)
        result0[...] = result[0:BLOCK]
        result1[...] = result[BLOCK:]
        cotangent = jnp.concatenate([cot0[...], cot1[...]], axis=0).astype(FLOAT)
        grad = norm_back(cotangent * gain2[...], unit, inverse)
        second_grad[...] = grad
        low_grad = grad.astype(LOW)
        rows = jnp.concatenate(
            [
                column_sum(cotangent * unit),
                column_sum(cotangent),
                column_sum(low_grad.astype(FLOAT)),
                jnp.zeros((5, WIDTH), FLOAT),
            ],
            axis=0,
        )
        sums[...] = rows
        feed_ext[0:OWN] = low_grad
        feed_ext[OWN:] = jnp.concatenate([rows, jnp.zeros_like(rows)], axis=0).astype(LOW)


def row_of(vector):
    return vector.reshape(1, vector.shape[0])


def forward(place, att, att_got, tokens, cotangents, weights, after=()):
    chunk = WIDTH

    def vector(name):
        return plain(row_of(weights[name]))

    units = ((16, DOWN_ROWS, OWN), LOW, pl.BlockSpec((4, DOWN_ROWS, OWN), lambda i, place: (i, 0, 0)))
    return call(
        forward_kernel,
        "forward",
        place,
        [
            plain(att),
            plain(att_got),
            (weights["out"], pl.BlockSpec((HALF, WIDTH), lambda i, place: (place[3], 0))),
            (weights["out"], pl.BlockSpec((HALF, WIDTH), lambda i, place: (1 - place[3], 0))),
            vector("out_bias"), plain(tokens[0]), plain(tokens[1]), vector("gain1"), vector("shift1"),
            (weights["up"], pl.BlockSpec((WIDTH, chunk), lambda i, place: (0, i))),
            (row_of(weights["up_bias"]), pl.BlockSpec((1, chunk), lambda i, place: (0, i))),
            (weights["down"], pl.BlockSpec((chunk, WIDTH), lambda i, place: (i, 0))),
            vector("down_bias"), vector("gain2"), vector("shift2"), plain(cotangents[0]), plain(cotangents[1]),
        ],
        [
            made((BLOCK, WIDTH), LOW), made((BLOCK, WIDTH), LOW), made((EXT, WIDTH), LOW),
            made((OWN, WIDTH), FLOAT), units, units,
            ((OWN, FF), LOW, pl.BlockSpec((OWN, chunk), lambda i, place: (0, i))),
            made((OWN, WIDTH), FLOAT), made((OWN, LANES), FLOAT), made((OWN, WIDTH), LOW),
            made((WIDTH, OWN), LOW), made((WIDTH, 512), LOW), made((8, WIDTH), FLOAT),
        ],
        scratch=[
            pltpu.VMEM((OWN, WIDTH), FLOAT),
            pltpu.VMEM((OWN, WIDTH), FLOAT),
            pltpu.VMEM((4, 2, DOWN_ROWS, OWN), LOW),
        ],
        grid=(FF // chunk,),
        after=after,
        work=cost(2.7e9, 20e6, 2e6),
    )


def split_units(place, units, px_send, px, qy_send, qy):
    y, x = place[1], place[2]
    half = units.shape[2] // 2
    for line in range(2):
        px[0, line] = units[line, x, 0:half]
        px_send[0, line] = units[line, 1 - x, 0:half]
    for side in range(2):
        qy[0, side] = units[y, side, half:]
        qy_send[0, side] = units[1 - y, side, half:]


def unit_outputs(rows, width):
    shape = (4, 2, rows // 2, width)
    return [(shape, LOW, pl.BlockSpec((1,) + shape[1:], lambda i, place: (i, 0, 0, 0)))] * 4


def down_kernel(place, act, act_got, feed, feed_got, px_send, px, qy_send, qy, units):
    shape = (4 * DOWN_ROWS, OWN)
    total = dot(act[...].reshape(shape), feed[0:OWN]) + dot(act_got[...].reshape(shape), feed_got[0:OWN])
    units[...] = total.astype(LOW).reshape(units.shape)
    split_units(place, units, px_send, px, qy_send, qy)


def down_units(place, act, act_got, feed, feed_got, after=()):
    block = pl.BlockSpec((4, DOWN_ROWS, OWN), lambda i, place: (i, 0, 0))
    return call(
        down_kernel,
        "down_units",
        place,
        [(act, block), (act_got, block), plain(feed), plain(feed_got)],
        unit_outputs(DOWN_ROWS, WIDTH),
        scratch=[pltpu.VMEM((2, 2, DOWN_ROWS, WIDTH), LOW)],
        grid=(4,),
        after=after,
        work=cost(0.6e9, 3.5e6),
    )


def backward_kernel(
    place, feed_ext, slope, up, down, second_grad, unit1, inverse1, gain1, wo_own, wo_other,
    inner0, inner1, send0, send1, first_grad, branch_own, back_own, misc, sums,
    normed_grad, branch,
):
    step = pl.program_id(0)
    c = place[3]

    @pl.when(step == 0)
    def _():
        normed_grad[...] = second_grad[...]
        sums[...] = jnp.zeros_like(sums)

    grad = (dot_nt(feed_ext[0:OWN], down[...]) * slope[...].astype(FLOAT)).astype(LOW)
    for target, index in ((inner0, c), (inner1, 2 + c), (send0, 1 - c), (send1, 3 - c)):

        @pl.when(step == index)
        def _(target=target):
            target[...] = grad

    sums[pl.ds(4 + step, 1), :] = column_sum(grad.astype(FLOAT))
    normed_grad[...] += dot_nt(grad, up[...])

    @pl.when(step == pl.num_programs(0) - 1)
    def _():
        total = normed_grad[...]
        unit = unit1[...]
        sums[0:1, :] = column_sum(total * unit)
        sums[1:2, :] = column_sum(total)
        grad1 = norm_back(total * gain1[...], unit, inverse1[:, 0:1])
        first_grad[...] = grad1
        low = grad1.astype(LOW)
        branch[...] = low
        sums[2:3, :] = column_sum(low.astype(FLOAT))
        branch_own[...] = branch[:, pl.ds(pl.multiple_of(c * HALF, LANES), HALF)]
        back_own[...] = dot_nt(low, wo_own[...]).astype(LOW)
        misc[0:OWN, 0:HALF] = branch[:, pl.ds(pl.multiple_of((1 - c) * HALF, LANES), HALF)]
        misc[0:OWN, HALF:] = dot_nt(low, wo_other[...]).astype(LOW)
        rows = sums[...]
        misc[OWN:] = jnp.concatenate([rows, jnp.zeros_like(rows)], axis=0).astype(LOW)


def backward(place, feed_ext, slope, second_grad, unit1, inverse1, weights, after=()):
    chunk = WIDTH
    return call(
        backward_kernel,
        "backward",
        place,
        [
            plain(feed_ext),
            (slope, pl.BlockSpec((OWN, chunk), lambda i, place: (0, i))),
            (weights["up"], pl.BlockSpec((WIDTH, chunk), lambda i, place: (0, i))),
            (weights["down"], pl.BlockSpec((chunk, WIDTH), lambda i, place: (i, 0))),
            plain(second_grad), plain(unit1), plain(inverse1), plain(row_of(weights["gain1"])),
            (weights["out"], pl.BlockSpec((HALF, WIDTH), lambda i, place: (place[3], 0))),
            (weights["out"], pl.BlockSpec((HALF, WIDTH), lambda i, place: (1 - place[3], 0))),
        ],
        [made((OWN, WIDTH), LOW)] * 4
        + [
            made((OWN, WIDTH), FLOAT), made((OWN, HALF), LOW), made((OWN, HALF), LOW), made((EXT, WIDTH), LOW),
            made((8, WIDTH), FLOAT),
        ],
        scratch=[pltpu.VMEM((OWN, WIDTH), FLOAT), pltpu.VMEM((OWN, WIDTH), LOW)],
        grid=(FF // chunk,),
        after=after,
        work=cost(2.7e9, 16e6),
    )


def up_kernel(
    place, normed_t, normed_got, inner0, inner1, got0, got1, att_t, branch, misc, sums0, sums1, feed_got,
    x_send, y_send, px, qy, units, normed_got_t,
):
    z = pl.program_id(0)
    y, x = place[1], place[2]

    @pl.when(z == 0)
    def _():
        normed_got_t[...] = jnp.transpose(normed_got[...].astype(FLOAT)).astype(LOW)

    theirs = normed_got_t[pl.ds(pl.multiple_of(z * 192, 32), 192), :]
    outer = dot(att_t[:, 0:OWN], branch[...]) + dot(att_t[:, OWN:], misc[0:OWN, 0:HALF])
    for side, inner, got, sums, pair in ((0, inner0, got0, sums0, feed_got), (1, inner1, got1, sums1, misc)):
        grad = dot(normed_t[...], inner[...]) + dot(theirs, got[...])
        vectors = sums[...] + pair[OWN:].astype(FLOAT)[0:8]
        for line in range(2):
            first = line * 96 + side * 48
            rest = jnp.concatenate([outer[first : first + 24], outer[first + 24 : first + 48]], axis=1)
            units[line, side] = jnp.concatenate(
                [grad[line * 96 : line * 96 + 96], rest, vectors], axis=0
            ).astype(LOW)
    half = UP_ROWS // 2
    for index in range(2):
        rows = pl.ds(pl.multiple_of(DOWN_SENT + (z * 2 + index) * half, half), half)
        px[0, index] = units[index, x, 0:half]
        x_send[rows, :] = units[index, 1 - x, 0:half]
        qy[0, index] = units[y, index, half:]
        y_send[rows, :] = units[1 - y, index, half:]


def up_units(place, normed_t, normed_got, inner, got, att_t, branch, misc, sums0, sums1, feed_got, after=()):
    rows = pl.BlockSpec((192, OWN), lambda i, place: (i, 0))
    return call(
        up_kernel,
        "up_units",
        place,
        [
            (normed_t, rows), plain(normed_got), plain(inner[0]), plain(inner[1]), plain(got[0]), plain(got[1]),
            (att_t, pl.BlockSpec((192, 512), lambda i, place: (i, 0))),
            plain(branch), plain(misc), plain(sums0), plain(sums1), plain(feed_got),
        ],
        [made((DOWN_SENT + 4 * UP_ROWS, WIDTH), LOW)] * 2 + unit_outputs(UP_ROWS, WIDTH)[:2],
        scratch=[pltpu.VMEM((2, 2, UP_ROWS, WIDTH), LOW), pltpu.VMEM((WIDTH, OWN), LOW)],
        grid=(4,),
        after=after,
        work=cost(0.9e9, 5e6),
    )


def attention_back_kernel(
    place, own_lengths, peer_lengths, q, k0, k1, v0, v1, log_total, att, back0, misc,
    dq_out, dk_out, dv_out, bias,
):
    bases = first_positions(place)
    ends = pair_ends(place, own_lengths, peer_lengths)
    query_ids = [pairs_along(base, ends, 1)[0:1] for base in bases[:4]]
    for j in range(8):
        key_ids = pairs_along(bases[j], ends, 0)
        for i in range(4):
            bias[pl.ds(j * BLOCK, BLOCK), pl.ds(i * BLOCK, BLOCK)] = jnp.where(
                key_ids == query_ids[i], 0.0, NEGATIVE
            )
    for pair in range(PAIRS_OF_HEADS):
        lanes = pl.ds(pair * LANES, LANES)
        keys = jnp.concatenate([k0[:, lanes], k1[:, lanes]], axis=0)
        values = jnp.concatenate([v0[:, lanes], v1[:, lanes]], axis=0)
        keys_t = jnp.transpose(keys.astype(FLOAT)).astype(LOW)
        key_grad = jnp.zeros((1024, LANES), FLOAT)
        value_grad = jnp.zeros((1024, LANES), FLOAT)
        left = head_mask(OWN)
        for part in range(2):
            rows = pl.ds(part * OWN, OWN)
            queries = q[rows, lanes]
            grads = back0[:, lanes] if part == 0 else misc[0:OWN, pl.ds(HALF + pair * LANES, LANES)]
            zeros = jnp.zeros_like(queries)
            product = jnp.transpose(grads.astype(FLOAT) * att[rows, lanes].astype(FLOAT))
            halves = []
            for half in range(2):
                if half == 0:
                    chosen, chosen_grads = jnp.where(left, queries, zeros), jnp.where(left, grads, zeros)
                else:
                    chosen, chosen_grads = jnp.where(left, zeros, queries), jnp.where(left, zeros, grads)
                delta = column_sum(product[half * HEAD_DIM : (half + 1) * HEAD_DIM])
                head = pair * 2 + half
                scores = dot_nt(keys, chosen) + bias[:, rows]
                weights = jnp.exp(scores - log_total[head : head + 1, rows])
                weight_grad = dot_nt(values, chosen_grads)
                score_grad = (weights * (weight_grad - delta)).astype(LOW)
                value_grad = value_grad + dot(weights.astype(LOW), chosen_grads)
                key_grad = key_grad + dot(score_grad, chosen)
                halves.append(dot(keys_t, score_grad))
            query_grad_t = jnp.concatenate([halves[0][0:HEAD_DIM], halves[1][HEAD_DIM:LANES]], axis=0)
            dq_out[rows, lanes] = (jnp.transpose(query_grad_t) * HEAD_DIM**-0.5).astype(LOW)
        dk_out[:, lanes] = key_grad.astype(LOW)
        dv_out[:, lanes] = value_grad.astype(LOW)


def attention_back(place, lengths, q, keys, values, log_total, att, back_own, misc, after=()):
    return call(
        attention_back_kernel,
        "attention_back",
        place,
        [plain(array) for array in (q, *keys, *values, log_total, att, back_own, misc)],
        [made((512, HALF), LOW), made((1024, HALF), LOW), made((1024, HALF), LOW)],
        scratch=[pltpu.VMEM((1024, 512), FLOAT)],
        scalars=lengths,
        after=after,
        work=cost(7e9, 6e6, 3e6),
    )


def token_kernel(place, dq, dk, dv, wq, wk, wv, own, own_send, far, far_send):
    for part, target in enumerate((own, own_send, far, far_send)):
        rows = pl.ds(part * OWN, OWN)
        total = dot_nt(dk[rows, :], wk[...]) + dot_nt(dv[rows, :], wv[...])
        if part < 2:
            total = total + dot_nt(dq[rows, :], wq[...])
        target[...] = total.astype(LOW)


def token_parts(place, dq, dk, dv, joint_weight, after=()):
    def columns(kind):
        return joint_weight, pl.BlockSpec((WIDTH, HALF), lambda i, place: (0, 2 * kind + place[3]))

    return call(
        token_kernel,
        "token_parts",
        place,
        [plain(dq), plain(dk), plain(dv), columns(0), columns(1), columns(2)],
        [made((OWN, WIDTH), LOW)] * 4,
        after=after,
        work=cost(1.5e9, 5e6),
    )


def token_last_kernel(place, own, own_got, across, first_grad, token0, token1):
    total = own[...].astype(FLOAT) + own_got[...].astype(FLOAT) + across[8 * JOINT_SECOND :].astype(FLOAT) + first_grad[...]
    total = total.astype(LOW)
    token0[...] = total[0:BLOCK]
    token1[...] = total[BLOCK:]


def token_last(place, arrays, after=()):
    return call(
        token_last_kernel,
        "token_last",
        place,
        [plain(array) for array in arrays],
        [made((BLOCK, WIDTH), LOW)] * 2,
        after=after,
        work=cost(1e6, 2e6),
    )


def back_rows_kernel(place, done0, done1, back0, back1, outputs, token_grad):
    odd = place[0] % 2
    outputs[odd] = done0[...]
    outputs[1 - odd] = done1[...]
    token_grad[odd] = back0[...].astype(FLOAT)
    token_grad[1 - odd] = back1[...].astype(FLOAT)


def back_rows(place, done, back, after=()):
    return call(
        back_rows_kernel,
        "back_rows",
        place,
        [plain(array) for array in (*done, *back)],
        [made((2, BLOCK, WIDTH), LOW), made((2, BLOCK, WIDTH), FLOAT)],
        after=after,
        work=cost(1e6, 2e6),
    )


def joint_kernel(
    place, t0, t1, t2, t3, t4, t5, t6, t7, dq, dk, dv, far, far_got, px_send, px, qy_send, qy, tokens_t, units
):
    y, x = place[1], place[2]
    qy_send[pl.ds(8 * JOINT_SECOND, OWN), :] = added(far[...], far_got[...])
    for index, block in enumerate((t0, t1, t2, t3, t4, t5, t6, t7)):
        tokens_t[:, pl.ds(index * BLOCK, BLOCK)] = jnp.transpose(block[...].astype(FLOAT)).astype(LOW)
    biases = jnp.concatenate([column_sum(dq[...].astype(FLOAT)), column_sum(dv[...].astype(FLOAT))], axis=1)
    biases = jnp.concatenate([biases, jnp.zeros((7, WIDTH), FLOAT)], axis=0)
    for z in range(4):
        rows = pl.ds(z * 192, 192)
        query = dot(tokens_t[rows, 0:512], dq[...])
        key = dot(tokens_t[rows, :], dk[...])
        value = dot(tokens_t[rows, :], dv[...])
        for line in range(2):
            for side in range(2):
                at = line * 96 + side * 48
                units[line, side, 0:JOINT_FIRST] = jnp.concatenate(
                    [query[at : at + 48], key[at : at + 48]], axis=1
                ).astype(LOW)
                rest = jnp.concatenate([value[at : at + 24], value[at + 24 : at + 48]], axis=1)
                units[line, side, JOINT_FIRST:] = jnp.concatenate([rest, biases], axis=0).astype(LOW)
        for line in range(2):
            px[z, line] = units[line, x, 0:JOINT_FIRST]
            px_send[z, line] = units[line, 1 - x, 0:JOINT_FIRST]
        for side in range(2):
            qy[z, side] = units[y, side, JOINT_FIRST:]
            qy_send[pl.ds((z * 2 + side) * JOINT_SECOND, JOINT_SECOND), :] = units[1 - y, side, JOINT_FIRST:]


def joint_units(place, blocks, dq, dk, dv, far, far_got, after=()):
    first, second = made((4, 2, JOINT_FIRST, WIDTH), LOW), made((4, 2, JOINT_SECOND, WIDTH), LOW)
    return call(
        joint_kernel,
        "joint_units",
        place,
        [plain(array) for array in (*blocks, dq, dk, dv, far, far_got)],
        [first, first, made((8 * JOINT_SECOND + OWN, WIDTH), LOW), second],
        scratch=[pltpu.VMEM((WIDTH, 1024), LOW), pltpu.VMEM((2, 2, JOINT_ROWS, WIDTH), LOW)],
        after=after,
        work=cost(1.5e9, 6e6),
    )


def added(left, right):
    return (left.astype(FLOAT) + right.astype(FLOAT)).astype(LOW)


def down_pair_kernel(place, px, px_got, qy, qy_got, x_in, y_in, x_send, y_send, p, q):
    y, x = place[1], place[2]
    p[0] = added(px[0, y], px_got[0, y])
    y_send[...] = added(px[0, 1 - y], px_got[0, 1 - y])
    q[0] = added(qy[0, x], qy_got[0, x])
    x_send[...] = added(qy[0, 1 - x], qy_got[0, 1 - x])


def down_pair_stage(place, arrays, x_send, y_send, after=()):
    half = DOWN_ROWS // 2
    block = pl.BlockSpec((1, 2, half, WIDTH), lambda i, place: (i, 0, 0, 0))
    sent = (x_send.shape, LOW, pl.BlockSpec((half, WIDTH), lambda i, place: (i, 0)))
    kept = ((4, half, WIDTH), LOW, pl.BlockSpec((1, half, WIDTH), lambda i, place: (i, 0, 0)))
    anywhere = pl.BlockSpec(memory_space=pl.ANY)
    return call(
        down_pair_kernel,
        "down_pair_stage",
        place,
        [(array, block) for array in arrays] + [(x_send, anywhere), (y_send, anywhere)],
        [sent, sent, kept, kept],
        grid=(4,),
        after=after,
        work=cost(1e6, 1e7),
        aliases=((4, 0), (5, 1)),
    )


def second_kernel(
    place, x_got, y_got, px, qy, down_p, down_q, x_send, y_send, p, q, down_send, down_keep
):
    z_here, y, x = place[0], place[1], place[2]
    half = UP_ROWS // 2
    for z in range(4):
        for got, have, own, keep, send in ((x_got, px, y, p, y_send), (y_got, qy, x, q, x_send)):
            at = DOWN_SENT + z * UP_ROWS
            mine = pl.ds(pl.multiple_of(at + own * half, half), half)
            other = pl.ds(pl.multiple_of(at + (1 - own) * half, half), half)
            keep[z] = added(have[z, own], got[mine, :])
            send[pl.ds(z * half, half), :] = added(have[z, 1 - own], got[other, :])
    low = z_here % 2
    small = DOWN_ROWS // 2
    for target, parity in ((down_keep, low), (down_send, 1 - low)):
        for high in range(2):
            index = 2 * high + parity
            rows = pl.ds(pl.multiple_of(index * small, small), small)
            target[high, 0:small] = added(down_p[index], y_got[rows, :])
            target[high, small:] = added(down_q[index], x_got[rows, :])


def second_stage(place, arrays, after=()):
    kept = made((4, UP_ROWS // 2, WIDTH), LOW)
    down = made((2, DOWN_ROWS, WIDTH), LOW)
    return call(
        second_kernel,
        "second_stage",
        place,
        [plain(array) for array in arrays],
        [made((OWN, WIDTH), LOW), made((OWN, WIDTH), LOW), kept, kept, down, down],
        after=after,
        work=cost(1e6, 1e7),
    )


def joint_pair_kernel(place, px, px_got, qy, qy_got, x_send, y_send, p, q):
    y, x = place[1], place[2]
    for z in range(4):
        p[z] = added(px[z, y], px_got[z, y])
        y_send[z] = added(px[z, 1 - y], px_got[z, 1 - y])


        def from_y(side):
            return qy_got[pl.ds(pl.multiple_of((z * 2 + side) * JOINT_SECOND, 32), JOINT_SECOND), :]

        q[z] = added(qy[z, x], from_y(x))
        x_send[z] = added(qy[z, 1 - x], from_y(1 - x))


def joint_pair_stage(place, arrays, after=()):
    first, second = made((4, JOINT_FIRST, WIDTH), LOW), made((4, JOINT_SECOND, WIDTH), LOW)
    return call(
        joint_pair_kernel,
        "joint_pair_stage",
        place,
        [plain(array) for array in arrays],
        [second, first, first, second],
        after=after,
        work=cost(1e6, 1e7),
    )


def up_line_kernel(place, x_got, y_got, p, q, down_two, down_got, send, keep, down_send, down_keep):
    low, high_here = place[0] % 2, place[0] // 2
    half = UP_ROWS // 2
    for target, parity in ((keep, low), (send, 1 - low)):
        for high in range(2):
            index = 2 * high + parity
            rows = pl.ds(pl.multiple_of(index * half, half), half)
            target[high, 0:half] = added(p[index], y_got[rows, :])
            target[high, half:] = added(q[index], x_got[rows, :])
    down_keep[...] = added(down_two[high_here], down_got[high_here])
    down_send[...] = added(down_two[1 - high_here], down_got[1 - high_here])


def up_line_stage(place, arrays, after=()):
    return call(
        up_line_kernel,
        "up_line_stage",
        place,
        [plain(array) for array in arrays],
        [made((2, UP_ROWS, WIDTH), LOW)] * 2 + [made((DOWN_ROWS, WIDTH), LOW)] * 2,
        after=after,
        work=cost(1e6, 1e7),
    )


def joint_line_kernel(place, x_got, y_got, p, q, send, keep):
    low = place[0] % 2
    for target, parity in ((keep, low), (send, 1 - low)):
        for high in range(2):
            index = 2 * high + parity
            target[high, 0:JOINT_FIRST] = added(p[index], y_got[index])
            target[high, JOINT_FIRST:] = added(q[index], x_got[index])


def joint_line_stage(place, arrays, after=()):
    return call(
        joint_line_kernel,
        "joint_line_stage",
        place,
        [plain(array) for array in arrays],
        [made((2, JOINT_ROWS, WIDTH), LOW)] * 2,
        after=after,
        work=cost(1e6, 1e6),
    )


def end_stage_kernel(place, keep_two, got, send, keep):
    high = place[0] // 2
    keep[...] = added(keep_two[high], got[high])
    send[...] = added(keep_two[1 - high], got[1 - high])


def end_stage(place, keep_two, got, after=()):
    return call(
        end_stage_kernel,
        "end_stage",
        place,
        [plain(keep_two), plain(got)],
        [made(keep_two.shape[1:], LOW)] * 2,
        after=after,
        work=cost(1e6, 1e6),
    )


def last_sum_kernel(place, *refs):
    out = refs[-1]
    at = 0
    for first, second in zip(refs[0:-1:2], refs[1:-1:2]):
        out[pl.ds(at, first.shape[0]), :] = added(first[...], second[...])
        at += first.shape[0]


def last_sum(place, pairs, after=()):
    arrays = [array for pair in pairs for array in pair]
    rows = sum(pair[0].shape[0] for pair in pairs)
    results, mark = call(
        last_sum_kernel,
        "last_sum",
        place,
        [plain(array) for array in arrays],
        [made((rows, arrays[0].shape[1]), LOW)],
        after=after,
        work=cost(1e6, 1e6),
    )
    return results[0], mark


def gathered(unit):
    across = x_swap(unit)
    return unit, core_swap(unit), across, core_swap(across)


def quarters(place):
    x, c = place[2], place[3]
    return (x, c), (x, 1 - c), (1 - x, c), (1 - x, 1 - c)


def line_shift(place):
    seq = place[0] * 2 + place[1]
    return lax.rem(WIDTH - seq * 96, WIDTH)


def dense_out_kernel(
    place, u0, u1, u2, u3, down, up, out, gain2, shift2, down_bias, gain1, shift1, out_bias, up_bias, heads, tails
):
    for unit, (x, c) in zip((u0, u1, u2, u3), quarters(place)):
        quarter = 2 * x + c
        down[pl.ds(pl.multiple_of(quarter * DOWN_ROWS, 32), DOWN_ROWS), :] = unit[0:DOWN_ROWS, :].astype(FLOAT)
        up[:, pl.ds(pl.multiple_of(quarter * WIDTH, LANES), WIDTH)] = unit[96:192, :].astype(FLOAT)
        rest = unit[192:224, :].astype(FLOAT)
        lanes = pl.ds(pl.multiple_of(c * HALF, LANES), HALF)
        out[pl.ds(pl.multiple_of(x * 48, 8), 24), lanes] = rest[0:24, 0:HALF]
        out[pl.ds(pl.multiple_of(x * 48 + 24, 8), 24), lanes] = rest[0:24, HALF:]

        @pl.when(x == 0)
        def _(rest=rest):
            heads[...] = rest[24:32]

        @pl.when(x == 1)
        def _(rest=rest):
            tails[...] = rest[24:32]

    seq = place[0] * 2 + place[1]
    shift = line_shift(place)
    head = pltpu.roll(heads[...], shift, 1)
    gain2[...] = head[0:1, 0:96]
    shift2[...] = head[1:2, 0:96]
    down_bias[...] = head[2:3, 0:96]
    tail = pltpu.roll(tails[...], shift, 1)
    gain1[...] = tail[0:1, 0:96]
    shift1[...] = tail[1:2, 0:96]
    out_bias[...] = tail[2:3, 0:96]
    wide = tails[pl.ds(4 + seq // 2, 1), :]
    up_bias[...] = jnp.where(seq % 2 == 0, wide[:, 0:HALF], wide[:, HALF:])


def dense_outputs(place, units, after=()):
    results, mark = call(
        dense_out_kernel,
        "dense_outputs",
        place,
        [plain(unit) for unit in units],
        [made((4 * DOWN_ROWS, WIDTH), FLOAT), made((96, FF), FLOAT), made((96, WIDTH), FLOAT)]
        + [made((1, 96), FLOAT)] * 6
        + [made((1, HALF), FLOAT)],
        scratch=[pltpu.VMEM((8, WIDTH), FLOAT)] * 2,
        after=after,
        work=cost(1e6, 3e6),
    )
    return (*results[:3], *(vector.reshape(-1) for vector in results[3:])), mark


def joint_out_kernel(place, u0, u1, u2, u3, joint, query_bias, value_bias, sums):
    for unit, (x, c) in zip((u0, u1, u2, u3), quarters(place)):

        def lanes(kind):
            return pl.ds(pl.multiple_of(kind * WIDTH + c * HALF, LANES), HALF)

        first = unit[0:JOINT_FIRST].astype(FLOAT)
        rest = unit[JOINT_FIRST:].astype(FLOAT)
        rows = pl.ds(pl.multiple_of(x * 48, 16), 48)
        joint[rows, lanes(0)] = first[:, 0:HALF]
        joint[rows, lanes(1)] = first[:, HALF:]
        joint[pl.ds(pl.multiple_of(x * 48, 8), 24), lanes(2)] = rest[0:24, 0:HALF]
        joint[pl.ds(pl.multiple_of(x * 48 + 24, 8), 24), lanes(2)] = rest[0:24, HALF:]

        @pl.when(x == 0)
        def _(rest=rest, c=c):
            half = pl.ds(pl.multiple_of(c * HALF, LANES), HALF)
            sums[0:1, half] = rest[24:25, 0:HALF]
            sums[1:2, half] = rest[24:25, HALF:]

    turned = pltpu.roll(sums[...], line_shift(place), 1)
    query_bias[...] = turned[0:1, 0:96]
    value_bias[...] = turned[1:2, 0:96]


def joint_outputs(place, units, after=()):
    results, mark = call(
        joint_out_kernel,
        "joint_outputs",
        place,
        [plain(unit) for unit in units],
        [made((96, 3 * WIDTH), FLOAT), made((1, 96), FLOAT), made((1, 96), FLOAT)],
        scratch=[pltpu.VMEM((8, WIDTH), FLOAT)],
        after=after,
        work=cost(1e6, 2e6),
    )
    return (results[0], results[1].reshape(-1), results[2].reshape(-1)), mark


def row_body(
    tokens,
    pair_lengths,
    joint_weight,
    query_bias,
    value_bias,
    out_weight,
    out_bias,
    first_gain,
    first_shift,
    up_weight,
    up_bias,
    down_weight,
    down_bias,
    second_gain,
    second_shift,
    cotangent,
):
    seq, rows = lax.axis_index("seq"), lax.axis_index("rows")
    z, y, x, c = seq // 2, seq % 2, rows // 2, rows % 2
    place = jnp.stack([z, y, x, c]).astype(jnp.int32)
    odd = z % 2
    weights = {
        "out": out_weight, "out_bias": out_bias, "gain1": first_gain, "shift1": first_shift,
        "up": up_weight, "up_bias": up_bias, "down": down_weight, "down_bias": down_bias,
        "gain2": second_gain, "shift2": second_shift,
    }

    def local_row(array, index):
        return lax.dynamic_index_in_dim(array, index, 0, keepdims=False)

    own = [row_swap(local_row(tokens, odd), 0), row_swap(local_row(tokens, 1 - odd), 1)]
    lengths = (pair_lengths, core_swap(pair_lengths))
    across = [y_swap(block) for block in own]
    here = own + [core_swap(block) for block in own]
    (q, k_here, v_here, summed, highest), mark = first_attention(
        place, lengths, here, joint_weight, query_bias, value_bias
    )
    across[0], across[1], mark = lax.optimization_barrier((across[0], across[1], mark))
    there = across + [core_swap(block) for block in across]
    blocks = here + there
    cotangents = [row_swap(local_row(cotangent, odd), 0), row_swap(local_row(cotangent, 1 - odd), 1)]
    (att, k_there, v_there, log_total), mark = attention(
        place, lengths, there, joint_weight, value_bias, q, summed, highest, (mark, *cotangents)
    )
    att_got = core_swap(att)
    results, mark = forward(place, att, att_got, own, cotangents, weights, (mark,))
    (
        result0, result1, feed, second_grad, act, act_send, slope, unit1, inverse1, normed, normed_t, att_t, sums0
    ) = results
    act_got, feed_got, normed_got = core_swap(act_send), core_swap(feed), core_swap(normed)
    done = (row_swap(result0, 0), row_swap(result1, 1))
    (px_send, px, qy_send, qy), mark = down_units(place, act, act_got, feed, feed_got, (mark,))
    down_pair = (px, x_swap(px_send), qy, y_swap(qy_send))
    results, mark = backward(place, feed, slope, second_grad, unit1, inverse1, weights, (mark, normed_got))
    inner0, inner1, send0, send1, first_grad, branch_own, back_own, misc_send, sums1 = results
    got, misc = (core_swap(send0), core_swap(send1)), core_swap(misc_send)
    (x_send, y_send, px, qy), mark = up_units(
        place, normed_t, normed_got, (inner0, inner1), got, att_t, branch_own, misc, sums0, sums1, feed_got, (mark,)
    )
    (x_send, y_send, down_p, down_q), mark = down_pair_stage(place, down_pair, x_send, y_send, (mark,))
    x_got, y_got = x_swap(x_send), y_swap(y_send)
    (dq, dk, dv), mark = attention_back(
        place, lengths, q, (k_here, k_there), (v_here, v_there), log_total, att, back_own, misc, (mark,)
    )
    (token_own, own_send, token_far, far_send), mark = token_parts(place, dq, dk, dv, joint_weight, (mark, *done))
    own_got, far_got = core_swap(own_send), core_swap(far_send)
    (px_send, joint_px, qy_send, joint_qy), mark = joint_units(
        place, blocks, dq, dk, dv, token_far, far_got, (mark,)
    )
    (x_send, y_send, p, q_, down_send, down_two), mark = second_stage(
        place, (x_got, y_got, px, qy, down_p, down_q), (mark,)
    )
    x_got, y_got, down_got = x_swap(x_send), y_swap(y_send), z_swap(down_send, 1)
    px_send, qy_send, mark = lax.optimization_barrier((px_send, qy_send, mark))
    across = y_swap(qy_send)
    joint_pair = (joint_px, x_swap(px_send), joint_qy, across)
    (up_send, up_two, down_send, down_keep), mark = up_line_stage(
        place, (x_got, y_got, p, q_, down_two, down_got), (mark,)
    )
    up_got, down_got = z_swap(up_send, 1), z_swap(down_send, 2)
    (up_send, up_keep), mark = end_stage(place, up_two, up_got, (mark, down_got))
    up_got = z_swap(up_send, 2)
    (x_send, y_send, joint_p, joint_q), mark = joint_pair_stage(place, joint_pair, (mark,))
    joint_x_got, joint_y_got = x_swap(x_send), y_swap(y_send)
    (token0, token1), mark = token_last(place, (token_own, own_got, across, first_grad), (mark,))
    back = (row_swap(token0, 0), row_swap(token1, 1))
    dense_unit, mark = last_sum(place, ((down_keep, down_got), (up_keep, up_got)), (mark,))
    dense_all = gathered(dense_unit)
    (joint_send, joint_two), mark = joint_line_stage(place, (joint_x_got, joint_y_got, joint_p, joint_q), (mark,))
    joint_got = z_swap(joint_send, 1)
    (joint_send, joint_keep), mark = end_stage(place, joint_two, joint_got, (mark,))
    joint_got = z_swap(joint_send, 2)
    (outputs, token_grad), mark = back_rows(place, done, back, (mark,))
    joint_unit, mark = last_sum(place, ((joint_keep, joint_got),), (mark,))
    joint_all = gathered(joint_unit)
    (
        down_grad, up_grad, out_grad, second_gain_grad, second_shift_grad, down_bias_grad, first_gain_grad,
        first_shift_grad, out_bias_grad, up_bias_grad,
    ), mark = dense_outputs(place, dense_all, (mark,))
    (joint_grad, query_bias_grad, value_bias_grad), mark = joint_outputs(place, joint_all, (mark,))
    return (
        outputs,
        token_grad,
        joint_grad,
        query_bias_grad,
        value_bias_grad,
        out_grad,
        out_bias_grad,
        first_gain_grad,
        first_shift_grad,
        up_grad,
        up_bias_grad,
        down_grad,
        down_bias_grad,
        second_gain_grad,
        second_shift_grad,
    )


def body(tokens, *others):
    if (lax.axis_size("seq"), lax.axis_size("rows")) == (8, 4) and tokens.shape == (2, BLOCK, WIDTH):
        return row_body(tokens, *others)
    return general_body(tokens, *others)


def solution(mesh):
    placed = (
        P("rows", "seq", None),
        P("rows", None),
        P(),
        P(),
        P(),
        P(),
        P(),
        P(),
        P(),
        P(),
        P(),
        P(),
        P(),
        P(),
        P(),
        P("rows", "seq", None),
    )
    return jax.shard_map(
        body,
        mesh=mesh,
        in_specs=placed,
        out_specs=(
            P("rows", "seq", None),
            P("rows", "seq", None),
            P("seq", None),
            P("seq"),
            P("seq"),
            P("seq", None),
            P("seq"),
            P("seq"),
            P("seq"),
            P("seq", None),
            P("seq"),
            P("seq", None),
            P("seq"),
            P("seq"),
            P("seq"),
        ),
        check_vma=False,
    )
```

```python
import functools
import math

import jax
import jax.numpy as jnp
from jax import lax
from jax.experimental import pallas as pl
from jax.experimental.pallas import tpu as pltpu
from jax.sharding import PartitionSpec as P

HEADS = 12
HEAD_DIM = 64


NEGATIVE = -1e30
EPSILON = 1e-12


def from_behind(value, axis, steps):
    count = lax.axis_size(axis)
    pairs = [(source, (source + steps) % count) for source in range(count)]
    return lax.ppermute(value, axis, pairs)


def layer_norm(value, gain, shift):
    mean = jnp.mean(value, axis=-1, keepdims=True)
    centred = value - mean
    spread = jnp.mean(centred * centred, axis=-1, keepdims=True)
    return centred * lax.rsqrt(spread + EPSILON) * gain + shift


def gelu_exact(value):
    return jax.nn.gelu(value, approximate=False)


def pair_index(positions, ends):
    return jnp.sum((positions[None, :, None] >= ends[:, None, :]).astype(jnp.int32), axis=2)


def split_heads(array):
    return array.reshape(array.shape[0], array.shape[1], HEADS, HEAD_DIM)


def online_block(state, query_heads, query_pairs, key_block, value_block, key_pairs):
    highest, total, summed = state
    scores = jnp.einsum(
        "rqhd,rkhd->rhqk", query_heads, split_heads(key_block), preferred_element_type=jnp.float32
    ) * HEAD_DIM ** (-0.5)
    allowed = query_pairs[:, None, :, None] == key_pairs[:, None, None, :]
    masked = jnp.where(allowed, scores, NEGATIVE)
    new_high = jnp.maximum(highest, jnp.max(masked, axis=3))
    weights = jnp.where(allowed, jnp.exp(masked - new_high[..., None]), 0.0)
    factor = jnp.exp(highest - new_high)
    total = total * factor + jnp.sum(weights, axis=3)
    summed = summed * jnp.swapaxes(factor, 1, 2)[..., None] + jnp.einsum(
        "rhqk,rkhd->rqhd",
        weights.astype(jnp.bfloat16),
        split_heads(value_block),
        preferred_element_type=jnp.float32,
    )
    return (new_high, total, summed)


def tile_terms(queries, out_grad, log_total, delta, query_pairs, keys, values, key_pairs):
    scale = HEAD_DIM ** (-0.5)
    query_heads = split_heads(queries)
    grad_heads = split_heads(out_grad)
    key_heads = split_heads(keys)
    value_heads = split_heads(values)
    scores = (
        jnp.einsum("rqhd,rkhd->rhqk", query_heads, key_heads, preferred_element_type=jnp.float32)
        * scale
    )
    allowed = query_pairs[:, None, :, None] == key_pairs[:, None, None, :]
    weights = jnp.where(
        allowed, jnp.exp(jnp.where(allowed, scores, NEGATIVE) - log_total[..., None]), 0.0
    )
    weight_grad = jnp.einsum(
        "rqhd,rkhd->rhqk", grad_heads, value_heads, preferred_element_type=jnp.float32
    )
    score_grad = (weights * (weight_grad - delta[..., None])).astype(jnp.bfloat16)
    query_term = (
        jnp.einsum("rhqk,rkhd->rqhd", score_grad, key_heads, preferred_element_type=jnp.float32)
        * scale
    )
    key_term = (
        jnp.einsum("rhqk,rqhd->rkhd", score_grad, query_heads, preferred_element_type=jnp.float32)
        * scale
    )
    value_term = jnp.einsum(
        "rhqk,rqhd->rkhd",
        weights.astype(jnp.bfloat16),
        grad_heads,
        preferred_element_type=jnp.float32,
    )
    return (
        query_term.reshape(queries.shape),
        key_term.reshape(keys.shape),
        value_term.reshape(values.shape),
    )


def general_body(
    tokens,
    pair_lengths,
    joint_weight,
    query_bias,
    value_bias,
    out_weight,
    out_bias,
    first_gain,
    first_shift,
    up_weight,
    up_bias,
    down_weight,
    down_bias,
    second_gain,
    second_shift,
    cotangent,
):
    rows_here, seq_here, width = tokens.shape
    count = lax.axis_size("seq")
    cycle_index = lax.axis_index("seq")
    ends = jnp.cumsum(pair_lengths, axis=1)
    offsets = jnp.arange(seq_here, dtype=jnp.int32)
    own_pairs = pair_index(cycle_index * seq_here + offsets, ends)
    block_shape = (rows_here, seq_here, width)
    flat = tokens.reshape(rows_here * seq_here, width)
    projected = jnp.dot(flat, joint_weight, preferred_element_type=jnp.float32)
    queries = (projected[:, :width] + query_bias).astype(jnp.bfloat16).reshape(block_shape)
    keys = projected[:, width : 2 * width].astype(jnp.bfloat16).reshape(block_shape)
    values = (projected[:, 2 * width :] + value_bias).astype(jnp.bfloat16).reshape(block_shape)
    query_heads = split_heads(queries)
    initial = (
        jnp.full((rows_here, HEADS, seq_here), NEGATIVE, jnp.float32),
        jnp.zeros((rows_here, HEADS, seq_here), jnp.float32),
        jnp.zeros((rows_here, seq_here, HEADS, HEAD_DIM), jnp.float32),
    )
    key_piece = lax.all_gather(keys, "seq", axis=1, tiled=True)
    value_piece = lax.all_gather(values, "seq", axis=1, tiled=True)
    length = key_piece.shape[1]
    block = math.gcd(length, seq_here)

    def one_block(index, inner_state):
        first = index * block
        key_block = lax.dynamic_slice_in_dim(key_piece, first, block, 1)
        value_block = lax.dynamic_slice_in_dim(value_piece, first, block, 1)
        key_pairs = pair_index(first + jnp.arange(block, dtype=jnp.int32), ends)
        return online_block(inner_state, query_heads, own_pairs, key_block, value_block, key_pairs)

    highest, total, summed = lax.fori_loop(0, length // block, one_block, initial)
    log_total = highest + jnp.log(total)
    attended = (
        (summed / jnp.swapaxes(total, 1, 2)[..., None]).astype(jnp.bfloat16).reshape(flat.shape)
    )
    branch = jnp.dot(attended, out_weight, preferred_element_type=jnp.float32) + out_bias
    first_sum = flat.astype(jnp.float32) + branch
    normed, first_back = jax.vjp(layer_norm, first_sum, first_gain, first_shift)
    normed_low = normed.astype(jnp.bfloat16)
    inner = jnp.dot(normed_low, up_weight, preferred_element_type=jnp.float32) + up_bias
    activated_full, gelu_back = jax.vjp(gelu_exact, inner)
    activated = activated_full.astype(jnp.bfloat16)
    feed = jnp.dot(activated, down_weight, preferred_element_type=jnp.float32) + down_bias
    second_sum = normed + feed
    result, second_back = jax.vjp(layer_norm, second_sum, second_gain, second_shift)
    outputs = result.astype(jnp.bfloat16).reshape(tokens.shape)
    second_grad, second_gain_grad, second_shift_grad = second_back(
        cotangent.astype(jnp.float32).reshape(flat.shape)
    )
    feed_grad = second_grad.astype(jnp.bfloat16)
    down_grad = jnp.einsum("ti,tj->ij", activated, feed_grad, preferred_element_type=jnp.float32)
    down_bias_grad = jnp.sum(feed_grad.astype(jnp.float32), axis=0)
    activated_grad = jnp.einsum(
        "tj,ij->ti", feed_grad, down_weight, preferred_element_type=jnp.float32
    )
    inner_grad = gelu_back(activated_grad)[0].astype(jnp.bfloat16)
    up_grad = jnp.einsum("ti,tj->ij", normed_low, inner_grad, preferred_element_type=jnp.float32)
    up_bias_grad = jnp.sum(inner_grad.astype(jnp.float32), axis=0)
    normed_grad = second_grad + jnp.einsum(
        "tj,ij->ti", inner_grad, up_weight, preferred_element_type=jnp.float32
    )
    first_grad, first_gain_grad, first_shift_grad = first_back(normed_grad)
    branch_grad = first_grad.astype(jnp.bfloat16)
    out_grad = jnp.einsum("ti,tj->ij", attended, branch_grad, preferred_element_type=jnp.float32)
    out_bias_grad = jnp.sum(branch_grad.astype(jnp.float32), axis=0)
    attended_grad = jnp.einsum(
        "tj,ij->ti", branch_grad, out_weight, preferred_element_type=jnp.float32
    ).astype(jnp.bfloat16)
    delta = jnp.sum(
        (attended_grad.astype(jnp.float32) * attended.astype(jnp.float32)).reshape(
            rows_here, seq_here, HEADS, HEAD_DIM
        ),
        axis=3,
    )
    delta = jnp.swapaxes(delta, 1, 2)
    attended_grad = attended_grad.reshape(block_shape)
    zeros_block = jnp.zeros(block_shape, jnp.float32)

    def send_key_sums(sums):
        return (
            from_behind(sums[0].astype(jnp.bfloat16), "seq", 1).astype(jnp.float32),
            from_behind(sums[1].astype(jnp.bfloat16), "seq", 1).astype(jnp.float32),
        )

    def key_work(turn, pair_block, sums, query_sum):
        anchor = (cycle_index - turn) % count
        key_pairs = pair_index(anchor * seq_here + offsets, ends)
        query_term, key_term, value_term = tile_terms(
            queries,
            attended_grad,
            log_total,
            delta,
            own_pairs,
            pair_block[0],
            pair_block[1],
            key_pairs,
        )
        return ((sums[0] + key_term, sums[1] + value_term), query_sum + query_term)

    def key_turn(turn, state):
        pair_block, sums, query_sum = state
        sums, query_sum = key_work(turn, pair_block, sums, query_sum)
        sums = send_key_sums(sums)
        pair_block = from_behind((pair_block[0], pair_block[1]), "seq", 1)
        return (pair_block, sums, query_sum)

    pair_block, sums, query_sum = lax.fori_loop(
        0, count - 1, key_turn, ((keys, values), (zeros_block, zeros_block), zeros_block)
    )
    sums, query_sum = key_work(count - 1, pair_block, sums, query_sum)
    key_sum, value_sum = send_key_sums(sums)
    query_low = query_sum.astype(jnp.bfloat16).reshape(flat.shape)
    key_low = key_sum.astype(jnp.bfloat16).reshape(flat.shape)
    value_low = value_sum.astype(jnp.bfloat16).reshape(flat.shape)
    joint_low = jnp.concatenate([query_low, key_low, value_low], axis=1)
    joint_grad = jnp.einsum("ti,tj->ij", flat, joint_low, preferred_element_type=jnp.float32)
    query_bias_grad = jnp.sum(query_low.astype(jnp.float32), axis=0)
    value_bias_grad = jnp.sum(value_low.astype(jnp.float32), axis=0)
    token_grad = first_grad + jnp.einsum(
        "tj,ij->ti", joint_low, joint_weight, preferred_element_type=jnp.float32
    )
    gradients = (
        joint_grad,
        query_bias_grad,
        value_bias_grad,
        out_grad,
        out_bias_grad,
        first_gain_grad,
        first_shift_grad,
        up_grad,
        up_bias_grad,
        down_grad,
        down_bias_grad,
        second_gain_grad,
        second_shift_grad,
    )
    shares = (
        lax.psum_scatter(
            gradients[0].astype(jnp.bfloat16), "seq", scatter_dimension=0, tiled=True
        ).astype(jnp.float32),
        lax.psum_scatter(
            gradients[1].astype(jnp.bfloat16), "seq", scatter_dimension=0, tiled=True
        ).astype(jnp.float32),
        lax.psum_scatter(
            gradients[2].astype(jnp.bfloat16), "seq", scatter_dimension=0, tiled=True
        ).astype(jnp.float32),
        lax.psum_scatter(
            gradients[3].astype(jnp.bfloat16), "seq", scatter_dimension=0, tiled=True
        ).astype(jnp.float32),
        lax.psum_scatter(
            gradients[4].astype(jnp.bfloat16), "seq", scatter_dimension=0, tiled=True
        ).astype(jnp.float32),
        lax.psum_scatter(
            gradients[5].astype(jnp.bfloat16), "seq", scatter_dimension=0, tiled=True
        ).astype(jnp.float32),
        lax.psum_scatter(
            gradients[6].astype(jnp.bfloat16), "seq", scatter_dimension=0, tiled=True
        ).astype(jnp.float32),
        lax.psum_scatter(
            gradients[7].astype(jnp.bfloat16), "seq", scatter_dimension=0, tiled=True
        ).astype(jnp.float32),
        lax.psum_scatter(
            gradients[8].astype(jnp.bfloat16), "seq", scatter_dimension=0, tiled=True
        ).astype(jnp.float32),
        lax.psum_scatter(
            gradients[9].astype(jnp.bfloat16), "seq", scatter_dimension=0, tiled=True
        ).astype(jnp.float32),
        lax.psum_scatter(
            gradients[10].astype(jnp.bfloat16), "seq", scatter_dimension=0, tiled=True
        ).astype(jnp.float32),
        lax.psum_scatter(
            gradients[11].astype(jnp.bfloat16), "seq", scatter_dimension=0, tiled=True
        ).astype(jnp.float32),
        lax.psum_scatter(
            gradients[12].astype(jnp.bfloat16), "seq", scatter_dimension=0, tiled=True
        ).astype(jnp.float32),
    )
    shares = (
        lax.psum(shares[0].astype(jnp.bfloat16), "rows").astype(jnp.float32),
        lax.psum(shares[1].astype(jnp.bfloat16), "rows").astype(jnp.float32),
        lax.psum(shares[2].astype(jnp.bfloat16), "rows").astype(jnp.float32),
        lax.psum(shares[3].astype(jnp.bfloat16), "rows").astype(jnp.float32),
        lax.psum(shares[4].astype(jnp.bfloat16), "rows").astype(jnp.float32),
        lax.psum(shares[5].astype(jnp.bfloat16), "rows").astype(jnp.float32),
        lax.psum(shares[6].astype(jnp.bfloat16), "rows").astype(jnp.float32),
        lax.psum(shares[7].astype(jnp.bfloat16), "rows").astype(jnp.float32),
        lax.psum(shares[8].astype(jnp.bfloat16), "rows").astype(jnp.float32),
        lax.psum(shares[9].astype(jnp.bfloat16), "rows").astype(jnp.float32),
        lax.psum(shares[10].astype(jnp.bfloat16), "rows").astype(jnp.float32),
        lax.psum(shares[11].astype(jnp.bfloat16), "rows").astype(jnp.float32),
        lax.psum(shares[12].astype(jnp.bfloat16), "rows").astype(jnp.float32),
    )
    return (outputs, token_grad.reshape(tokens.shape)) + tuple(shares)


WIDTH = HEADS * HEAD_DIM
HALF = WIDTH // 2
FF = 4 * WIDTH
BLOCK = 128
OWN = 2 * BLOCK
LANES = 128
PAIRS_OF_HEADS = HALF // LANES
JOINT_ROWS = 80
JOINT_FIRST = 48
JOINT_SECOND = JOINT_ROWS - JOINT_FIRST
UP_ROWS = 128
DOWN_ROWS = 96
EXT = OWN + 16
DOWN_SENT = 2 * DOWN_ROWS
FLOAT = jnp.float32
LOW = jnp.bfloat16
AXES = ("seq", "rows")


def kernel_params(megabytes):
    return pltpu.CompilerParams(vmem_limit_bytes=megabytes << 20)


def shaped(shape, kind):
    return jax.ShapeDtypeStruct(shape, kind)


def whole(shape):
    return pl.BlockSpec(shape, lambda *_: (0,) * len(shape))


def cost(flops, moved, exps=0):
    return pl.CostEstimate(flops=1024, bytes_accessed=1024, transcendentals=0)


def dot(left, right):
    return lax.dot_general(left, right, (((1,), (0,)), ((), ())), preferred_element_type=FLOAT)


def dot_nt(left, right):
    return lax.dot_general(left, right, (((1,), (1,)), ((), ())), preferred_element_type=FLOAT)


def call(kernel, name, place, inputs, outputs, scratch=(), grid=(1,), scalars=(), after=(), megabytes=28, work=None, aliases=()):
    prefetch = 1 + len(scalars)
    given, made = len(inputs), len(outputs)

    def ordered(*refs):
        first = prefetch + given
        mark = refs[first + len(after) + made]
        mark[...] = jnp.zeros_like(mark)
        kernel(*refs[:first], *refs[first + len(after) : first + len(after) + made], *refs[first + len(after) + made + 1 :])

    results = pl.pallas_call(
        ordered,
        grid_spec=pltpu.PrefetchScalarGridSpec(
            num_scalar_prefetch=prefetch,
            grid=grid,
            in_specs=[spec for _, spec in inputs] + [pl.BlockSpec(memory_space=pl.ANY)] * len(after),
            out_specs=[spec for _, _, spec in outputs] + [whole((8, LANES))],
            scratch_shapes=list(scratch),
        ),
        out_shape=[shaped(shape, kind) for shape, kind, _ in outputs] + [shaped((8, LANES), FLOAT)],
        compiler_params=kernel_params(megabytes),
        cost_estimate=work,
        input_output_aliases={prefetch + source: target for source, target in aliases},
        name=name,
    )(place, *scalars, *[array for array, _ in inputs], *after)
    return results[:-1], results[-1]


def plain(array):
    return array, whole(array.shape)


def made(shape, kind):
    return shape, kind, whole(shape)


def device_at(z, y, x, c):
    return ((z * 2 + y) * 2 + x) * 2 + c


def permute(value, target):
    pairs = []
    for z in range(4):
        for y in range(2):
            for x in range(2):
                for c in range(2):
                    pairs.append((device_at(z, y, x, c), device_at(*target(z, y, x, c))))
    return lax.ppermute(value, AXES, pairs)


def core_swap(value):
    return permute(value, lambda z, y, x, c: (z, y, x, 1 - c))


def x_swap(value):
    return permute(value, lambda z, y, x, c: (z, y, 1 - x, c))


def y_swap(value):
    return permute(value, lambda z, y, x, c: (z, 1 - y, x, c))


def z_swap(value, bits):
    return permute(value, lambda z, y, x, c: (z ^ bits, y, x, c))


def row_swap(value, second):
    return permute(value, lambda z, y, x, c: (2 * c + (z % 2 ^ second), y, x, z // 2))


def first_positions(place):
    z, y, c = place[0], place[1], place[3]
    bases = []
    for core, line in ((c, y), (1 - c, y), (c, 1 - y), (1 - c, 1 - y)):
        for second in (0, 1):
            parity = z % 2
            parity = 1 - parity if second else parity
            bases.append((2 * (2 * core + parity) + line) * BLOCK)
    return bases


def pair_ends(place, own_lengths, peer_lengths):
    z, c = place[0], place[3]
    here = (z // 2) == c
    line = z % 2
    ends, end = [], 0
    for pair in range(own_lengths.shape[1]):
        end = end + jnp.where(here, own_lengths[line, pair], peer_lengths[line, pair])
        ends.append(end)
    return ends


def pairs_along(base, ends, axis):
    shape = (8, BLOCK) if axis == 1 else (BLOCK, LANES)
    position = base + lax.broadcasted_iota(jnp.int32, shape, axis)
    ids = jnp.zeros(shape, jnp.int32)
    for end in ends:
        ids = ids + (position >= end).astype(jnp.int32)
    return ids


def head_mask(rows):
    return lax.broadcasted_iota(jnp.int32, (rows, LANES), 1) < HEAD_DIM


def columns_kernel(place, columns, query_bias, value_bias, out, query_row, value_row):
    out[0] = columns[...]
    query_row[...] = query_bias[...]
    value_row[...] = value_bias[...]


def own_columns(place, joint_weight, query_bias, value_bias):
    half_row = pl.BlockSpec((1, HALF), lambda i, place: (0, place[3]))
    results, _ = call(
        columns_kernel,
        "own_columns",
        place,
        [
            (joint_weight, pl.BlockSpec((WIDTH, HALF), lambda i, place: (0, 2 * i + place[3]))),
            (row_of(query_bias), half_row),
            (row_of(value_bias), half_row),
        ],
        [((3, WIDTH, HALF), LOW, pl.BlockSpec((1, WIDTH, HALF), lambda i, place: (i, 0, 0)))]
        + [made((1, HALF), FLOAT)] * 2,
        grid=(3,),
        work=cost(1e6, 4e6),
    )
    return results


def first_attention_kernel(
    place, own_lengths, peer_lengths, t0, t1, t2, t3, columns, qb, vb, q_out, k_out, v_out, summed, stats, bias
):
    bases = first_positions(place)
    ends = pair_ends(place, own_lengths, peer_lengths)
    tokens = jnp.concatenate([block[...] for block in (t0, t1, t2, t3)], axis=0)
    queries = dot(tokens, columns[0]) + qb[...]
    q_out[...] = (queries.astype(LOW).astype(FLOAT) * HEAD_DIM**-0.5).astype(LOW)
    k_out[...] = dot(tokens, columns[1]).astype(LOW)
    v_out[...] = (dot(tokens, columns[2]) + vb[...]).astype(LOW)
    fill_bias(bias, bases[:4], bases[:4], ends)
    stats[...] = jnp.zeros_like(stats)
    for pair in range(PAIRS_OF_HEADS):
        lanes = pl.ds(pair * LANES, LANES)
        scores = masked_scores(k_out[:, lanes], q_out[:, lanes], bias)
        highest = jnp.max(scores, axis=0, keepdims=True)
        weights = jnp.exp(scores - highest)
        summed[pair] = dot(turned(v_out[:, lanes]), weights.astype(LOW))
        stats[2 * pair : 2 * pair + 1, :] = highest
        stats[2 * pair + 1 : 2 * pair + 2, :] = column_sum(weights)


def turned(array):
    return jnp.transpose(array.astype(FLOAT)).astype(LOW)


def masked_scores(keys, queries, bias):
    mask = bias[...]
    chosen = jnp.concatenate(halves_of(queries), axis=0)
    return dot_nt(keys, chosen) + jnp.concatenate([mask, mask], axis=1)


def fill_bias(bias, query_bases, key_bases, ends):
    key_ids = [pairs_along(base, ends, 1)[0:1] for base in key_bases]
    for i, base in enumerate(query_bases):
        query_ids = pairs_along(base, ends, 0)
        for j in range(len(key_bases)):
            bias[pl.ds(i * BLOCK, BLOCK), pl.ds(j * BLOCK, BLOCK)] = jnp.where(query_ids == key_ids[j], 0.0, NEGATIVE)


def halves_of(array):
    left = head_mask(array.shape[0])
    zeros = jnp.zeros_like(array)
    return jnp.where(left, array, zeros), jnp.where(left, zeros, array)


def first_attention(place, lengths, blocks, columns, query_bias, value_bias, after=()):
    return call(
        first_attention_kernel,
        "first_attention",
        place,
        [plain(array) for array in (*blocks, columns, query_bias, value_bias)],
        [made((512, HALF), LOW)] * 3 + [made((PAIRS_OF_HEADS, LANES, 1024), FLOAT), made((8, 1024), FLOAT)],
        scratch=[pltpu.VMEM((512, 512), FLOAT)],
        scalars=lengths,
        after=after,
        work=cost(4e9, 8e6, 3e6),
    )


def attention_kernel(
    place, own_lengths, peer_lengths, t0, t1, t2, t3, columns, vb, q, summed, stats,
    att_out, k_out, v_out, log_out, bias,
):
    bases = first_positions(place)
    ends = pair_ends(place, own_lengths, peer_lengths)
    tokens = jnp.concatenate([block[...] for block in (t0, t1, t2, t3)], axis=0)
    k_out[...] = dot(tokens, columns[1]).astype(LOW)
    v_out[...] = (dot(tokens, columns[2]) + vb[...]).astype(LOW)
    fill_bias(bias, bases[4:], bases[:4], ends)
    log_out[...] = jnp.zeros_like(log_out)
    top = lax.broadcasted_iota(jnp.int32, (LANES, 512), 0) < HEAD_DIM
    for pair in range(PAIRS_OF_HEADS):
        lanes = pl.ds(pair * LANES, LANES)
        scores = masked_scores(k_out[:, lanes], q[:, lanes], bias)
        before = stats[2 * pair : 2 * pair + 1, :]
        highest = jnp.maximum(before, jnp.max(scores, axis=0, keepdims=True))
        weights = jnp.exp(scores - highest)
        shrink = jnp.exp(before - highest)
        sums = column_sum(weights) + shrink * stats[2 * pair + 1 : 2 * pair + 2, :]
        total = (dot(turned(v_out[:, lanes]), weights.astype(LOW)) + shrink * summed[pair]) / sums
        att_out[:, lanes] = jnp.transpose(jnp.where(top, total[:, 0:512], total[:, 512:])).astype(LOW)
        logs = highest + jnp.log(sums)
        log_out[2 * pair : 2 * pair + 1, :] = logs[:, 0:512]
        log_out[2 * pair + 1 : 2 * pair + 2, :] = logs[:, 512:]


def attention(place, lengths, blocks, columns, value_bias, q, summed, stats, after=()):
    return call(
        attention_kernel,
        "attention",
        place,
        [plain(array) for array in (*blocks, columns, value_bias, q, summed, stats)],
        [made((512, HALF), LOW)] * 3 + [made((8, 512), FLOAT)],
        scratch=[pltpu.VMEM((512, 512), FLOAT)],
        scalars=lengths,
        after=after,
        work=cost(4e9, 8e6, 3e6),
    )


def centred_norm(value):
    mean = jnp.mean(value, axis=-1, keepdims=True)
    centred = value - mean
    spread = jnp.mean(centred * centred, axis=-1, keepdims=True)
    inverse = lax.rsqrt(spread + EPSILON)
    return centred * inverse, inverse


def norm_back(grad, unit, inverse):
    mean = jnp.mean(grad, axis=-1, keepdims=True)
    along = jnp.mean(grad * unit, axis=-1, keepdims=True)
    return (grad - mean - unit * along) * inverse


def column_sum(value):
    return jnp.sum(value, axis=0, keepdims=True)


def forward_kernel(
    place, att, att_got, wo_own, wo_other, out_bias, x0, x1, gain1, shift1, up, up_bias, down,
    down_bias, gain2, shift2, cot0, cot1,
    result0, result1, feed_ext, second_grad, act_keep, act_send, slope, unit1, inverse1, normed_low, normed_t, att_t, sums,
    normed, feed, act_t,
):
    step = pl.program_id(0)
    c = place[3]

    @pl.when(step == 0)
    def _():
        tokens = jnp.concatenate([x0[...], x1[...]], axis=0).astype(FLOAT)
        att_own, att_other = att[0:OWN], att_got[OWN:]
        branch = dot(att_own, wo_own[...]) + dot(att_other, wo_other[...]) + out_bias[...]
        unit, inverse = centred_norm(tokens + branch)
        unit1[...] = unit
        inverse1[...] = jnp.broadcast_to(inverse, (OWN, LANES))
        value = unit * gain1[...] + shift1[...]
        normed[...] = value
        normed_low[...] = value.astype(LOW)
        normed_t[...] = jnp.transpose(value).astype(LOW)
        mine = pl.ds(pl.multiple_of(c * HALF, HALF), HALF)
        other = pl.ds(pl.multiple_of((1 - c) * HALF, HALF), HALF)
        att_t[mine, :] = jnp.transpose(att[...].astype(FLOAT)).astype(LOW)
        att_t[other, 0:OWN] = jnp.transpose(att_other.astype(FLOAT)).astype(LOW)
        att_t[other, OWN:] = jnp.transpose(att_got[0:OWN].astype(FLOAT)).astype(LOW)
        feed[...] = jnp.zeros_like(feed)

    inner = dot(normed_low[...], up[...]) + up_bias[...]
    below = 0.5 + 0.5 * lax.erf(inner * math.sqrt(0.5))
    density = jnp.exp(inner * inner * -0.5) * (1.0 / math.sqrt(2.0 * math.pi))
    activated = inner * below
    slope[...] = (below + inner * density).astype(LOW)
    low = activated.astype(LOW)
    act_t[...] = jnp.transpose(activated).astype(LOW).reshape(4, 2, DOWN_ROWS, OWN)
    act_keep[...] = act_t[:, c]
    act_send[...] = act_t[:, 1 - c]
    feed[...] += dot(low, down[...])

    @pl.when(step == pl.num_programs(0) - 1)
    def _():
        unit, inverse = centred_norm(normed[...] + feed[...] + down_bias[...])
        result = (unit * gain2[...] + shift2[...]).astype(LOW)
        result0[...] = result[0:BLOCK]
        result1[...] = result[BLOCK:]
        cotangent = jnp.concatenate([cot0[0:BLOCK], cot1[0:BLOCK]], axis=0).astype(FLOAT)
        grad = norm_back(cotangent * gain2[...], unit, inverse)
        second_grad[...] = grad
        low_grad = grad.astype(LOW)
        rows = jnp.concatenate(
            [
                column_sum(cotangent * unit),
                column_sum(cotangent),
                column_sum(low_grad.astype(FLOAT)),
                jnp.zeros((5, WIDTH), FLOAT),
            ],
            axis=0,
        )
        sums[...] = rows
        feed_ext[0:OWN] = low_grad
        feed_ext[OWN:] = jnp.concatenate([rows, jnp.zeros_like(rows)], axis=0).astype(LOW)


def row_of(vector):
    return vector.reshape(1, vector.shape[0])


def forward(place, att, att_got, tokens, cotangents, weights, after=()):
    chunk = WIDTH

    def vector(name):
        return plain(row_of(weights[name]))

    units = ((16, DOWN_ROWS, OWN), LOW, pl.BlockSpec((4, DOWN_ROWS, OWN), lambda i, place: (i, 0, 0)))
    return call(
        forward_kernel,
        "forward",
        place,
        [
            plain(att),
            plain(att_got),
            (weights["out"], pl.BlockSpec((HALF, WIDTH), lambda i, place: (place[3], 0))),
            (weights["out"], pl.BlockSpec((HALF, WIDTH), lambda i, place: (1 - place[3], 0))),
            vector("out_bias"), plain(tokens[0]), plain(tokens[1]), vector("gain1"), vector("shift1"),
            (weights["up"], pl.BlockSpec((WIDTH, chunk), lambda i, place: (0, i))),
            (row_of(weights["up_bias"]), pl.BlockSpec((1, chunk), lambda i, place: (0, i))),
            (weights["down"], pl.BlockSpec((chunk, WIDTH), lambda i, place: (i, 0))),
            vector("down_bias"), vector("gain2"), vector("shift2"), plain(cotangents[0]), plain(cotangents[1]),
        ],
        [
            made((BLOCK, WIDTH), LOW), made((BLOCK, WIDTH), LOW), made((EXT, WIDTH), LOW),
            made((OWN, WIDTH), FLOAT), units, units,
            ((OWN, FF), LOW, pl.BlockSpec((OWN, chunk), lambda i, place: (0, i))),
            made((OWN, WIDTH), FLOAT), made((OWN, LANES), FLOAT), made((OWN, WIDTH), LOW),
            made((WIDTH, OWN), LOW), made((WIDTH, 512), LOW), made((8, WIDTH), FLOAT),
        ],
        scratch=[
            pltpu.VMEM((OWN, WIDTH), FLOAT),
            pltpu.VMEM((OWN, WIDTH), FLOAT),
            pltpu.VMEM((4, 2, DOWN_ROWS, OWN), LOW),
        ],
        grid=(FF // chunk,),
        after=after,
        work=cost(2.7e9, 20e6, 2e6),
    )


def split_units(place, units, px_send, px, qy_send, qy):
    y, x = place[1], place[2]
    half = units.shape[2] // 2
    for line in range(2):
        px[0, line] = units[line, x, 0:half]
        px_send[0, line] = units[line, 1 - x, 0:half]
    for side in range(2):
        qy[0, side] = units[y, side, half:]
        qy_send[0, side] = units[1 - y, side, half:]


def unit_outputs(rows, width):
    shape = (4, 2, rows // 2, width)
    return [(shape, LOW, pl.BlockSpec((1,) + shape[1:], lambda i, place: (i, 0, 0, 0)))] * 4


def down_kernel(place, act, act_got, feed, feed_got, px_send, px, qy_send, qy, units):
    shape = (4 * DOWN_ROWS, OWN)
    total = dot(act[...].reshape(shape), feed[0:OWN]) + dot(act_got[...].reshape(shape), feed_got[0:OWN])
    units[...] = total.astype(LOW).reshape(units.shape)
    split_units(place, units, px_send, px, qy_send, qy)


def down_units(place, act, act_got, feed, feed_got, after=()):
    block = pl.BlockSpec((4, DOWN_ROWS, OWN), lambda i, place: (i, 0, 0))
    return call(
        down_kernel,
        "down_units",
        place,
        [(act, block), (act_got, block), plain(feed), plain(feed_got)],
        unit_outputs(DOWN_ROWS, WIDTH),
        scratch=[pltpu.VMEM((2, 2, DOWN_ROWS, WIDTH), LOW)],
        grid=(4,),
        after=after,
        work=cost(0.6e9, 3.5e6),
    )


def backward_kernel(
    place, feed_ext, slope, up, down, second_grad, unit1, inverse1, gain1, wo_own, wo_other,
    inner0, inner1, send0, send1, first_grad, branch_own, back_own, misc, sums,
    normed_grad, branch,
):
    step = pl.program_id(0)
    c = place[3]

    @pl.when(step == 0)
    def _():
        normed_grad[...] = second_grad[...]
        sums[...] = jnp.zeros_like(sums)

    grad = (dot_nt(feed_ext[0:OWN], down[...]) * slope[...].astype(FLOAT)).astype(LOW)
    for target, index in ((inner0, c), (inner1, 2 + c), (send0, 1 - c), (send1, 3 - c)):

        @pl.when(step == index)
        def _(target=target):
            target[...] = grad

    sums[pl.ds(4 + step, 1), :] = column_sum(grad.astype(FLOAT))
    normed_grad[...] += dot_nt(grad, up[...])

    @pl.when(step == pl.num_programs(0) - 1)
    def _():
        total = normed_grad[...]
        unit = unit1[...]
        sums[0:1, :] = column_sum(total * unit)
        sums[1:2, :] = column_sum(total)
        grad1 = norm_back(total * gain1[...], unit, inverse1[:, 0:1])
        first_grad[...] = grad1
        low = grad1.astype(LOW)
        branch[...] = low
        sums[2:3, :] = column_sum(low.astype(FLOAT))
        branch_own[...] = branch[:, pl.ds(pl.multiple_of(c * HALF, LANES), HALF)]
        back_own[...] = dot_nt(low, wo_own[...]).astype(LOW)
        misc[0:OWN, 0:HALF] = branch[:, pl.ds(pl.multiple_of((1 - c) * HALF, LANES), HALF)]
        misc[0:OWN, HALF:] = dot_nt(low, wo_other[...]).astype(LOW)
        rows = sums[...]
        misc[OWN:] = jnp.concatenate([rows, jnp.zeros_like(rows)], axis=0).astype(LOW)


def backward(place, feed_ext, slope, second_grad, unit1, inverse1, weights, after=()):
    chunk = WIDTH
    return call(
        backward_kernel,
        "backward",
        place,
        [
            plain(feed_ext),
            (slope, pl.BlockSpec((OWN, chunk), lambda i, place: (0, i))),
            (weights["up"], pl.BlockSpec((WIDTH, chunk), lambda i, place: (0, i))),
            (weights["down"], pl.BlockSpec((chunk, WIDTH), lambda i, place: (i, 0))),
            plain(second_grad), plain(unit1), plain(inverse1), plain(row_of(weights["gain1"])),
            (weights["out"], pl.BlockSpec((HALF, WIDTH), lambda i, place: (place[3], 0))),
            (weights["out"], pl.BlockSpec((HALF, WIDTH), lambda i, place: (1 - place[3], 0))),
        ],
        [made((OWN, WIDTH), LOW)] * 4
        + [
            made((OWN, WIDTH), FLOAT), made((OWN, HALF), LOW), made((OWN, HALF), LOW), made((EXT, WIDTH), LOW),
            made((8, WIDTH), FLOAT),
        ],
        scratch=[pltpu.VMEM((OWN, WIDTH), FLOAT), pltpu.VMEM((OWN, WIDTH), LOW)],
        grid=(FF // chunk,),
        after=after,
        work=cost(2.7e9, 16e6),
    )


def up_kernel(
    place, normed_t, normed_got, inner0, inner1, got0, got1, att_t, branch, misc, sums0, sums1, feed_got,
    x_send, y_send, px, qy, units, normed_got_t,
):
    z = pl.program_id(0)
    y, x = place[1], place[2]

    @pl.when(z == 0)
    def _():
        normed_got_t[...] = jnp.transpose(normed_got[...].astype(FLOAT)).astype(LOW)

    theirs = normed_got_t[pl.ds(pl.multiple_of(z * 192, 32), 192), :]
    outer = dot(att_t[:, 0:OWN], branch[...]) + dot(att_t[:, OWN:], misc[0:OWN, 0:HALF])
    for side, inner, got, sums, pair in ((0, inner0, got0, sums0, feed_got), (1, inner1, got1, sums1, misc)):
        grad = dot(normed_t[...], inner[...]) + dot(theirs, got[...])
        vectors = sums[...] + pair[OWN:].astype(FLOAT)[0:8]
        for line in range(2):
            first = line * 96 + side * 48
            rest = jnp.concatenate([outer[first : first + 24], outer[first + 24 : first + 48]], axis=1)
            units[line, side] = jnp.concatenate(
                [grad[line * 96 : line * 96 + 96], rest, vectors], axis=0
            ).astype(LOW)
    half = UP_ROWS // 2
    for index in range(2):
        rows = pl.ds(pl.multiple_of(DOWN_SENT + (z * 2 + index) * half, half), half)
        px[0, index] = units[index, x, 0:half]
        x_send[rows, :] = units[index, 1 - x, 0:half]
        qy[0, index] = units[y, index, half:]
        y_send[rows, :] = units[1 - y, index, half:]


def up_units(place, normed_t, normed_got, inner, got, att_t, branch, misc, sums0, sums1, feed_got, after=()):
    rows = pl.BlockSpec((192, OWN), lambda i, place: (i, 0))
    return call(
        up_kernel,
        "up_units",
        place,
        [
            (normed_t, rows), plain(normed_got), plain(inner[0]), plain(inner[1]), plain(got[0]), plain(got[1]),
            (att_t, pl.BlockSpec((192, 512), lambda i, place: (i, 0))),
            plain(branch), plain(misc), plain(sums0), plain(sums1), plain(feed_got),
        ],
        [made((DOWN_SENT + 4 * UP_ROWS, WIDTH), LOW)] * 2 + unit_outputs(UP_ROWS, WIDTH)[:2],
        scratch=[pltpu.VMEM((2, 2, UP_ROWS, WIDTH), LOW), pltpu.VMEM((WIDTH, OWN), LOW)],
        grid=(4,),
        after=after,
        work=cost(0.9e9, 5e6),
    )


def attention_back_kernel(
    place, own_lengths, peer_lengths, q, k0, k1, v0, v1, log_total, att, back0, misc,
    dq_out, dk_out, dv_out, bias,
):
    bases = first_positions(place)
    ends = pair_ends(place, own_lengths, peer_lengths)
    query_ids = [pairs_along(base, ends, 1)[0:1] for base in bases[:4]]
    for j in range(8):
        key_ids = pairs_along(bases[j], ends, 0)
        for i in range(4):
            bias[pl.ds(j * BLOCK, BLOCK), pl.ds(i * BLOCK, BLOCK)] = jnp.where(
                key_ids == query_ids[i], 0.0, NEGATIVE
            )
    for pair in range(PAIRS_OF_HEADS):
        lanes = pl.ds(pair * LANES, LANES)
        keys = jnp.concatenate([k0[:, lanes], k1[:, lanes]], axis=0)
        values = jnp.concatenate([v0[:, lanes], v1[:, lanes]], axis=0)
        keys_t = jnp.transpose(keys.astype(FLOAT)).astype(LOW)
        key_grad = jnp.zeros((1024, LANES), FLOAT)
        value_grad = jnp.zeros((1024, LANES), FLOAT)
        left = head_mask(OWN)
        for part in range(2):
            rows = pl.ds(part * OWN, OWN)
            queries = q[rows, lanes]
            grads = back0[:, lanes] if part == 0 else misc[0:OWN, pl.ds(HALF + pair * LANES, LANES)]
            zeros = jnp.zeros_like(queries)
            product = jnp.transpose(grads.astype(FLOAT) * att[rows, lanes].astype(FLOAT))
            halves = []
            for half in range(2):
                if half == 0:
                    chosen, chosen_grads = jnp.where(left, queries, zeros), jnp.where(left, grads, zeros)
                else:
                    chosen, chosen_grads = jnp.where(left, zeros, queries), jnp.where(left, zeros, grads)
                delta = column_sum(product[half * HEAD_DIM : (half + 1) * HEAD_DIM])
                head = pair * 2 + half
                scores = dot_nt(keys, chosen) + bias[:, rows]
                weights = jnp.exp(scores - log_total[head : head + 1, rows])
                weight_grad = dot_nt(values, chosen_grads)
                score_grad = (weights * (weight_grad - delta)).astype(LOW)
                value_grad = value_grad + dot(weights.astype(LOW), chosen_grads)
                key_grad = key_grad + dot(score_grad, chosen)
                halves.append(dot(keys_t, score_grad))
            query_grad_t = jnp.concatenate([halves[0][0:HEAD_DIM], halves[1][HEAD_DIM:LANES]], axis=0)
            dq_out[rows, lanes] = (jnp.transpose(query_grad_t) * HEAD_DIM**-0.5).astype(LOW)
        dk_out[:, lanes] = key_grad.astype(LOW)
        dv_out[:, lanes] = value_grad.astype(LOW)


def attention_back(place, lengths, q, keys, values, log_total, att, back_own, misc, after=()):
    return call(
        attention_back_kernel,
        "attention_back",
        place,
        [plain(array) for array in (q, *keys, *values, log_total, att, back_own, misc)],
        [made((512, HALF), LOW), made((1024, HALF), LOW), made((1024, HALF), LOW)],
        scratch=[pltpu.VMEM((1024, 512), FLOAT)],
        scalars=lengths,
        after=after,
        work=cost(7e9, 6e6, 3e6),
    )


def token_kernel(place, dq, dk, dv, columns, own, own_send, far, far_send):
    for part, target in enumerate((own, own_send, far, far_send)):
        rows = pl.ds(part * OWN, OWN)
        total = dot_nt(dk[rows, :], columns[1]) + dot_nt(dv[rows, :], columns[2])
        if part < 2:
            total = total + dot_nt(dq[rows, :], columns[0])
        target[...] = total.astype(LOW)


def token_parts(place, dq, dk, dv, columns, after=()):
    return call(
        token_kernel,
        "token_parts",
        place,
        [plain(dq), plain(dk), plain(dv), plain(columns)],
        [made((OWN, WIDTH), LOW)] * 4,
        after=after,
        work=cost(1.5e9, 5e6),
    )


def token_last_kernel(place, own, own_got, across, first_grad, token0, token1):
    total = own[...].astype(FLOAT) + own_got[...].astype(FLOAT) + across[8 * JOINT_SECOND :].astype(FLOAT) + first_grad[...]
    total = total.astype(LOW)
    token0[...] = total[0:BLOCK]
    token1[...] = total[BLOCK:]


def token_last(place, arrays, after=()):
    return call(
        token_last_kernel,
        "token_last",
        place,
        [plain(array) for array in arrays],
        [made((BLOCK, WIDTH), LOW)] * 2,
        after=after,
        work=cost(1e6, 2e6),
    )


def back_rows_kernel(place, done0, done1, back0, back1, outputs, token_grad):
    odd = place[0] % 2
    outputs[odd] = done0[...]
    outputs[1 - odd] = done1[...]
    token_grad[odd] = back0[...].astype(FLOAT)
    token_grad[1 - odd] = back1[...].astype(FLOAT)


def back_rows(place, done, back, after=()):
    return call(
        back_rows_kernel,
        "back_rows",
        place,
        [plain(array) for array in (*done, *back)],
        [made((2, BLOCK, WIDTH), LOW), made((2, BLOCK, WIDTH), FLOAT)],
        after=after,
        work=cost(1e6, 2e6),
    )


def joint_kernel(
    place, t0, t1, t2, t3, t4, t5, t6, t7, dq, dk, dv, far, far_got, px_send, px, qy_send, qy, tokens_t, units
):
    y, x = place[1], place[2]
    qy_send[pl.ds(8 * JOINT_SECOND, OWN), :] = added(far[...], far_got[...])
    for index, block in enumerate((t0, t1, t2, t3, t4, t5, t6, t7)):
        tokens_t[:, pl.ds(index * BLOCK, BLOCK)] = jnp.transpose(block[...].astype(FLOAT)).astype(LOW)
    biases = jnp.concatenate([column_sum(dq[...].astype(FLOAT)), column_sum(dv[...].astype(FLOAT))], axis=1)
    biases = jnp.concatenate([biases, jnp.zeros((7, WIDTH), FLOAT)], axis=0)
    for z in range(4):
        rows = pl.ds(z * 192, 192)
        query = dot(tokens_t[rows, 0:512], dq[...])
        key = dot(tokens_t[rows, :], dk[...])
        value = dot(tokens_t[rows, :], dv[...])
        for line in range(2):
            for side in range(2):
                at = line * 96 + side * 48
                units[line, side, 0:JOINT_FIRST] = jnp.concatenate(
                    [query[at : at + 48], key[at : at + 48]], axis=1
                ).astype(LOW)
                rest = jnp.concatenate([value[at : at + 24], value[at + 24 : at + 48]], axis=1)
                units[line, side, JOINT_FIRST:] = jnp.concatenate([rest, biases], axis=0).astype(LOW)
        for line in range(2):
            px[z, line] = units[line, x, 0:JOINT_FIRST]
            px_send[z, line] = units[line, 1 - x, 0:JOINT_FIRST]
        for side in range(2):
            qy[z, side] = units[y, side, JOINT_FIRST:]
            qy_send[pl.ds((z * 2 + side) * JOINT_SECOND, JOINT_SECOND), :] = units[1 - y, side, JOINT_FIRST:]


def joint_units(place, blocks, dq, dk, dv, far, far_got, after=()):
    first, second = made((4, 2, JOINT_FIRST, WIDTH), LOW), made((4, 2, JOINT_SECOND, WIDTH), LOW)
    return call(
        joint_kernel,
        "joint_units",
        place,
        [plain(array) for array in (*blocks, dq, dk, dv, far, far_got)],
        [first, first, made((8 * JOINT_SECOND + OWN, WIDTH), LOW), second],
        scratch=[pltpu.VMEM((WIDTH, 1024), LOW), pltpu.VMEM((2, 2, JOINT_ROWS, WIDTH), LOW)],
        after=after,
        work=cost(1.5e9, 6e6),
    )


def added(left, right):
    return (left.astype(FLOAT) + right.astype(FLOAT)).astype(LOW)


def down_pair_kernel(place, px, px_got, qy, qy_got, x_in, y_in, x_send, y_send, p, q):
    y, x = place[1], place[2]
    p[0] = added(px[0, y], px_got[0, y])
    y_send[...] = added(px[0, 1 - y], px_got[0, 1 - y])
    q[0] = added(qy[0, x], qy_got[0, x])
    x_send[...] = added(qy[0, 1 - x], qy_got[0, 1 - x])


def down_pair_stage(place, arrays, x_send, y_send, after=()):
    half = DOWN_ROWS // 2
    block = pl.BlockSpec((1, 2, half, WIDTH), lambda i, place: (i, 0, 0, 0))
    sent = (x_send.shape, LOW, pl.BlockSpec((half, WIDTH), lambda i, place: (i, 0)))
    kept = ((4, half, WIDTH), LOW, pl.BlockSpec((1, half, WIDTH), lambda i, place: (i, 0, 0)))
    anywhere = pl.BlockSpec(memory_space=pl.ANY)
    return call(
        down_pair_kernel,
        "down_pair_stage",
        place,
        [(array, block) for array in arrays] + [(x_send, anywhere), (y_send, anywhere)],
        [sent, sent, kept, kept],
        grid=(4,),
        after=after,
        work=cost(1e6, 1e7),
        aliases=((4, 0), (5, 1)),
    )


def second_kernel(
    place, x_got, y_got, px, qy, down_p, down_q, x_send, y_send, p, q, down_send, down_keep
):
    z_here, y, x = place[0], place[1], place[2]
    half = UP_ROWS // 2
    for z in range(4):
        for got, have, own, keep, send in ((x_got, px, y, p, y_send), (y_got, qy, x, q, x_send)):
            at = DOWN_SENT + z * UP_ROWS
            mine = pl.ds(pl.multiple_of(at + own * half, half), half)
            other = pl.ds(pl.multiple_of(at + (1 - own) * half, half), half)
            keep[z] = added(have[z, own], got[mine, :])
            send[pl.ds(z * half, half), :] = added(have[z, 1 - own], got[other, :])
    low = z_here % 2
    small = DOWN_ROWS // 2
    for target, parity in ((down_keep, low), (down_send, 1 - low)):
        for high in range(2):
            index = 2 * high + parity
            rows = pl.ds(pl.multiple_of(index * small, small), small)
            target[high, 0:small] = added(down_p[index], y_got[rows, :])
            target[high, small:] = added(down_q[index], x_got[rows, :])


def second_stage(place, arrays, after=()):
    kept = made((4, UP_ROWS // 2, WIDTH), LOW)
    down = made((2, DOWN_ROWS, WIDTH), LOW)
    return call(
        second_kernel,
        "second_stage",
        place,
        [plain(array) for array in arrays],
        [made((OWN, WIDTH), LOW), made((OWN, WIDTH), LOW), kept, kept, down, down],
        after=after,
        work=cost(1e6, 1e7),
    )


def joint_pair_kernel(place, px, px_got, qy, qy_got, x_send, y_send, p, q):
    y, x = place[1], place[2]
    for z in range(4):
        p[z] = added(px[z, y], px_got[z, y])
        y_send[z] = added(px[z, 1 - y], px_got[z, 1 - y])


        def from_y(side):
            return qy_got[pl.ds(pl.multiple_of((z * 2 + side) * JOINT_SECOND, 32), JOINT_SECOND), :]

        q[z] = added(qy[z, x], from_y(x))
        x_send[z] = added(qy[z, 1 - x], from_y(1 - x))


def joint_pair_stage(place, arrays, after=()):
    first, second = made((4, JOINT_FIRST, WIDTH), LOW), made((4, JOINT_SECOND, WIDTH), LOW)
    return call(
        joint_pair_kernel,
        "joint_pair_stage",
        place,
        [plain(array) for array in arrays],
        [second, first, first, second],
        after=after,
        work=cost(1e6, 1e7),
    )


def up_line_kernel(place, x_got, y_got, p, q, down_two, down_got, send, keep, down_send, down_keep):
    low, high_here = place[0] % 2, place[0] // 2
    half = UP_ROWS // 2
    for target, parity in ((keep, low), (send, 1 - low)):
        for high in range(2):
            index = 2 * high + parity
            rows = pl.ds(pl.multiple_of(index * half, half), half)
            target[high, 0:half] = added(p[index], y_got[rows, :])
            target[high, half:] = added(q[index], x_got[rows, :])
    down_keep[...] = added(down_two[high_here], down_got[high_here])
    down_send[...] = added(down_two[1 - high_here], down_got[1 - high_here])


def up_line_stage(place, arrays, after=()):
    return call(
        up_line_kernel,
        "up_line_stage",
        place,
        [plain(array) for array in arrays],
        [made((2, UP_ROWS, WIDTH), LOW)] * 2 + [made((DOWN_ROWS, WIDTH), LOW)] * 2,
        after=after,
        work=cost(1e6, 1e7),
    )


def joint_line_kernel(place, x_got, y_got, p, q, send, keep):
    low = place[0] % 2
    for target, parity in ((keep, low), (send, 1 - low)):
        for high in range(2):
            index = 2 * high + parity
            target[high, 0:JOINT_FIRST] = added(p[index], y_got[index])
            target[high, JOINT_FIRST:] = added(q[index], x_got[index])


def joint_line_stage(place, arrays, after=()):
    return call(
        joint_line_kernel,
        "joint_line_stage",
        place,
        [plain(array) for array in arrays],
        [made((2, JOINT_ROWS, WIDTH), LOW)] * 2,
        after=after,
        work=cost(1e6, 1e6),
    )


def end_stage_kernel(place, keep_two, got, send, keep):
    high = place[0] // 2
    keep[...] = added(keep_two[high], got[high])
    send[...] = added(keep_two[1 - high], got[1 - high])


def end_stage(place, keep_two, got, after=()):
    return call(
        end_stage_kernel,
        "end_stage",
        place,
        [plain(keep_two), plain(got)],
        [made(keep_two.shape[1:], LOW)] * 2,
        after=after,
        work=cost(1e6, 1e6),
    )


def last_sum_kernel(place, *refs):
    count = len(refs) // 3
    for index in range(count):
        refs[2 * count + index][...] = added(refs[2 * index][...], refs[2 * index + 1][...])


def last_sum(place, pairs, after=()):
    return call(
        last_sum_kernel,
        "last_sum",
        place,
        [plain(array) for pair in pairs for array in pair],
        [made(pair[0].shape, LOW) for pair in pairs],
        after=after,
        work=cost(1e6, 1e6),
    )


def gathered(unit, mark=None):
    across = x_swap(unit)
    if mark is not None:
        across, mark = lax.optimization_barrier((across, mark))
    return unit, core_swap(unit), across, core_swap(across)


def quarters(place):
    x, c = place[2], place[3]
    return (x, c), (x, 1 - c), (1 - x, c), (1 - x, 1 - c)


def line_shift(place):
    seq = place[0] * 2 + place[1]
    return lax.rem(WIDTH - seq * 96, WIDTH)


def dense_out_kernel(
    place, d0, d1, d2, d3, u0, u1, u2, u3,
    down, up, out, gain2, shift2, down_bias, gain1, shift1, out_bias, up_bias, heads, tails,
):
    for down_unit, unit, (x, c) in zip((d0, d1, d2, d3), (u0, u1, u2, u3), quarters(place)):
        quarter = 2 * x + c
        down[pl.ds(pl.multiple_of(quarter * DOWN_ROWS, 32), DOWN_ROWS), :] = down_unit[...].astype(FLOAT)
        up[:, pl.ds(pl.multiple_of(quarter * WIDTH, LANES), WIDTH)] = unit[0:96, :].astype(FLOAT)
        rest = unit[96:128, :].astype(FLOAT)
        lanes = pl.ds(pl.multiple_of(c * HALF, LANES), HALF)
        out[pl.ds(pl.multiple_of(x * 48, 8), 24), lanes] = rest[0:24, 0:HALF]
        out[pl.ds(pl.multiple_of(x * 48 + 24, 8), 24), lanes] = rest[0:24, HALF:]

        @pl.when(x == 0)
        def _(rest=rest):
            heads[...] = rest[24:32]

        @pl.when(x == 1)
        def _(rest=rest):
            tails[...] = rest[24:32]

    seq = place[0] * 2 + place[1]
    shift = line_shift(place)
    head = pltpu.roll(heads[...], shift, 1)
    gain2[...] = head[0:1, 0:96]
    shift2[...] = head[1:2, 0:96]
    down_bias[...] = head[2:3, 0:96]
    tail = pltpu.roll(tails[...], shift, 1)
    gain1[...] = tail[0:1, 0:96]
    shift1[...] = tail[1:2, 0:96]
    out_bias[...] = tail[2:3, 0:96]
    wide = tails[pl.ds(4 + seq // 2, 1), :]
    up_bias[...] = jnp.where(seq % 2 == 0, wide[:, 0:HALF], wide[:, HALF:])


def dense_outputs(place, units, after=()):
    results, mark = call(
        dense_out_kernel,
        "dense_outputs",
        place,
        [plain(unit) for unit in units],
        [made((4 * DOWN_ROWS, WIDTH), FLOAT), made((96, FF), FLOAT), made((96, WIDTH), FLOAT)]
        + [made((1, 96), FLOAT)] * 6
        + [made((1, HALF), FLOAT)],
        scratch=[pltpu.VMEM((8, WIDTH), FLOAT)] * 2,
        after=after,
        work=cost(1e6, 3e6),
    )
    return (*results[:3], *(vector.reshape(-1) for vector in results[3:])), mark


def joint_out_kernel(place, u0, u1, u2, u3, joint, query_bias, value_bias, sums):
    for unit, (x, c) in zip((u0, u1, u2, u3), quarters(place)):

        def lanes(kind):
            return pl.ds(pl.multiple_of(kind * WIDTH + c * HALF, LANES), HALF)

        first = unit[0:JOINT_FIRST].astype(FLOAT)
        rest = unit[JOINT_FIRST:].astype(FLOAT)
        rows = pl.ds(pl.multiple_of(x * 48, 16), 48)
        joint[rows, lanes(0)] = first[:, 0:HALF]
        joint[rows, lanes(1)] = first[:, HALF:]
        joint[pl.ds(pl.multiple_of(x * 48, 8), 24), lanes(2)] = rest[0:24, 0:HALF]
        joint[pl.ds(pl.multiple_of(x * 48 + 24, 8), 24), lanes(2)] = rest[0:24, HALF:]

        @pl.when(x == 0)
        def _(rest=rest, c=c):
            half = pl.ds(pl.multiple_of(c * HALF, LANES), HALF)
            sums[0:1, half] = rest[24:25, 0:HALF]
            sums[1:2, half] = rest[24:25, HALF:]

    turned = pltpu.roll(sums[...], line_shift(place), 1)
    query_bias[...] = turned[0:1, 0:96]
    value_bias[...] = turned[1:2, 0:96]


def joint_outputs(place, units, after=()):
    results, mark = call(
        joint_out_kernel,
        "joint_outputs",
        place,
        [plain(unit) for unit in units],
        [made((96, 3 * WIDTH), FLOAT), made((1, 96), FLOAT), made((1, 96), FLOAT)],
        scratch=[pltpu.VMEM((8, WIDTH), FLOAT)],
        after=after,
        work=cost(1e6, 2e6),
    )
    return (results[0], results[1].reshape(-1), results[2].reshape(-1)), mark


def row_body(
    tokens,
    pair_lengths,
    joint_weight,
    query_bias,
    value_bias,
    out_weight,
    out_bias,
    first_gain,
    first_shift,
    up_weight,
    up_bias,
    down_weight,
    down_bias,
    second_gain,
    second_shift,
    cotangent,
):
    seq, rows = lax.axis_index("seq"), lax.axis_index("rows")
    z, y, x, c = seq // 2, seq % 2, rows // 2, rows % 2
    place = jnp.stack([z, y, x, c]).astype(jnp.int32)
    odd = z % 2
    weights = {
        "out": out_weight, "out_bias": out_bias, "gain1": first_gain, "shift1": first_shift,
        "up": up_weight, "up_bias": up_bias, "down": down_weight, "down_bias": down_bias,
        "gain2": second_gain, "shift2": second_shift,
    }

    def local_row(array, index):
        return lax.dynamic_index_in_dim(array, index, 0, keepdims=False)

    columns, query_row, value_row = own_columns(place, joint_weight, query_bias, value_bias)
    lengths = (pair_lengths, core_swap(pair_lengths))
    own = [row_swap(local_row(tokens, odd), 0), row_swap(local_row(tokens, 1 - odd), 1)]
    *own, columns, lengths = lax.optimization_barrier((*own, columns, lengths))
    across = [y_swap(block) for block in own]
    here = own + [core_swap(block) for block in own]
    (q, k_here, v_here, summed, stats), mark = first_attention(
        place, lengths, here, columns, query_row, value_row
    )
    padding = jnp.zeros((16, WIDTH), LOW)
    cotangents = [
        row_swap(jnp.concatenate([local_row(cotangent, index), padding], axis=0), second)
        for second, index in ((0, odd), (1, 1 - odd))
    ]
    across[0], across[1], mark, cotangents[0] = lax.optimization_barrier((across[0], across[1], mark, cotangents[0]))
    there = across + [core_swap(block) for block in across]
    blocks = here + there
    (att, k_there, v_there, log_total), mark = attention(
        place, lengths, there, columns, value_row, q, summed, stats, (mark,)
    )
    att, cotangents[1] = lax.optimization_barrier((att, cotangents[1]))
    att_got = core_swap(att)
    results, mark = forward(place, att, att_got, own, cotangents, weights, (mark,))
    (
        result0, result1, feed, second_grad, act, act_send, slope, unit1, inverse1, normed, normed_t, att_t, sums0
    ) = results
    act_got, feed_got, normed_got = core_swap(act_send), core_swap(feed), core_swap(normed)
    done = (row_swap(result0, 0), row_swap(result1, 1))
    (px_send, px, qy_send, qy), mark = down_units(place, act, act_got, feed, feed_got, (mark,))
    down_pair = (px, x_swap(px_send), qy, y_swap(qy_send))
    results, mark = backward(place, feed, slope, second_grad, unit1, inverse1, weights, (mark, normed_got))
    inner0, inner1, send0, send1, first_grad, branch_own, back_own, misc_send, sums1 = results
    got, misc = (core_swap(send0), core_swap(send1)), core_swap(misc_send)
    (x_send, y_send, px, qy), mark = up_units(
        place, normed_t, normed_got, (inner0, inner1), got, att_t, branch_own, misc, sums0, sums1, feed_got, (mark,)
    )
    (x_send, y_send, down_p, down_q), mark = down_pair_stage(place, down_pair, x_send, y_send, (mark,))
    x_got, y_got = x_swap(x_send), y_swap(y_send)
    (dq, dk, dv), mark = attention_back(
        place, lengths, q, (k_here, k_there), (v_here, v_there), log_total, att, back_own, misc, (mark,)
    )
    (token_own, own_send, token_far, far_send), mark = token_parts(place, dq, dk, dv, columns, (mark, *done))
    own_got, far_got = core_swap(own_send), core_swap(far_send)
    (px_send, joint_px, qy_send, joint_qy), mark = joint_units(
        place, blocks, dq, dk, dv, token_far, far_got, (mark,)
    )
    (x_send, y_send, p, q_, down_send, down_two), mark = second_stage(
        place, (x_got, y_got, px, qy, down_p, down_q), (mark,)
    )
    x_got, y_got, down_got = x_swap(x_send), y_swap(y_send), z_swap(down_send, 1)
    px_send, qy_send, mark = lax.optimization_barrier((px_send, qy_send, mark))
    across = y_swap(qy_send)
    joint_pair = (joint_px, x_swap(px_send), joint_qy, across)
    (up_send, up_two, down_send, down_keep), mark = up_line_stage(
        place, (x_got, y_got, p, q_, down_two, down_got), (mark,)
    )
    up_got, down_got = z_swap(up_send, 1), z_swap(down_send, 2)
    (up_send, up_keep), mark = end_stage(place, up_two, up_got, (mark, down_got))
    up_got = z_swap(up_send, 2)
    (x_send, y_send, joint_p, joint_q), mark = joint_pair_stage(place, joint_pair, (mark,))
    joint_x_got, joint_y_got = x_swap(x_send), y_swap(y_send)
    (token0, token1), mark = token_last(place, (token_own, own_got, across, first_grad), (mark,))
    back = (row_swap(token0, 0), row_swap(token1, 1))
    (down_unit, up_unit), mark = last_sum(place, ((down_keep, down_got), (up_keep, up_got)), (mark,))
    dense_all = (*gathered(down_unit), *gathered(up_unit))
    (joint_send, joint_two), mark = joint_line_stage(place, (joint_x_got, joint_y_got, joint_p, joint_q), (mark,))
    joint_got = z_swap(joint_send, 1)
    (joint_send, joint_keep), mark = end_stage(place, joint_two, joint_got, (mark,))
    joint_got = z_swap(joint_send, 2)
    (
        down_grad, up_grad, out_grad, second_gain_grad, second_shift_grad, down_bias_grad, first_gain_grad,
        first_shift_grad, out_bias_grad, up_bias_grad,
    ), mark = dense_outputs(place, dense_all, (mark,))
    (joint_unit,), mark = last_sum(place, ((joint_keep, joint_got),), (mark,))
    (outputs, token_grad), mark = back_rows(place, done, back, (mark,))
    joint_all = gathered(joint_unit, mark)
    (joint_grad, query_bias_grad, value_bias_grad), mark = joint_outputs(place, joint_all, (mark,))
    return (
        outputs,
        token_grad,
        joint_grad,
        query_bias_grad,
        value_bias_grad,
        out_grad,
        out_bias_grad,
        first_gain_grad,
        first_shift_grad,
        up_grad,
        up_bias_grad,
        down_grad,
        down_bias_grad,
        second_gain_grad,
        second_shift_grad,
    )


def body(tokens, *others):
    if (lax.axis_size("seq"), lax.axis_size("rows")) == (8, 4) and tokens.shape == (2, BLOCK, WIDTH):
        return row_body(tokens, *others)
    return general_body(tokens, *others)


def solution(mesh):
    placed = (
        P("rows", "seq", None),
        P("rows", None),
        P(),
        P(),
        P(),
        P(),
        P(),
        P(),
        P(),
        P(),
        P(),
        P(),
        P(),
        P(),
        P(),
        P("rows", "seq", None),
    )
    return jax.shard_map(
        body,
        mesh=mesh,
        in_specs=placed,
        out_specs=(
            P("rows", "seq", None),
            P("rows", "seq", None),
            P("seq", None),
            P("seq"),
            P("seq"),
            P("seq", None),
            P("seq"),
            P("seq"),
            P("seq"),
            P("seq", None),
            P("seq"),
            P("seq", None),
            P("seq"),
            P("seq"),
            P("seq"),
        ),
        check_vma=False,
    )
```

```python
import functools
import math

import jax
import jax.numpy as jnp
from jax import lax
from jax.experimental import pallas as pl
from jax.experimental.pallas import tpu as pltpu
from jax.sharding import PartitionSpec as P

HEADS = 12
HEAD_DIM = 64


NEGATIVE = -1e30
EPSILON = 1e-12


def from_behind(value, axis, steps):
    count = lax.axis_size(axis)
    pairs = [(source, (source + steps) % count) for source in range(count)]
    return lax.ppermute(value, axis, pairs)


def layer_norm(value, gain, shift):
    mean = jnp.mean(value, axis=-1, keepdims=True)
    centred = value - mean
    spread = jnp.mean(centred * centred, axis=-1, keepdims=True)
    return centred * lax.rsqrt(spread + EPSILON) * gain + shift


def gelu_exact(value):
    return jax.nn.gelu(value, approximate=False)


def pair_index(positions, ends):
    return jnp.sum((positions[None, :, None] >= ends[:, None, :]).astype(jnp.int32), axis=2)


def split_heads(array):
    return array.reshape(array.shape[0], array.shape[1], HEADS, HEAD_DIM)


def online_block(state, query_heads, query_pairs, key_block, value_block, key_pairs):
    highest, total, summed = state
    scores = jnp.einsum(
        "rqhd,rkhd->rhqk", query_heads, split_heads(key_block), preferred_element_type=jnp.float32
    ) * HEAD_DIM ** (-0.5)
    allowed = query_pairs[:, None, :, None] == key_pairs[:, None, None, :]
    masked = jnp.where(allowed, scores, NEGATIVE)
    new_high = jnp.maximum(highest, jnp.max(masked, axis=3))
    weights = jnp.where(allowed, jnp.exp(masked - new_high[..., None]), 0.0)
    factor = jnp.exp(highest - new_high)
    total = total * factor + jnp.sum(weights, axis=3)
    summed = summed * jnp.swapaxes(factor, 1, 2)[..., None] + jnp.einsum(
        "rhqk,rkhd->rqhd",
        weights.astype(jnp.bfloat16),
        split_heads(value_block),
        preferred_element_type=jnp.float32,
    )
    return (new_high, total, summed)


def tile_terms(queries, out_grad, log_total, delta, query_pairs, keys, values, key_pairs):
    scale = HEAD_DIM ** (-0.5)
    query_heads = split_heads(queries)
    grad_heads = split_heads(out_grad)
    key_heads = split_heads(keys)
    value_heads = split_heads(values)
    scores = (
        jnp.einsum("rqhd,rkhd->rhqk", query_heads, key_heads, preferred_element_type=jnp.float32)
        * scale
    )
    allowed = query_pairs[:, None, :, None] == key_pairs[:, None, None, :]
    weights = jnp.where(
        allowed, jnp.exp(jnp.where(allowed, scores, NEGATIVE) - log_total[..., None]), 0.0
    )
    weight_grad = jnp.einsum(
        "rqhd,rkhd->rhqk", grad_heads, value_heads, preferred_element_type=jnp.float32
    )
    score_grad = (weights * (weight_grad - delta[..., None])).astype(jnp.bfloat16)
    query_term = (
        jnp.einsum("rhqk,rkhd->rqhd", score_grad, key_heads, preferred_element_type=jnp.float32)
        * scale
    )
    key_term = (
        jnp.einsum("rhqk,rqhd->rkhd", score_grad, query_heads, preferred_element_type=jnp.float32)
        * scale
    )
    value_term = jnp.einsum(
        "rhqk,rqhd->rkhd",
        weights.astype(jnp.bfloat16),
        grad_heads,
        preferred_element_type=jnp.float32,
    )
    return (
        query_term.reshape(queries.shape),
        key_term.reshape(keys.shape),
        value_term.reshape(values.shape),
    )


def general_body(
    tokens,
    pair_lengths,
    joint_weight,
    query_bias,
    value_bias,
    out_weight,
    out_bias,
    first_gain,
    first_shift,
    up_weight,
    up_bias,
    down_weight,
    down_bias,
    second_gain,
    second_shift,
    cotangent,
):
    rows_here, seq_here, width = tokens.shape
    count = lax.axis_size("seq")
    cycle_index = lax.axis_index("seq")
    ends = jnp.cumsum(pair_lengths, axis=1)
    offsets = jnp.arange(seq_here, dtype=jnp.int32)
    own_pairs = pair_index(cycle_index * seq_here + offsets, ends)
    block_shape = (rows_here, seq_here, width)
    flat = tokens.reshape(rows_here * seq_here, width)
    projected = jnp.dot(flat, joint_weight, preferred_element_type=jnp.float32)
    queries = (projected[:, :width] + query_bias).astype(jnp.bfloat16).reshape(block_shape)
    keys = projected[:, width : 2 * width].astype(jnp.bfloat16).reshape(block_shape)
    values = (projected[:, 2 * width :] + value_bias).astype(jnp.bfloat16).reshape(block_shape)
    query_heads = split_heads(queries)
    initial = (
        jnp.full((rows_here, HEADS, seq_here), NEGATIVE, jnp.float32),
        jnp.zeros((rows_here, HEADS, seq_here), jnp.float32),
        jnp.zeros((rows_here, seq_here, HEADS, HEAD_DIM), jnp.float32),
    )
    key_piece = lax.all_gather(keys, "seq", axis=1, tiled=True)
    value_piece = lax.all_gather(values, "seq", axis=1, tiled=True)
    length = key_piece.shape[1]
    block = math.gcd(length, seq_here)

    def one_block(index, inner_state):
        first = index * block
        key_block = lax.dynamic_slice_in_dim(key_piece, first, block, 1)
        value_block = lax.dynamic_slice_in_dim(value_piece, first, block, 1)
        key_pairs = pair_index(first + jnp.arange(block, dtype=jnp.int32), ends)
        return online_block(inner_state, query_heads, own_pairs, key_block, value_block, key_pairs)

    highest, total, summed = lax.fori_loop(0, length // block, one_block, initial)
    log_total = highest + jnp.log(total)
    attended = (
        (summed / jnp.swapaxes(total, 1, 2)[..., None]).astype(jnp.bfloat16).reshape(flat.shape)
    )
    branch = jnp.dot(attended, out_weight, preferred_element_type=jnp.float32) + out_bias
    first_sum = flat.astype(jnp.float32) + branch
    normed, first_back = jax.vjp(layer_norm, first_sum, first_gain, first_shift)
    normed_low = normed.astype(jnp.bfloat16)
    inner = jnp.dot(normed_low, up_weight, preferred_element_type=jnp.float32) + up_bias
    activated_full, gelu_back = jax.vjp(gelu_exact, inner)
    activated = activated_full.astype(jnp.bfloat16)
    feed = jnp.dot(activated, down_weight, preferred_element_type=jnp.float32) + down_bias
    second_sum = normed + feed
    result, second_back = jax.vjp(layer_norm, second_sum, second_gain, second_shift)
    outputs = result.astype(jnp.bfloat16).reshape(tokens.shape)
    second_grad, second_gain_grad, second_shift_grad = second_back(
        cotangent.astype(jnp.float32).reshape(flat.shape)
    )
    feed_grad = second_grad.astype(jnp.bfloat16)
    down_grad = jnp.einsum("ti,tj->ij", activated, feed_grad, preferred_element_type=jnp.float32)
    down_bias_grad = jnp.sum(feed_grad.astype(jnp.float32), axis=0)
    activated_grad = jnp.einsum(
        "tj,ij->ti", feed_grad, down_weight, preferred_element_type=jnp.float32
    )
    inner_grad = gelu_back(activated_grad)[0].astype(jnp.bfloat16)
    up_grad = jnp.einsum("ti,tj->ij", normed_low, inner_grad, preferred_element_type=jnp.float32)
    up_bias_grad = jnp.sum(inner_grad.astype(jnp.float32), axis=0)
    normed_grad = second_grad + jnp.einsum(
        "tj,ij->ti", inner_grad, up_weight, preferred_element_type=jnp.float32
    )
    first_grad, first_gain_grad, first_shift_grad = first_back(normed_grad)
    branch_grad = first_grad.astype(jnp.bfloat16)
    out_grad = jnp.einsum("ti,tj->ij", attended, branch_grad, preferred_element_type=jnp.float32)
    out_bias_grad = jnp.sum(branch_grad.astype(jnp.float32), axis=0)
    attended_grad = jnp.einsum(
        "tj,ij->ti", branch_grad, out_weight, preferred_element_type=jnp.float32
    ).astype(jnp.bfloat16)
    delta = jnp.sum(
        (attended_grad.astype(jnp.float32) * attended.astype(jnp.float32)).reshape(
            rows_here, seq_here, HEADS, HEAD_DIM
        ),
        axis=3,
    )
    delta = jnp.swapaxes(delta, 1, 2)
    attended_grad = attended_grad.reshape(block_shape)
    zeros_block = jnp.zeros(block_shape, jnp.float32)

    def send_key_sums(sums):
        return (
            from_behind(sums[0].astype(jnp.bfloat16), "seq", 1).astype(jnp.float32),
            from_behind(sums[1].astype(jnp.bfloat16), "seq", 1).astype(jnp.float32),
        )

    def key_work(turn, pair_block, sums, query_sum):
        anchor = (cycle_index - turn) % count
        key_pairs = pair_index(anchor * seq_here + offsets, ends)
        query_term, key_term, value_term = tile_terms(
            queries,
            attended_grad,
            log_total,
            delta,
            own_pairs,
            pair_block[0],
            pair_block[1],
            key_pairs,
        )
        return ((sums[0] + key_term, sums[1] + value_term), query_sum + query_term)

    def key_turn(turn, state):
        pair_block, sums, query_sum = state
        sums, query_sum = key_work(turn, pair_block, sums, query_sum)
        sums = send_key_sums(sums)
        pair_block = from_behind((pair_block[0], pair_block[1]), "seq", 1)
        return (pair_block, sums, query_sum)

    pair_block, sums, query_sum = lax.fori_loop(
        0, count - 1, key_turn, ((keys, values), (zeros_block, zeros_block), zeros_block)
    )
    sums, query_sum = key_work(count - 1, pair_block, sums, query_sum)
    key_sum, value_sum = send_key_sums(sums)
    query_low = query_sum.astype(jnp.bfloat16).reshape(flat.shape)
    key_low = key_sum.astype(jnp.bfloat16).reshape(flat.shape)
    value_low = value_sum.astype(jnp.bfloat16).reshape(flat.shape)
    joint_low = jnp.concatenate([query_low, key_low, value_low], axis=1)
    joint_grad = jnp.einsum("ti,tj->ij", flat, joint_low, preferred_element_type=jnp.float32)
    query_bias_grad = jnp.sum(query_low.astype(jnp.float32), axis=0)
    value_bias_grad = jnp.sum(value_low.astype(jnp.float32), axis=0)
    token_grad = first_grad + jnp.einsum(
        "tj,ij->ti", joint_low, joint_weight, preferred_element_type=jnp.float32
    )
    gradients = (
        joint_grad,
        query_bias_grad,
        value_bias_grad,
        out_grad,
        out_bias_grad,
        first_gain_grad,
        first_shift_grad,
        up_grad,
        up_bias_grad,
        down_grad,
        down_bias_grad,
        second_gain_grad,
        second_shift_grad,
    )
    shares = (
        lax.psum_scatter(
            gradients[0].astype(jnp.bfloat16), "seq", scatter_dimension=0, tiled=True
        ).astype(jnp.float32),
        lax.psum_scatter(
            gradients[1].astype(jnp.bfloat16), "seq", scatter_dimension=0, tiled=True
        ).astype(jnp.float32),
        lax.psum_scatter(
            gradients[2].astype(jnp.bfloat16), "seq", scatter_dimension=0, tiled=True
        ).astype(jnp.float32),
        lax.psum_scatter(
            gradients[3].astype(jnp.bfloat16), "seq", scatter_dimension=0, tiled=True
        ).astype(jnp.float32),
        lax.psum_scatter(
            gradients[4].astype(jnp.bfloat16), "seq", scatter_dimension=0, tiled=True
        ).astype(jnp.float32),
        lax.psum_scatter(
            gradients[5].astype(jnp.bfloat16), "seq", scatter_dimension=0, tiled=True
        ).astype(jnp.float32),
        lax.psum_scatter(
            gradients[6].astype(jnp.bfloat16), "seq", scatter_dimension=0, tiled=True
        ).astype(jnp.float32),
        lax.psum_scatter(
            gradients[7].astype(jnp.bfloat16), "seq", scatter_dimension=0, tiled=True
        ).astype(jnp.float32),
        lax.psum_scatter(
            gradients[8].astype(jnp.bfloat16), "seq", scatter_dimension=0, tiled=True
        ).astype(jnp.float32),
        lax.psum_scatter(
            gradients[9].astype(jnp.bfloat16), "seq", scatter_dimension=0, tiled=True
        ).astype(jnp.float32),
        lax.psum_scatter(
            gradients[10].astype(jnp.bfloat16), "seq", scatter_dimension=0, tiled=True
        ).astype(jnp.float32),
        lax.psum_scatter(
            gradients[11].astype(jnp.bfloat16), "seq", scatter_dimension=0, tiled=True
        ).astype(jnp.float32),
        lax.psum_scatter(
            gradients[12].astype(jnp.bfloat16), "seq", scatter_dimension=0, tiled=True
        ).astype(jnp.float32),
    )
    shares = (
        lax.psum(shares[0].astype(jnp.bfloat16), "rows").astype(jnp.float32),
        lax.psum(shares[1].astype(jnp.bfloat16), "rows").astype(jnp.float32),
        lax.psum(shares[2].astype(jnp.bfloat16), "rows").astype(jnp.float32),
        lax.psum(shares[3].astype(jnp.bfloat16), "rows").astype(jnp.float32),
        lax.psum(shares[4].astype(jnp.bfloat16), "rows").astype(jnp.float32),
        lax.psum(shares[5].astype(jnp.bfloat16), "rows").astype(jnp.float32),
        lax.psum(shares[6].astype(jnp.bfloat16), "rows").astype(jnp.float32),
        lax.psum(shares[7].astype(jnp.bfloat16), "rows").astype(jnp.float32),
        lax.psum(shares[8].astype(jnp.bfloat16), "rows").astype(jnp.float32),
        lax.psum(shares[9].astype(jnp.bfloat16), "rows").astype(jnp.float32),
        lax.psum(shares[10].astype(jnp.bfloat16), "rows").astype(jnp.float32),
        lax.psum(shares[11].astype(jnp.bfloat16), "rows").astype(jnp.float32),
        lax.psum(shares[12].astype(jnp.bfloat16), "rows").astype(jnp.float32),
    )
    return (outputs, token_grad.reshape(tokens.shape)) + tuple(shares)


WIDTH = HEADS * HEAD_DIM
HALF = WIDTH // 2
FF = 4 * WIDTH
BLOCK = 128
OWN = 2 * BLOCK
LANES = 128
PAIRS_OF_HEADS = HALF // LANES
JOINT_ROWS = 80
JOINT_FIRST = 48
JOINT_SECOND = JOINT_ROWS - JOINT_FIRST
UP_ROWS = 128
DOWN_ROWS = 96
EXT = OWN + 16
DOWN_SENT = 2 * DOWN_ROWS
FLOAT = jnp.float32
LOW = jnp.bfloat16
AXES = ("seq", "rows")


def kernel_params(megabytes):
    return pltpu.CompilerParams(vmem_limit_bytes=megabytes << 20)


def shaped(shape, kind):
    return jax.ShapeDtypeStruct(shape, kind)


def whole(shape):
    return pl.BlockSpec(shape, lambda *_: (0,) * len(shape))


def cost(flops, moved, exps=0):
    return pl.CostEstimate(flops=1024, bytes_accessed=1024, transcendentals=0)


def dot(left, right):
    return lax.dot_general(left, right, (((1,), (0,)), ((), ())), preferred_element_type=FLOAT)


def dot_nt(left, right):
    return lax.dot_general(left, right, (((1,), (1,)), ((), ())), preferred_element_type=FLOAT)


def call(kernel, name, place, inputs, outputs, scratch=(), grid=(1,), scalars=(), after=(), megabytes=28, work=None, aliases=()):
    prefetch = 1 + len(scalars)
    given, made = len(inputs), len(outputs)

    def ordered(*refs):
        first = prefetch + given
        mark = refs[first + len(after) + made]
        mark[...] = jnp.zeros_like(mark)
        kernel(*refs[:first], *refs[first + len(after) : first + len(after) + made], *refs[first + len(after) + made + 1 :])

    results = pl.pallas_call(
        ordered,
        grid_spec=pltpu.PrefetchScalarGridSpec(
            num_scalar_prefetch=prefetch,
            grid=grid,
            in_specs=[spec for _, spec in inputs] + [pl.BlockSpec(memory_space=pl.ANY)] * len(after),
            out_specs=[spec for _, _, spec in outputs] + [whole((8, LANES))],
            scratch_shapes=list(scratch),
        ),
        out_shape=[shaped(shape, kind) for shape, kind, _ in outputs] + [shaped((8, LANES), FLOAT)],
        compiler_params=kernel_params(megabytes),
        cost_estimate=work,
        input_output_aliases={prefetch + source: target for source, target in aliases},
        name=name,
    )(place, *scalars, *[array for array, _ in inputs], *after)
    return results[:-1], results[-1]


def plain(array):
    return array, whole(array.shape)


def made(shape, kind):
    return shape, kind, whole(shape)


def device_at(z, y, x, c):
    return ((z * 2 + y) * 2 + x) * 2 + c


def permute(value, target):
    pairs = []
    for z in range(4):
        for y in range(2):
            for x in range(2):
                for c in range(2):
                    pairs.append((device_at(z, y, x, c), device_at(*target(z, y, x, c))))
    return lax.ppermute(value, AXES, pairs)


def core_swap(value):
    return permute(value, lambda z, y, x, c: (z, y, x, 1 - c))


def x_swap(value):
    return permute(value, lambda z, y, x, c: (z, y, 1 - x, c))


def y_swap(value):
    return permute(value, lambda z, y, x, c: (z, 1 - y, x, c))


def z_swap(value, bits):
    return permute(value, lambda z, y, x, c: (z ^ bits, y, x, c))


def row_swap(value, second):
    return permute(value, lambda z, y, x, c: (2 * c + (z % 2 ^ second), y, x, z // 2))


def first_positions(place):
    z, y, c = place[0], place[1], place[3]
    bases = []
    for core, line in ((c, y), (1 - c, y), (c, 1 - y), (1 - c, 1 - y)):
        for second in (0, 1):
            parity = z % 2
            parity = 1 - parity if second else parity
            bases.append((2 * (2 * core + parity) + line) * BLOCK)
    return bases


def pair_ends(place, own_lengths, peer_lengths):
    z, c = place[0], place[3]
    here = (z // 2) == c
    line = z % 2
    ends, end = [], 0
    for pair in range(own_lengths.shape[1]):
        end = end + jnp.where(here, own_lengths[line, pair], peer_lengths[line, pair])
        ends.append(end)
    return ends


def pairs_along(base, ends, axis):
    shape = (8, BLOCK) if axis == 1 else (BLOCK, LANES)
    position = base + lax.broadcasted_iota(jnp.int32, shape, axis)
    ids = jnp.zeros(shape, jnp.int32)
    for end in ends:
        ids = ids + (position >= end).astype(jnp.int32)
    return ids


def head_mask(rows):
    return lax.broadcasted_iota(jnp.int32, (rows, LANES), 1) < HEAD_DIM


def columns_kernel(place, columns, query_bias, value_bias, out, query_row, value_row):
    out[0] = columns[...]
    query_row[...] = query_bias[...]
    value_row[...] = value_bias[...]


def own_columns(place, joint_weight, query_bias, value_bias):
    half_row = pl.BlockSpec((1, HALF), lambda i, place: (0, place[3]))
    results, _ = call(
        columns_kernel,
        "own_columns",
        place,
        [
            (joint_weight, pl.BlockSpec((WIDTH, HALF), lambda i, place: (0, 2 * i + place[3]))),
            (row_of(query_bias), half_row),
            (row_of(value_bias), half_row),
        ],
        [((3, WIDTH, HALF), LOW, pl.BlockSpec((1, WIDTH, HALF), lambda i, place: (i, 0, 0)))]
        + [made((1, HALF), FLOAT)] * 2,
        grid=(3,),
        work=cost(1e6, 4e6),
    )
    return results


def first_attention_kernel(
    place, own_lengths, peer_lengths, t0, t1, t2, t3, columns, qb, vb, q_out, k_out, v_out, summed, stats, bias
):
    bases = first_positions(place)
    ends = pair_ends(place, own_lengths, peer_lengths)
    tokens = jnp.concatenate([block[...] for block in (t0, t1, t2, t3)], axis=0)
    queries = dot(tokens, columns[0]) + qb[...]
    q_out[...] = (queries.astype(LOW).astype(FLOAT) * HEAD_DIM**-0.5).astype(LOW)
    k_out[...] = dot(tokens, columns[1]).astype(LOW)
    v_out[...] = (dot(tokens, columns[2]) + vb[...]).astype(LOW)
    fill_bias(bias, bases[:4], bases[:4], ends)
    stats[...] = jnp.zeros_like(stats)
    for pair in range(PAIRS_OF_HEADS):
        lanes = pl.ds(pair * LANES, LANES)
        scores = masked_scores(k_out[:, lanes], q_out[:, lanes], bias)
        highest = jnp.max(scores, axis=0, keepdims=True)
        weights = jnp.exp(scores - highest)
        summed[pair] = dot(turned(v_out[:, lanes]), weights.astype(LOW))
        stats[2 * pair : 2 * pair + 1, :] = highest
        stats[2 * pair + 1 : 2 * pair + 2, :] = column_sum(weights)


def turned(array):
    return jnp.transpose(array.astype(FLOAT)).astype(LOW)


def masked_scores(keys, queries, bias):
    mask = bias[...]
    chosen = jnp.concatenate(halves_of(queries), axis=0)
    return dot_nt(keys, chosen) + jnp.concatenate([mask, mask], axis=1)


def fill_bias(bias, query_bases, key_bases, ends):
    key_ids = [pairs_along(base, ends, 1)[0:1] for base in key_bases]
    for i, base in enumerate(query_bases):
        query_ids = pairs_along(base, ends, 0)
        for j in range(len(key_bases)):
            bias[pl.ds(i * BLOCK, BLOCK), pl.ds(j * BLOCK, BLOCK)] = jnp.where(query_ids == key_ids[j], 0.0, NEGATIVE)


def halves_of(array):
    left = head_mask(array.shape[0])
    zeros = jnp.zeros_like(array)
    return jnp.where(left, array, zeros), jnp.where(left, zeros, array)


def first_attention(place, lengths, blocks, columns, query_bias, value_bias, after=()):
    return call(
        first_attention_kernel,
        "first_attention",
        place,
        [plain(array) for array in (*blocks, columns, query_bias, value_bias)],
        [made((512, HALF), LOW)] * 3 + [made((PAIRS_OF_HEADS, LANES, 1024), FLOAT), made((8, 1024), FLOAT)],
        scratch=[pltpu.VMEM((512, 512), FLOAT)],
        scalars=lengths,
        after=after,
        work=cost(4e9, 8e6, 3e6),
    )


def attention_kernel(
    place, own_lengths, peer_lengths, t0, t1, t2, t3, columns, vb, q, summed, stats,
    att_out, k_out, v_out, log_out, bias,
):
    bases = first_positions(place)
    ends = pair_ends(place, own_lengths, peer_lengths)
    tokens = jnp.concatenate([block[...] for block in (t0, t1, t2, t3)], axis=0)
    k_out[...] = dot(tokens, columns[1]).astype(LOW)
    v_out[...] = (dot(tokens, columns[2]) + vb[...]).astype(LOW)
    fill_bias(bias, bases[4:], bases[:4], ends)
    log_out[...] = jnp.zeros_like(log_out)
    top = lax.broadcasted_iota(jnp.int32, (LANES, 512), 0) < HEAD_DIM
    for pair in range(PAIRS_OF_HEADS):
        lanes = pl.ds(pair * LANES, LANES)
        scores = masked_scores(k_out[:, lanes], q[:, lanes], bias)
        before = stats[2 * pair : 2 * pair + 1, :]
        highest = jnp.maximum(before, jnp.max(scores, axis=0, keepdims=True))
        weights = jnp.exp(scores - highest)
        shrink = jnp.exp(before - highest)
        sums = column_sum(weights) + shrink * stats[2 * pair + 1 : 2 * pair + 2, :]
        total = (dot(turned(v_out[:, lanes]), weights.astype(LOW)) + shrink * summed[pair]) / sums
        att_out[:, lanes] = jnp.transpose(jnp.where(top, total[:, 0:512], total[:, 512:])).astype(LOW)
        logs = highest + jnp.log(sums)
        log_out[2 * pair : 2 * pair + 1, :] = logs[:, 0:512]
        log_out[2 * pair + 1 : 2 * pair + 2, :] = logs[:, 512:]


def attention(place, lengths, blocks, columns, value_bias, q, summed, stats, after=()):
    return call(
        attention_kernel,
        "attention",
        place,
        [plain(array) for array in (*blocks, columns, value_bias, q, summed, stats)],
        [made((512, HALF), LOW)] * 3 + [made((8, 512), FLOAT)],
        scratch=[pltpu.VMEM((512, 512), FLOAT)],
        scalars=lengths,
        after=after,
        work=cost(4e9, 8e6, 3e6),
    )


def centred_norm(value):
    mean = jnp.mean(value, axis=-1, keepdims=True)
    centred = value - mean
    spread = jnp.mean(centred * centred, axis=-1, keepdims=True)
    inverse = lax.rsqrt(spread + EPSILON)
    return centred * inverse, inverse


def norm_back(grad, unit, inverse):
    mean = jnp.mean(grad, axis=-1, keepdims=True)
    along = jnp.mean(grad * unit, axis=-1, keepdims=True)
    return (grad - mean - unit * along) * inverse


def column_sum(value):
    return jnp.sum(value, axis=0, keepdims=True)


def forward_kernel(
    place, att, att_got, wo_own, wo_other, out_bias, x0, x1, gain1, shift1, up, up_bias, down,
    down_bias, gain2, shift2, cot0, cot1,
    result0, result1, feed_ext, second_grad, act_keep, act_send, slope, unit1, inverse1, normed_low, normed_t, att_t, sums,
    act_t,
):
    c = place[3]
    tokens = jnp.concatenate([x0[...], x1[...]], axis=0).astype(FLOAT)
    att_own, att_other = att[0:OWN], att_got[OWN:]
    branch = dot(att_own, wo_own[...]) + dot(att_other, wo_other[...]) + out_bias[...]
    unit, inverse = centred_norm(tokens + branch)
    unit1[...] = unit
    inverse1[...] = jnp.broadcast_to(inverse, (OWN, LANES))
    normed = unit * gain1[...] + shift1[...]
    low = normed.astype(LOW)
    normed_low[...] = low
    normed_t[...] = jnp.transpose(normed).astype(LOW)
    mine = pl.ds(pl.multiple_of(c * HALF, HALF), HALF)
    other = pl.ds(pl.multiple_of((1 - c) * HALF, HALF), HALF)
    att_t[mine, :] = jnp.transpose(att[...].astype(FLOAT)).astype(LOW)
    att_t[other, 0:OWN] = jnp.transpose(att_other.astype(FLOAT)).astype(LOW)
    att_t[other, OWN:] = jnp.transpose(att_got[0:OWN].astype(FLOAT)).astype(LOW)
    inner = dot(low, up[...]) + up_bias[...]
    below = 0.5 + 0.5 * lax.erf(inner * math.sqrt(0.5))
    density = jnp.exp(inner * inner * -0.5) * (1.0 / math.sqrt(2.0 * math.pi))
    activated = inner * below
    slope[...] = (below + inner * density).astype(LOW)
    act_t[...] = jnp.transpose(activated).astype(LOW).reshape(16, 2, DOWN_ROWS, OWN)
    act_keep[...] = act_t[:, c]
    act_send[...] = act_t[:, 1 - c]
    feed = dot(activated.astype(LOW), down[...])
    unit, inverse = centred_norm(normed + feed + down_bias[...])
    result = (unit * gain2[...] + shift2[...]).astype(LOW)
    result0[...] = result[0:BLOCK]
    result1[...] = result[BLOCK:]
    cotangent = jnp.concatenate([cot0[0:BLOCK], cot1[0:BLOCK]], axis=0).astype(FLOAT)
    grad = norm_back(cotangent * gain2[...], unit, inverse)
    second_grad[...] = grad
    low_grad = grad.astype(LOW)
    rows = jnp.concatenate(
        [
            column_sum(cotangent * unit),
            column_sum(cotangent),
            column_sum(low_grad.astype(FLOAT)),
            jnp.zeros((5, WIDTH), FLOAT),
        ],
        axis=0,
    )
    sums[...] = rows
    feed_ext[0:OWN] = low_grad
    feed_ext[OWN:] = jnp.concatenate([rows, jnp.zeros_like(rows)], axis=0).astype(LOW)


def row_of(vector):
    return vector.reshape(1, vector.shape[0])


def forward(place, att, att_got, tokens, cotangents, weights, after=()):
    chunk = FF

    def vector(name):
        return plain(row_of(weights[name]))

    units = ((16, DOWN_ROWS, OWN), LOW, pl.BlockSpec((16, DOWN_ROWS, OWN), lambda i, place: (i, 0, 0)))
    return call(
        forward_kernel,
        "forward",
        place,
        [
            plain(att),
            plain(att_got),
            (weights["out"], pl.BlockSpec((HALF, WIDTH), lambda i, place: (place[3], 0))),
            (weights["out"], pl.BlockSpec((HALF, WIDTH), lambda i, place: (1 - place[3], 0))),
            vector("out_bias"), plain(tokens[0]), plain(tokens[1]), vector("gain1"), vector("shift1"),
            (weights["up"], pl.BlockSpec((WIDTH, chunk), lambda i, place: (0, i))),
            (row_of(weights["up_bias"]), pl.BlockSpec((1, chunk), lambda i, place: (0, i))),
            (weights["down"], pl.BlockSpec((chunk, WIDTH), lambda i, place: (i, 0))),
            vector("down_bias"), vector("gain2"), vector("shift2"), plain(cotangents[0]), plain(cotangents[1]),
        ],
        [
            made((BLOCK, WIDTH), LOW), made((BLOCK, WIDTH), LOW), made((EXT, WIDTH), LOW),
            made((OWN, WIDTH), FLOAT), units, units,
            ((OWN, FF), LOW, pl.BlockSpec((OWN, chunk), lambda i, place: (0, i))),
            made((OWN, WIDTH), FLOAT), made((OWN, LANES), FLOAT), made((OWN, WIDTH), LOW),
            made((WIDTH, OWN), LOW), made((WIDTH, 512), LOW), made((8, WIDTH), FLOAT),
        ],
        scratch=[pltpu.VMEM((16, 2, DOWN_ROWS, OWN), LOW)],
        after=after,
        work=cost(2.7e9, 20e6, 2e6),
    )


def split_units(place, units, px_send, px, qy_send, qy):
    y, x = place[1], place[2]
    half = units.shape[2] // 2
    for line in range(2):
        px[0, line] = units[line, x, 0:half]
        px_send[0, line] = units[line, 1 - x, 0:half]
    for side in range(2):
        qy[0, side] = units[y, side, half:]
        qy_send[0, side] = units[1 - y, side, half:]


def unit_outputs(rows, width):
    shape = (4, 2, rows // 2, width)
    return [(shape, LOW, pl.BlockSpec((1,) + shape[1:], lambda i, place: (i, 0, 0, 0)))] * 4


def down_kernel(place, act, act_got, feed, feed_got, px_send, px, qy_send, qy, units):
    shape = (4 * DOWN_ROWS, OWN)
    total = dot(act[...].reshape(shape), feed[0:OWN]) + dot(act_got[...].reshape(shape), feed_got[0:OWN])
    units[...] = total.astype(LOW).reshape(units.shape)
    split_units(place, units, px_send, px, qy_send, qy)


def down_units(place, act, act_got, feed, feed_got, after=()):
    block = pl.BlockSpec((4, DOWN_ROWS, OWN), lambda i, place: (i, 0, 0))
    return call(
        down_kernel,
        "down_units",
        place,
        [(act, block), (act_got, block), plain(feed), plain(feed_got)],
        unit_outputs(DOWN_ROWS, WIDTH),
        scratch=[pltpu.VMEM((2, 2, DOWN_ROWS, WIDTH), LOW)],
        grid=(4,),
        after=after,
        work=cost(0.6e9, 3.5e6),
    )


def backward_kernel(
    place, feed_ext, slope, up, down, second_grad, unit1, inverse1, gain1, wo_own, wo_other,
    inner0, inner1, send0, send1, first_grad, branch_own, back_own, misc, sums,
    inner, branch,
):
    c = place[3]
    grad = (dot_nt(feed_ext[0:OWN], down[...]) * slope[...].astype(FLOAT)).astype(LOW)
    inner[...] = grad
    for target, index in ((inner0, c), (inner1, 2 + c), (send0, 1 - c), (send1, 3 - c)):
        target[...] = inner[:, pl.ds(pl.multiple_of(index * WIDTH, LANES), WIDTH)]
    inner_sum = column_sum(grad.astype(FLOAT))
    total = second_grad[...] + dot_nt(grad, up[...])
    unit = unit1[...]
    grad1 = norm_back(total * gain1[...], unit, inverse1[:, 0:1])
    first_grad[...] = grad1
    low = grad1.astype(LOW)
    branch[...] = low
    rows = jnp.concatenate(
        [
            column_sum(total * unit),
            column_sum(total),
            column_sum(low.astype(FLOAT)),
            jnp.zeros((1, WIDTH), FLOAT),
        ]
        + [inner_sum[:, index * WIDTH : (index + 1) * WIDTH] for index in range(4)],
        axis=0,
    )
    sums[...] = rows
    branch_own[...] = branch[:, pl.ds(pl.multiple_of(c * HALF, LANES), HALF)]
    back_own[...] = dot_nt(low, wo_own[...]).astype(LOW)
    misc[0:OWN, 0:HALF] = branch[:, pl.ds(pl.multiple_of((1 - c) * HALF, LANES), HALF)]
    misc[0:OWN, HALF:] = dot_nt(low, wo_other[...]).astype(LOW)
    misc[OWN:] = jnp.concatenate([rows, jnp.zeros_like(rows)], axis=0).astype(LOW)


def backward(place, feed_ext, slope, second_grad, unit1, inverse1, weights, after=()):
    chunk = FF
    return call(
        backward_kernel,
        "backward",
        place,
        [
            plain(feed_ext),
            (slope, pl.BlockSpec((OWN, chunk), lambda i, place: (0, i))),
            (weights["up"], pl.BlockSpec((WIDTH, chunk), lambda i, place: (0, i))),
            (weights["down"], pl.BlockSpec((chunk, WIDTH), lambda i, place: (i, 0))),
            plain(second_grad), plain(unit1), plain(inverse1), plain(row_of(weights["gain1"])),
            (weights["out"], pl.BlockSpec((HALF, WIDTH), lambda i, place: (place[3], 0))),
            (weights["out"], pl.BlockSpec((HALF, WIDTH), lambda i, place: (1 - place[3], 0))),
        ],
        [made((OWN, WIDTH), LOW)] * 4
        + [
            made((OWN, WIDTH), FLOAT), made((OWN, HALF), LOW), made((OWN, HALF), LOW), made((EXT, WIDTH), LOW),
            made((8, WIDTH), FLOAT),
        ],
        scratch=[pltpu.VMEM((OWN, FF), LOW), pltpu.VMEM((OWN, WIDTH), LOW)],
        after=after,
        work=cost(2.7e9, 16e6),
    )


def up_kernel(
    place, normed_t, normed_got, inner0, inner1, got0, got1, att_t, branch, misc, sums0, sums1, feed_got,
    x_send, y_send, px, qy, units, normed_got_t,
):
    z = pl.program_id(0)
    y, x = place[1], place[2]

    @pl.when(z == 0)
    def _():
        normed_got_t[...] = jnp.transpose(normed_got[...].astype(FLOAT)).astype(LOW)

    theirs = normed_got_t[pl.ds(pl.multiple_of(z * 192, 32), 192), :]
    outer = dot(att_t[:, 0:OWN], branch[...]) + dot(att_t[:, OWN:], misc[0:OWN, 0:HALF])
    for side, inner, got, sums, pair in ((0, inner0, got0, sums0, feed_got), (1, inner1, got1, sums1, misc)):
        grad = dot(normed_t[...], inner[...]) + dot(theirs, got[...])
        vectors = sums[...] + pair[OWN:].astype(FLOAT)[0:8]
        for line in range(2):
            first = line * 96 + side * 48
            rest = jnp.concatenate([outer[first : first + 24], outer[first + 24 : first + 48]], axis=1)
            units[line, side] = jnp.concatenate(
                [grad[line * 96 : line * 96 + 96], rest, vectors], axis=0
            ).astype(LOW)
    half = UP_ROWS // 2
    for index in range(2):
        rows = pl.ds(pl.multiple_of(DOWN_SENT + (z * 2 + index) * half, half), half)
        px[0, index] = units[index, x, 0:half]
        x_send[rows, :] = units[index, 1 - x, 0:half]
        qy[0, index] = units[y, index, half:]
        y_send[rows, :] = units[1 - y, index, half:]


def up_units(place, normed_t, normed_got, inner, got, att_t, branch, misc, sums0, sums1, feed_got, after=()):
    rows = pl.BlockSpec((192, OWN), lambda i, place: (i, 0))
    return call(
        up_kernel,
        "up_units",
        place,
        [
            (normed_t, rows), plain(normed_got), plain(inner[0]), plain(inner[1]), plain(got[0]), plain(got[1]),
            (att_t, pl.BlockSpec((192, 512), lambda i, place: (i, 0))),
            plain(branch), plain(misc), plain(sums0), plain(sums1), plain(feed_got),
        ],
        [made((DOWN_SENT + 4 * UP_ROWS, WIDTH), LOW)] * 2 + unit_outputs(UP_ROWS, WIDTH)[:2],
        scratch=[pltpu.VMEM((2, 2, UP_ROWS, WIDTH), LOW), pltpu.VMEM((WIDTH, OWN), LOW)],
        grid=(4,),
        after=after,
        work=cost(0.9e9, 5e6),
    )


def attention_back_kernel(
    place, own_lengths, peer_lengths, q, k0, k1, v0, v1, log_total, att, back0, misc,
    dq_out, dk_out, dv_out, bias,
):
    bases = first_positions(place)
    ends = pair_ends(place, own_lengths, peer_lengths)
    query_ids = [pairs_along(base, ends, 1)[0:1] for base in bases[:4]]
    for j in range(8):
        key_ids = pairs_along(bases[j], ends, 0)
        for i in range(4):
            bias[pl.ds(j * BLOCK, BLOCK), pl.ds(i * BLOCK, BLOCK)] = jnp.where(
                key_ids == query_ids[i], 0.0, NEGATIVE
            )
    for pair in range(PAIRS_OF_HEADS):
        lanes = pl.ds(pair * LANES, LANES)
        keys = jnp.concatenate([k0[:, lanes], k1[:, lanes]], axis=0)
        values = jnp.concatenate([v0[:, lanes], v1[:, lanes]], axis=0)
        keys_t = jnp.transpose(keys.astype(FLOAT)).astype(LOW)
        key_grad = jnp.zeros((1024, LANES), FLOAT)
        value_grad = jnp.zeros((1024, LANES), FLOAT)
        left = head_mask(OWN)
        for part in range(2):
            rows = pl.ds(part * OWN, OWN)
            queries = q[rows, lanes]
            grads = back0[:, lanes] if part == 0 else misc[0:OWN, pl.ds(HALF + pair * LANES, LANES)]
            zeros = jnp.zeros_like(queries)
            product = jnp.transpose(grads.astype(FLOAT) * att[rows, lanes].astype(FLOAT))
            halves = []
            for half in range(2):
                if half == 0:
                    chosen, chosen_grads = jnp.where(left, queries, zeros), jnp.where(left, grads, zeros)
                else:
                    chosen, chosen_grads = jnp.where(left, zeros, queries), jnp.where(left, zeros, grads)
                delta = column_sum(product[half * HEAD_DIM : (half + 1) * HEAD_DIM])
                head = pair * 2 + half
                scores = dot_nt(keys, chosen) + bias[:, rows]
                weights = jnp.exp(scores - log_total[head : head + 1, rows])
                weight_grad = dot_nt(values, chosen_grads)
                score_grad = (weights * (weight_grad - delta)).astype(LOW)
                value_grad = value_grad + dot(weights.astype(LOW), chosen_grads)
                key_grad = key_grad + dot(score_grad, chosen)
                halves.append(dot(keys_t, score_grad))
            query_grad_t = jnp.concatenate([halves[0][0:HEAD_DIM], halves[1][HEAD_DIM:LANES]], axis=0)
            dq_out[rows, lanes] = (jnp.transpose(query_grad_t) * HEAD_DIM**-0.5).astype(LOW)
        dk_out[:, lanes] = key_grad.astype(LOW)
        dv_out[:, lanes] = value_grad.astype(LOW)


def attention_back(place, lengths, q, keys, values, log_total, att, back_own, misc, after=()):
    return call(
        attention_back_kernel,
        "attention_back",
        place,
        [plain(array) for array in (q, *keys, *values, log_total, att, back_own, misc)],
        [made((512, HALF), LOW), made((1024, HALF), LOW), made((1024, HALF), LOW)],
        scratch=[pltpu.VMEM((1024, 512), FLOAT)],
        scalars=lengths,
        after=after,
        work=cost(7e9, 6e6, 3e6),
    )


def token_kernel(place, dq, dk, dv, columns, own, own_send, far, far_send):
    for part, target in enumerate((own, own_send, far, far_send)):
        rows = pl.ds(part * OWN, OWN)
        total = dot_nt(dk[rows, :], columns[1]) + dot_nt(dv[rows, :], columns[2])
        if part < 2:
            total = total + dot_nt(dq[rows, :], columns[0])
        target[...] = total.astype(LOW)


def token_parts(place, dq, dk, dv, columns, after=()):
    return call(
        token_kernel,
        "token_parts",
        place,
        [plain(dq), plain(dk), plain(dv), plain(columns)],
        [made((OWN, WIDTH), LOW)] * 4,
        after=after,
        work=cost(1.5e9, 5e6),
    )


def token_last_kernel(place, own, own_got, across, first_grad, token0, token1):
    total = own[...].astype(FLOAT) + own_got[...].astype(FLOAT) + across[8 * JOINT_SECOND :].astype(FLOAT) + first_grad[...]
    total = total.astype(LOW)
    token0[...] = total[0:BLOCK]
    token1[...] = total[BLOCK:]


def token_last(place, arrays, after=()):
    return call(
        token_last_kernel,
        "token_last",
        place,
        [plain(array) for array in arrays],
        [made((BLOCK, WIDTH), LOW)] * 2,
        after=after,
        work=cost(1e6, 2e6),
    )


def back_rows_kernel(place, done0, done1, back0, back1, outputs, token_grad):
    odd = place[0] % 2
    outputs[odd] = done0[...]
    outputs[1 - odd] = done1[...]
    token_grad[odd] = back0[...].astype(FLOAT)
    token_grad[1 - odd] = back1[...].astype(FLOAT)


def back_rows(place, done, back, after=()):
    return call(
        back_rows_kernel,
        "back_rows",
        place,
        [plain(array) for array in (*done, *back)],
        [made((2, BLOCK, WIDTH), LOW), made((2, BLOCK, WIDTH), FLOAT)],
        after=after,
        work=cost(1e6, 2e6),
    )


def joint_kernel(
    place, t0, t1, t2, t3, t4, t5, t6, t7, dq, dk, dv, far, far_got, px_send, px, qy_send, qy, tokens_t, units
):
    y, x = place[1], place[2]
    qy_send[pl.ds(8 * JOINT_SECOND, OWN), :] = added(far[...], far_got[...])
    for index, block in enumerate((t0, t1, t2, t3, t4, t5, t6, t7)):
        tokens_t[:, pl.ds(index * BLOCK, BLOCK)] = jnp.transpose(block[...].astype(FLOAT)).astype(LOW)
    biases = jnp.concatenate([column_sum(dq[...].astype(FLOAT)), column_sum(dv[...].astype(FLOAT))], axis=1)
    biases = jnp.concatenate([biases, jnp.zeros((7, WIDTH), FLOAT)], axis=0)
    for z in range(4):
        rows = pl.ds(z * 192, 192)
        query = dot(tokens_t[rows, 0:512], dq[...])
        key = dot(tokens_t[rows, :], dk[...])
        value = dot(tokens_t[rows, :], dv[...])
        for line in range(2):
            for side in range(2):
                at = line * 96 + side * 48
                units[line, side, 0:JOINT_FIRST] = jnp.concatenate(
                    [query[at : at + 48], key[at : at + 48]], axis=1
                ).astype(LOW)
                rest = jnp.concatenate([value[at : at + 24], value[at + 24 : at + 48]], axis=1)
                units[line, side, JOINT_FIRST:] = jnp.concatenate([rest, biases], axis=0).astype(LOW)
        for line in range(2):
            px[z, line] = units[line, x, 0:JOINT_FIRST]
            px_send[z, line] = units[line, 1 - x, 0:JOINT_FIRST]
        for side in range(2):
            qy[z, side] = units[y, side, JOINT_FIRST:]
            qy_send[pl.ds((z * 2 + side) * JOINT_SECOND, JOINT_SECOND), :] = units[1 - y, side, JOINT_FIRST:]


def joint_units(place, blocks, dq, dk, dv, far, far_got, after=()):
    first, second = made((4, 2, JOINT_FIRST, WIDTH), LOW), made((4, 2, JOINT_SECOND, WIDTH), LOW)
    return call(
        joint_kernel,
        "joint_units",
        place,
        [plain(array) for array in (*blocks, dq, dk, dv, far, far_got)],
        [first, first, made((8 * JOINT_SECOND + OWN, WIDTH), LOW), second],
        scratch=[pltpu.VMEM((WIDTH, 1024), LOW), pltpu.VMEM((2, 2, JOINT_ROWS, WIDTH), LOW)],
        after=after,
        work=cost(1.5e9, 6e6),
    )


def added(left, right):
    return (left.astype(FLOAT) + right.astype(FLOAT)).astype(LOW)


def down_pair_kernel(place, px, px_got, qy, qy_got, x_in, y_in, x_send, y_send, p, q):
    y, x = place[1], place[2]
    p[0] = added(px[0, y], px_got[0, y])
    y_send[...] = added(px[0, 1 - y], px_got[0, 1 - y])
    q[0] = added(qy[0, x], qy_got[0, x])
    x_send[...] = added(qy[0, 1 - x], qy_got[0, 1 - x])


def down_pair_stage(place, arrays, x_send, y_send, after=()):
    half = DOWN_ROWS // 2
    block = pl.BlockSpec((1, 2, half, WIDTH), lambda i, place: (i, 0, 0, 0))
    sent = (x_send.shape, LOW, pl.BlockSpec((half, WIDTH), lambda i, place: (i, 0)))
    kept = ((4, half, WIDTH), LOW, pl.BlockSpec((1, half, WIDTH), lambda i, place: (i, 0, 0)))
    anywhere = pl.BlockSpec(memory_space=pl.ANY)
    return call(
        down_pair_kernel,
        "down_pair_stage",
        place,
        [(array, block) for array in arrays] + [(x_send, anywhere), (y_send, anywhere)],
        [sent, sent, kept, kept],
        grid=(4,),
        after=after,
        work=cost(1e6, 1e7),
        aliases=((4, 0), (5, 1)),
    )


def second_kernel(
    place, x_got, y_got, px, qy, down_p, down_q, x_send, y_send, p, q, down_send, down_keep
):
    z_here, y, x = place[0], place[1], place[2]
    half = UP_ROWS // 2
    for z in range(4):
        for got, have, own, keep, send in ((x_got, px, y, p, y_send), (y_got, qy, x, q, x_send)):
            at = DOWN_SENT + z * UP_ROWS
            mine = pl.ds(pl.multiple_of(at + own * half, half), half)
            other = pl.ds(pl.multiple_of(at + (1 - own) * half, half), half)
            keep[z] = added(have[z, own], got[mine, :])
            send[pl.ds(z * half, half), :] = added(have[z, 1 - own], got[other, :])
    low = z_here % 2
    small = DOWN_ROWS // 2
    for target, parity in ((down_keep, low), (down_send, 1 - low)):
        for high in range(2):
            index = 2 * high + parity
            rows = pl.ds(pl.multiple_of(index * small, small), small)
            target[high, 0:small] = added(down_p[index], y_got[rows, :])
            target[high, small:] = added(down_q[index], x_got[rows, :])


def second_stage(place, arrays, after=()):
    kept = made((4, UP_ROWS // 2, WIDTH), LOW)
    down = made((2, DOWN_ROWS, WIDTH), LOW)
    return call(
        second_kernel,
        "second_stage",
        place,
        [plain(array) for array in arrays],
        [made((OWN, WIDTH), LOW), made((OWN, WIDTH), LOW), kept, kept, down, down],
        after=after,
        work=cost(1e6, 1e7),
    )


def joint_pair_kernel(place, px, px_got, qy, qy_got, x_send, y_send, p, q):
    y, x = place[1], place[2]
    for z in range(4):
        p[z] = added(px[z, y], px_got[z, y])
        y_send[z] = added(px[z, 1 - y], px_got[z, 1 - y])


        def from_y(side):
            return qy_got[pl.ds(pl.multiple_of((z * 2 + side) * JOINT_SECOND, 32), JOINT_SECOND), :]

        q[z] = added(qy[z, x], from_y(x))
        x_send[z] = added(qy[z, 1 - x], from_y(1 - x))


def joint_pair_stage(place, arrays, after=()):
    first, second = made((4, JOINT_FIRST, WIDTH), LOW), made((4, JOINT_SECOND, WIDTH), LOW)
    return call(
        joint_pair_kernel,
        "joint_pair_stage",
        place,
        [plain(array) for array in arrays],
        [second, first, first, second],
        after=after,
        work=cost(1e6, 1e7),
    )


def up_line_kernel(place, x_got, y_got, p, q, down_two, down_got, send, keep, down_send, down_keep):
    low, high_here = place[0] % 2, place[0] // 2
    half = UP_ROWS // 2
    for target, parity in ((keep, low), (send, 1 - low)):
        for high in range(2):
            index = 2 * high + parity
            rows = pl.ds(pl.multiple_of(index * half, half), half)
            target[high, 0:half] = added(p[index], y_got[rows, :])
            target[high, half:] = added(q[index], x_got[rows, :])
    down_keep[...] = added(down_two[high_here], down_got[high_here])
    down_send[...] = added(down_two[1 - high_here], down_got[1 - high_here])


def up_line_stage(place, arrays, after=()):
    return call(
        up_line_kernel,
        "up_line_stage",
        place,
        [plain(array) for array in arrays],
        [made((2, UP_ROWS, WIDTH), LOW)] * 2 + [made((DOWN_ROWS, WIDTH), LOW)] * 2,
        after=after,
        work=cost(1e6, 1e7),
    )


def joint_line_kernel(place, x_got, y_got, p, q, keep, one, two, three):
    low, high = place[0] % 2, place[0] // 2
    for target, index in (
        (keep, 2 * high + low), (one, 2 * high + 1 - low), (two, 2 * (1 - high) + low), (three, 2 * (1 - high) + 1 - low)
    ):
        target[0:JOINT_FIRST] = added(p[index], y_got[index])
        target[JOINT_FIRST:] = added(q[index], x_got[index])


def joint_line_stage(place, arrays, after=()):
    return call(
        joint_line_kernel,
        "joint_line_stage",
        place,
        [plain(array) for array in arrays],
        [made((JOINT_ROWS, WIDTH), LOW)] * 4,
        after=after,
        work=cost(1e6, 1e6),
    )


def end_stage_kernel(place, keep_two, got, send, keep):
    high = place[0] // 2
    keep[...] = added(keep_two[high], got[high])
    send[...] = added(keep_two[1 - high], got[1 - high])


def end_stage(place, keep_two, got, after=()):
    return call(
        end_stage_kernel,
        "end_stage",
        place,
        [plain(keep_two), plain(got)],
        [made(keep_two.shape[1:], LOW)] * 2,
        after=after,
        work=cost(1e6, 1e6),
    )


def joint_sum_kernel(place, first, second, third, fourth, out):
    total = (first[...].astype(FLOAT) + second[...].astype(FLOAT)) + (third[...].astype(FLOAT) + fourth[...].astype(FLOAT))
    out[...] = total.astype(LOW)


def joint_sum(place, arrays, after=()):
    results, mark = call(
        joint_sum_kernel,
        "joint_sum",
        place,
        [plain(array) for array in arrays],
        [made((JOINT_ROWS, WIDTH), LOW)],
        after=after,
        work=cost(1e6, 1e6),
    )
    return results[0], mark


def last_sum_kernel(place, *refs):
    count = len(refs) // 3
    for index in range(count):
        refs[2 * count + index][...] = added(refs[2 * index][...], refs[2 * index + 1][...])


def last_sum(place, pairs, after=()):
    return call(
        last_sum_kernel,
        "last_sum",
        place,
        [plain(array) for pair in pairs for array in pair],
        [made(pair[0].shape, LOW) for pair in pairs],
        after=after,
        work=cost(1e6, 1e6),
    )


def gathered(unit, mark=None):
    across = x_swap(unit)
    if mark is not None:
        across, mark = lax.optimization_barrier((across, mark))
    return unit, core_swap(unit), across, core_swap(across)


def quarters(place):
    x, c = place[2], place[3]
    return (x, c), (x, 1 - c), (1 - x, c), (1 - x, 1 - c)


def line_shift(place):
    seq = place[0] * 2 + place[1]
    return lax.rem(WIDTH - seq * 96, WIDTH)


def dense_out_kernel(
    place, d0, d1, d2, d3, u0, u1, u2, u3,
    down, up, out, gain2, shift2, down_bias, gain1, shift1, out_bias, up_bias, heads, tails,
):
    for down_unit, unit, (x, c) in zip((d0, d1, d2, d3), (u0, u1, u2, u3), quarters(place)):
        quarter = 2 * x + c
        down[pl.ds(pl.multiple_of(quarter * DOWN_ROWS, 32), DOWN_ROWS), :] = down_unit[...].astype(FLOAT)
        up[:, pl.ds(pl.multiple_of(quarter * WIDTH, LANES), WIDTH)] = unit[0:96, :].astype(FLOAT)
        rest = unit[96:128, :].astype(FLOAT)
        lanes = pl.ds(pl.multiple_of(c * HALF, LANES), HALF)
        out[pl.ds(pl.multiple_of(x * 48, 8), 24), lanes] = rest[0:24, 0:HALF]
        out[pl.ds(pl.multiple_of(x * 48 + 24, 8), 24), lanes] = rest[0:24, HALF:]

        @pl.when(x == 0)
        def _(rest=rest):
            heads[...] = rest[24:32]

        @pl.when(x == 1)
        def _(rest=rest):
            tails[...] = rest[24:32]

    seq = place[0] * 2 + place[1]
    shift = line_shift(place)
    head = pltpu.roll(heads[...], shift, 1)
    gain2[...] = head[0:1, 0:96]
    shift2[...] = head[1:2, 0:96]
    down_bias[...] = head[2:3, 0:96]
    tail = pltpu.roll(tails[...], shift, 1)
    gain1[...] = tail[0:1, 0:96]
    shift1[...] = tail[1:2, 0:96]
    out_bias[...] = tail[2:3, 0:96]
    wide = tails[pl.ds(4 + seq // 2, 1), :]
    up_bias[...] = jnp.where(seq % 2 == 0, wide[:, 0:HALF], wide[:, HALF:])


def dense_outputs(place, units, after=()):
    results, mark = call(
        dense_out_kernel,
        "dense_outputs",
        place,
        [plain(unit) for unit in units],
        [made((4 * DOWN_ROWS, WIDTH), FLOAT), made((96, FF), FLOAT), made((96, WIDTH), FLOAT)]
        + [made((1, 96), FLOAT)] * 6
        + [made((1, HALF), FLOAT)],
        scratch=[pltpu.VMEM((8, WIDTH), FLOAT)] * 2,
        after=after,
        work=cost(1e6, 3e6),
    )
    return (*results[:3], *(vector.reshape(-1) for vector in results[3:])), mark


def joint_out_kernel(place, u0, u1, u2, u3, joint, query_bias, value_bias, sums):
    for unit, (x, c) in zip((u0, u1, u2, u3), quarters(place)):

        def lanes(kind):
            return pl.ds(pl.multiple_of(kind * WIDTH + c * HALF, LANES), HALF)

        first = unit[0:JOINT_FIRST].astype(FLOAT)
        rest = unit[JOINT_FIRST:].astype(FLOAT)
        rows = pl.ds(pl.multiple_of(x * 48, 16), 48)
        joint[rows, lanes(0)] = first[:, 0:HALF]
        joint[rows, lanes(1)] = first[:, HALF:]
        joint[pl.ds(pl.multiple_of(x * 48, 8), 24), lanes(2)] = rest[0:24, 0:HALF]
        joint[pl.ds(pl.multiple_of(x * 48 + 24, 8), 24), lanes(2)] = rest[0:24, HALF:]

        @pl.when(x == 0)
        def _(rest=rest, c=c):
            half = pl.ds(pl.multiple_of(c * HALF, LANES), HALF)
            sums[0:1, half] = rest[24:25, 0:HALF]
            sums[1:2, half] = rest[24:25, HALF:]

    turned = pltpu.roll(sums[...], line_shift(place), 1)
    query_bias[...] = turned[0:1, 0:96]
    value_bias[...] = turned[1:2, 0:96]


def joint_outputs(place, units, after=()):
    results, mark = call(
        joint_out_kernel,
        "joint_outputs",
        place,
        [plain(unit) for unit in units],
        [made((96, 3 * WIDTH), FLOAT), made((1, 96), FLOAT), made((1, 96), FLOAT)],
        scratch=[pltpu.VMEM((8, WIDTH), FLOAT)],
        after=after,
        work=cost(1e6, 2e6),
    )
    return (results[0], results[1].reshape(-1), results[2].reshape(-1)), mark


def row_body(
    tokens,
    pair_lengths,
    joint_weight,
    query_bias,
    value_bias,
    out_weight,
    out_bias,
    first_gain,
    first_shift,
    up_weight,
    up_bias,
    down_weight,
    down_bias,
    second_gain,
    second_shift,
    cotangent,
):
    seq, rows = lax.axis_index("seq"), lax.axis_index("rows")
    z, y, x, c = seq // 2, seq % 2, rows // 2, rows % 2
    place = jnp.stack([z, y, x, c]).astype(jnp.int32)
    odd = z % 2
    weights = {
        "out": out_weight, "out_bias": out_bias, "gain1": first_gain, "shift1": first_shift,
        "up": up_weight, "up_bias": up_bias, "down": down_weight, "down_bias": down_bias,
        "gain2": second_gain, "shift2": second_shift,
    }

    def local_row(array, index):
        return lax.dynamic_index_in_dim(array, index, 0, keepdims=False)

    columns, query_row, value_row = own_columns(place, joint_weight, query_bias, value_bias)
    lengths = (pair_lengths, core_swap(pair_lengths))
    own = [row_swap(local_row(tokens, odd), 0), row_swap(local_row(tokens, 1 - odd), 1)]
    *own, columns, lengths = lax.optimization_barrier((*own, columns, lengths))
    across = [y_swap(block) for block in own]
    here = own + [core_swap(block) for block in own]
    (q, k_here, v_here, summed, stats), mark = first_attention(
        place, lengths, here, columns, query_row, value_row
    )
    padding = jnp.zeros((16, WIDTH), LOW)
    cotangents = [
        row_swap(jnp.concatenate([local_row(cotangent, index), padding], axis=0), second)
        for second, index in ((0, odd), (1, 1 - odd))
    ]
    across[0], across[1], mark, cotangents[0] = lax.optimization_barrier((across[0], across[1], mark, cotangents[0]))
    there = across + [core_swap(block) for block in across]
    blocks = here + there
    (att, k_there, v_there, log_total), mark = attention(
        place, lengths, there, columns, value_row, q, summed, stats, (mark,)
    )
    att, cotangents[1] = lax.optimization_barrier((att, cotangents[1]))
    att_got = core_swap(att)
    results, mark = forward(place, att, att_got, own, cotangents, weights, (mark,))
    (
        result0, result1, feed, second_grad, act, act_send, slope, unit1, inverse1, normed, normed_t, att_t, sums0
    ) = results
    act_got, feed_got, normed_got = core_swap(act_send), core_swap(feed), core_swap(normed)
    done = (row_swap(result0, 0), row_swap(result1, 1))
    (px_send, px, qy_send, qy), mark = down_units(place, act, act_got, feed, feed_got, (mark,))
    down_pair = (px, x_swap(px_send), qy, y_swap(qy_send))
    results, mark = backward(place, feed, slope, second_grad, unit1, inverse1, weights, (mark, normed_got))
    inner0, inner1, send0, send1, first_grad, branch_own, back_own, misc_send, sums1 = results
    got, misc = (core_swap(send0), core_swap(send1)), core_swap(misc_send)
    (x_send, y_send, px, qy), mark = up_units(
        place, normed_t, normed_got, (inner0, inner1), got, att_t, branch_own, misc, sums0, sums1, feed_got, (mark,)
    )
    (x_send, y_send, down_p, down_q), mark = down_pair_stage(place, down_pair, x_send, y_send, (mark,))
    x_got, y_got = x_swap(x_send), y_swap(y_send)
    (dq, dk, dv), mark = attention_back(
        place, lengths, q, (k_here, k_there), (v_here, v_there), log_total, att, back_own, misc, (mark,)
    )
    (token_own, own_send, token_far, far_send), mark = token_parts(place, dq, dk, dv, columns, (mark, *done))
    own_got, far_got = core_swap(own_send), core_swap(far_send)
    (px_send, joint_px, qy_send, joint_qy), mark = joint_units(
        place, blocks, dq, dk, dv, token_far, far_got, (mark,)
    )
    (x_send, y_send, p, q_, down_send, down_two), mark = second_stage(
        place, (x_got, y_got, px, qy, down_p, down_q), (mark,)
    )
    x_got, y_got, down_got = x_swap(x_send), y_swap(y_send), z_swap(down_send, 1)
    px_send, qy_send, mark = lax.optimization_barrier((px_send, qy_send, mark))
    across = y_swap(qy_send)
    joint_pair = (joint_px, x_swap(px_send), joint_qy, across)
    (up_send, up_two, down_send, down_keep), mark = up_line_stage(
        place, (x_got, y_got, p, q_, down_two, down_got), (mark,)
    )
    up_got, down_got = z_swap(up_send, 1), z_swap(down_send, 2)
    (up_send, up_keep), mark = end_stage(place, up_two, up_got, (mark, down_got))
    up_got = z_swap(up_send, 2)
    (down_unit,), mark = last_sum(place, ((down_keep, down_got),), (mark,))
    down_all = gathered(down_unit)
    (x_send, y_send, joint_p, joint_q), mark = joint_pair_stage(place, joint_pair, (mark,))
    joint_x_got, joint_y_got = x_swap(x_send), y_swap(y_send)
    (token0, token1), mark = token_last(place, (token_own, own_got, across, first_grad), (mark,))
    back = (row_swap(token0, 0), row_swap(token1, 1))
    (keep, one, two, three), mark = joint_line_stage(
        place, (joint_x_got, joint_y_got, joint_p, joint_q), (mark,)
    )
    joint_last = (keep, z_swap(one, 1), z_swap(two, 2), z_swap(three, 3))
    (up_unit,), mark = last_sum(place, ((up_keep, up_got),), (mark, *down_all[1:]))
    up_all = gathered(up_unit)
    joint_unit, mark = joint_sum(place, joint_last, (mark,))
    (
        down_grad, up_grad, out_grad, second_gain_grad, second_shift_grad, down_bias_grad, first_gain_grad,
        first_shift_grad, out_bias_grad, up_bias_grad,
    ), mark = dense_outputs(place, (*down_all, *up_all), (mark,))
    joint_all = gathered(joint_unit, mark)
    (joint_grad, query_bias_grad, value_bias_grad), mark = joint_outputs(place, joint_all, (mark,))
    (outputs, token_grad), mark = back_rows(place, done, back, (mark,))
    return (
        outputs,
        token_grad,
        joint_grad,
        query_bias_grad,
        value_bias_grad,
        out_grad,
        out_bias_grad,
        first_gain_grad,
        first_shift_grad,
        up_grad,
        up_bias_grad,
        down_grad,
        down_bias_grad,
        second_gain_grad,
        second_shift_grad,
    )


def body(tokens, *others):
    if (lax.axis_size("seq"), lax.axis_size("rows")) == (8, 4) and tokens.shape == (2, BLOCK, WIDTH):
        return row_body(tokens, *others)
    return general_body(tokens, *others)


def solution(mesh):
    placed = (
        P("rows", "seq", None),
        P("rows", None),
        P(),
        P(),
        P(),
        P(),
        P(),
        P(),
        P(),
        P(),
        P(),
        P(),
        P(),
        P(),
        P(),
        P("rows", "seq", None),
    )
    return jax.shard_map(
        body,
        mesh=mesh,
        in_specs=placed,
        out_specs=(
            P("rows", "seq", None),
            P("rows", "seq", None),
            P("seq", None),
            P("seq"),
            P("seq"),
            P("seq", None),
            P("seq"),
            P("seq"),
            P("seq"),
            P("seq", None),
            P("seq"),
            P("seq", None),
            P("seq"),
            P("seq"),
            P("seq"),
        ),
        check_vma=False,
    )
```

```python
import functools
import math

import jax
import jax.numpy as jnp
from jax import lax
from jax.experimental import pallas as pl
from jax.experimental.pallas import tpu as pltpu
from jax.sharding import PartitionSpec as P

HEADS = 12
HEAD_DIM = 64


NEGATIVE = -1e30
EPSILON = 1e-12


def from_behind(value, axis, steps):
    count = lax.axis_size(axis)
    pairs = [(source, (source + steps) % count) for source in range(count)]
    return lax.ppermute(value, axis, pairs)


def layer_norm(value, gain, shift):
    mean = jnp.mean(value, axis=-1, keepdims=True)
    centred = value - mean
    spread = jnp.mean(centred * centred, axis=-1, keepdims=True)
    return centred * lax.rsqrt(spread + EPSILON) * gain + shift


def gelu_exact(value):
    return jax.nn.gelu(value, approximate=False)


def pair_index(positions, ends):
    return jnp.sum((positions[None, :, None] >= ends[:, None, :]).astype(jnp.int32), axis=2)


def split_heads(array):
    return array.reshape(array.shape[0], array.shape[1], HEADS, HEAD_DIM)


def online_block(state, query_heads, query_pairs, key_block, value_block, key_pairs):
    highest, total, summed = state
    scores = jnp.einsum(
        "rqhd,rkhd->rhqk", query_heads, split_heads(key_block), preferred_element_type=jnp.float32
    ) * HEAD_DIM ** (-0.5)
    allowed = query_pairs[:, None, :, None] == key_pairs[:, None, None, :]
    masked = jnp.where(allowed, scores, NEGATIVE)
    new_high = jnp.maximum(highest, jnp.max(masked, axis=3))
    weights = jnp.where(allowed, jnp.exp(masked - new_high[..., None]), 0.0)
    factor = jnp.exp(highest - new_high)
    total = total * factor + jnp.sum(weights, axis=3)
    summed = summed * jnp.swapaxes(factor, 1, 2)[..., None] + jnp.einsum(
        "rhqk,rkhd->rqhd",
        weights.astype(jnp.bfloat16),
        split_heads(value_block),
        preferred_element_type=jnp.float32,
    )
    return (new_high, total, summed)


def tile_terms(queries, out_grad, log_total, delta, query_pairs, keys, values, key_pairs):
    scale = HEAD_DIM ** (-0.5)
    query_heads = split_heads(queries)
    grad_heads = split_heads(out_grad)
    key_heads = split_heads(keys)
    value_heads = split_heads(values)
    scores = (
        jnp.einsum("rqhd,rkhd->rhqk", query_heads, key_heads, preferred_element_type=jnp.float32)
        * scale
    )
    allowed = query_pairs[:, None, :, None] == key_pairs[:, None, None, :]
    weights = jnp.where(
        allowed, jnp.exp(jnp.where(allowed, scores, NEGATIVE) - log_total[..., None]), 0.0
    )
    weight_grad = jnp.einsum(
        "rqhd,rkhd->rhqk", grad_heads, value_heads, preferred_element_type=jnp.float32
    )
    score_grad = (weights * (weight_grad - delta[..., None])).astype(jnp.bfloat16)
    query_term = (
        jnp.einsum("rhqk,rkhd->rqhd", score_grad, key_heads, preferred_element_type=jnp.float32)
        * scale
    )
    key_term = (
        jnp.einsum("rhqk,rqhd->rkhd", score_grad, query_heads, preferred_element_type=jnp.float32)
        * scale
    )
    value_term = jnp.einsum(
        "rhqk,rqhd->rkhd",
        weights.astype(jnp.bfloat16),
        grad_heads,
        preferred_element_type=jnp.float32,
    )
    return (
        query_term.reshape(queries.shape),
        key_term.reshape(keys.shape),
        value_term.reshape(values.shape),
    )


def general_body(
    tokens,
    pair_lengths,
    joint_weight,
    query_bias,
    value_bias,
    out_weight,
    out_bias,
    first_gain,
    first_shift,
    up_weight,
    up_bias,
    down_weight,
    down_bias,
    second_gain,
    second_shift,
    cotangent,
):
    rows_here, seq_here, width = tokens.shape
    count = lax.axis_size("seq")
    cycle_index = lax.axis_index("seq")
    ends = jnp.cumsum(pair_lengths, axis=1)
    offsets = jnp.arange(seq_here, dtype=jnp.int32)
    own_pairs = pair_index(cycle_index * seq_here + offsets, ends)
    block_shape = (rows_here, seq_here, width)
    flat = tokens.reshape(rows_here * seq_here, width)
    projected = jnp.dot(flat, joint_weight, preferred_element_type=jnp.float32)
    queries = (projected[:, :width] + query_bias).astype(jnp.bfloat16).reshape(block_shape)
    keys = projected[:, width : 2 * width].astype(jnp.bfloat16).reshape(block_shape)
    values = (projected[:, 2 * width :] + value_bias).astype(jnp.bfloat16).reshape(block_shape)
    query_heads = split_heads(queries)
    initial = (
        jnp.full((rows_here, HEADS, seq_here), NEGATIVE, jnp.float32),
        jnp.zeros((rows_here, HEADS, seq_here), jnp.float32),
        jnp.zeros((rows_here, seq_here, HEADS, HEAD_DIM), jnp.float32),
    )
    key_piece = lax.all_gather(keys, "seq", axis=1, tiled=True)
    value_piece = lax.all_gather(values, "seq", axis=1, tiled=True)
    length = key_piece.shape[1]
    block = math.gcd(length, seq_here)

    def one_block(index, inner_state):
        first = index * block
        key_block = lax.dynamic_slice_in_dim(key_piece, first, block, 1)
        value_block = lax.dynamic_slice_in_dim(value_piece, first, block, 1)
        key_pairs = pair_index(first + jnp.arange(block, dtype=jnp.int32), ends)
        return online_block(inner_state, query_heads, own_pairs, key_block, value_block, key_pairs)

    highest, total, summed = lax.fori_loop(0, length // block, one_block, initial)
    log_total = highest + jnp.log(total)
    attended = (
        (summed / jnp.swapaxes(total, 1, 2)[..., None]).astype(jnp.bfloat16).reshape(flat.shape)
    )
    branch = jnp.dot(attended, out_weight, preferred_element_type=jnp.float32) + out_bias
    first_sum = flat.astype(jnp.float32) + branch
    normed, first_back = jax.vjp(layer_norm, first_sum, first_gain, first_shift)
    normed_low = normed.astype(jnp.bfloat16)
    inner = jnp.dot(normed_low, up_weight, preferred_element_type=jnp.float32) + up_bias
    activated_full, gelu_back = jax.vjp(gelu_exact, inner)
    activated = activated_full.astype(jnp.bfloat16)
    feed = jnp.dot(activated, down_weight, preferred_element_type=jnp.float32) + down_bias
    second_sum = normed + feed
    result, second_back = jax.vjp(layer_norm, second_sum, second_gain, second_shift)
    outputs = result.astype(jnp.bfloat16).reshape(tokens.shape)
    second_grad, second_gain_grad, second_shift_grad = second_back(
        cotangent.astype(jnp.float32).reshape(flat.shape)
    )
    feed_grad = second_grad.astype(jnp.bfloat16)
    down_grad = jnp.einsum("ti,tj->ij", activated, feed_grad, preferred_element_type=jnp.float32)
    down_bias_grad = jnp.sum(feed_grad.astype(jnp.float32), axis=0)
    activated_grad = jnp.einsum(
        "tj,ij->ti", feed_grad, down_weight, preferred_element_type=jnp.float32
    )
    inner_grad = gelu_back(activated_grad)[0].astype(jnp.bfloat16)
    up_grad = jnp.einsum("ti,tj->ij", normed_low, inner_grad, preferred_element_type=jnp.float32)
    up_bias_grad = jnp.sum(inner_grad.astype(jnp.float32), axis=0)
    normed_grad = second_grad + jnp.einsum(
        "tj,ij->ti", inner_grad, up_weight, preferred_element_type=jnp.float32
    )
    first_grad, first_gain_grad, first_shift_grad = first_back(normed_grad)
    branch_grad = first_grad.astype(jnp.bfloat16)
    out_grad = jnp.einsum("ti,tj->ij", attended, branch_grad, preferred_element_type=jnp.float32)
    out_bias_grad = jnp.sum(branch_grad.astype(jnp.float32), axis=0)
    attended_grad = jnp.einsum(
        "tj,ij->ti", branch_grad, out_weight, preferred_element_type=jnp.float32
    ).astype(jnp.bfloat16)
    delta = jnp.sum(
        (attended_grad.astype(jnp.float32) * attended.astype(jnp.float32)).reshape(
            rows_here, seq_here, HEADS, HEAD_DIM
        ),
        axis=3,
    )
    delta = jnp.swapaxes(delta, 1, 2)
    attended_grad = attended_grad.reshape(block_shape)
    zeros_block = jnp.zeros(block_shape, jnp.float32)

    def send_key_sums(sums):
        return (
            from_behind(sums[0].astype(jnp.bfloat16), "seq", 1).astype(jnp.float32),
            from_behind(sums[1].astype(jnp.bfloat16), "seq", 1).astype(jnp.float32),
        )

    def key_work(turn, pair_block, sums, query_sum):
        anchor = (cycle_index - turn) % count
        key_pairs = pair_index(anchor * seq_here + offsets, ends)
        query_term, key_term, value_term = tile_terms(
            queries,
            attended_grad,
            log_total,
            delta,
            own_pairs,
            pair_block[0],
            pair_block[1],
            key_pairs,
        )
        return ((sums[0] + key_term, sums[1] + value_term), query_sum + query_term)

    def key_turn(turn, state):
        pair_block, sums, query_sum = state
        sums, query_sum = key_work(turn, pair_block, sums, query_sum)
        sums = send_key_sums(sums)
        pair_block = from_behind((pair_block[0], pair_block[1]), "seq", 1)
        return (pair_block, sums, query_sum)

    pair_block, sums, query_sum = lax.fori_loop(
        0, count - 1, key_turn, ((keys, values), (zeros_block, zeros_block), zeros_block)
    )
    sums, query_sum = key_work(count - 1, pair_block, sums, query_sum)
    key_sum, value_sum = send_key_sums(sums)
    query_low = query_sum.astype(jnp.bfloat16).reshape(flat.shape)
    key_low = key_sum.astype(jnp.bfloat16).reshape(flat.shape)
    value_low = value_sum.astype(jnp.bfloat16).reshape(flat.shape)
    joint_low = jnp.concatenate([query_low, key_low, value_low], axis=1)
    joint_grad = jnp.einsum("ti,tj->ij", flat, joint_low, preferred_element_type=jnp.float32)
    query_bias_grad = jnp.sum(query_low.astype(jnp.float32), axis=0)
    value_bias_grad = jnp.sum(value_low.astype(jnp.float32), axis=0)
    token_grad = first_grad + jnp.einsum(
        "tj,ij->ti", joint_low, joint_weight, preferred_element_type=jnp.float32
    )
    gradients = (
        joint_grad,
        query_bias_grad,
        value_bias_grad,
        out_grad,
        out_bias_grad,
        first_gain_grad,
        first_shift_grad,
        up_grad,
        up_bias_grad,
        down_grad,
        down_bias_grad,
        second_gain_grad,
        second_shift_grad,
    )
    shares = (
        lax.psum_scatter(
            gradients[0].astype(jnp.bfloat16), "seq", scatter_dimension=0, tiled=True
        ).astype(jnp.float32),
        lax.psum_scatter(
            gradients[1].astype(jnp.bfloat16), "seq", scatter_dimension=0, tiled=True
        ).astype(jnp.float32),
        lax.psum_scatter(
            gradients[2].astype(jnp.bfloat16), "seq", scatter_dimension=0, tiled=True
        ).astype(jnp.float32),
        lax.psum_scatter(
            gradients[3].astype(jnp.bfloat16), "seq", scatter_dimension=0, tiled=True
        ).astype(jnp.float32),
        lax.psum_scatter(
            gradients[4].astype(jnp.bfloat16), "seq", scatter_dimension=0, tiled=True
        ).astype(jnp.float32),
        lax.psum_scatter(
            gradients[5].astype(jnp.bfloat16), "seq", scatter_dimension=0, tiled=True
        ).astype(jnp.float32),
        lax.psum_scatter(
            gradients[6].astype(jnp.bfloat16), "seq", scatter_dimension=0, tiled=True
        ).astype(jnp.float32),
        lax.psum_scatter(
            gradients[7].astype(jnp.bfloat16), "seq", scatter_dimension=0, tiled=True
        ).astype(jnp.float32),
        lax.psum_scatter(
            gradients[8].astype(jnp.bfloat16), "seq", scatter_dimension=0, tiled=True
        ).astype(jnp.float32),
        lax.psum_scatter(
            gradients[9].astype(jnp.bfloat16), "seq", scatter_dimension=0, tiled=True
        ).astype(jnp.float32),
        lax.psum_scatter(
            gradients[10].astype(jnp.bfloat16), "seq", scatter_dimension=0, tiled=True
        ).astype(jnp.float32),
        lax.psum_scatter(
            gradients[11].astype(jnp.bfloat16), "seq", scatter_dimension=0, tiled=True
        ).astype(jnp.float32),
        lax.psum_scatter(
            gradients[12].astype(jnp.bfloat16), "seq", scatter_dimension=0, tiled=True
        ).astype(jnp.float32),
    )
    shares = (
        lax.psum(shares[0].astype(jnp.bfloat16), "rows").astype(jnp.float32),
        lax.psum(shares[1].astype(jnp.bfloat16), "rows").astype(jnp.float32),
        lax.psum(shares[2].astype(jnp.bfloat16), "rows").astype(jnp.float32),
        lax.psum(shares[3].astype(jnp.bfloat16), "rows").astype(jnp.float32),
        lax.psum(shares[4].astype(jnp.bfloat16), "rows").astype(jnp.float32),
        lax.psum(shares[5].astype(jnp.bfloat16), "rows").astype(jnp.float32),
        lax.psum(shares[6].astype(jnp.bfloat16), "rows").astype(jnp.float32),
        lax.psum(shares[7].astype(jnp.bfloat16), "rows").astype(jnp.float32),
        lax.psum(shares[8].astype(jnp.bfloat16), "rows").astype(jnp.float32),
        lax.psum(shares[9].astype(jnp.bfloat16), "rows").astype(jnp.float32),
        lax.psum(shares[10].astype(jnp.bfloat16), "rows").astype(jnp.float32),
        lax.psum(shares[11].astype(jnp.bfloat16), "rows").astype(jnp.float32),
        lax.psum(shares[12].astype(jnp.bfloat16), "rows").astype(jnp.float32),
    )
    return (outputs, token_grad.reshape(tokens.shape)) + tuple(shares)


WIDTH = HEADS * HEAD_DIM
HALF = WIDTH // 2
FF = 4 * WIDTH
BLOCK = 128
OWN = 2 * BLOCK
LANES = 128
PAIRS_OF_HEADS = HALF // LANES
JOINT_ROWS = 80
JOINT_FIRST = 48
JOINT_SECOND = JOINT_ROWS - JOINT_FIRST
UP_ROWS = 128
DOWN_ROWS = 96
EXT = OWN + 16
DOWN_SENT = 2 * DOWN_ROWS
FLOAT = jnp.float32
LOW = jnp.bfloat16
AXES = ("seq", "rows")


def kernel_params(megabytes):
    return pltpu.CompilerParams(vmem_limit_bytes=megabytes << 20)


def shaped(shape, kind):
    return jax.ShapeDtypeStruct(shape, kind)


def whole(shape):
    return pl.BlockSpec(shape, lambda *_: (0,) * len(shape))


def cost(flops, moved, exps=0):
    return pl.CostEstimate(flops=1024, bytes_accessed=1024, transcendentals=0)


def dot(left, right):
    return lax.dot_general(left, right, (((1,), (0,)), ((), ())), preferred_element_type=FLOAT)


def dot_nt(left, right):
    return lax.dot_general(left, right, (((1,), (1,)), ((), ())), preferred_element_type=FLOAT)


def call(kernel, name, place, inputs, outputs, scratch=(), grid=(1,), scalars=(), after=(), megabytes=28, work=None, aliases=()):
    prefetch = 1 + len(scalars)
    given, made = len(inputs), len(outputs)

    def ordered(*refs):
        first = prefetch + given
        mark = refs[first + len(after) + made]
        mark[...] = jnp.zeros_like(mark)
        kernel(*refs[:first], *refs[first + len(after) : first + len(after) + made], *refs[first + len(after) + made + 1 :])

    results = pl.pallas_call(
        ordered,
        grid_spec=pltpu.PrefetchScalarGridSpec(
            num_scalar_prefetch=prefetch,
            grid=grid,
            in_specs=[spec for _, spec in inputs] + [pl.BlockSpec(memory_space=pl.ANY)] * len(after),
            out_specs=[spec for _, _, spec in outputs] + [whole((8, LANES))],
            scratch_shapes=list(scratch),
        ),
        out_shape=[shaped(shape, kind) for shape, kind, _ in outputs] + [shaped((8, LANES), FLOAT)],
        compiler_params=kernel_params(megabytes),
        cost_estimate=work,
        input_output_aliases={prefetch + source: target for source, target in aliases},
        name=name,
    )(place, *scalars, *[array for array, _ in inputs], *after)
    return results[:-1], results[-1]


def plain(array):
    return array, whole(array.shape)


def made(shape, kind):
    return shape, kind, whole(shape)


def device_at(z, y, x, c):
    return ((z * 2 + y) * 2 + x) * 2 + c


def permute(value, target):
    pairs = []
    for z in range(4):
        for y in range(2):
            for x in range(2):
                for c in range(2):
                    pairs.append((device_at(z, y, x, c), device_at(*target(z, y, x, c))))
    return lax.ppermute(value, AXES, pairs)


def core_swap(value):
    return permute(value, lambda z, y, x, c: (z, y, x, 1 - c))


def x_swap(value):
    return permute(value, lambda z, y, x, c: (z, y, 1 - x, c))


def y_swap(value):
    return permute(value, lambda z, y, x, c: (z, 1 - y, x, c))


def z_swap(value, bits):
    return permute(value, lambda z, y, x, c: (z ^ bits, y, x, c))


def row_swap(value, second):
    return permute(value, lambda z, y, x, c: (2 * c + (z % 2 ^ second), y, x, z // 2))


def first_positions(place):
    z, y, c = place[0], place[1], place[3]
    bases = []
    for core, line in ((c, y), (1 - c, y), (c, 1 - y), (1 - c, 1 - y)):
        for second in (0, 1):
            parity = z % 2
            parity = 1 - parity if second else parity
            bases.append((2 * (2 * core + parity) + line) * BLOCK)
    return bases


def pair_ends(place, own_lengths, peer_lengths):
    z, c = place[0], place[3]
    here = (z // 2) == c
    line = z % 2
    ends, end = [], 0
    for pair in range(own_lengths.shape[1]):
        end = end + jnp.where(here, own_lengths[line, pair], peer_lengths[line, pair])
        ends.append(end)
    return ends


def pairs_along(base, ends, axis):
    shape = (8, BLOCK) if axis == 1 else (BLOCK, LANES)
    position = base + lax.broadcasted_iota(jnp.int32, shape, axis)
    ids = jnp.zeros(shape, jnp.int32)
    for end in ends:
        ids = ids + (position >= end).astype(jnp.int32)
    return ids


def head_mask(rows):
    return lax.broadcasted_iota(jnp.int32, (rows, LANES), 1) < HEAD_DIM


def columns_kernel(place, columns, query_bias, value_bias, out, query_row, value_row):
    out[0] = columns[...]
    query_row[...] = query_bias[...]
    value_row[...] = value_bias[...]


def own_columns(place, joint_weight, query_bias, value_bias):
    half_row = pl.BlockSpec((1, HALF), lambda i, place: (0, place[3]))
    results, _ = call(
        columns_kernel,
        "own_columns",
        place,
        [
            (joint_weight, pl.BlockSpec((WIDTH, HALF), lambda i, place: (0, 2 * i + place[3]))),
            (row_of(query_bias), half_row),
            (row_of(value_bias), half_row),
        ],
        [((3, WIDTH, HALF), LOW, pl.BlockSpec((1, WIDTH, HALF), lambda i, place: (i, 0, 0)))]
        + [made((1, HALF), FLOAT)] * 2,
        grid=(3,),
        work=cost(1e6, 4e6),
    )
    return results


def first_attention_kernel(
    place, own_lengths, peer_lengths, t0, t1, t2, t3, columns, qb, vb, q_out, k_out, v_out, summed, stats, bias
):
    bases = first_positions(place)
    ends = pair_ends(place, own_lengths, peer_lengths)
    tokens = jnp.concatenate([block[...] for block in (t0, t1, t2, t3)], axis=0)
    queries = dot(tokens, columns[0]) + qb[...]
    q_out[...] = (queries.astype(LOW).astype(FLOAT) * HEAD_DIM**-0.5).astype(LOW)
    k_out[...] = dot(tokens, columns[1]).astype(LOW)
    v_out[...] = (dot(tokens, columns[2]) + vb[...]).astype(LOW)
    fill_bias(bias, bases[:4], bases[:4], ends)
    stats[...] = jnp.zeros_like(stats)
    for pair in range(PAIRS_OF_HEADS):
        lanes = pl.ds(pair * LANES, LANES)
        scores = masked_scores(k_out[:, lanes], q_out[:, lanes], bias)
        highest = jnp.max(scores, axis=0, keepdims=True)
        weights = jnp.exp(scores - highest)
        summed[pair] = dot(turned(v_out[:, lanes]), weights.astype(LOW))
        stats[2 * pair : 2 * pair + 1, :] = highest
        stats[2 * pair + 1 : 2 * pair + 2, :] = column_sum(weights)


def turned(array):
    return jnp.transpose(array.astype(FLOAT)).astype(LOW)


def masked_scores(keys, queries, bias):
    mask = bias[...]
    chosen = jnp.concatenate(halves_of(queries), axis=0)
    return dot_nt(keys, chosen) + jnp.concatenate([mask, mask], axis=1)


def fill_bias(bias, query_bases, key_bases, ends):
    key_ids = [pairs_along(base, ends, 1)[0:1] for base in key_bases]
    for i, base in enumerate(query_bases):
        query_ids = pairs_along(base, ends, 0)
        for j in range(len(key_bases)):
            bias[pl.ds(i * BLOCK, BLOCK), pl.ds(j * BLOCK, BLOCK)] = jnp.where(query_ids == key_ids[j], 0.0, NEGATIVE)


def halves_of(array):
    left = head_mask(array.shape[0])
    zeros = jnp.zeros_like(array)
    return jnp.where(left, array, zeros), jnp.where(left, zeros, array)


def first_attention(place, lengths, blocks, columns, query_bias, value_bias, after=()):
    return call(
        first_attention_kernel,
        "first_attention",
        place,
        [plain(array) for array in (*blocks, columns, query_bias, value_bias)],
        [made((512, HALF), LOW)] * 3 + [made((PAIRS_OF_HEADS, LANES, 1024), FLOAT), made((8, 1024), FLOAT)],
        scratch=[pltpu.VMEM((512, 512), FLOAT)],
        scalars=lengths,
        after=after,
        work=cost(4e9, 8e6, 3e6),
    )


def attention_kernel(
    place, own_lengths, peer_lengths, t0, t1, t2, t3, columns, vb, q, summed, stats,
    att_out, k_out, v_out, log_out, bias,
):
    bases = first_positions(place)
    ends = pair_ends(place, own_lengths, peer_lengths)
    tokens = jnp.concatenate([block[...] for block in (t0, t1, t2, t3)], axis=0)
    k_out[...] = dot(tokens, columns[1]).astype(LOW)
    v_out[...] = (dot(tokens, columns[2]) + vb[...]).astype(LOW)
    fill_bias(bias, bases[4:], bases[:4], ends)
    log_out[...] = jnp.zeros_like(log_out)
    top = lax.broadcasted_iota(jnp.int32, (LANES, 512), 0) < HEAD_DIM
    for pair in range(PAIRS_OF_HEADS):
        lanes = pl.ds(pair * LANES, LANES)
        scores = masked_scores(k_out[:, lanes], q[:, lanes], bias)
        before = stats[2 * pair : 2 * pair + 1, :]
        highest = jnp.maximum(before, jnp.max(scores, axis=0, keepdims=True))
        weights = jnp.exp(scores - highest)
        shrink = jnp.exp(before - highest)
        sums = column_sum(weights) + shrink * stats[2 * pair + 1 : 2 * pair + 2, :]
        total = (dot(turned(v_out[:, lanes]), weights.astype(LOW)) + shrink * summed[pair]) / sums
        att_out[:, lanes] = jnp.transpose(jnp.where(top, total[:, 0:512], total[:, 512:])).astype(LOW)
        logs = highest + jnp.log(sums)
        log_out[2 * pair : 2 * pair + 1, :] = logs[:, 0:512]
        log_out[2 * pair + 1 : 2 * pair + 2, :] = logs[:, 512:]


def attention(place, lengths, blocks, columns, value_bias, q, summed, stats, after=()):
    return call(
        attention_kernel,
        "attention",
        place,
        [plain(array) for array in (*blocks, columns, value_bias, q, summed, stats)],
        [made((512, HALF), LOW)] * 3 + [made((8, 512), FLOAT)],
        scratch=[pltpu.VMEM((512, 512), FLOAT)],
        scalars=lengths,
        after=after,
        work=cost(4e9, 8e6, 3e6),
    )


def centred_norm(value):
    mean = jnp.mean(value, axis=-1, keepdims=True)
    centred = value - mean
    spread = jnp.mean(centred * centred, axis=-1, keepdims=True)
    inverse = lax.rsqrt(spread + EPSILON)
    return centred * inverse, inverse


def norm_back(grad, unit, inverse):
    mean = jnp.mean(grad, axis=-1, keepdims=True)
    along = jnp.mean(grad * unit, axis=-1, keepdims=True)
    return (grad - mean - unit * along) * inverse


def column_sum(value):
    return jnp.sum(value, axis=0, keepdims=True)


def forward_kernel(
    place, att, att_got, wo_own, wo_other, out_bias, x0, x1, gain1, shift1, up, up_bias, down,
    down_bias, gain2, shift2, cot0, cot1,
    result0, result1, feed_ext, second_grad, act_keep, act_send, slope, unit1, inverse1, normed_low, normed_t, att_t, sums,
    act_t,
):
    c = place[3]
    tokens = jnp.concatenate([x0[...], x1[...]], axis=0).astype(FLOAT)
    att_own, att_other = att[0:OWN], att_got[OWN:]
    branch = dot(att_own, wo_own[...]) + dot(att_other, wo_other[...]) + out_bias[...]
    unit, inverse = centred_norm(tokens + branch)
    unit1[...] = unit
    inverse1[...] = jnp.broadcast_to(inverse, (OWN, LANES))
    normed = unit * gain1[...] + shift1[...]
    low = normed.astype(LOW)
    normed_low[...] = low
    normed_t[...] = jnp.transpose(normed).astype(LOW)
    mine = pl.ds(pl.multiple_of(c * HALF, HALF), HALF)
    other = pl.ds(pl.multiple_of((1 - c) * HALF, HALF), HALF)
    att_t[mine, :] = jnp.transpose(att[...].astype(FLOAT)).astype(LOW)
    att_t[other, 0:OWN] = jnp.transpose(att_other.astype(FLOAT)).astype(LOW)
    att_t[other, OWN:] = jnp.transpose(att_got[0:OWN].astype(FLOAT)).astype(LOW)
    inner = dot(low, up[...]) + up_bias[...]
    below = 0.5 + 0.5 * lax.erf(inner * math.sqrt(0.5))
    density = jnp.exp(inner * inner * -0.5) * (1.0 / math.sqrt(2.0 * math.pi))
    activated = inner * below
    slope[...] = (below + inner * density).astype(LOW)
    act_t[...] = jnp.transpose(activated).astype(LOW).reshape(16, 2, DOWN_ROWS, OWN)
    act_keep[...] = act_t[:, c]
    act_send[...] = act_t[:, 1 - c]
    feed = dot(activated.astype(LOW), down[...])
    unit, inverse = centred_norm(normed + feed + down_bias[...])
    result = (unit * gain2[...] + shift2[...]).astype(LOW)
    result0[...] = result[0:BLOCK]
    result1[...] = result[BLOCK:]
    cotangent = jnp.concatenate([cot0[0:BLOCK], cot1[0:BLOCK]], axis=0).astype(FLOAT)
    grad = norm_back(cotangent * gain2[...], unit, inverse)
    second_grad[...] = grad
    low_grad = grad.astype(LOW)
    rows = jnp.concatenate(
        [
            column_sum(cotangent * unit),
            column_sum(cotangent),
            column_sum(low_grad.astype(FLOAT)),
            jnp.zeros((5, WIDTH), FLOAT),
        ],
        axis=0,
    )
    sums[...] = rows
    feed_ext[0:OWN] = low_grad
    feed_ext[OWN:] = jnp.concatenate([rows, jnp.zeros_like(rows)], axis=0).astype(LOW)


def row_of(vector):
    return vector.reshape(1, vector.shape[0])


def forward(place, att, att_got, tokens, cotangents, weights, after=()):
    chunk = FF

    def vector(name):
        return plain(row_of(weights[name]))

    units = ((16, DOWN_ROWS, OWN), LOW, pl.BlockSpec((16, DOWN_ROWS, OWN), lambda i, place: (i, 0, 0)))
    return call(
        forward_kernel,
        "forward",
        place,
        [
            plain(att),
            plain(att_got),
            (weights["out"], pl.BlockSpec((HALF, WIDTH), lambda i, place: (place[3], 0))),
            (weights["out"], pl.BlockSpec((HALF, WIDTH), lambda i, place: (1 - place[3], 0))),
            vector("out_bias"), plain(tokens[0]), plain(tokens[1]), vector("gain1"), vector("shift1"),
            (weights["up"], pl.BlockSpec((WIDTH, chunk), lambda i, place: (0, i))),
            (row_of(weights["up_bias"]), pl.BlockSpec((1, chunk), lambda i, place: (0, i))),
            (weights["down"], pl.BlockSpec((chunk, WIDTH), lambda i, place: (i, 0))),
            vector("down_bias"), vector("gain2"), vector("shift2"), plain(cotangents[0]), plain(cotangents[1]),
        ],
        [
            made((BLOCK, WIDTH), LOW), made((BLOCK, WIDTH), LOW), made((EXT, WIDTH), LOW),
            made((OWN, WIDTH), FLOAT), units, units,
            ((OWN, FF), LOW, pl.BlockSpec((OWN, chunk), lambda i, place: (0, i))),
            made((OWN, WIDTH), FLOAT), made((OWN, LANES), FLOAT), made((OWN, WIDTH), LOW),
            made((WIDTH, OWN), LOW), made((WIDTH, 512), LOW), made((8, WIDTH), FLOAT),
        ],
        scratch=[pltpu.VMEM((16, 2, DOWN_ROWS, OWN), LOW)],
        after=after,
        work=cost(2.7e9, 20e6, 2e6),
    )


def split_units(place, units, px_send, px, qy_send, qy):
    y, x = place[1], place[2]
    half = units.shape[2] // 2
    for line in range(2):
        px[0, line] = units[line, x, 0:half]
        px_send[0, line] = units[line, 1 - x, 0:half]
    for side in range(2):
        qy[0, side] = units[y, side, half:]
        qy_send[0, side] = units[1 - y, side, half:]


def unit_outputs(rows, width):
    shape = (4, 2, rows // 2, width)
    return [(shape, LOW, pl.BlockSpec((1,) + shape[1:], lambda i, place: (i, 0, 0, 0)))] * 4


def down_kernel(place, act, act_got, feed, feed_got, px_send, px, qy_send, qy, units):
    shape = (4 * DOWN_ROWS, OWN)
    total = dot(act[...].reshape(shape), feed[0:OWN]) + dot(act_got[...].reshape(shape), feed_got[0:OWN])
    units[...] = total.astype(LOW).reshape(units.shape)
    split_units(place, units, px_send, px, qy_send, qy)


def down_units(place, act, act_got, feed, feed_got, after=()):
    block = pl.BlockSpec((4, DOWN_ROWS, OWN), lambda i, place: (i, 0, 0))
    return call(
        down_kernel,
        "down_units",
        place,
        [(act, block), (act_got, block), plain(feed), plain(feed_got)],
        unit_outputs(DOWN_ROWS, WIDTH),
        scratch=[pltpu.VMEM((2, 2, DOWN_ROWS, WIDTH), LOW)],
        grid=(4,),
        after=after,
        work=cost(0.6e9, 3.5e6),
    )


def backward_kernel(
    place, feed_ext, slope, up, down, second_grad, unit1, inverse1, gain1, wo_own, wo_other,
    inner0, inner1, send0, send1, first_grad, branch_own, back_own, misc, sums,
    inner, branch,
):
    c = place[3]
    grad = (dot_nt(feed_ext[0:OWN], down[...]) * slope[...].astype(FLOAT)).astype(LOW)
    inner[...] = grad
    for target, index in ((inner0, c), (inner1, 2 + c), (send0, 1 - c), (send1, 3 - c)):
        target[...] = inner[:, pl.ds(pl.multiple_of(index * WIDTH, LANES), WIDTH)]
    inner_sum = column_sum(grad.astype(FLOAT))
    total = second_grad[...] + dot_nt(grad, up[...])
    unit = unit1[...]
    grad1 = norm_back(total * gain1[...], unit, inverse1[:, 0:1])
    first_grad[...] = grad1
    low = grad1.astype(LOW)
    branch[...] = low
    rows = jnp.concatenate(
        [
            column_sum(total * unit),
            column_sum(total),
            column_sum(low.astype(FLOAT)),
            jnp.zeros((1, WIDTH), FLOAT),
        ]
        + [inner_sum[:, index * WIDTH : (index + 1) * WIDTH] for index in range(4)],
        axis=0,
    )
    sums[...] = rows
    branch_own[...] = branch[:, pl.ds(pl.multiple_of(c * HALF, LANES), HALF)]
    back_own[...] = dot_nt(low, wo_own[...]).astype(LOW)
    misc[0:OWN, 0:HALF] = branch[:, pl.ds(pl.multiple_of((1 - c) * HALF, LANES), HALF)]
    misc[0:OWN, HALF:] = dot_nt(low, wo_other[...]).astype(LOW)
    misc[OWN:] = jnp.concatenate([rows, jnp.zeros_like(rows)], axis=0).astype(LOW)


def backward(place, feed_ext, slope, second_grad, unit1, inverse1, weights, after=()):
    chunk = FF
    return call(
        backward_kernel,
        "backward",
        place,
        [
            plain(feed_ext),
            (slope, pl.BlockSpec((OWN, chunk), lambda i, place: (0, i))),
            (weights["up"], pl.BlockSpec((WIDTH, chunk), lambda i, place: (0, i))),
            (weights["down"], pl.BlockSpec((chunk, WIDTH), lambda i, place: (i, 0))),
            plain(second_grad), plain(unit1), plain(inverse1), plain(row_of(weights["gain1"])),
            (weights["out"], pl.BlockSpec((HALF, WIDTH), lambda i, place: (place[3], 0))),
            (weights["out"], pl.BlockSpec((HALF, WIDTH), lambda i, place: (1 - place[3], 0))),
        ],
        [made((OWN, WIDTH), LOW)] * 4
        + [
            made((OWN, WIDTH), FLOAT), made((OWN, HALF), LOW), made((OWN, HALF), LOW), made((EXT, WIDTH), LOW),
            made((8, WIDTH), FLOAT),
        ],
        scratch=[pltpu.VMEM((OWN, FF), LOW), pltpu.VMEM((OWN, WIDTH), LOW)],
        after=after,
        work=cost(2.7e9, 16e6),
    )


def up_kernel(
    place, normed_t, normed_got, inner0, inner1, got0, got1, att_t, branch, misc, sums0, sums1, feed_got,
    x_send, y_send, px, qy, units, normed_got_t,
):
    z = pl.program_id(0)
    y, x = place[1], place[2]

    @pl.when(z == 0)
    def _():
        normed_got_t[...] = jnp.transpose(normed_got[...].astype(FLOAT)).astype(LOW)

    theirs = normed_got_t[pl.ds(pl.multiple_of(z * 192, 32), 192), :]
    outer = dot(att_t[:, 0:OWN], branch[...]) + dot(att_t[:, OWN:], misc[0:OWN, 0:HALF])
    for side, inner, got, sums, pair in ((0, inner0, got0, sums0, feed_got), (1, inner1, got1, sums1, misc)):
        grad = dot(normed_t[...], inner[...]) + dot(theirs, got[...])
        vectors = sums[...] + pair[OWN:].astype(FLOAT)[0:8]
        for line in range(2):
            first = line * 96 + side * 48
            rest = jnp.concatenate([outer[first : first + 24], outer[first + 24 : first + 48]], axis=1)
            units[line, side] = jnp.concatenate(
                [grad[line * 96 : line * 96 + 96], rest, vectors], axis=0
            ).astype(LOW)
    half = UP_ROWS // 2
    for index in range(2):
        rows = pl.ds(pl.multiple_of(DOWN_SENT + (z * 2 + index) * half, half), half)
        px[0, index] = units[index, x, 0:half]
        x_send[rows, :] = units[index, 1 - x, 0:half]
        qy[0, index] = units[y, index, half:]
        y_send[rows, :] = units[1 - y, index, half:]


def up_units(place, normed_t, normed_got, inner, got, att_t, branch, misc, sums0, sums1, feed_got, after=()):
    rows = pl.BlockSpec((192, OWN), lambda i, place: (i, 0))
    return call(
        up_kernel,
        "up_units",
        place,
        [
            (normed_t, rows), plain(normed_got), plain(inner[0]), plain(inner[1]), plain(got[0]), plain(got[1]),
            (att_t, pl.BlockSpec((192, 512), lambda i, place: (i, 0))),
            plain(branch), plain(misc), plain(sums0), plain(sums1), plain(feed_got),
        ],
        [made((DOWN_SENT + 4 * UP_ROWS, WIDTH), LOW)] * 2 + unit_outputs(UP_ROWS, WIDTH)[:2],
        scratch=[pltpu.VMEM((2, 2, UP_ROWS, WIDTH), LOW), pltpu.VMEM((WIDTH, OWN), LOW)],
        grid=(4,),
        after=after,
        work=cost(0.9e9, 5e6),
    )


def attention_back_kernel(
    place, own_lengths, peer_lengths, q, k0, k1, v0, v1, log_total, att, back0, misc,
    dq_out, dk_out, dv_out, bias,
):
    bases = first_positions(place)
    ends = pair_ends(place, own_lengths, peer_lengths)
    query_ids = [pairs_along(base, ends, 1)[0:1] for base in bases[:4]]
    for j in range(8):
        key_ids = pairs_along(bases[j], ends, 0)
        for i in range(4):
            bias[pl.ds(j * BLOCK, BLOCK), pl.ds(i * BLOCK, BLOCK)] = jnp.where(
                key_ids == query_ids[i], 0.0, NEGATIVE
            )

    def one_pair(pair, carry):
        lanes = pl.ds(pl.multiple_of(pair * LANES, LANES), LANES)
        keys = jnp.concatenate([k0[:, lanes], k1[:, lanes]], axis=0)
        values = jnp.concatenate([v0[:, lanes], v1[:, lanes]], axis=0)
        keys_t = turned(keys)
        key_grad = jnp.zeros((1024, LANES), FLOAT)
        value_grad = jnp.zeros((1024, LANES), FLOAT)
        far = pl.ds(pl.multiple_of(HALF + pair * LANES, LANES), LANES)
        for part, back in ((0, back0[:, lanes]), (1, misc[0:OWN, far])):
            rows = pl.ds(part * OWN, OWN)
            product = jnp.transpose(back.astype(FLOAT) * att[rows, lanes].astype(FLOAT))
            delta = jnp.concatenate([column_sum(product[0:HEAD_DIM]), column_sum(product[HEAD_DIM:])], axis=1)
            logs = jnp.concatenate(
                [log_total[pl.ds(2 * pair, 1), rows], log_total[pl.ds(2 * pair + 1, 1), rows]], axis=1
            )
            chosen = jnp.concatenate(halves_of(q[rows, lanes]), axis=0)
            grads = jnp.concatenate(halves_of(back), axis=0)
            mask = bias[:, rows]
            weights = jnp.exp(dot_nt(keys, chosen) + jnp.concatenate([mask, mask], axis=1) - logs)
            score_grad = (weights * (dot_nt(values, grads) - delta)).astype(LOW)
            value_grad = value_grad + dot(weights.astype(LOW), grads)
            key_grad = key_grad + dot(score_grad, chosen)
            both = dot(keys_t, score_grad)
            query_grad_t = jnp.concatenate([both[0:HEAD_DIM, 0:OWN], both[HEAD_DIM:, OWN:]], axis=0)
            dq_out[rows, lanes] = (jnp.transpose(query_grad_t) * HEAD_DIM**-0.5).astype(LOW)
        dk_out[:, lanes] = key_grad.astype(LOW)
        dv_out[:, lanes] = value_grad.astype(LOW)
        return carry

    lax.fori_loop(0, PAIRS_OF_HEADS, one_pair, 0)


def attention_back(place, lengths, q, keys, values, log_total, att, back_own, misc, after=()):
    return call(
        attention_back_kernel,
        "attention_back",
        place,
        [plain(array) for array in (q, *keys, *values, log_total, att, back_own, misc)],
        [made((512, HALF), LOW), made((1024, HALF), LOW), made((1024, HALF), LOW)],
        scratch=[pltpu.VMEM((1024, 512), FLOAT)],
        scalars=lengths,
        after=after,
        work=cost(7e9, 6e6, 3e6),
    )


def token_kernel(place, dq, dk, dv, columns, own, own_send, far, far_send):
    for part, target in enumerate((own, own_send, far, far_send)):
        rows = pl.ds(part * OWN, OWN)
        total = dot_nt(dk[rows, :], columns[1]) + dot_nt(dv[rows, :], columns[2])
        if part < 2:
            total = total + dot_nt(dq[rows, :], columns[0])
        target[...] = total.astype(LOW)


def token_parts(place, dq, dk, dv, columns, after=()):
    return call(
        token_kernel,
        "token_parts",
        place,
        [plain(dq), plain(dk), plain(dv), plain(columns)],
        [made((OWN, WIDTH), LOW)] * 4,
        after=after,
        work=cost(1.5e9, 5e6),
    )


def token_last_kernel(place, own, own_got, across, first_grad, token0, token1):
    total = own[...].astype(FLOAT) + own_got[...].astype(FLOAT) + across[8 * JOINT_SECOND :].astype(FLOAT) + first_grad[...]
    total = total.astype(LOW)
    token0[...] = total[0:BLOCK]
    token1[...] = total[BLOCK:]


def token_last(place, arrays, after=()):
    return call(
        token_last_kernel,
        "token_last",
        place,
        [plain(array) for array in arrays],
        [made((BLOCK, WIDTH), LOW)] * 2,
        after=after,
        work=cost(1e6, 2e6),
    )


def back_rows_kernel(place, done0, done1, back0, back1, outputs, token_grad):
    odd = place[0] % 2
    outputs[odd] = done0[...]
    outputs[1 - odd] = done1[...]
    token_grad[odd] = back0[...].astype(FLOAT)
    token_grad[1 - odd] = back1[...].astype(FLOAT)


def back_rows(place, done, back, after=()):
    return call(
        back_rows_kernel,
        "back_rows",
        place,
        [plain(array) for array in (*done, *back)],
        [made((2, BLOCK, WIDTH), LOW), made((2, BLOCK, WIDTH), FLOAT)],
        after=after,
        work=cost(1e6, 2e6),
    )


def joint_kernel(
    place, t0, t1, t2, t3, t4, t5, t6, t7, dq, dk, dv, far, far_got, px_send, px, qy_send, qy, tokens_t, units
):
    y, x = place[1], place[2]
    qy_send[pl.ds(8 * JOINT_SECOND, OWN), :] = added(far[...], far_got[...])
    for index, block in enumerate((t0, t1, t2, t3, t4, t5, t6, t7)):
        tokens_t[:, pl.ds(index * BLOCK, BLOCK)] = jnp.transpose(block[...].astype(FLOAT)).astype(LOW)
    biases = jnp.concatenate([column_sum(dq[...].astype(FLOAT)), column_sum(dv[...].astype(FLOAT))], axis=1)
    biases = jnp.concatenate([biases, jnp.zeros((7, WIDTH), FLOAT)], axis=0)
    for z in range(4):
        rows = pl.ds(z * 192, 192)
        query = dot(tokens_t[rows, 0:512], dq[...])
        key = dot(tokens_t[rows, :], dk[...])
        value = dot(tokens_t[rows, :], dv[...])
        for line in range(2):
            for side in range(2):
                at = line * 96 + side * 48
                units[line, side, 0:JOINT_FIRST] = jnp.concatenate(
                    [query[at : at + 48], key[at : at + 48]], axis=1
                ).astype(LOW)
                rest = jnp.concatenate([value[at : at + 24], value[at + 24 : at + 48]], axis=1)
                units[line, side, JOINT_FIRST:] = jnp.concatenate([rest, biases], axis=0).astype(LOW)
        for line in range(2):
            px[z, line] = units[line, x, 0:JOINT_FIRST]
            px_send[z, line] = units[line, 1 - x, 0:JOINT_FIRST]
        for side in range(2):
            qy[z, side] = units[y, side, JOINT_FIRST:]
            qy_send[pl.ds((z * 2 + side) * JOINT_SECOND, JOINT_SECOND), :] = units[1 - y, side, JOINT_FIRST:]


def joint_units(place, blocks, dq, dk, dv, far, far_got, after=()):
    first, second = made((4, 2, JOINT_FIRST, WIDTH), LOW), made((4, 2, JOINT_SECOND, WIDTH), LOW)
    return call(
        joint_kernel,
        "joint_units",
        place,
        [plain(array) for array in (*blocks, dq, dk, dv, far, far_got)],
        [first, first, made((8 * JOINT_SECOND + OWN, WIDTH), LOW), second],
        scratch=[pltpu.VMEM((WIDTH, 1024), LOW), pltpu.VMEM((2, 2, JOINT_ROWS, WIDTH), LOW)],
        after=after,
        work=cost(1.5e9, 6e6),
    )


def added(left, right):
    return (left.astype(FLOAT) + right.astype(FLOAT)).astype(LOW)


def down_pair_kernel(place, px, px_got, qy, qy_got, x_in, y_in, x_send, y_send, p, q):
    y, x = place[1], place[2]
    p[0] = added(px[0, y], px_got[0, y])
    y_send[...] = added(px[0, 1 - y], px_got[0, 1 - y])
    q[0] = added(qy[0, x], qy_got[0, x])
    x_send[...] = added(qy[0, 1 - x], qy_got[0, 1 - x])


def down_pair_stage(place, arrays, x_send, y_send, after=()):
    half = DOWN_ROWS // 2
    block = pl.BlockSpec((1, 2, half, WIDTH), lambda i, place: (i, 0, 0, 0))
    sent = (x_send.shape, LOW, pl.BlockSpec((half, WIDTH), lambda i, place: (i, 0)))
    kept = ((4, half, WIDTH), LOW, pl.BlockSpec((1, half, WIDTH), lambda i, place: (i, 0, 0)))
    anywhere = pl.BlockSpec(memory_space=pl.ANY)
    return call(
        down_pair_kernel,
        "down_pair_stage",
        place,
        [(array, block) for array in arrays] + [(x_send, anywhere), (y_send, anywhere)],
        [sent, sent, kept, kept],
        grid=(4,),
        after=after,
        work=cost(1e6, 1e7),
        aliases=((4, 0), (5, 1)),
    )


def second_kernel(
    place, x_got, y_got, px, qy, down_p, down_q, x_send, y_send, p, q, down_send, down_keep
):
    z_here, y, x = place[0], place[1], place[2]
    half = UP_ROWS // 2
    for z in range(4):
        for got, have, own, keep, send in ((x_got, px, y, p, y_send), (y_got, qy, x, q, x_send)):
            at = DOWN_SENT + z * UP_ROWS
            mine = pl.ds(pl.multiple_of(at + own * half, half), half)
            other = pl.ds(pl.multiple_of(at + (1 - own) * half, half), half)
            keep[z] = added(have[z, own], got[mine, :])
            send[pl.ds(z * half, half), :] = added(have[z, 1 - own], got[other, :])
    low = z_here % 2
    small = DOWN_ROWS // 2
    for target, parity in ((down_keep, low), (down_send, 1 - low)):
        for high in range(2):
            index = 2 * high + parity
            rows = pl.ds(pl.multiple_of(index * small, small), small)
            target[high, 0:small] = added(down_p[index], y_got[rows, :])
            target[high, small:] = added(down_q[index], x_got[rows, :])


def second_stage(place, arrays, after=()):
    kept = made((4, UP_ROWS // 2, WIDTH), LOW)
    down = made((2, DOWN_ROWS, WIDTH), LOW)
    return call(
        second_kernel,
        "second_stage",
        place,
        [plain(array) for array in arrays],
        [made((OWN, WIDTH), LOW), made((OWN, WIDTH), LOW), kept, kept, down, down],
        after=after,
        work=cost(1e6, 1e7),
    )


def joint_pair_kernel(place, px, px_got, qy, qy_got, x_send, y_send, p, q):
    y, x = place[1], place[2]
    for z in range(4):
        p[z] = added(px[z, y], px_got[z, y])
        y_send[z] = added(px[z, 1 - y], px_got[z, 1 - y])


        def from_y(side):
            return qy_got[pl.ds(pl.multiple_of((z * 2 + side) * JOINT_SECOND, 32), JOINT_SECOND), :]

        q[z] = added(qy[z, x], from_y(x))
        x_send[z] = added(qy[z, 1 - x], from_y(1 - x))


def joint_pair_stage(place, arrays, after=()):
    first, second = made((4, JOINT_FIRST, WIDTH), LOW), made((4, JOINT_SECOND, WIDTH), LOW)
    return call(
        joint_pair_kernel,
        "joint_pair_stage",
        place,
        [plain(array) for array in arrays],
        [second, first, first, second],
        after=after,
        work=cost(1e6, 1e7),
    )


def up_line_kernel(place, x_got, y_got, p, q, down_two, down_got, send, keep, down_send, down_keep):
    low, high_here = place[0] % 2, place[0] // 2
    half = UP_ROWS // 2
    for target, parity in ((keep, low), (send, 1 - low)):
        for high in range(2):
            index = 2 * high + parity
            rows = pl.ds(pl.multiple_of(index * half, half), half)
            target[high, 0:half] = added(p[index], y_got[rows, :])
            target[high, half:] = added(q[index], x_got[rows, :])
    down_keep[...] = added(down_two[high_here], down_got[high_here])
    down_send[...] = added(down_two[1 - high_here], down_got[1 - high_here])


def up_line_stage(place, arrays, after=()):
    return call(
        up_line_kernel,
        "up_line_stage",
        place,
        [plain(array) for array in arrays],
        [made((2, UP_ROWS, WIDTH), LOW)] * 2 + [made((DOWN_ROWS, WIDTH), LOW)] * 2,
        after=after,
        work=cost(1e6, 1e7),
    )


def joint_line_kernel(place, x_got, y_got, p, q, keep, one, two, three):
    low, high = place[0] % 2, place[0] // 2
    for target, index in (
        (keep, 2 * high + low), (one, 2 * high + 1 - low), (two, 2 * (1 - high) + low), (three, 2 * (1 - high) + 1 - low)
    ):
        target[0:JOINT_FIRST] = added(p[index], y_got[index])
        target[JOINT_FIRST:] = added(q[index], x_got[index])


def joint_line_stage(place, arrays, after=()):
    return call(
        joint_line_kernel,
        "joint_line_stage",
        place,
        [plain(array) for array in arrays],
        [made((JOINT_ROWS, WIDTH), LOW)] * 4,
        after=after,
        work=cost(1e6, 1e6),
    )


def end_stage_kernel(place, keep_two, got, send, keep):
    high = place[0] // 2
    keep[...] = added(keep_two[high], got[high])
    send[...] = added(keep_two[1 - high], got[1 - high])


def end_stage(place, keep_two, got, after=()):
    return call(
        end_stage_kernel,
        "end_stage",
        place,
        [plain(keep_two), plain(got)],
        [made(keep_two.shape[1:], LOW)] * 2,
        after=after,
        work=cost(1e6, 1e6),
    )


def joint_sum_kernel(place, first, second, third, fourth, out):
    total = (first[...].astype(FLOAT) + second[...].astype(FLOAT)) + (third[...].astype(FLOAT) + fourth[...].astype(FLOAT))
    out[...] = total.astype(LOW)


def joint_sum(place, arrays, after=()):
    results, mark = call(
        joint_sum_kernel,
        "joint_sum",
        place,
        [plain(array) for array in arrays],
        [made((JOINT_ROWS, WIDTH), LOW)],
        after=after,
        work=cost(1e6, 1e6),
    )
    return results[0], mark


def last_sum_kernel(place, *refs):
    count = len(refs) // 3
    for index in range(count):
        refs[2 * count + index][...] = added(refs[2 * index][...], refs[2 * index + 1][...])


def last_sum(place, pairs, after=()):
    return call(
        last_sum_kernel,
        "last_sum",
        place,
        [plain(array) for pair in pairs for array in pair],
        [made(pair[0].shape, LOW) for pair in pairs],
        after=after,
        work=cost(1e6, 1e6),
    )


def gathered(unit, mark=None):
    across = x_swap(unit)
    if mark is not None:
        across, mark = lax.optimization_barrier((across, mark))
    return unit, core_swap(unit), across, core_swap(across)


def quarters(place):
    x, c = place[2], place[3]
    return (x, c), (x, 1 - c), (1 - x, c), (1 - x, 1 - c)


def line_shift(place):
    seq = place[0] * 2 + place[1]
    return lax.rem(WIDTH - seq * 96, WIDTH)


def dense_out_kernel(
    place, d0, d1, d2, d3, u0, u1, u2, u3,
    down, up, out, gain2, shift2, down_bias, gain1, shift1, out_bias, up_bias, heads, tails,
):
    for down_unit, unit, (x, c) in zip((d0, d1, d2, d3), (u0, u1, u2, u3), quarters(place)):
        quarter = 2 * x + c
        down[pl.ds(pl.multiple_of(quarter * DOWN_ROWS, 32), DOWN_ROWS), :] = down_unit[...].astype(FLOAT)
        up[:, pl.ds(pl.multiple_of(quarter * WIDTH, LANES), WIDTH)] = unit[0:96, :].astype(FLOAT)
        rest = unit[96:128, :].astype(FLOAT)
        lanes = pl.ds(pl.multiple_of(c * HALF, LANES), HALF)
        out[pl.ds(pl.multiple_of(x * 48, 8), 24), lanes] = rest[0:24, 0:HALF]
        out[pl.ds(pl.multiple_of(x * 48 + 24, 8), 24), lanes] = rest[0:24, HALF:]

        @pl.when(x == 0)
        def _(rest=rest):
            heads[...] = rest[24:32]

        @pl.when(x == 1)
        def _(rest=rest):
            tails[...] = rest[24:32]

    seq = place[0] * 2 + place[1]
    shift = line_shift(place)
    head = pltpu.roll(heads[...], shift, 1)
    gain2[...] = head[0:1, 0:96]
    shift2[...] = head[1:2, 0:96]
    down_bias[...] = head[2:3, 0:96]
    tail = pltpu.roll(tails[...], shift, 1)
    gain1[...] = tail[0:1, 0:96]
    shift1[...] = tail[1:2, 0:96]
    out_bias[...] = tail[2:3, 0:96]
    wide = tails[pl.ds(4 + seq // 2, 1), :]
    up_bias[...] = jnp.where(seq % 2 == 0, wide[:, 0:HALF], wide[:, HALF:])


def dense_outputs(place, units, after=()):
    results, mark = call(
        dense_out_kernel,
        "dense_outputs",
        place,
        [plain(unit) for unit in units],
        [made((4 * DOWN_ROWS, WIDTH), FLOAT), made((96, FF), FLOAT), made((96, WIDTH), FLOAT)]
        + [made((1, 96), FLOAT)] * 6
        + [made((1, HALF), FLOAT)],
        scratch=[pltpu.VMEM((8, WIDTH), FLOAT)] * 2,
        after=after,
        work=cost(1e6, 3e6),
    )
    return (*results[:3], *(vector.reshape(-1) for vector in results[3:])), mark


def joint_out_kernel(place, u0, u1, u2, u3, joint, query_bias, value_bias, sums):
    for unit, (x, c) in zip((u0, u1, u2, u3), quarters(place)):

        def lanes(kind):
            return pl.ds(pl.multiple_of(kind * WIDTH + c * HALF, LANES), HALF)

        first = unit[0:JOINT_FIRST].astype(FLOAT)
        rest = unit[JOINT_FIRST:].astype(FLOAT)
        rows = pl.ds(pl.multiple_of(x * 48, 16), 48)
        joint[rows, lanes(0)] = first[:, 0:HALF]
        joint[rows, lanes(1)] = first[:, HALF:]
        joint[pl.ds(pl.multiple_of(x * 48, 8), 24), lanes(2)] = rest[0:24, 0:HALF]
        joint[pl.ds(pl.multiple_of(x * 48 + 24, 8), 24), lanes(2)] = rest[0:24, HALF:]

        @pl.when(x == 0)
        def _(rest=rest, c=c):
            half = pl.ds(pl.multiple_of(c * HALF, LANES), HALF)
            sums[0:1, half] = rest[24:25, 0:HALF]
            sums[1:2, half] = rest[24:25, HALF:]

    turned = pltpu.roll(sums[...], line_shift(place), 1)
    query_bias[...] = turned[0:1, 0:96]
    value_bias[...] = turned[1:2, 0:96]


def joint_outputs(place, units, after=()):
    results, mark = call(
        joint_out_kernel,
        "joint_outputs",
        place,
        [plain(unit) for unit in units],
        [made((96, 3 * WIDTH), FLOAT), made((1, 96), FLOAT), made((1, 96), FLOAT)],
        scratch=[pltpu.VMEM((8, WIDTH), FLOAT)],
        after=after,
        work=cost(1e6, 2e6),
    )
    return (results[0], results[1].reshape(-1), results[2].reshape(-1)), mark


def row_body(
    tokens,
    pair_lengths,
    joint_weight,
    query_bias,
    value_bias,
    out_weight,
    out_bias,
    first_gain,
    first_shift,
    up_weight,
    up_bias,
    down_weight,
    down_bias,
    second_gain,
    second_shift,
    cotangent,
):
    seq, rows = lax.axis_index("seq"), lax.axis_index("rows")
    z, y, x, c = seq // 2, seq % 2, rows // 2, rows % 2
    place = jnp.stack([z, y, x, c]).astype(jnp.int32)
    odd = z % 2
    weights = {
        "out": out_weight, "out_bias": out_bias, "gain1": first_gain, "shift1": first_shift,
        "up": up_weight, "up_bias": up_bias, "down": down_weight, "down_bias": down_bias,
        "gain2": second_gain, "shift2": second_shift,
    }

    def local_row(array, index):
        return lax.dynamic_index_in_dim(array, index, 0, keepdims=False)

    columns, query_row, value_row = own_columns(place, joint_weight, query_bias, value_bias)
    lengths = (pair_lengths, core_swap(pair_lengths))
    own = [row_swap(local_row(tokens, odd), 0), row_swap(local_row(tokens, 1 - odd), 1)]
    *own, columns, lengths = lax.optimization_barrier((*own, columns, lengths))
    across = [y_swap(block) for block in own]
    here = own + [core_swap(block) for block in own]
    (q, k_here, v_here, summed, stats), mark = first_attention(
        place, lengths, here, columns, query_row, value_row
    )
    padding = jnp.zeros((16, WIDTH), LOW)
    cotangents = [
        row_swap(jnp.concatenate([local_row(cotangent, index), padding], axis=0), second)
        for second, index in ((0, odd), (1, 1 - odd))
    ]
    across[0], across[1], mark, cotangents[0] = lax.optimization_barrier((across[0], across[1], mark, cotangents[0]))
    there = across + [core_swap(block) for block in across]
    blocks = here + there
    (att, k_there, v_there, log_total), mark = attention(
        place, lengths, there, columns, value_row, q, summed, stats, (mark,)
    )
    att, cotangents[1] = lax.optimization_barrier((att, cotangents[1]))
    att_got = core_swap(att)
    results, mark = forward(place, att, att_got, own, cotangents, weights, (mark,))
    (
        result0, result1, feed, second_grad, act, act_send, slope, unit1, inverse1, normed, normed_t, att_t, sums0
    ) = results
    act_got, feed_got, normed_got = core_swap(act_send), core_swap(feed), core_swap(normed)
    done = (row_swap(result0, 0), row_swap(result1, 1))
    (px_send, px, qy_send, qy), mark = down_units(place, act, act_got, feed, feed_got, (mark,))
    down_pair = (px, x_swap(px_send), qy, y_swap(qy_send))
    results, mark = backward(place, feed, slope, second_grad, unit1, inverse1, weights, (mark, normed_got))
    inner0, inner1, send0, send1, first_grad, branch_own, back_own, misc_send, sums1 = results
    got, misc = (core_swap(send0), core_swap(send1)), core_swap(misc_send)
    (x_send, y_send, px, qy), mark = up_units(
        place, normed_t, normed_got, (inner0, inner1), got, att_t, branch_own, misc, sums0, sums1, feed_got, (mark,)
    )
    (x_send, y_send, down_p, down_q), mark = down_pair_stage(place, down_pair, x_send, y_send, (mark,))
    x_got, y_got = x_swap(x_send), y_swap(y_send)
    (dq, dk, dv), mark = attention_back(
        place, lengths, q, (k_here, k_there), (v_here, v_there), log_total, att, back_own, misc, (mark,)
    )
    (token_own, own_send, token_far, far_send), mark = token_parts(place, dq, dk, dv, columns, (mark, *done))
    own_got, far_got = core_swap(own_send), core_swap(far_send)
    (px_send, joint_px, qy_send, joint_qy), mark = joint_units(
        place, blocks, dq, dk, dv, token_far, far_got, (mark,)
    )
    (x_send, y_send, p, q_, down_send, down_two), mark = second_stage(
        place, (x_got, y_got, px, qy, down_p, down_q), (mark,)
    )
    x_got, y_got, down_got = x_swap(x_send), y_swap(y_send), z_swap(down_send, 1)
    px_send, qy_send, mark = lax.optimization_barrier((px_send, qy_send, mark))
    across = y_swap(qy_send)
    joint_pair = (joint_px, x_swap(px_send), joint_qy, across)
    (up_send, up_two, down_send, down_keep), mark = up_line_stage(
        place, (x_got, y_got, p, q_, down_two, down_got), (mark,)
    )
    up_got, down_got = z_swap(up_send, 1), z_swap(down_send, 2)
    (up_send, up_keep), mark = end_stage(place, up_two, up_got, (mark, down_got))
    up_got = z_swap(up_send, 2)
    (down_unit,), mark = last_sum(place, ((down_keep, down_got),), (mark,))
    down_all = gathered(down_unit)
    (x_send, y_send, joint_p, joint_q), mark = joint_pair_stage(place, joint_pair, (mark,))
    joint_x_got, joint_y_got = x_swap(x_send), y_swap(y_send)
    (token0, token1), mark = token_last(place, (token_own, own_got, across, first_grad), (mark,))
    back = (row_swap(token0, 0), row_swap(token1, 1))
    (keep, one, two, three), mark = joint_line_stage(
        place, (joint_x_got, joint_y_got, joint_p, joint_q), (mark,)
    )
    joint_last = (keep, z_swap(one, 1), z_swap(two, 2), z_swap(three, 3))
    (up_unit,), mark = last_sum(place, ((up_keep, up_got),), (mark, *down_all[1:]))
    up_all = gathered(up_unit)
    joint_unit, mark = joint_sum(place, joint_last, (mark,))
    (
        down_grad, up_grad, out_grad, second_gain_grad, second_shift_grad, down_bias_grad, first_gain_grad,
        first_shift_grad, out_bias_grad, up_bias_grad,
    ), mark = dense_outputs(place, (*down_all, *up_all), (mark,))
    joint_all = gathered(joint_unit, mark)
    (joint_grad, query_bias_grad, value_bias_grad), mark = joint_outputs(place, joint_all, (mark,))
    (outputs, token_grad), mark = back_rows(place, done, back, (mark,))
    return (
        outputs,
        token_grad,
        joint_grad,
        query_bias_grad,
        value_bias_grad,
        out_grad,
        out_bias_grad,
        first_gain_grad,
        first_shift_grad,
        up_grad,
        up_bias_grad,
        down_grad,
        down_bias_grad,
        second_gain_grad,
        second_shift_grad,
    )


def body(tokens, *others):
    if (lax.axis_size("seq"), lax.axis_size("rows")) == (8, 4) and tokens.shape == (2, BLOCK, WIDTH):
        return row_body(tokens, *others)
    return general_body(tokens, *others)


def solution(mesh):
    placed = (
        P("rows", "seq", None),
        P("rows", None),
        P(),
        P(),
        P(),
        P(),
        P(),
        P(),
        P(),
        P(),
        P(),
        P(),
        P(),
        P(),
        P(),
        P("rows", "seq", None),
    )
    return jax.shard_map(
        body,
        mesh=mesh,
        in_specs=placed,
        out_specs=(
            P("rows", "seq", None),
            P("rows", "seq", None),
            P("seq", None),
            P("seq"),
            P("seq"),
            P("seq", None),
            P("seq"),
            P("seq"),
            P("seq"),
            P("seq", None),
            P("seq"),
            P("seq", None),
            P("seq"),
            P("seq"),
            P("seq"),
        ),
        check_vma=False,
    )
```

```python
import functools
import math

import jax
import jax.numpy as jnp
from jax import lax
from jax.experimental import pallas as pl
from jax.experimental.pallas import tpu as pltpu
from jax.sharding import PartitionSpec as P

HEADS = 12
HEAD_DIM = 64


NEGATIVE = -1e30
EPSILON = 1e-12


def from_behind(value, axis, steps):
    count = lax.axis_size(axis)
    pairs = [(source, (source + steps) % count) for source in range(count)]
    return lax.ppermute(value, axis, pairs)


def layer_norm(value, gain, shift):
    mean = jnp.mean(value, axis=-1, keepdims=True)
    centred = value - mean
    spread = jnp.mean(centred * centred, axis=-1, keepdims=True)
    return centred * lax.rsqrt(spread + EPSILON) * gain + shift


def gelu_exact(value):
    return jax.nn.gelu(value, approximate=False)


def pair_index(positions, ends):
    return jnp.sum((positions[None, :, None] >= ends[:, None, :]).astype(jnp.int32), axis=2)


def split_heads(array):
    return array.reshape(array.shape[0], array.shape[1], HEADS, HEAD_DIM)


def online_block(state, query_heads, query_pairs, key_block, value_block, key_pairs):
    highest, total, summed = state
    scores = jnp.einsum(
        "rqhd,rkhd->rhqk", query_heads, split_heads(key_block), preferred_element_type=jnp.float32
    ) * HEAD_DIM ** (-0.5)
    allowed = query_pairs[:, None, :, None] == key_pairs[:, None, None, :]
    masked = jnp.where(allowed, scores, NEGATIVE)
    new_high = jnp.maximum(highest, jnp.max(masked, axis=3))
    weights = jnp.where(allowed, jnp.exp(masked - new_high[..., None]), 0.0)
    factor = jnp.exp(highest - new_high)
    total = total * factor + jnp.sum(weights, axis=3)
    summed = summed * jnp.swapaxes(factor, 1, 2)[..., None] + jnp.einsum(
        "rhqk,rkhd->rqhd",
        weights.astype(jnp.bfloat16),
        split_heads(value_block),
        preferred_element_type=jnp.float32,
    )
    return (new_high, total, summed)


def tile_terms(queries, out_grad, log_total, delta, query_pairs, keys, values, key_pairs):
    scale = HEAD_DIM ** (-0.5)
    query_heads = split_heads(queries)
    grad_heads = split_heads(out_grad)
    key_heads = split_heads(keys)
    value_heads = split_heads(values)
    scores = (
        jnp.einsum("rqhd,rkhd->rhqk", query_heads, key_heads, preferred_element_type=jnp.float32)
        * scale
    )
    allowed = query_pairs[:, None, :, None] == key_pairs[:, None, None, :]
    weights = jnp.where(
        allowed, jnp.exp(jnp.where(allowed, scores, NEGATIVE) - log_total[..., None]), 0.0
    )
    weight_grad = jnp.einsum(
        "rqhd,rkhd->rhqk", grad_heads, value_heads, preferred_element_type=jnp.float32
    )
    score_grad = (weights * (weight_grad - delta[..., None])).astype(jnp.bfloat16)
    query_term = (
        jnp.einsum("rhqk,rkhd->rqhd", score_grad, key_heads, preferred_element_type=jnp.float32)
        * scale
    )
    key_term = (
        jnp.einsum("rhqk,rqhd->rkhd", score_grad, query_heads, preferred_element_type=jnp.float32)
        * scale
    )
    value_term = jnp.einsum(
        "rhqk,rqhd->rkhd",
        weights.astype(jnp.bfloat16),
        grad_heads,
        preferred_element_type=jnp.float32,
    )
    return (
        query_term.reshape(queries.shape),
        key_term.reshape(keys.shape),
        value_term.reshape(values.shape),
    )


def general_body(
    tokens,
    pair_lengths,
    joint_weight,
    query_bias,
    value_bias,
    out_weight,
    out_bias,
    first_gain,
    first_shift,
    up_weight,
    up_bias,
    down_weight,
    down_bias,
    second_gain,
    second_shift,
    cotangent,
):
    rows_here, seq_here, width = tokens.shape
    count = lax.axis_size("seq")
    cycle_index = lax.axis_index("seq")
    ends = jnp.cumsum(pair_lengths, axis=1)
    offsets = jnp.arange(seq_here, dtype=jnp.int32)
    own_pairs = pair_index(cycle_index * seq_here + offsets, ends)
    block_shape = (rows_here, seq_here, width)
    flat = tokens.reshape(rows_here * seq_here, width)
    projected = jnp.dot(flat, joint_weight, preferred_element_type=jnp.float32)
    queries = (projected[:, :width] + query_bias).astype(jnp.bfloat16).reshape(block_shape)
    keys = projected[:, width : 2 * width].astype(jnp.bfloat16).reshape(block_shape)
    values = (projected[:, 2 * width :] + value_bias).astype(jnp.bfloat16).reshape(block_shape)
    query_heads = split_heads(queries)
    initial = (
        jnp.full((rows_here, HEADS, seq_here), NEGATIVE, jnp.float32),
        jnp.zeros((rows_here, HEADS, seq_here), jnp.float32),
        jnp.zeros((rows_here, seq_here, HEADS, HEAD_DIM), jnp.float32),
    )
    key_piece = lax.all_gather(keys, "seq", axis=1, tiled=True)
    value_piece = lax.all_gather(values, "seq", axis=1, tiled=True)
    length = key_piece.shape[1]
    block = math.gcd(length, seq_here)

    def one_block(index, inner_state):
        first = index * block
        key_block = lax.dynamic_slice_in_dim(key_piece, first, block, 1)
        value_block = lax.dynamic_slice_in_dim(value_piece, first, block, 1)
        key_pairs = pair_index(first + jnp.arange(block, dtype=jnp.int32), ends)
        return online_block(inner_state, query_heads, own_pairs, key_block, value_block, key_pairs)

    highest, total, summed = lax.fori_loop(0, length // block, one_block, initial)
    log_total = highest + jnp.log(total)
    attended = (
        (summed / jnp.swapaxes(total, 1, 2)[..., None]).astype(jnp.bfloat16).reshape(flat.shape)
    )
    branch = jnp.dot(attended, out_weight, preferred_element_type=jnp.float32) + out_bias
    first_sum = flat.astype(jnp.float32) + branch
    normed, first_back = jax.vjp(layer_norm, first_sum, first_gain, first_shift)
    normed_low = normed.astype(jnp.bfloat16)
    inner = jnp.dot(normed_low, up_weight, preferred_element_type=jnp.float32) + up_bias
    activated_full, gelu_back = jax.vjp(gelu_exact, inner)
    activated = activated_full.astype(jnp.bfloat16)
    feed = jnp.dot(activated, down_weight, preferred_element_type=jnp.float32) + down_bias
    second_sum = normed + feed
    result, second_back = jax.vjp(layer_norm, second_sum, second_gain, second_shift)
    outputs = result.astype(jnp.bfloat16).reshape(tokens.shape)
    second_grad, second_gain_grad, second_shift_grad = second_back(
        cotangent.astype(jnp.float32).reshape(flat.shape)
    )
    feed_grad = second_grad.astype(jnp.bfloat16)
    down_grad = jnp.einsum("ti,tj->ij", activated, feed_grad, preferred_element_type=jnp.float32)
    down_bias_grad = jnp.sum(feed_grad.astype(jnp.float32), axis=0)
    activated_grad = jnp.einsum(
        "tj,ij->ti", feed_grad, down_weight, preferred_element_type=jnp.float32
    )
    inner_grad = gelu_back(activated_grad)[0].astype(jnp.bfloat16)
    up_grad = jnp.einsum("ti,tj->ij", normed_low, inner_grad, preferred_element_type=jnp.float32)
    up_bias_grad = jnp.sum(inner_grad.astype(jnp.float32), axis=0)
    normed_grad = second_grad + jnp.einsum(
        "tj,ij->ti", inner_grad, up_weight, preferred_element_type=jnp.float32
    )
    first_grad, first_gain_grad, first_shift_grad = first_back(normed_grad)
    branch_grad = first_grad.astype(jnp.bfloat16)
    out_grad = jnp.einsum("ti,tj->ij", attended, branch_grad, preferred_element_type=jnp.float32)
    out_bias_grad = jnp.sum(branch_grad.astype(jnp.float32), axis=0)
    attended_grad = jnp.einsum(
        "tj,ij->ti", branch_grad, out_weight, preferred_element_type=jnp.float32
    ).astype(jnp.bfloat16)
    delta = jnp.sum(
        (attended_grad.astype(jnp.float32) * attended.astype(jnp.float32)).reshape(
            rows_here, seq_here, HEADS, HEAD_DIM
        ),
        axis=3,
    )
    delta = jnp.swapaxes(delta, 1, 2)
    attended_grad = attended_grad.reshape(block_shape)
    zeros_block = jnp.zeros(block_shape, jnp.float32)

    def send_key_sums(sums):
        return (
            from_behind(sums[0].astype(jnp.bfloat16), "seq", 1).astype(jnp.float32),
            from_behind(sums[1].astype(jnp.bfloat16), "seq", 1).astype(jnp.float32),
        )

    def key_work(turn, pair_block, sums, query_sum):
        anchor = (cycle_index - turn) % count
        key_pairs = pair_index(anchor * seq_here + offsets, ends)
        query_term, key_term, value_term = tile_terms(
            queries,
            attended_grad,
            log_total,
            delta,
            own_pairs,
            pair_block[0],
            pair_block[1],
            key_pairs,
        )
        return ((sums[0] + key_term, sums[1] + value_term), query_sum + query_term)

    def key_turn(turn, state):
        pair_block, sums, query_sum = state
        sums, query_sum = key_work(turn, pair_block, sums, query_sum)
        sums = send_key_sums(sums)
        pair_block = from_behind((pair_block[0], pair_block[1]), "seq", 1)
        return (pair_block, sums, query_sum)

    pair_block, sums, query_sum = lax.fori_loop(
        0, count - 1, key_turn, ((keys, values), (zeros_block, zeros_block), zeros_block)
    )
    sums, query_sum = key_work(count - 1, pair_block, sums, query_sum)
    key_sum, value_sum = send_key_sums(sums)
    query_low = query_sum.astype(jnp.bfloat16).reshape(flat.shape)
    key_low = key_sum.astype(jnp.bfloat16).reshape(flat.shape)
    value_low = value_sum.astype(jnp.bfloat16).reshape(flat.shape)
    joint_low = jnp.concatenate([query_low, key_low, value_low], axis=1)
    joint_grad = jnp.einsum("ti,tj->ij", flat, joint_low, preferred_element_type=jnp.float32)
    query_bias_grad = jnp.sum(query_low.astype(jnp.float32), axis=0)
    value_bias_grad = jnp.sum(value_low.astype(jnp.float32), axis=0)
    token_grad = first_grad + jnp.einsum(
        "tj,ij->ti", joint_low, joint_weight, preferred_element_type=jnp.float32
    )
    gradients = (
        joint_grad,
        query_bias_grad,
        value_bias_grad,
        out_grad,
        out_bias_grad,
        first_gain_grad,
        first_shift_grad,
        up_grad,
        up_bias_grad,
        down_grad,
        down_bias_grad,
        second_gain_grad,
        second_shift_grad,
    )
    shares = (
        lax.psum_scatter(
            gradients[0].astype(jnp.bfloat16), "seq", scatter_dimension=0, tiled=True
        ).astype(jnp.float32),
        lax.psum_scatter(
            gradients[1].astype(jnp.bfloat16), "seq", scatter_dimension=0, tiled=True
        ).astype(jnp.float32),
        lax.psum_scatter(
            gradients[2].astype(jnp.bfloat16), "seq", scatter_dimension=0, tiled=True
        ).astype(jnp.float32),
        lax.psum_scatter(
            gradients[3].astype(jnp.bfloat16), "seq", scatter_dimension=0, tiled=True
        ).astype(jnp.float32),
        lax.psum_scatter(
            gradients[4].astype(jnp.bfloat16), "seq", scatter_dimension=0, tiled=True
        ).astype(jnp.float32),
        lax.psum_scatter(
            gradients[5].astype(jnp.bfloat16), "seq", scatter_dimension=0, tiled=True
        ).astype(jnp.float32),
        lax.psum_scatter(
            gradients[6].astype(jnp.bfloat16), "seq", scatter_dimension=0, tiled=True
        ).astype(jnp.float32),
        lax.psum_scatter(
            gradients[7].astype(jnp.bfloat16), "seq", scatter_dimension=0, tiled=True
        ).astype(jnp.float32),
        lax.psum_scatter(
            gradients[8].astype(jnp.bfloat16), "seq", scatter_dimension=0, tiled=True
        ).astype(jnp.float32),
        lax.psum_scatter(
            gradients[9].astype(jnp.bfloat16), "seq", scatter_dimension=0, tiled=True
        ).astype(jnp.float32),
        lax.psum_scatter(
            gradients[10].astype(jnp.bfloat16), "seq", scatter_dimension=0, tiled=True
        ).astype(jnp.float32),
        lax.psum_scatter(
            gradients[11].astype(jnp.bfloat16), "seq", scatter_dimension=0, tiled=True
        ).astype(jnp.float32),
        lax.psum_scatter(
            gradients[12].astype(jnp.bfloat16), "seq", scatter_dimension=0, tiled=True
        ).astype(jnp.float32),
    )
    shares = (
        lax.psum(shares[0].astype(jnp.bfloat16), "rows").astype(jnp.float32),
        lax.psum(shares[1].astype(jnp.bfloat16), "rows").astype(jnp.float32),
        lax.psum(shares[2].astype(jnp.bfloat16), "rows").astype(jnp.float32),
        lax.psum(shares[3].astype(jnp.bfloat16), "rows").astype(jnp.float32),
        lax.psum(shares[4].astype(jnp.bfloat16), "rows").astype(jnp.float32),
        lax.psum(shares[5].astype(jnp.bfloat16), "rows").astype(jnp.float32),
        lax.psum(shares[6].astype(jnp.bfloat16), "rows").astype(jnp.float32),
        lax.psum(shares[7].astype(jnp.bfloat16), "rows").astype(jnp.float32),
        lax.psum(shares[8].astype(jnp.bfloat16), "rows").astype(jnp.float32),
        lax.psum(shares[9].astype(jnp.bfloat16), "rows").astype(jnp.float32),
        lax.psum(shares[10].astype(jnp.bfloat16), "rows").astype(jnp.float32),
        lax.psum(shares[11].astype(jnp.bfloat16), "rows").astype(jnp.float32),
        lax.psum(shares[12].astype(jnp.bfloat16), "rows").astype(jnp.float32),
    )
    return (outputs, token_grad.reshape(tokens.shape)) + tuple(shares)


WIDTH = HEADS * HEAD_DIM
HALF = WIDTH // 2
FF = 4 * WIDTH
BLOCK = 128
OWN = 2 * BLOCK
LANES = 128
PAIRS_OF_HEADS = HALF // LANES
JOINT_ROWS = 80
JOINT_FIRST = 48
JOINT_SECOND = JOINT_ROWS - JOINT_FIRST
UP_ROWS = 128
DOWN_ROWS = 96
EXT = OWN + 16
DOWN_SENT = 2 * DOWN_ROWS
FLOAT = jnp.float32
LOW = jnp.bfloat16
AXES = ("seq", "rows")


def kernel_params(megabytes):
    return pltpu.CompilerParams(vmem_limit_bytes=megabytes << 20)


def shaped(shape, kind):
    return jax.ShapeDtypeStruct(shape, kind)


def whole(shape):
    return pl.BlockSpec(shape, lambda *_: (0,) * len(shape))


def cost(flops, moved, exps=0):
    return pl.CostEstimate(flops=1024, bytes_accessed=1024, transcendentals=0)


def dot(left, right):
    return lax.dot_general(left, right, (((1,), (0,)), ((), ())), preferred_element_type=FLOAT)


def dot_nt(left, right):
    return lax.dot_general(left, right, (((1,), (1,)), ((), ())), preferred_element_type=FLOAT)


def call(kernel, name, place, inputs, outputs, scratch=(), grid=(1,), scalars=(), after=(), megabytes=28, work=None, aliases=()):
    prefetch = 1 + len(scalars)
    given, made = len(inputs), len(outputs)

    def ordered(*refs):
        first = prefetch + given
        mark = refs[first + len(after) + made]
        mark[...] = jnp.zeros_like(mark)
        kernel(*refs[:first], *refs[first + len(after) : first + len(after) + made], *refs[first + len(after) + made + 1 :])

    results = pl.pallas_call(
        ordered,
        grid_spec=pltpu.PrefetchScalarGridSpec(
            num_scalar_prefetch=prefetch,
            grid=grid,
            in_specs=[spec for _, spec in inputs] + [pl.BlockSpec(memory_space=pl.ANY)] * len(after),
            out_specs=[spec for _, _, spec in outputs] + [whole((8, LANES))],
            scratch_shapes=list(scratch),
        ),
        out_shape=[shaped(shape, kind) for shape, kind, _ in outputs] + [shaped((8, LANES), FLOAT)],
        compiler_params=kernel_params(megabytes),
        cost_estimate=work,
        input_output_aliases={prefetch + source: target for source, target in aliases},
        name=name,
    )(place, *scalars, *[array for array, _ in inputs], *after)
    return results[:-1], results[-1]


def plain(array):
    return array, whole(array.shape)


def made(shape, kind):
    return shape, kind, whole(shape)


def device_at(z, y, x, c):
    return ((z * 2 + y) * 2 + x) * 2 + c


def permute(value, target):
    pairs = []
    for z in range(4):
        for y in range(2):
            for x in range(2):
                for c in range(2):
                    pairs.append((device_at(z, y, x, c), device_at(*target(z, y, x, c))))
    return lax.ppermute(value, AXES, pairs)


def core_swap(value):
    return permute(value, lambda z, y, x, c: (z, y, x, 1 - c))


def x_swap(value):
    return permute(value, lambda z, y, x, c: (z, y, 1 - x, c))


def y_swap(value):
    return permute(value, lambda z, y, x, c: (z, 1 - y, x, c))


def z_swap(value, bits):
    return permute(value, lambda z, y, x, c: (z ^ bits, y, x, c))


def row_swap(value, second):
    return permute(value, lambda z, y, x, c: (2 * c + (z % 2 ^ second), y, x, z // 2))


def first_positions(place):
    z, y, c = place[0], place[1], place[3]
    bases = []
    for core, line in ((c, y), (1 - c, y), (c, 1 - y), (1 - c, 1 - y)):
        for second in (0, 1):
            parity = z % 2
            parity = 1 - parity if second else parity
            bases.append((2 * (2 * core + parity) + line) * BLOCK)
    return bases


def pair_ends(place, own_lengths, peer_lengths):
    z, c = place[0], place[3]
    here = (z // 2) == c
    line = z % 2
    ends, end = [], 0
    for pair in range(own_lengths.shape[1]):
        end = end + jnp.where(here, own_lengths[line, pair], peer_lengths[line, pair])
        ends.append(end)
    return ends


def pairs_along(base, ends, axis):
    shape = (8, BLOCK) if axis == 1 else (BLOCK, LANES)
    position = base + lax.broadcasted_iota(jnp.int32, shape, axis)
    ids = jnp.zeros(shape, jnp.int32)
    for end in ends:
        ids = ids + (position >= end).astype(jnp.int32)
    return ids


def head_mask(rows):
    return lax.broadcasted_iota(jnp.int32, (rows, LANES), 1) < HEAD_DIM


def columns_kernel(place, columns, query_bias, value_bias, out, query_row, value_row):
    out[0] = columns[...]
    query_row[...] = query_bias[...]
    value_row[...] = value_bias[...]


def own_columns(place, joint_weight, query_bias, value_bias):
    half_row = pl.BlockSpec((1, HALF), lambda i, place: (0, place[3]))
    results, _ = call(
        columns_kernel,
        "own_columns",
        place,
        [
            (joint_weight, pl.BlockSpec((WIDTH, HALF), lambda i, place: (0, 2 * i + place[3]))),
            (row_of(query_bias), half_row),
            (row_of(value_bias), half_row),
        ],
        [((3, WIDTH, HALF), LOW, pl.BlockSpec((1, WIDTH, HALF), lambda i, place: (i, 0, 0)))]
        + [made((1, HALF), FLOAT)] * 2,
        grid=(3,),
        work=cost(1e6, 4e6),
    )
    return results


def first_attention_kernel(
    place, own_lengths, peer_lengths, t0, t1, t2, t3, columns, qb, vb, q_out, k_out, v_out, summed, stats, bias
):
    bases = first_positions(place)
    ends = pair_ends(place, own_lengths, peer_lengths)
    tokens = jnp.concatenate([block[...] for block in (t0, t1, t2, t3)], axis=0)
    queries = dot(tokens, columns[0]) + qb[...]
    q_out[...] = (queries.astype(LOW).astype(FLOAT) * HEAD_DIM**-0.5).astype(LOW)
    k_out[...] = dot(tokens, columns[1]).astype(LOW)
    v_out[...] = (dot(tokens, columns[2]) + vb[...]).astype(LOW)
    fill_bias(bias, bases[:4], bases[:4], ends)
    stats[...] = jnp.zeros_like(stats)
    for pair in range(PAIRS_OF_HEADS):
        lanes = pl.ds(pair * LANES, LANES)
        scores = masked_scores(k_out[:, lanes], q_out[:, lanes], bias)
        highest = jnp.max(scores, axis=0, keepdims=True)
        weights = jnp.exp(scores - highest)
        summed[pair] = dot(turned(v_out[:, lanes]), weights.astype(LOW))
        stats[2 * pair : 2 * pair + 1, :] = highest
        stats[2 * pair + 1 : 2 * pair + 2, :] = column_sum(weights)


def turned(array):
    return jnp.transpose(array.astype(FLOAT)).astype(LOW)


def masked_scores(keys, queries, bias):
    mask = bias[...]
    chosen = jnp.concatenate(halves_of(queries), axis=0)
    return dot_nt(keys, chosen) + jnp.concatenate([mask, mask], axis=1)


def fill_bias(bias, query_bases, key_bases, ends):
    key_ids = [pairs_along(base, ends, 1)[0:1] for base in key_bases]
    for i, base in enumerate(query_bases):
        query_ids = pairs_along(base, ends, 0)
        for j in range(len(key_bases)):
            bias[pl.ds(i * BLOCK, BLOCK), pl.ds(j * BLOCK, BLOCK)] = jnp.where(query_ids == key_ids[j], 0.0, NEGATIVE)


def halves_of(array):
    left = head_mask(array.shape[0])
    zeros = jnp.zeros_like(array)
    return jnp.where(left, array, zeros), jnp.where(left, zeros, array)


def first_attention(place, lengths, blocks, columns, query_bias, value_bias, after=()):
    return call(
        first_attention_kernel,
        "first_attention",
        place,
        [plain(array) for array in (*blocks, columns, query_bias, value_bias)],
        [made((512, HALF), LOW)] * 3 + [made((PAIRS_OF_HEADS, LANES, 1024), FLOAT), made((8, 1024), FLOAT)],
        scratch=[pltpu.VMEM((512, 512), FLOAT)],
        scalars=lengths,
        after=after,
        work=cost(4e9, 8e6, 3e6),
    )


def attention_kernel(
    place, own_lengths, peer_lengths, t0, t1, t2, t3, columns, vb, q, summed, stats,
    att_out, k_out, v_out, log_out, bias,
):
    bases = first_positions(place)
    ends = pair_ends(place, own_lengths, peer_lengths)
    tokens = jnp.concatenate([block[...] for block in (t0, t1, t2, t3)], axis=0)
    k_out[...] = dot(tokens, columns[1]).astype(LOW)
    v_out[...] = (dot(tokens, columns[2]) + vb[...]).astype(LOW)
    fill_bias(bias, bases[4:], bases[:4], ends)
    log_out[...] = jnp.zeros_like(log_out)
    top = lax.broadcasted_iota(jnp.int32, (LANES, 512), 0) < HEAD_DIM
    for pair in range(PAIRS_OF_HEADS):
        lanes = pl.ds(pair * LANES, LANES)
        scores = masked_scores(k_out[:, lanes], q[:, lanes], bias)
        before = stats[2 * pair : 2 * pair + 1, :]
        highest = jnp.maximum(before, jnp.max(scores, axis=0, keepdims=True))
        weights = jnp.exp(scores - highest)
        shrink = jnp.exp(before - highest)
        sums = column_sum(weights) + shrink * stats[2 * pair + 1 : 2 * pair + 2, :]
        total = (dot(turned(v_out[:, lanes]), weights.astype(LOW)) + shrink * summed[pair]) / sums
        att_out[:, lanes] = jnp.transpose(jnp.where(top, total[:, 0:512], total[:, 512:])).astype(LOW)
        logs = highest + jnp.log(sums)
        log_out[2 * pair : 2 * pair + 1, :] = logs[:, 0:512]
        log_out[2 * pair + 1 : 2 * pair + 2, :] = logs[:, 512:]


def attention(place, lengths, blocks, columns, value_bias, q, summed, stats, after=()):
    return call(
        attention_kernel,
        "attention",
        place,
        [plain(array) for array in (*blocks, columns, value_bias, q, summed, stats)],
        [made((512, HALF), LOW)] * 3 + [made((8, 512), FLOAT)],
        scratch=[pltpu.VMEM((512, 512), FLOAT)],
        scalars=lengths,
        after=after,
        work=cost(4e9, 8e6, 3e6),
    )


def centred_norm(value):
    mean = jnp.mean(value, axis=-1, keepdims=True)
    centred = value - mean
    spread = jnp.mean(centred * centred, axis=-1, keepdims=True)
    inverse = lax.rsqrt(spread + EPSILON)
    return centred * inverse, inverse


def norm_back(grad, unit, inverse):
    mean = jnp.mean(grad, axis=-1, keepdims=True)
    along = jnp.mean(grad * unit, axis=-1, keepdims=True)
    return (grad - mean - unit * along) * inverse


def column_sum(value):
    return jnp.sum(value, axis=0, keepdims=True)


def forward_kernel(
    place, att, att_got, wo_own, wo_other, out_bias, x0, x1, gain1, shift1, up, up_bias, down,
    down_bias, gain2, shift2, cot0, cot1,
    result0, result1, feed_ext, second_grad, act_keep, act_send, slope, unit1, inverse1, normed_low, normed_t, att_t, sums,
    act_t,
):
    c = place[3]
    tokens = jnp.concatenate([x0[...], x1[...]], axis=0).astype(FLOAT)
    att_own, att_other = att[0:OWN], att_got[OWN:]
    branch = dot(att_own, wo_own[...]) + dot(att_other, wo_other[...]) + out_bias[...]
    unit, inverse = centred_norm(tokens + branch)
    unit1[...] = unit
    inverse1[...] = jnp.broadcast_to(inverse, (OWN, LANES))
    normed = unit * gain1[...] + shift1[...]
    low = normed.astype(LOW)
    normed_low[...] = low
    normed_t[...] = jnp.transpose(normed).astype(LOW)
    mine = pl.ds(pl.multiple_of(c * HALF, HALF), HALF)
    other = pl.ds(pl.multiple_of((1 - c) * HALF, HALF), HALF)
    att_t[mine, :] = jnp.transpose(att[...].astype(FLOAT)).astype(LOW)
    att_t[other, 0:OWN] = jnp.transpose(att_other.astype(FLOAT)).astype(LOW)
    att_t[other, OWN:] = jnp.transpose(att_got[0:OWN].astype(FLOAT)).astype(LOW)
    inner = dot(low, up[...]) + up_bias[...]
    below = 0.5 + 0.5 * lax.erf(inner * math.sqrt(0.5))
    density = jnp.exp(inner * inner * -0.5) * (1.0 / math.sqrt(2.0 * math.pi))
    activated = inner * below
    slope[...] = (below + inner * density).astype(LOW)
    act_t[...] = jnp.transpose(activated).astype(LOW).reshape(16, 2, DOWN_ROWS, OWN)
    act_keep[...] = act_t[:, c]
    act_send[...] = act_t[:, 1 - c]
    feed = dot(activated.astype(LOW), down[...])
    unit, inverse = centred_norm(normed + feed + down_bias[...])
    result = (unit * gain2[...] + shift2[...]).astype(LOW)
    result0[...] = result[0:BLOCK]
    result1[...] = result[BLOCK:]
    cotangent = jnp.concatenate([cot0[0:BLOCK], cot1[0:BLOCK]], axis=0).astype(FLOAT)
    grad = norm_back(cotangent * gain2[...], unit, inverse)
    second_grad[...] = grad
    low_grad = grad.astype(LOW)
    rows = jnp.concatenate(
        [
            column_sum(cotangent * unit),
            column_sum(cotangent),
            column_sum(low_grad.astype(FLOAT)),
            jnp.zeros((5, WIDTH), FLOAT),
        ],
        axis=0,
    )
    sums[...] = rows
    feed_ext[0:OWN] = low_grad
    feed_ext[OWN:] = jnp.concatenate([rows, jnp.zeros_like(rows)], axis=0).astype(LOW)


def row_of(vector):
    return vector.reshape(1, vector.shape[0])


def forward(place, att, att_got, tokens, cotangents, weights, after=()):
    chunk = FF

    def vector(name):
        return plain(row_of(weights[name]))

    units = ((16, DOWN_ROWS, OWN), LOW, pl.BlockSpec((16, DOWN_ROWS, OWN), lambda i, place: (i, 0, 0)))
    return call(
        forward_kernel,
        "forward",
        place,
        [
            plain(att),
            plain(att_got),
            (weights["out"], pl.BlockSpec((HALF, WIDTH), lambda i, place: (place[3], 0))),
            (weights["out"], pl.BlockSpec((HALF, WIDTH), lambda i, place: (1 - place[3], 0))),
            vector("out_bias"), plain(tokens[0]), plain(tokens[1]), vector("gain1"), vector("shift1"),
            (weights["up"], pl.BlockSpec((WIDTH, chunk), lambda i, place: (0, i))),
            (row_of(weights["up_bias"]), pl.BlockSpec((1, chunk), lambda i, place: (0, i))),
            (weights["down"], pl.BlockSpec((chunk, WIDTH), lambda i, place: (i, 0))),
            vector("down_bias"), vector("gain2"), vector("shift2"), plain(cotangents[0]), plain(cotangents[1]),
        ],
        [
            made((BLOCK, WIDTH), LOW), made((BLOCK, WIDTH), LOW), made((EXT, WIDTH), LOW),
            made((OWN, WIDTH), FLOAT), units, units,
            ((OWN, FF), LOW, pl.BlockSpec((OWN, chunk), lambda i, place: (0, i))),
            made((OWN, WIDTH), FLOAT), made((OWN, LANES), FLOAT), made((OWN, WIDTH), LOW),
            made((WIDTH, OWN), LOW), made((WIDTH, 512), LOW), made((8, WIDTH), FLOAT),
        ],
        scratch=[pltpu.VMEM((16, 2, DOWN_ROWS, OWN), LOW)],
        after=after,
        work=cost(2.7e9, 20e6, 2e6),
    )


def split_units(place, units, px_send, px, qy_send, qy):
    y, x = place[1], place[2]
    half = units.shape[2] // 2
    for line in range(2):
        px[0, line] = units[line, x, 0:half]
        px_send[0, line] = units[line, 1 - x, 0:half]
    for side in range(2):
        qy[0, side] = units[y, side, half:]
        qy_send[0, side] = units[1 - y, side, half:]


def unit_outputs(rows, width):
    shape = (4, 2, rows // 2, width)
    return [(shape, LOW, pl.BlockSpec((1,) + shape[1:], lambda i, place: (i, 0, 0, 0)))] * 4


def down_kernel(place, act, act_got, feed, feed_got, px_send, px, qy_send, qy, units):
    shape = (4 * DOWN_ROWS, OWN)
    total = dot(act[...].reshape(shape), feed[0:OWN]) + dot(act_got[...].reshape(shape), feed_got[0:OWN])
    units[...] = total.astype(LOW).reshape(units.shape)
    split_units(place, units, px_send, px, qy_send, qy)


def down_units(place, act, act_got, feed, feed_got, after=()):
    block = pl.BlockSpec((4, DOWN_ROWS, OWN), lambda i, place: (i, 0, 0))
    return call(
        down_kernel,
        "down_units",
        place,
        [(act, block), (act_got, block), plain(feed), plain(feed_got)],
        unit_outputs(DOWN_ROWS, WIDTH),
        scratch=[pltpu.VMEM((2, 2, DOWN_ROWS, WIDTH), LOW)],
        grid=(4,),
        after=after,
        work=cost(0.6e9, 3.5e6),
    )


def backward_kernel(
    place, feed_ext, slope, up, down, second_grad, unit1, inverse1, gain1, wo_own, wo_other,
    inner0, inner1, send0, send1, first_grad, branch_own, back_own, misc, sums,
    inner, branch,
):
    c = place[3]
    grad = (dot_nt(feed_ext[0:OWN], down[...]) * slope[...].astype(FLOAT)).astype(LOW)
    inner[...] = grad
    for target, index in ((inner0, c), (inner1, 2 + c), (send0, 1 - c), (send1, 3 - c)):
        target[...] = inner[:, pl.ds(pl.multiple_of(index * WIDTH, LANES), WIDTH)]
    inner_sum = column_sum(grad.astype(FLOAT))
    total = second_grad[...] + dot_nt(grad, up[...])
    unit = unit1[...]
    grad1 = norm_back(total * gain1[...], unit, inverse1[:, 0:1])
    first_grad[...] = grad1
    low = grad1.astype(LOW)
    branch[...] = low
    rows = jnp.concatenate(
        [
            column_sum(total * unit),
            column_sum(total),
            column_sum(low.astype(FLOAT)),
            jnp.zeros((1, WIDTH), FLOAT),
        ]
        + [inner_sum[:, index * WIDTH : (index + 1) * WIDTH] for index in range(4)],
        axis=0,
    )
    sums[...] = rows
    branch_own[...] = branch[:, pl.ds(pl.multiple_of(c * HALF, LANES), HALF)]
    back_own[...] = dot_nt(low, wo_own[...]).astype(LOW)
    misc[0:OWN, 0:HALF] = branch[:, pl.ds(pl.multiple_of((1 - c) * HALF, LANES), HALF)]
    misc[0:OWN, HALF:] = dot_nt(low, wo_other[...]).astype(LOW)
    misc[OWN:] = jnp.concatenate([rows, jnp.zeros_like(rows)], axis=0).astype(LOW)


def backward(place, feed_ext, slope, second_grad, unit1, inverse1, weights, after=()):
    chunk = FF
    return call(
        backward_kernel,
        "backward",
        place,
        [
            plain(feed_ext),
            (slope, pl.BlockSpec((OWN, chunk), lambda i, place: (0, i))),
            (weights["up"], pl.BlockSpec((WIDTH, chunk), lambda i, place: (0, i))),
            (weights["down"], pl.BlockSpec((chunk, WIDTH), lambda i, place: (i, 0))),
            plain(second_grad), plain(unit1), plain(inverse1), plain(row_of(weights["gain1"])),
            (weights["out"], pl.BlockSpec((HALF, WIDTH), lambda i, place: (place[3], 0))),
            (weights["out"], pl.BlockSpec((HALF, WIDTH), lambda i, place: (1 - place[3], 0))),
        ],
        [made((OWN, WIDTH), LOW)] * 4
        + [
            made((OWN, WIDTH), FLOAT), made((OWN, HALF), LOW), made((OWN, HALF), LOW), made((EXT, WIDTH), LOW),
            made((8, WIDTH), FLOAT),
        ],
        scratch=[pltpu.VMEM((OWN, FF), LOW), pltpu.VMEM((OWN, WIDTH), LOW)],
        after=after,
        work=cost(2.7e9, 16e6),
    )


def up_kernel(
    place, normed_t, normed_got, inner0, inner1, got0, got1, att_t, branch, misc, sums0, sums1, feed_got,
    x_send, y_send, px, qy, units, normed_got_t,
):
    z = pl.program_id(0)
    y, x = place[1], place[2]

    @pl.when(z == 0)
    def _():
        normed_got_t[...] = jnp.transpose(normed_got[...].astype(FLOAT)).astype(LOW)

    theirs = normed_got_t[pl.ds(pl.multiple_of(z * 192, 32), 192), :]
    outer = dot(att_t[:, 0:OWN], branch[...]) + dot(att_t[:, OWN:], misc[0:OWN, 0:HALF])
    for side, inner, got, sums, pair in ((0, inner0, got0, sums0, feed_got), (1, inner1, got1, sums1, misc)):
        grad = dot(normed_t[...], inner[...]) + dot(theirs, got[...])
        vectors = sums[...] + pair[OWN:].astype(FLOAT)[0:8]
        for line in range(2):
            first = line * 96 + side * 48
            rest = jnp.concatenate([outer[first : first + 24], outer[first + 24 : first + 48]], axis=1)
            units[line, side] = jnp.concatenate(
                [grad[line * 96 : line * 96 + 96], rest, vectors], axis=0
            ).astype(LOW)
    half = UP_ROWS // 2
    for index in range(2):
        rows = pl.ds(pl.multiple_of(DOWN_SENT + (z * 2 + index) * half, half), half)
        px[0, index] = units[index, x, 0:half]
        x_send[rows, :] = units[index, 1 - x, 0:half]
        qy[0, index] = units[y, index, half:]
        y_send[rows, :] = units[1 - y, index, half:]


def up_units(place, normed_t, normed_got, inner, got, att_t, branch, misc, sums0, sums1, feed_got, after=()):
    rows = pl.BlockSpec((192, OWN), lambda i, place: (i, 0))
    return call(
        up_kernel,
        "up_units",
        place,
        [
            (normed_t, rows), plain(normed_got), plain(inner[0]), plain(inner[1]), plain(got[0]), plain(got[1]),
            (att_t, pl.BlockSpec((192, 512), lambda i, place: (i, 0))),
            plain(branch), plain(misc), plain(sums0), plain(sums1), plain(feed_got),
        ],
        [made((DOWN_SENT + 4 * UP_ROWS, WIDTH), LOW)] * 2 + unit_outputs(UP_ROWS, WIDTH)[:2],
        scratch=[pltpu.VMEM((2, 2, UP_ROWS, WIDTH), LOW), pltpu.VMEM((WIDTH, OWN), LOW)],
        grid=(4,),
        after=after,
        work=cost(0.9e9, 5e6),
    )


def attention_back_kernel(
    place, own_lengths, peer_lengths, q, k0, k1, v0, v1, log_total, att, back0, misc,
    dq_out, dk_out, dv_out, bias,
):
    bases = first_positions(place)
    ends = pair_ends(place, own_lengths, peer_lengths)
    query_ids = [pairs_along(base, ends, 1)[0:1] for base in bases[:4]]
    for j in range(8):
        key_ids = pairs_along(bases[j], ends, 0)
        for i in range(4):
            bias[pl.ds(j * BLOCK, BLOCK), pl.ds(i * BLOCK, BLOCK)] = jnp.where(
                key_ids == query_ids[i], 0.0, NEGATIVE
            )

    def one_pair(pair, carry):
        lanes = pl.ds(pl.multiple_of(pair * LANES, LANES), LANES)
        keys = jnp.concatenate([k0[:, lanes], k1[:, lanes]], axis=0)
        values = jnp.concatenate([v0[:, lanes], v1[:, lanes]], axis=0)
        keys_t = turned(keys)
        key_grad = jnp.zeros((1024, LANES), FLOAT)
        value_grad = jnp.zeros((1024, LANES), FLOAT)
        far = pl.ds(pl.multiple_of(HALF + pair * LANES, LANES), LANES)
        for part, back in ((0, back0[:, lanes]), (1, misc[0:OWN, far])):
            rows = pl.ds(part * OWN, OWN)
            product = jnp.transpose(back.astype(FLOAT) * att[rows, lanes].astype(FLOAT))
            delta = jnp.concatenate([column_sum(product[0:HEAD_DIM]), column_sum(product[HEAD_DIM:])], axis=1)
            logs = jnp.concatenate(
                [log_total[pl.ds(2 * pair, 1), rows], log_total[pl.ds(2 * pair + 1, 1), rows]], axis=1
            )
            chosen = jnp.concatenate(halves_of(q[rows, lanes]), axis=0)
            grads = jnp.concatenate(halves_of(back), axis=0)
            mask = bias[:, rows]
            weights = jnp.exp(dot_nt(keys, chosen) + jnp.concatenate([mask, mask], axis=1) - logs)
            score_grad = (weights * (dot_nt(values, grads) - delta)).astype(LOW)
            value_grad = value_grad + dot(weights.astype(LOW), grads)
            key_grad = key_grad + dot(score_grad, chosen)
            both = dot(keys_t, score_grad)
            query_grad_t = jnp.concatenate([both[0:HEAD_DIM, 0:OWN], both[HEAD_DIM:, OWN:]], axis=0)
            dq_out[rows, lanes] = (jnp.transpose(query_grad_t) * HEAD_DIM**-0.5).astype(LOW)
        dk_out[:, lanes] = key_grad.astype(LOW)
        dv_out[:, lanes] = value_grad.astype(LOW)
        return carry

    lax.fori_loop(0, PAIRS_OF_HEADS, one_pair, 0)


def attention_back(place, lengths, q, keys, values, log_total, att, back_own, misc, after=()):
    return call(
        attention_back_kernel,
        "attention_back",
        place,
        [plain(array) for array in (q, *keys, *values, log_total, att, back_own, misc)],
        [made((512, HALF), LOW), made((1024, HALF), LOW), made((1024, HALF), LOW)],
        scratch=[pltpu.VMEM((1024, 512), FLOAT)],
        scalars=lengths,
        after=after,
        work=cost(7e9, 6e6, 3e6),
    )


def token_kernel(place, dq, dk, dv, columns, own, own_send, far, far_send):
    for part, target in enumerate((own, own_send, far, far_send)):
        rows = pl.ds(part * OWN, OWN)
        total = dot_nt(dk[rows, :], columns[1]) + dot_nt(dv[rows, :], columns[2])
        if part < 2:
            total = total + dot_nt(dq[rows, :], columns[0])
        target[...] = total.astype(LOW)


def token_parts(place, dq, dk, dv, columns, after=()):
    return call(
        token_kernel,
        "token_parts",
        place,
        [plain(dq), plain(dk), plain(dv), plain(columns)],
        [made((OWN, WIDTH), LOW)] * 4,
        after=after,
        work=cost(1.5e9, 5e6),
    )


def token_last_kernel(place, own, own_got, across, first_grad, token0, token1):
    total = own[...].astype(FLOAT) + own_got[...].astype(FLOAT) + across[8 * JOINT_SECOND :].astype(FLOAT) + first_grad[...]
    total = total.astype(LOW)
    token0[...] = total[0:BLOCK]
    token1[...] = total[BLOCK:]


def token_last(place, arrays, after=()):
    return call(
        token_last_kernel,
        "token_last",
        place,
        [plain(array) for array in arrays],
        [made((BLOCK, WIDTH), LOW)] * 2,
        after=after,
        work=cost(1e6, 2e6),
    )


def back_rows_kernel(place, done0, done1, back0, back1, outputs, token_grad):
    odd = place[0] % 2
    outputs[odd] = done0[...]
    outputs[1 - odd] = done1[...]
    token_grad[odd] = back0[...].astype(FLOAT)
    token_grad[1 - odd] = back1[...].astype(FLOAT)


def back_rows(place, done, back, after=()):
    return call(
        back_rows_kernel,
        "back_rows",
        place,
        [plain(array) for array in (*done, *back)],
        [made((2, BLOCK, WIDTH), LOW), made((2, BLOCK, WIDTH), FLOAT)],
        after=after,
        work=cost(1e6, 2e6),
    )


def joint_kernel(
    place, t0, t1, t2, t3, t4, t5, t6, t7, dq, dk, dv, far, far_got, px_send, px, qy_send, qy, tokens_t, units
):
    y, x = place[1], place[2]
    qy_send[pl.ds(8 * JOINT_SECOND, OWN), :] = added(far[...], far_got[...])
    for index, block in enumerate((t0, t1, t2, t3, t4, t5, t6, t7)):
        tokens_t[:, pl.ds(index * BLOCK, BLOCK)] = jnp.transpose(block[...].astype(FLOAT)).astype(LOW)
    biases = jnp.concatenate([column_sum(dq[...].astype(FLOAT)), column_sum(dv[...].astype(FLOAT))], axis=1)
    biases = jnp.concatenate([biases, jnp.zeros((7, WIDTH), FLOAT)], axis=0)
    for z in range(4):
        rows = pl.ds(z * 192, 192)
        query = dot(tokens_t[rows, 0:512], dq[...])
        key = dot(tokens_t[rows, :], dk[...])
        value = dot(tokens_t[rows, :], dv[...])
        for line in range(2):
            for side in range(2):
                at = line * 96 + side * 48
                units[line, side, 0:JOINT_FIRST] = jnp.concatenate(
                    [query[at : at + 48], key[at : at + 48]], axis=1
                ).astype(LOW)
                rest = jnp.concatenate([value[at : at + 24], value[at + 24 : at + 48]], axis=1)
                units[line, side, JOINT_FIRST:] = jnp.concatenate([rest, biases], axis=0).astype(LOW)
        for line in range(2):
            px[z, line] = units[line, x, 0:JOINT_FIRST]
            px_send[z, line] = units[line, 1 - x, 0:JOINT_FIRST]
        for side in range(2):
            qy[z, side] = units[y, side, JOINT_FIRST:]
            qy_send[pl.ds((z * 2 + side) * JOINT_SECOND, JOINT_SECOND), :] = units[1 - y, side, JOINT_FIRST:]


def joint_units(place, blocks, dq, dk, dv, far, far_got, after=()):
    first, second = made((4, 2, JOINT_FIRST, WIDTH), LOW), made((4, 2, JOINT_SECOND, WIDTH), LOW)
    return call(
        joint_kernel,
        "joint_units",
        place,
        [plain(array) for array in (*blocks, dq, dk, dv, far, far_got)],
        [first, first, made((8 * JOINT_SECOND + OWN, WIDTH), LOW), second],
        scratch=[pltpu.VMEM((WIDTH, 1024), LOW), pltpu.VMEM((2, 2, JOINT_ROWS, WIDTH), LOW)],
        after=after,
        work=cost(1.5e9, 6e6),
    )


def added(left, right):
    return (left.astype(FLOAT) + right.astype(FLOAT)).astype(LOW)


def down_pair_kernel(place, px, px_got, qy, qy_got, x_in, y_in, x_send, y_send, p, q):
    y, x = place[1], place[2]
    p[0] = added(px[0, y], px_got[0, y])
    y_send[...] = added(px[0, 1 - y], px_got[0, 1 - y])
    q[0] = added(qy[0, x], qy_got[0, x])
    x_send[...] = added(qy[0, 1 - x], qy_got[0, 1 - x])


def down_pair_stage(place, arrays, x_send, y_send, after=()):
    half = DOWN_ROWS // 2
    block = pl.BlockSpec((1, 2, half, WIDTH), lambda i, place: (i, 0, 0, 0))
    sent = (x_send.shape, LOW, pl.BlockSpec((half, WIDTH), lambda i, place: (i, 0)))
    kept = ((4, half, WIDTH), LOW, pl.BlockSpec((1, half, WIDTH), lambda i, place: (i, 0, 0)))
    anywhere = pl.BlockSpec(memory_space=pl.ANY)
    return call(
        down_pair_kernel,
        "down_pair_stage",
        place,
        [(array, block) for array in arrays] + [(x_send, anywhere), (y_send, anywhere)],
        [sent, sent, kept, kept],
        grid=(4,),
        after=after,
        work=cost(1e6, 1e7),
        aliases=((4, 0), (5, 1)),
    )


def second_kernel(
    place, x_got, y_got, px, qy, down_p, down_q, x_send, y_send, p, q, down_send, down_keep
):
    z_here, y, x = place[0], place[1], place[2]
    half = UP_ROWS // 2
    for z in range(4):
        for got, have, own, keep, send in ((x_got, px, y, p, y_send), (y_got, qy, x, q, x_send)):
            at = DOWN_SENT + z * UP_ROWS
            mine = pl.ds(pl.multiple_of(at + own * half, half), half)
            other = pl.ds(pl.multiple_of(at + (1 - own) * half, half), half)
            keep[z] = added(have[z, own], got[mine, :])
            send[pl.ds(z * half, half), :] = added(have[z, 1 - own], got[other, :])
    low = z_here % 2
    small = DOWN_ROWS // 2
    for target, parity in ((down_keep, low), (down_send, 1 - low)):
        for high in range(2):
            index = 2 * high + parity
            rows = pl.ds(pl.multiple_of(index * small, small), small)
            target[high, 0:small] = added(down_p[index], y_got[rows, :])
            target[high, small:] = added(down_q[index], x_got[rows, :])


def second_stage(place, arrays, after=()):
    kept = made((4, UP_ROWS // 2, WIDTH), LOW)
    down = made((2, DOWN_ROWS, WIDTH), LOW)
    return call(
        second_kernel,
        "second_stage",
        place,
        [plain(array) for array in arrays],
        [made((OWN, WIDTH), LOW), made((OWN, WIDTH), LOW), kept, kept, down, down],
        after=after,
        work=cost(1e6, 1e7),
    )


def joint_pair_kernel(place, px, px_got, qy, qy_got, x_send, y_send, p, q):
    y, x = place[1], place[2]
    for z in range(4):
        p[z] = added(px[z, y], px_got[z, y])
        y_send[z] = added(px[z, 1 - y], px_got[z, 1 - y])


        def from_y(side):
            return qy_got[pl.ds(pl.multiple_of((z * 2 + side) * JOINT_SECOND, 32), JOINT_SECOND), :]

        q[z] = added(qy[z, x], from_y(x))
        x_send[z] = added(qy[z, 1 - x], from_y(1 - x))


def joint_pair_stage(place, arrays, after=()):
    first, second = made((4, JOINT_FIRST, WIDTH), LOW), made((4, JOINT_SECOND, WIDTH), LOW)
    return call(
        joint_pair_kernel,
        "joint_pair_stage",
        place,
        [plain(array) for array in arrays],
        [second, first, first, second],
        after=after,
        work=cost(1e6, 1e7),
    )


def up_line_kernel(place, x_got, y_got, p, q, down_two, down_got, send, keep, down_send, down_keep):
    low, high_here = place[0] % 2, place[0] // 2
    half = UP_ROWS // 2
    for target, parity in ((keep, low), (send, 1 - low)):
        for high in range(2):
            index = 2 * high + parity
            rows = pl.ds(pl.multiple_of(index * half, half), half)
            target[high, 0:half] = added(p[index], y_got[rows, :])
            target[high, half:] = added(q[index], x_got[rows, :])
    down_keep[...] = added(down_two[high_here], down_got[high_here])
    down_send[...] = added(down_two[1 - high_here], down_got[1 - high_here])


def up_line_stage(place, arrays, after=()):
    return call(
        up_line_kernel,
        "up_line_stage",
        place,
        [plain(array) for array in arrays],
        [made((2, UP_ROWS, WIDTH), LOW)] * 2 + [made((DOWN_ROWS, WIDTH), LOW)] * 2,
        after=after,
        work=cost(1e6, 1e7),
    )


def joint_line_kernel(place, x_got, y_got, p, q, keep, one, two, three):
    low, high = place[0] % 2, place[0] // 2
    for target, index in (
        (keep, 2 * high + low), (one, 2 * high + 1 - low), (two, 2 * (1 - high) + low), (three, 2 * (1 - high) + 1 - low)
    ):
        target[0:JOINT_FIRST] = added(p[index], y_got[index])
        target[JOINT_FIRST:] = added(q[index], x_got[index])


def joint_line_stage(place, arrays, after=()):
    return call(
        joint_line_kernel,
        "joint_line_stage",
        place,
        [plain(array) for array in arrays],
        [made((JOINT_ROWS, WIDTH), LOW)] * 4,
        after=after,
        work=cost(1e6, 1e6),
    )


def end_stage_kernel(place, keep_two, got, send, keep):
    high = place[0] // 2
    keep[...] = added(keep_two[high], got[high])
    send[...] = added(keep_two[1 - high], got[1 - high])


def end_stage(place, keep_two, got, after=()):
    return call(
        end_stage_kernel,
        "end_stage",
        place,
        [plain(keep_two), plain(got)],
        [made(keep_two.shape[1:], LOW)] * 2,
        after=after,
        work=cost(1e6, 1e6),
    )


def joint_sum_kernel(place, first, second, third, fourth, out):
    total = (first[...].astype(FLOAT) + second[...].astype(FLOAT)) + (third[...].astype(FLOAT) + fourth[...].astype(FLOAT))
    out[...] = total.astype(LOW)


def joint_sum(place, arrays, after=()):
    results, mark = call(
        joint_sum_kernel,
        "joint_sum",
        place,
        [plain(array) for array in arrays],
        [made((JOINT_ROWS, WIDTH), LOW)],
        after=after,
        work=cost(1e6, 1e6),
    )
    return results[0], mark


def last_sum_kernel(place, *refs):
    count = len(refs) // 3
    for index in range(count):
        refs[2 * count + index][...] = added(refs[2 * index][...], refs[2 * index + 1][...])


def last_sum(place, pairs, after=()):
    return call(
        last_sum_kernel,
        "last_sum",
        place,
        [plain(array) for pair in pairs for array in pair],
        [made(pair[0].shape, LOW) for pair in pairs],
        after=after,
        work=cost(1e6, 1e6),
    )


def gathered(unit, mark=None):
    across = x_swap(unit)
    if mark is not None:
        across, mark = lax.optimization_barrier((across, mark))
    return unit, core_swap(unit), across, core_swap(across)


def quarters(place):
    x, c = place[2], place[3]
    return (x, c), (x, 1 - c), (1 - x, c), (1 - x, 1 - c)


def line_shift(place):
    seq = place[0] * 2 + place[1]
    return lax.rem(WIDTH - seq * 96, WIDTH)


def dense_out_kernel(
    place, d0, d1, d2, d3, u0, u1, u2, u3,
    down, up, out, gain2, shift2, down_bias, gain1, shift1, out_bias, up_bias, heads, tails,
):
    for down_unit, unit, (x, c) in zip((d0, d1, d2, d3), (u0, u1, u2, u3), quarters(place)):
        quarter = 2 * x + c
        down[pl.ds(pl.multiple_of(quarter * DOWN_ROWS, 32), DOWN_ROWS), :] = down_unit[...].astype(FLOAT)
        up[:, pl.ds(pl.multiple_of(quarter * WIDTH, LANES), WIDTH)] = unit[0:96, :].astype(FLOAT)
        rest = unit[96:128, :].astype(FLOAT)
        lanes = pl.ds(pl.multiple_of(c * HALF, LANES), HALF)
        out[pl.ds(pl.multiple_of(x * 48, 8), 24), lanes] = rest[0:24, 0:HALF]
        out[pl.ds(pl.multiple_of(x * 48 + 24, 8), 24), lanes] = rest[0:24, HALF:]

        @pl.when(x == 0)
        def _(rest=rest):
            heads[...] = rest[24:32]

        @pl.when(x == 1)
        def _(rest=rest):
            tails[...] = rest[24:32]

    seq = place[0] * 2 + place[1]
    shift = line_shift(place)
    head = pltpu.roll(heads[...], shift, 1)
    gain2[...] = head[0:1, 0:96]
    shift2[...] = head[1:2, 0:96]
    down_bias[...] = head[2:3, 0:96]
    tail = pltpu.roll(tails[...], shift, 1)
    gain1[...] = tail[0:1, 0:96]
    shift1[...] = tail[1:2, 0:96]
    out_bias[...] = tail[2:3, 0:96]
    wide = tails[pl.ds(4 + seq // 2, 1), :]
    up_bias[...] = jnp.where(seq % 2 == 0, wide[:, 0:HALF], wide[:, HALF:])


def dense_outputs(place, units, after=()):
    results, mark = call(
        dense_out_kernel,
        "dense_outputs",
        place,
        [plain(unit) for unit in units],
        [made((4 * DOWN_ROWS, WIDTH), FLOAT), made((96, FF), FLOAT), made((96, WIDTH), FLOAT)]
        + [made((1, 96), FLOAT)] * 6
        + [made((1, HALF), FLOAT)],
        scratch=[pltpu.VMEM((8, WIDTH), FLOAT)] * 2,
        after=after,
        work=cost(1e6, 3e6),
    )
    return (*results[:3], *(vector.reshape(-1) for vector in results[3:])), mark


def joint_out_kernel(place, u0, u1, u2, u3, joint, query_bias, value_bias, sums):
    for unit, (x, c) in zip((u0, u1, u2, u3), quarters(place)):

        def lanes(kind):
            return pl.ds(pl.multiple_of(kind * WIDTH + c * HALF, LANES), HALF)

        first = unit[0:JOINT_FIRST].astype(FLOAT)
        rest = unit[JOINT_FIRST:].astype(FLOAT)
        rows = pl.ds(pl.multiple_of(x * 48, 16), 48)
        joint[rows, lanes(0)] = first[:, 0:HALF]
        joint[rows, lanes(1)] = first[:, HALF:]
        joint[pl.ds(pl.multiple_of(x * 48, 8), 24), lanes(2)] = rest[0:24, 0:HALF]
        joint[pl.ds(pl.multiple_of(x * 48 + 24, 8), 24), lanes(2)] = rest[0:24, HALF:]

        @pl.when(x == 0)
        def _(rest=rest, c=c):
            half = pl.ds(pl.multiple_of(c * HALF, LANES), HALF)
            sums[0:1, half] = rest[24:25, 0:HALF]
            sums[1:2, half] = rest[24:25, HALF:]

    turned = pltpu.roll(sums[...], line_shift(place), 1)
    query_bias[...] = turned[0:1, 0:96]
    value_bias[...] = turned[1:2, 0:96]


def joint_outputs(place, units, after=()):
    results, mark = call(
        joint_out_kernel,
        "joint_outputs",
        place,
        [plain(unit) for unit in units],
        [made((96, 3 * WIDTH), FLOAT), made((1, 96), FLOAT), made((1, 96), FLOAT)],
        scratch=[pltpu.VMEM((8, WIDTH), FLOAT)],
        after=after,
        work=cost(1e6, 2e6),
    )
    return (results[0], results[1].reshape(-1), results[2].reshape(-1)), mark


def row_body(
    tokens,
    pair_lengths,
    joint_weight,
    query_bias,
    value_bias,
    out_weight,
    out_bias,
    first_gain,
    first_shift,
    up_weight,
    up_bias,
    down_weight,
    down_bias,
    second_gain,
    second_shift,
    cotangent,
):
    seq, rows = lax.axis_index("seq"), lax.axis_index("rows")
    z, y, x, c = seq // 2, seq % 2, rows // 2, rows % 2
    place = jnp.stack([z, y, x, c]).astype(jnp.int32)
    odd = z % 2
    weights = {
        "out": out_weight, "out_bias": out_bias, "gain1": first_gain, "shift1": first_shift,
        "up": up_weight, "up_bias": up_bias, "down": down_weight, "down_bias": down_bias,
        "gain2": second_gain, "shift2": second_shift,
    }

    def local_row(array, index):
        return lax.dynamic_index_in_dim(array, index, 0, keepdims=False)

    columns, query_row, value_row = own_columns(place, joint_weight, query_bias, value_bias)
    lengths = (pair_lengths, core_swap(pair_lengths))
    own = [row_swap(local_row(tokens, odd), 0), row_swap(local_row(tokens, 1 - odd), 1)]
    *own, columns, lengths = lax.optimization_barrier((*own, columns, lengths))
    across = [y_swap(block) for block in own]
    here = own + [core_swap(block) for block in own]
    (q, k_here, v_here, summed, stats), mark = first_attention(
        place, lengths, here, columns, query_row, value_row
    )
    padding = jnp.zeros((16, WIDTH), LOW)
    cotangents = [
        row_swap(jnp.concatenate([local_row(cotangent, index), padding], axis=0), second)
        for second, index in ((0, odd), (1, 1 - odd))
    ]
    across[0], across[1], mark = lax.optimization_barrier((across[0], across[1], mark))
    there = across + [core_swap(block) for block in across]
    blocks = here + there
    (att, k_there, v_there, log_total), mark = attention(
        place, lengths, there, columns, value_row, q, summed, stats, (mark,)
    )
    att, *cotangents = lax.optimization_barrier((att, *cotangents))
    att_got = core_swap(att)
    results, mark = forward(place, att, att_got, own, cotangents, weights, (mark,))
    (
        result0, result1, feed, second_grad, act, act_send, slope, unit1, inverse1, normed, normed_t, att_t, sums0
    ) = results
    act_got, feed_got, normed_got = core_swap(act_send), core_swap(feed), core_swap(normed)
    done = (row_swap(result0, 0), row_swap(result1, 1))
    (px_send, px, qy_send, qy), mark = down_units(place, act, act_got, feed, feed_got, (mark,))
    down_pair = (px, x_swap(px_send), qy, y_swap(qy_send))
    results, mark = backward(place, feed, slope, second_grad, unit1, inverse1, weights, (mark, normed_got))
    inner0, inner1, send0, send1, first_grad, branch_own, back_own, misc_send, sums1 = results
    got, misc = (core_swap(send0), core_swap(send1)), core_swap(misc_send)
    (x_send, y_send, px, qy), mark = up_units(
        place, normed_t, normed_got, (inner0, inner1), got, att_t, branch_own, misc, sums0, sums1, feed_got, (mark,)
    )
    (x_send, y_send, down_p, down_q), mark = down_pair_stage(place, down_pair, x_send, y_send, (mark,))
    x_got, y_got = x_swap(x_send), y_swap(y_send)
    (dq, dk, dv), mark = attention_back(
        place, lengths, q, (k_here, k_there), (v_here, v_there), log_total, att, back_own, misc, (mark,)
    )
    (token_own, own_send, token_far, far_send), mark = token_parts(place, dq, dk, dv, columns, (mark, *done))
    own_got, far_got = core_swap(own_send), core_swap(far_send)
    (px_send, joint_px, qy_send, joint_qy), mark = joint_units(
        place, blocks, dq, dk, dv, token_far, far_got, (mark,)
    )
    (x_send, y_send, p, q_, down_send, down_two), mark = second_stage(
        place, (x_got, y_got, px, qy, down_p, down_q), (mark, own_got)
    )
    x_got, y_got, down_got = x_swap(x_send), y_swap(y_send), z_swap(down_send, 1)
    px_send, qy_send, mark = lax.optimization_barrier((px_send, qy_send, mark))
    across = y_swap(qy_send)
    joint_pair = (joint_px, x_swap(px_send), joint_qy, across)
    (up_send, up_two, down_send, down_keep), mark = up_line_stage(
        place, (x_got, y_got, p, q_, down_two, down_got), (mark,)
    )
    up_got, down_got = z_swap(up_send, 1), z_swap(down_send, 2)
    (up_send, up_keep), mark = end_stage(place, up_two, up_got, (mark, down_got))
    up_got = z_swap(up_send, 2)
    (down_unit,), mark = last_sum(place, ((down_keep, down_got),), (mark,))
    down_across = x_swap(down_unit)
    (x_send, y_send, joint_p, joint_q), mark = joint_pair_stage(place, joint_pair, (mark,))
    joint_x_got, joint_y_got = x_swap(x_send), y_swap(y_send)
    down_own, up_got = lax.optimization_barrier((down_unit, up_got))
    down_all = (down_unit, core_swap(down_own), down_across, core_swap(down_across))
    (token0, token1), mark = token_last(place, (token_own, own_got, across, first_grad), (mark,))
    back = (row_swap(token0, 0), row_swap(token1, 1))
    (up_unit,), mark = last_sum(place, ((up_keep, up_got),), (mark,))
    up_all = gathered(up_unit)
    (keep, one, two, three), mark = joint_line_stage(
        place, (joint_x_got, joint_y_got, joint_p, joint_q), (mark, *down_all[1:])
    )
    joint_last = (keep, z_swap(one, 1), z_swap(two, 2), z_swap(three, 3))
    joint_unit, mark = joint_sum(place, joint_last, (mark,))
    joint_across = x_swap(joint_unit)
    joint_across, first_back = lax.optimization_barrier((joint_across, back[0]))
    joint_all = (joint_unit, core_swap(joint_unit), joint_across, core_swap(joint_across))
    (
        down_grad, up_grad, out_grad, second_gain_grad, second_shift_grad, down_bias_grad, first_gain_grad,
        first_shift_grad, out_bias_grad, up_bias_grad,
    ), mark = dense_outputs(place, (*down_all, *up_all), (mark,))
    (joint_grad, query_bias_grad, value_bias_grad), mark = joint_outputs(place, joint_all, (mark,))
    (outputs, token_grad), mark = back_rows(place, done, (first_back, back[1]), (mark,))
    return (
        outputs,
        token_grad,
        joint_grad,
        query_bias_grad,
        value_bias_grad,
        out_grad,
        out_bias_grad,
        first_gain_grad,
        first_shift_grad,
        up_grad,
        up_bias_grad,
        down_grad,
        down_bias_grad,
        second_gain_grad,
        second_shift_grad,
    )


def body(tokens, *others):
    if (lax.axis_size("seq"), lax.axis_size("rows")) == (8, 4) and tokens.shape == (2, BLOCK, WIDTH):
        return row_body(tokens, *others)
    return general_body(tokens, *others)


def solution(mesh):
    placed = (
        P("rows", "seq", None),
        P("rows", None),
        P(),
        P(),
        P(),
        P(),
        P(),
        P(),
        P(),
        P(),
        P(),
        P(),
        P(),
        P(),
        P(),
        P("rows", "seq", None),
    )
    return jax.shard_map(
        body,
        mesh=mesh,
        in_specs=placed,
        out_specs=(
            P("rows", "seq", None),
            P("rows", "seq", None),
            P("seq", None),
            P("seq"),
            P("seq"),
            P("seq", None),
            P("seq"),
            P("seq"),
            P("seq"),
            P("seq", None),
            P("seq"),
            P("seq", None),
            P("seq"),
            P("seq"),
            P("seq"),
        ),
        check_vma=False,
    )
```

```python
import functools
import math

import jax
import jax.numpy as jnp
from jax import lax
from jax.experimental import pallas as pl
from jax.experimental.pallas import tpu as pltpu
from jax.sharding import PartitionSpec as P

HEADS = 12
HEAD_DIM = 64


NEGATIVE = -1e30
EPSILON = 1e-12


def from_behind(value, axis, steps):
    count = lax.axis_size(axis)
    pairs = [(source, (source + steps) % count) for source in range(count)]
    return lax.ppermute(value, axis, pairs)


def layer_norm(value, gain, shift):
    mean = jnp.mean(value, axis=-1, keepdims=True)
    centred = value - mean
    spread = jnp.mean(centred * centred, axis=-1, keepdims=True)
    return centred * lax.rsqrt(spread + EPSILON) * gain + shift


def gelu_exact(value):
    return jax.nn.gelu(value, approximate=False)


def pair_index(positions, ends):
    return jnp.sum((positions[None, :, None] >= ends[:, None, :]).astype(jnp.int32), axis=2)


def split_heads(array):
    return array.reshape(array.shape[0], array.shape[1], HEADS, HEAD_DIM)


def online_block(state, query_heads, query_pairs, key_block, value_block, key_pairs):
    highest, total, summed = state
    scores = jnp.einsum(
        "rqhd,rkhd->rhqk", query_heads, split_heads(key_block), preferred_element_type=jnp.float32
    ) * HEAD_DIM ** (-0.5)
    allowed = query_pairs[:, None, :, None] == key_pairs[:, None, None, :]
    masked = jnp.where(allowed, scores, NEGATIVE)
    new_high = jnp.maximum(highest, jnp.max(masked, axis=3))
    weights = jnp.where(allowed, jnp.exp(masked - new_high[..., None]), 0.0)
    factor = jnp.exp(highest - new_high)
    total = total * factor + jnp.sum(weights, axis=3)
    summed = summed * jnp.swapaxes(factor, 1, 2)[..., None] + jnp.einsum(
        "rhqk,rkhd->rqhd",
        weights.astype(jnp.bfloat16),
        split_heads(value_block),
        preferred_element_type=jnp.float32,
    )
    return (new_high, total, summed)


def tile_terms(queries, out_grad, log_total, delta, query_pairs, keys, values, key_pairs):
    scale = HEAD_DIM ** (-0.5)
    query_heads = split_heads(queries)
    grad_heads = split_heads(out_grad)
    key_heads = split_heads(keys)
    value_heads = split_heads(values)
    scores = (
        jnp.einsum("rqhd,rkhd->rhqk", query_heads, key_heads, preferred_element_type=jnp.float32)
        * scale
    )
    allowed = query_pairs[:, None, :, None] == key_pairs[:, None, None, :]
    weights = jnp.where(
        allowed, jnp.exp(jnp.where(allowed, scores, NEGATIVE) - log_total[..., None]), 0.0
    )
    weight_grad = jnp.einsum(
        "rqhd,rkhd->rhqk", grad_heads, value_heads, preferred_element_type=jnp.float32
    )
    score_grad = (weights * (weight_grad - delta[..., None])).astype(jnp.bfloat16)
    query_term = (
        jnp.einsum("rhqk,rkhd->rqhd", score_grad, key_heads, preferred_element_type=jnp.float32)
        * scale
    )
    key_term = (
        jnp.einsum("rhqk,rqhd->rkhd", score_grad, query_heads, preferred_element_type=jnp.float32)
        * scale
    )
    value_term = jnp.einsum(
        "rhqk,rqhd->rkhd",
        weights.astype(jnp.bfloat16),
        grad_heads,
        preferred_element_type=jnp.float32,
    )
    return (
        query_term.reshape(queries.shape),
        key_term.reshape(keys.shape),
        value_term.reshape(values.shape),
    )


def general_body(
    tokens,
    pair_lengths,
    joint_weight,
    query_bias,
    value_bias,
    out_weight,
    out_bias,
    first_gain,
    first_shift,
    up_weight,
    up_bias,
    down_weight,
    down_bias,
    second_gain,
    second_shift,
    cotangent,
):
    rows_here, seq_here, width = tokens.shape
    count = lax.axis_size("seq")
    cycle_index = lax.axis_index("seq")
    ends = jnp.cumsum(pair_lengths, axis=1)
    offsets = jnp.arange(seq_here, dtype=jnp.int32)
    own_pairs = pair_index(cycle_index * seq_here + offsets, ends)
    block_shape = (rows_here, seq_here, width)
    flat = tokens.reshape(rows_here * seq_here, width)
    projected = jnp.dot(flat, joint_weight, preferred_element_type=jnp.float32)
    queries = (projected[:, :width] + query_bias).astype(jnp.bfloat16).reshape(block_shape)
    keys = projected[:, width : 2 * width].astype(jnp.bfloat16).reshape(block_shape)
    values = (projected[:, 2 * width :] + value_bias).astype(jnp.bfloat16).reshape(block_shape)
    query_heads = split_heads(queries)
    initial = (
        jnp.full((rows_here, HEADS, seq_here), NEGATIVE, jnp.float32),
        jnp.zeros((rows_here, HEADS, seq_here), jnp.float32),
        jnp.zeros((rows_here, seq_here, HEADS, HEAD_DIM), jnp.float32),
    )
    key_piece = lax.all_gather(keys, "seq", axis=1, tiled=True)
    value_piece = lax.all_gather(values, "seq", axis=1, tiled=True)
    length = key_piece.shape[1]
    block = math.gcd(length, seq_here)

    def one_block(index, inner_state):
        first = index * block
        key_block = lax.dynamic_slice_in_dim(key_piece, first, block, 1)
        value_block = lax.dynamic_slice_in_dim(value_piece, first, block, 1)
        key_pairs = pair_index(first + jnp.arange(block, dtype=jnp.int32), ends)
        return online_block(inner_state, query_heads, own_pairs, key_block, value_block, key_pairs)

    highest, total, summed = lax.fori_loop(0, length // block, one_block, initial)
    log_total = highest + jnp.log(total)
    attended = (
        (summed / jnp.swapaxes(total, 1, 2)[..., None]).astype(jnp.bfloat16).reshape(flat.shape)
    )
    branch = jnp.dot(attended, out_weight, preferred_element_type=jnp.float32) + out_bias
    first_sum = flat.astype(jnp.float32) + branch
    normed, first_back = jax.vjp(layer_norm, first_sum, first_gain, first_shift)
    normed_low = normed.astype(jnp.bfloat16)
    inner = jnp.dot(normed_low, up_weight, preferred_element_type=jnp.float32) + up_bias
    activated_full, gelu_back = jax.vjp(gelu_exact, inner)
    activated = activated_full.astype(jnp.bfloat16)
    feed = jnp.dot(activated, down_weight, preferred_element_type=jnp.float32) + down_bias
    second_sum = normed + feed
    result, second_back = jax.vjp(layer_norm, second_sum, second_gain, second_shift)
    outputs = result.astype(jnp.bfloat16).reshape(tokens.shape)
    second_grad, second_gain_grad, second_shift_grad = second_back(
        cotangent.astype(jnp.float32).reshape(flat.shape)
    )
    feed_grad = second_grad.astype(jnp.bfloat16)
    down_grad = jnp.einsum("ti,tj->ij", activated, feed_grad, preferred_element_type=jnp.float32)
    down_bias_grad = jnp.sum(feed_grad.astype(jnp.float32), axis=0)
    activated_grad = jnp.einsum(
        "tj,ij->ti", feed_grad, down_weight, preferred_element_type=jnp.float32
    )
    inner_grad = gelu_back(activated_grad)[0].astype(jnp.bfloat16)
    up_grad = jnp.einsum("ti,tj->ij", normed_low, inner_grad, preferred_element_type=jnp.float32)
    up_bias_grad = jnp.sum(inner_grad.astype(jnp.float32), axis=0)
    normed_grad = second_grad + jnp.einsum(
        "tj,ij->ti", inner_grad, up_weight, preferred_element_type=jnp.float32
    )
    first_grad, first_gain_grad, first_shift_grad = first_back(normed_grad)
    branch_grad = first_grad.astype(jnp.bfloat16)
    out_grad = jnp.einsum("ti,tj->ij", attended, branch_grad, preferred_element_type=jnp.float32)
    out_bias_grad = jnp.sum(branch_grad.astype(jnp.float32), axis=0)
    attended_grad = jnp.einsum(
        "tj,ij->ti", branch_grad, out_weight, preferred_element_type=jnp.float32
    ).astype(jnp.bfloat16)
    delta = jnp.sum(
        (attended_grad.astype(jnp.float32) * attended.astype(jnp.float32)).reshape(
            rows_here, seq_here, HEADS, HEAD_DIM
        ),
        axis=3,
    )
    delta = jnp.swapaxes(delta, 1, 2)
    attended_grad = attended_grad.reshape(block_shape)
    zeros_block = jnp.zeros(block_shape, jnp.float32)

    def send_key_sums(sums):
        return (
            from_behind(sums[0].astype(jnp.bfloat16), "seq", 1).astype(jnp.float32),
            from_behind(sums[1].astype(jnp.bfloat16), "seq", 1).astype(jnp.float32),
        )

    def key_work(turn, pair_block, sums, query_sum):
        anchor = (cycle_index - turn) % count
        key_pairs = pair_index(anchor * seq_here + offsets, ends)
        query_term, key_term, value_term = tile_terms(
            queries,
            attended_grad,
            log_total,
            delta,
            own_pairs,
            pair_block[0],
            pair_block[1],
            key_pairs,
        )
        return ((sums[0] + key_term, sums[1] + value_term), query_sum + query_term)

    def key_turn(turn, state):
        pair_block, sums, query_sum = state
        sums, query_sum = key_work(turn, pair_block, sums, query_sum)
        sums = send_key_sums(sums)
        pair_block = from_behind((pair_block[0], pair_block[1]), "seq", 1)
        return (pair_block, sums, query_sum)

    pair_block, sums, query_sum = lax.fori_loop(
        0, count - 1, key_turn, ((keys, values), (zeros_block, zeros_block), zeros_block)
    )
    sums, query_sum = key_work(count - 1, pair_block, sums, query_sum)
    key_sum, value_sum = send_key_sums(sums)
    query_low = query_sum.astype(jnp.bfloat16).reshape(flat.shape)
    key_low = key_sum.astype(jnp.bfloat16).reshape(flat.shape)
    value_low = value_sum.astype(jnp.bfloat16).reshape(flat.shape)
    joint_low = jnp.concatenate([query_low, key_low, value_low], axis=1)
    joint_grad = jnp.einsum("ti,tj->ij", flat, joint_low, preferred_element_type=jnp.float32)
    query_bias_grad = jnp.sum(query_low.astype(jnp.float32), axis=0)
    value_bias_grad = jnp.sum(value_low.astype(jnp.float32), axis=0)
    token_grad = first_grad + jnp.einsum(
        "tj,ij->ti", joint_low, joint_weight, preferred_element_type=jnp.float32
    )
    gradients = (
        joint_grad,
        query_bias_grad,
        value_bias_grad,
        out_grad,
        out_bias_grad,
        first_gain_grad,
        first_shift_grad,
        up_grad,
        up_bias_grad,
        down_grad,
        down_bias_grad,
        second_gain_grad,
        second_shift_grad,
    )
    shares = (
        lax.psum_scatter(
            gradients[0].astype(jnp.bfloat16), "seq", scatter_dimension=0, tiled=True
        ).astype(jnp.float32),
        lax.psum_scatter(
            gradients[1].astype(jnp.bfloat16), "seq", scatter_dimension=0, tiled=True
        ).astype(jnp.float32),
        lax.psum_scatter(
            gradients[2].astype(jnp.bfloat16), "seq", scatter_dimension=0, tiled=True
        ).astype(jnp.float32),
        lax.psum_scatter(
            gradients[3].astype(jnp.bfloat16), "seq", scatter_dimension=0, tiled=True
        ).astype(jnp.float32),
        lax.psum_scatter(
            gradients[4].astype(jnp.bfloat16), "seq", scatter_dimension=0, tiled=True
        ).astype(jnp.float32),
        lax.psum_scatter(
            gradients[5].astype(jnp.bfloat16), "seq", scatter_dimension=0, tiled=True
        ).astype(jnp.float32),
        lax.psum_scatter(
            gradients[6].astype(jnp.bfloat16), "seq", scatter_dimension=0, tiled=True
        ).astype(jnp.float32),
        lax.psum_scatter(
            gradients[7].astype(jnp.bfloat16), "seq", scatter_dimension=0, tiled=True
        ).astype(jnp.float32),
        lax.psum_scatter(
            gradients[8].astype(jnp.bfloat16), "seq", scatter_dimension=0, tiled=True
        ).astype(jnp.float32),
        lax.psum_scatter(
            gradients[9].astype(jnp.bfloat16), "seq", scatter_dimension=0, tiled=True
        ).astype(jnp.float32),
        lax.psum_scatter(
            gradients[10].astype(jnp.bfloat16), "seq", scatter_dimension=0, tiled=True
        ).astype(jnp.float32),
        lax.psum_scatter(
            gradients[11].astype(jnp.bfloat16), "seq", scatter_dimension=0, tiled=True
        ).astype(jnp.float32),
        lax.psum_scatter(
            gradients[12].astype(jnp.bfloat16), "seq", scatter_dimension=0, tiled=True
        ).astype(jnp.float32),
    )
    shares = (
        lax.psum(shares[0].astype(jnp.bfloat16), "rows").astype(jnp.float32),
        lax.psum(shares[1].astype(jnp.bfloat16), "rows").astype(jnp.float32),
        lax.psum(shares[2].astype(jnp.bfloat16), "rows").astype(jnp.float32),
        lax.psum(shares[3].astype(jnp.bfloat16), "rows").astype(jnp.float32),
        lax.psum(shares[4].astype(jnp.bfloat16), "rows").astype(jnp.float32),
        lax.psum(shares[5].astype(jnp.bfloat16), "rows").astype(jnp.float32),
        lax.psum(shares[6].astype(jnp.bfloat16), "rows").astype(jnp.float32),
        lax.psum(shares[7].astype(jnp.bfloat16), "rows").astype(jnp.float32),
        lax.psum(shares[8].astype(jnp.bfloat16), "rows").astype(jnp.float32),
        lax.psum(shares[9].astype(jnp.bfloat16), "rows").astype(jnp.float32),
        lax.psum(shares[10].astype(jnp.bfloat16), "rows").astype(jnp.float32),
        lax.psum(shares[11].astype(jnp.bfloat16), "rows").astype(jnp.float32),
        lax.psum(shares[12].astype(jnp.bfloat16), "rows").astype(jnp.float32),
    )
    return (outputs, token_grad.reshape(tokens.shape)) + tuple(shares)


WIDTH = HEADS * HEAD_DIM
HALF = WIDTH // 2
FF = 4 * WIDTH
BLOCK = 128
OWN = 2 * BLOCK
LANES = 128
PAIRS_OF_HEADS = HALF // LANES
JOINT_ROWS = 80
JOINT_FIRST = 48
JOINT_SECOND = JOINT_ROWS - JOINT_FIRST
UP_ROWS = 128
DOWN_ROWS = 96
EXT = OWN + 16
DOWN_SENT = 2 * DOWN_ROWS
FLOAT = jnp.float32
LOW = jnp.bfloat16
AXES = ("seq", "rows")


def kernel_params(megabytes):
    return pltpu.CompilerParams(vmem_limit_bytes=megabytes << 20)


def shaped(shape, kind):
    return jax.ShapeDtypeStruct(shape, kind)


def whole(shape):
    return pl.BlockSpec(shape, lambda *_: (0,) * len(shape))


def cost(flops, moved, exps=0):
    return pl.CostEstimate(flops=1024, bytes_accessed=1024, transcendentals=0)


def dot(left, right):
    return lax.dot_general(left, right, (((1,), (0,)), ((), ())), preferred_element_type=FLOAT)


def dot_nt(left, right):
    return lax.dot_general(left, right, (((1,), (1,)), ((), ())), preferred_element_type=FLOAT)


def call(kernel, name, place, inputs, outputs, scratch=(), grid=(1,), scalars=(), after=(), megabytes=28, work=None, aliases=()):
    prefetch = 1 + len(scalars)
    given, made = len(inputs), len(outputs)

    def ordered(*refs):
        first = prefetch + given
        mark = refs[first + len(after) + made]
        mark[...] = jnp.zeros_like(mark)
        kernel(*refs[:first], *refs[first + len(after) : first + len(after) + made], *refs[first + len(after) + made + 1 :])

    results = pl.pallas_call(
        ordered,
        grid_spec=pltpu.PrefetchScalarGridSpec(
            num_scalar_prefetch=prefetch,
            grid=grid,
            in_specs=[spec for _, spec in inputs] + [pl.BlockSpec(memory_space=pl.ANY)] * len(after),
            out_specs=[spec for _, _, spec in outputs] + [whole((8, LANES))],
            scratch_shapes=list(scratch),
        ),
        out_shape=[shaped(shape, kind) for shape, kind, _ in outputs] + [shaped((8, LANES), FLOAT)],
        compiler_params=kernel_params(megabytes),
        cost_estimate=work,
        input_output_aliases={prefetch + source: target for source, target in aliases},
        name=name,
    )(place, *scalars, *[array for array, _ in inputs], *after)
    return results[:-1], results[-1]


def plain(array):
    return array, whole(array.shape)


def made(shape, kind):
    return shape, kind, whole(shape)


def device_at(z, y, x, c):
    return ((z * 2 + y) * 2 + x) * 2 + c


def permute(value, target):
    pairs = []
    for z in range(4):
        for y in range(2):
            for x in range(2):
                for c in range(2):
                    pairs.append((device_at(z, y, x, c), device_at(*target(z, y, x, c))))
    return lax.ppermute(value, AXES, pairs)


def core_swap(value):
    return permute(value, lambda z, y, x, c: (z, y, x, 1 - c))


def x_swap(value):
    return permute(value, lambda z, y, x, c: (z, y, 1 - x, c))


def y_swap(value):
    return permute(value, lambda z, y, x, c: (z, 1 - y, x, c))


def z_swap(value, bits):
    return permute(value, lambda z, y, x, c: (z ^ bits, y, x, c))


def row_swap(value, second):
    return permute(value, lambda z, y, x, c: (2 * c + (z % 2 ^ second), y, x, z // 2))


def first_positions(place):
    z, y, c = place[0], place[1], place[3]
    bases = []
    for core, line in ((c, y), (1 - c, y), (c, 1 - y), (1 - c, 1 - y)):
        for second in (0, 1):
            parity = z % 2
            parity = 1 - parity if second else parity
            bases.append((2 * (2 * core + parity) + line) * BLOCK)
    return bases


def pair_ends(place, own_lengths, peer_lengths):
    z, c = place[0], place[3]
    here = (z // 2) == c
    line = z % 2
    ends, end = [], 0
    for pair in range(own_lengths.shape[1]):
        end = end + jnp.where(here, own_lengths[line, pair], peer_lengths[line, pair])
        ends.append(end)
    return ends


def pairs_along(base, ends, axis):
    shape = (8, BLOCK) if axis == 1 else (BLOCK, LANES)
    position = base + lax.broadcasted_iota(jnp.int32, shape, axis)
    ids = jnp.zeros(shape, jnp.int32)
    for end in ends:
        ids = ids + (position >= end).astype(jnp.int32)
    return ids


def head_mask(rows):
    return lax.broadcasted_iota(jnp.int32, (rows, LANES), 1) < HEAD_DIM


def columns_kernel(place, columns, query_bias, value_bias, out, query_row, value_row):
    out[0] = columns[...]
    query_row[...] = query_bias[...]
    value_row[...] = value_bias[...]


def own_columns(place, joint_weight, query_bias, value_bias):
    half_row = pl.BlockSpec((1, HALF), lambda i, place: (0, place[3]))
    results, _ = call(
        columns_kernel,
        "own_columns",
        place,
        [
            (joint_weight, pl.BlockSpec((WIDTH, HALF), lambda i, place: (0, 2 * i + place[3]))),
            (row_of(query_bias), half_row),
            (row_of(value_bias), half_row),
        ],
        [((3, WIDTH, HALF), LOW, pl.BlockSpec((1, WIDTH, HALF), lambda i, place: (i, 0, 0)))]
        + [made((1, HALF), FLOAT)] * 2,
        grid=(3,),
        work=cost(1e6, 4e6),
    )
    return results


def first_attention_kernel(
    place, own_lengths, peer_lengths, t0, t1, t2, t3, columns, qb, vb, q_out, k_out, v_out, summed, stats, bias
):
    bases = first_positions(place)
    ends = pair_ends(place, own_lengths, peer_lengths)
    tokens = jnp.concatenate([block[...] for block in (t0, t1, t2, t3)], axis=0)
    queries = dot(tokens, columns[0]) + qb[...]
    q_out[...] = (queries.astype(LOW).astype(FLOAT) * HEAD_DIM**-0.5).astype(LOW)
    k_out[...] = dot(tokens, columns[1]).astype(LOW)
    v_out[...] = (dot(tokens, columns[2]) + vb[...]).astype(LOW)
    fill_bias(bias, bases[:4], bases[:4], ends)
    stats[...] = jnp.zeros_like(stats)
    for pair in range(PAIRS_OF_HEADS):
        lanes = pl.ds(pair * LANES, LANES)
        scores = masked_scores(k_out[:, lanes], q_out[:, lanes], bias)
        highest = jnp.max(scores, axis=0, keepdims=True)
        weights = jnp.exp(scores - highest)
        summed[pair] = dot(turned(v_out[:, lanes]), weights.astype(LOW))
        stats[2 * pair : 2 * pair + 1, :] = highest
        stats[2 * pair + 1 : 2 * pair + 2, :] = column_sum(weights)


def turned(array):
    return jnp.transpose(array.astype(FLOAT)).astype(LOW)


def masked_scores(keys, queries, bias):
    mask = bias[...]
    chosen = jnp.concatenate(halves_of(queries), axis=0)
    return dot_nt(keys, chosen) + jnp.concatenate([mask, mask], axis=1)


def fill_bias(bias, query_bases, key_bases, ends):
    key_ids = [pairs_along(base, ends, 1)[0:1] for base in key_bases]
    for i, base in enumerate(query_bases):
        query_ids = pairs_along(base, ends, 0)
        for j in range(len(key_bases)):
            bias[pl.ds(i * BLOCK, BLOCK), pl.ds(j * BLOCK, BLOCK)] = jnp.where(query_ids == key_ids[j], 0.0, NEGATIVE)


def halves_of(array):
    left = head_mask(array.shape[0])
    zeros = jnp.zeros_like(array)
    return jnp.where(left, array, zeros), jnp.where(left, zeros, array)


def first_attention(place, lengths, blocks, columns, query_bias, value_bias, after=()):
    return call(
        first_attention_kernel,
        "first_attention",
        place,
        [plain(array) for array in (*blocks, columns, query_bias, value_bias)],
        [made((512, HALF), LOW)] * 3 + [made((PAIRS_OF_HEADS, LANES, 1024), FLOAT), made((8, 1024), FLOAT)],
        scratch=[pltpu.VMEM((512, 512), FLOAT)],
        scalars=lengths,
        after=after,
        work=cost(4e9, 8e6, 3e6),
    )


def attention_kernel(
    place, own_lengths, peer_lengths, t0, t1, t2, t3, columns, vb, q, summed, stats,
    att_out, k_out, v_out, log_out, bias,
):
    bases = first_positions(place)
    ends = pair_ends(place, own_lengths, peer_lengths)
    tokens = jnp.concatenate([block[...] for block in (t0, t1, t2, t3)], axis=0)
    k_out[...] = dot(tokens, columns[1]).astype(LOW)
    v_out[...] = (dot(tokens, columns[2]) + vb[...]).astype(LOW)
    fill_bias(bias, bases[4:], bases[:4], ends)
    log_out[...] = jnp.zeros_like(log_out)
    top = lax.broadcasted_iota(jnp.int32, (LANES, 512), 0) < HEAD_DIM
    for pair in range(PAIRS_OF_HEADS):
        lanes = pl.ds(pair * LANES, LANES)
        scores = masked_scores(k_out[:, lanes], q[:, lanes], bias)
        before = stats[2 * pair : 2 * pair + 1, :]
        highest = jnp.maximum(before, jnp.max(scores, axis=0, keepdims=True))
        weights = jnp.exp(scores - highest)
        shrink = jnp.exp(before - highest)
        sums = column_sum(weights) + shrink * stats[2 * pair + 1 : 2 * pair + 2, :]
        total = (dot(turned(v_out[:, lanes]), weights.astype(LOW)) + shrink * summed[pair]) / sums
        att_out[:, lanes] = jnp.transpose(jnp.where(top, total[:, 0:512], total[:, 512:])).astype(LOW)
        logs = highest + jnp.log(sums)
        log_out[2 * pair : 2 * pair + 1, :] = logs[:, 0:512]
        log_out[2 * pair + 1 : 2 * pair + 2, :] = logs[:, 512:]


def attention(place, lengths, blocks, columns, value_bias, q, summed, stats, after=()):
    return call(
        attention_kernel,
        "attention",
        place,
        [plain(array) for array in (*blocks, columns, value_bias, q, summed, stats)],
        [made((512, HALF), LOW)] * 3 + [made((8, 512), FLOAT)],
        scratch=[pltpu.VMEM((512, 512), FLOAT)],
        scalars=lengths,
        after=after,
        work=cost(4e9, 8e6, 3e6),
    )


def centred_norm(value):
    mean = jnp.mean(value, axis=-1, keepdims=True)
    centred = value - mean
    spread = jnp.mean(centred * centred, axis=-1, keepdims=True)
    inverse = lax.rsqrt(spread + EPSILON)
    return centred * inverse, inverse


def norm_back(grad, unit, inverse):
    mean = jnp.mean(grad, axis=-1, keepdims=True)
    along = jnp.mean(grad * unit, axis=-1, keepdims=True)
    return (grad - mean - unit * along) * inverse


def column_sum(value):
    return jnp.sum(value, axis=0, keepdims=True)


def forward_kernel(
    place, att, att_got, wo_own, wo_other, out_bias, x0, x1, gain1, shift1, up, up_bias, down,
    down_bias, gain2, shift2, cot0, cot1,
    result0, result1, feed_ext, second_grad, act_keep, act_send, slope, unit1, inverse1, normed_low, normed_t, att_t, sums,
    act_t,
):
    c = place[3]
    tokens = jnp.concatenate([x0[...], x1[...]], axis=0).astype(FLOAT)
    att_own, att_other = att[0:OWN], att_got[OWN:]
    branch = dot(att_own, wo_own[...]) + dot(att_other, wo_other[...]) + out_bias[...]
    unit, inverse = centred_norm(tokens + branch)
    unit1[...] = unit
    inverse1[...] = jnp.broadcast_to(inverse, (OWN, LANES))
    normed = unit * gain1[...] + shift1[...]
    low = normed.astype(LOW)
    normed_low[...] = low
    normed_t[...] = jnp.transpose(normed).astype(LOW)
    mine = pl.ds(pl.multiple_of(c * HALF, HALF), HALF)
    other = pl.ds(pl.multiple_of((1 - c) * HALF, HALF), HALF)
    att_t[mine, :] = jnp.transpose(att[...].astype(FLOAT)).astype(LOW)
    att_t[other, 0:OWN] = jnp.transpose(att_other.astype(FLOAT)).astype(LOW)
    att_t[other, OWN:] = jnp.transpose(att_got[0:OWN].astype(FLOAT)).astype(LOW)
    inner = dot(low, up[...]) + up_bias[...]
    below = 0.5 + 0.5 * lax.erf(inner * math.sqrt(0.5))
    density = jnp.exp(inner * inner * -0.5) * (1.0 / math.sqrt(2.0 * math.pi))
    activated = inner * below
    slope[...] = (below + inner * density).astype(LOW)
    act_t[...] = jnp.transpose(activated).astype(LOW).reshape(16, 2, DOWN_ROWS, OWN)
    act_keep[...] = act_t[:, c]
    act_send[...] = act_t[:, 1 - c]
    feed = dot(activated.astype(LOW), down[...])
    unit, inverse = centred_norm(normed + feed + down_bias[...])
    result = (unit * gain2[...] + shift2[...]).astype(LOW)
    result0[...] = result[0:BLOCK]
    result1[...] = result[BLOCK:]
    cotangent = jnp.concatenate([cot0[0:BLOCK], cot1[0:BLOCK]], axis=0).astype(FLOAT)
    grad = norm_back(cotangent * gain2[...], unit, inverse)
    second_grad[...] = grad
    low_grad = grad.astype(LOW)
    rows = jnp.concatenate(
        [
            column_sum(cotangent * unit),
            column_sum(cotangent),
            column_sum(low_grad.astype(FLOAT)),
            jnp.zeros((5, WIDTH), FLOAT),
        ],
        axis=0,
    )
    sums[...] = rows
    feed_ext[0:OWN] = low_grad
    feed_ext[OWN:] = jnp.concatenate([rows, jnp.zeros_like(rows)], axis=0).astype(LOW)


def row_of(vector):
    return vector.reshape(1, vector.shape[0])


def forward(place, att, att_got, tokens, cotangents, weights, after=()):
    chunk = FF

    def vector(name):
        return plain(row_of(weights[name]))

    units = ((16, DOWN_ROWS, OWN), LOW, pl.BlockSpec((16, DOWN_ROWS, OWN), lambda i, place: (i, 0, 0)))
    return call(
        forward_kernel,
        "forward",
        place,
        [
            plain(att),
            plain(att_got),
            (weights["out"], pl.BlockSpec((HALF, WIDTH), lambda i, place: (place[3], 0))),
            (weights["out"], pl.BlockSpec((HALF, WIDTH), lambda i, place: (1 - place[3], 0))),
            vector("out_bias"), plain(tokens[0]), plain(tokens[1]), vector("gain1"), vector("shift1"),
            (weights["up"], pl.BlockSpec((WIDTH, chunk), lambda i, place: (0, i))),
            (row_of(weights["up_bias"]), pl.BlockSpec((1, chunk), lambda i, place: (0, i))),
            (weights["down"], pl.BlockSpec((chunk, WIDTH), lambda i, place: (i, 0))),
            vector("down_bias"), vector("gain2"), vector("shift2"), plain(cotangents[0]), plain(cotangents[1]),
        ],
        [
            made((BLOCK, WIDTH), LOW), made((BLOCK, WIDTH), LOW), made((EXT, WIDTH), LOW),
            made((OWN, WIDTH), FLOAT), units, units,
            ((OWN, FF), LOW, pl.BlockSpec((OWN, chunk), lambda i, place: (0, i))),
            made((OWN, WIDTH), FLOAT), made((OWN, LANES), FLOAT), made((OWN, WIDTH), LOW),
            made((WIDTH, OWN), LOW), made((WIDTH, 512), LOW), made((8, WIDTH), FLOAT),
        ],
        scratch=[pltpu.VMEM((16, 2, DOWN_ROWS, OWN), LOW)],
        after=after,
        work=cost(2.7e9, 20e6, 2e6),
    )


def split_units(place, units, px_send, px, qy_send, qy):
    y, x = place[1], place[2]
    half = units.shape[2] // 2
    for line in range(2):
        px[0, line] = units[line, x, 0:half]
        px_send[0, line] = units[line, 1 - x, 0:half]
    for side in range(2):
        qy[0, side] = units[y, side, half:]
        qy_send[0, side] = units[1 - y, side, half:]


def unit_outputs(rows, width):
    shape = (4, 2, rows // 2, width)
    return [(shape, LOW, pl.BlockSpec((1,) + shape[1:], lambda i, place: (i, 0, 0, 0)))] * 4


def down_kernel(place, act, act_got, feed, feed_got, px_send, px, qy_send, qy, units):
    shape = (4 * DOWN_ROWS, OWN)
    total = dot(act[...].reshape(shape), feed[0:OWN]) + dot(act_got[...].reshape(shape), feed_got[0:OWN])
    units[...] = total.astype(LOW).reshape(units.shape)
    split_units(place, units, px_send, px, qy_send, qy)


def down_units(place, act, act_got, feed, feed_got, after=()):
    block = pl.BlockSpec((4, DOWN_ROWS, OWN), lambda i, place: (i, 0, 0))
    return call(
        down_kernel,
        "down_units",
        place,
        [(act, block), (act_got, block), plain(feed), plain(feed_got)],
        unit_outputs(DOWN_ROWS, WIDTH),
        scratch=[pltpu.VMEM((2, 2, DOWN_ROWS, WIDTH), LOW)],
        grid=(4,),
        after=after,
        work=cost(0.6e9, 3.5e6),
    )


def backward_kernel(
    place, feed_ext, slope, up, down, second_grad, unit1, inverse1, gain1, wo_own, wo_other,
    inner0, inner1, send0, send1, first_grad, branch_own, back_own, misc, sums,
    inner, branch,
):
    c = place[3]
    grad = (dot_nt(feed_ext[0:OWN], down[...]) * slope[...].astype(FLOAT)).astype(LOW)
    inner[...] = grad
    for target, index in ((inner0, c), (inner1, 2 + c), (send0, 1 - c), (send1, 3 - c)):
        target[...] = inner[:, pl.ds(pl.multiple_of(index * WIDTH, LANES), WIDTH)]
    inner_sum = column_sum(grad.astype(FLOAT))
    total = second_grad[...] + dot_nt(grad, up[...])
    unit = unit1[...]
    grad1 = norm_back(total * gain1[...], unit, inverse1[:, 0:1])
    first_grad[...] = grad1
    low = grad1.astype(LOW)
    branch[...] = low
    rows = jnp.concatenate(
        [
            column_sum(total * unit),
            column_sum(total),
            column_sum(low.astype(FLOAT)),
            jnp.zeros((1, WIDTH), FLOAT),
        ]
        + [inner_sum[:, index * WIDTH : (index + 1) * WIDTH] for index in range(4)],
        axis=0,
    )
    sums[...] = rows
    branch_own[...] = branch[:, pl.ds(pl.multiple_of(c * HALF, LANES), HALF)]
    back_own[...] = dot_nt(low, wo_own[...]).astype(LOW)
    misc[0:OWN, 0:HALF] = branch[:, pl.ds(pl.multiple_of((1 - c) * HALF, LANES), HALF)]
    misc[0:OWN, HALF:] = dot_nt(low, wo_other[...]).astype(LOW)
    misc[OWN:] = jnp.concatenate([rows, jnp.zeros_like(rows)], axis=0).astype(LOW)


def backward(place, feed_ext, slope, second_grad, unit1, inverse1, weights, after=()):
    chunk = FF
    return call(
        backward_kernel,
        "backward",
        place,
        [
            plain(feed_ext),
            (slope, pl.BlockSpec((OWN, chunk), lambda i, place: (0, i))),
            (weights["up"], pl.BlockSpec((WIDTH, chunk), lambda i, place: (0, i))),
            (weights["down"], pl.BlockSpec((chunk, WIDTH), lambda i, place: (i, 0))),
            plain(second_grad), plain(unit1), plain(inverse1), plain(row_of(weights["gain1"])),
            (weights["out"], pl.BlockSpec((HALF, WIDTH), lambda i, place: (place[3], 0))),
            (weights["out"], pl.BlockSpec((HALF, WIDTH), lambda i, place: (1 - place[3], 0))),
        ],
        [made((OWN, WIDTH), LOW)] * 4
        + [
            made((OWN, WIDTH), FLOAT), made((OWN, HALF), LOW), made((OWN, HALF), LOW), made((EXT, WIDTH), LOW),
            made((8, WIDTH), FLOAT),
        ],
        scratch=[pltpu.VMEM((OWN, FF), LOW), pltpu.VMEM((OWN, WIDTH), LOW)],
        after=after,
        work=cost(2.7e9, 16e6),
    )


def up_kernel(
    place, normed_t, normed_got, inner0, inner1, got0, got1, att_t, branch, misc, sums0, sums1, feed_got,
    x_send, y_send, px, qy, units, normed_got_t,
):
    z = pl.program_id(0)
    y, x = place[1], place[2]

    @pl.when(z == 0)
    def _():
        normed_got_t[...] = jnp.transpose(normed_got[...].astype(FLOAT)).astype(LOW)

    theirs = normed_got_t[pl.ds(pl.multiple_of(z * 192, 32), 192), :]
    outer = dot(att_t[:, 0:OWN], branch[...]) + dot(att_t[:, OWN:], misc[0:OWN, 0:HALF])
    for side, inner, got, sums, pair in ((0, inner0, got0, sums0, feed_got), (1, inner1, got1, sums1, misc)):
        grad = dot(normed_t[...], inner[...]) + dot(theirs, got[...])
        vectors = sums[...] + pair[OWN:].astype(FLOAT)[0:8]
        for line in range(2):
            first = line * 96 + side * 48
            rest = jnp.concatenate([outer[first : first + 24], outer[first + 24 : first + 48]], axis=1)
            units[line, side] = jnp.concatenate(
                [grad[line * 96 : line * 96 + 96], rest, vectors], axis=0
            ).astype(LOW)
    half = UP_ROWS // 2
    for index in range(2):
        rows = pl.ds(pl.multiple_of(DOWN_SENT + (z * 2 + index) * half, half), half)
        px[0, index] = units[index, x, 0:half]
        x_send[rows, :] = units[index, 1 - x, 0:half]
        qy[0, index] = units[y, index, half:]
        y_send[rows, :] = units[1 - y, index, half:]


def up_units(place, normed_t, normed_got, inner, got, att_t, branch, misc, sums0, sums1, feed_got, after=()):
    rows = pl.BlockSpec((192, OWN), lambda i, place: (i, 0))
    return call(
        up_kernel,
        "up_units",
        place,
        [
            (normed_t, rows), plain(normed_got), plain(inner[0]), plain(inner[1]), plain(got[0]), plain(got[1]),
            (att_t, pl.BlockSpec((192, 512), lambda i, place: (i, 0))),
            plain(branch), plain(misc), plain(sums0), plain(sums1), plain(feed_got),
        ],
        [made((DOWN_SENT + 4 * UP_ROWS, WIDTH), LOW)] * 2 + unit_outputs(UP_ROWS, WIDTH)[:2],
        scratch=[pltpu.VMEM((2, 2, UP_ROWS, WIDTH), LOW), pltpu.VMEM((WIDTH, OWN), LOW)],
        grid=(4,),
        after=after,
        work=cost(0.9e9, 5e6),
    )


def attention_back_kernel(
    place, own_lengths, peer_lengths, q, k0, k1, v0, v1, log_total, att, back0, misc,
    dq_out, dk_out, dv_out, bias,
):
    bases = first_positions(place)
    ends = pair_ends(place, own_lengths, peer_lengths)
    query_ids = [pairs_along(base, ends, 1)[0:1] for base in bases[:4]]
    for j in range(8):
        key_ids = pairs_along(bases[j], ends, 0)
        for i in range(4):
            bias[pl.ds(j * BLOCK, BLOCK), pl.ds(i * BLOCK, BLOCK)] = jnp.where(
                key_ids == query_ids[i], 0.0, NEGATIVE
            )

    def one_pair(pair, carry):
        lanes = pl.ds(pl.multiple_of(pair * LANES, LANES), LANES)
        keys = jnp.concatenate([k0[:, lanes], k1[:, lanes]], axis=0)
        values = jnp.concatenate([v0[:, lanes], v1[:, lanes]], axis=0)
        keys_t = turned(keys)
        key_grad = jnp.zeros((1024, LANES), FLOAT)
        value_grad = jnp.zeros((1024, LANES), FLOAT)
        far = pl.ds(pl.multiple_of(HALF + pair * LANES, LANES), LANES)
        for part, back in ((0, back0[:, lanes]), (1, misc[0:OWN, far])):
            rows = pl.ds(part * OWN, OWN)
            product = jnp.transpose(back.astype(FLOAT) * att[rows, lanes].astype(FLOAT))
            delta = jnp.concatenate([column_sum(product[0:HEAD_DIM]), column_sum(product[HEAD_DIM:])], axis=1)
            logs = jnp.concatenate(
                [log_total[pl.ds(2 * pair, 1), rows], log_total[pl.ds(2 * pair + 1, 1), rows]], axis=1
            )
            chosen = jnp.concatenate(halves_of(q[rows, lanes]), axis=0)
            grads = jnp.concatenate(halves_of(back), axis=0)
            mask = bias[:, rows]
            weights = jnp.exp(dot_nt(keys, chosen) + jnp.concatenate([mask, mask], axis=1) - logs)
            score_grad = (weights * (dot_nt(values, grads) - delta)).astype(LOW)
            value_grad = value_grad + dot(weights.astype(LOW), grads)
            key_grad = key_grad + dot(score_grad, chosen)
            both = dot(keys_t, score_grad)
            query_grad_t = jnp.concatenate([both[0:HEAD_DIM, 0:OWN], both[HEAD_DIM:, OWN:]], axis=0)
            dq_out[rows, lanes] = (jnp.transpose(query_grad_t) * HEAD_DIM**-0.5).astype(LOW)
        dk_out[:, lanes] = key_grad.astype(LOW)
        dv_out[:, lanes] = value_grad.astype(LOW)
        return carry

    lax.fori_loop(0, PAIRS_OF_HEADS, one_pair, 0)


def attention_back(place, lengths, q, keys, values, log_total, att, back_own, misc, after=()):
    return call(
        attention_back_kernel,
        "attention_back",
        place,
        [plain(array) for array in (q, *keys, *values, log_total, att, back_own, misc)],
        [made((512, HALF), LOW), made((1024, HALF), LOW), made((1024, HALF), LOW)],
        scratch=[pltpu.VMEM((1024, 512), FLOAT)],
        scalars=lengths,
        after=after,
        work=cost(7e9, 6e6, 3e6),
    )


def token_kernel(place, dq, dk, dv, columns, own, own_send, far, far_send):
    for part, target in enumerate((own, own_send, far, far_send)):
        rows = pl.ds(part * OWN, OWN)
        total = dot_nt(dk[rows, :], columns[1]) + dot_nt(dv[rows, :], columns[2])
        if part < 2:
            total = total + dot_nt(dq[rows, :], columns[0])
        target[...] = total.astype(LOW)


def token_parts(place, dq, dk, dv, columns, after=()):
    return call(
        token_kernel,
        "token_parts",
        place,
        [plain(dq), plain(dk), plain(dv), plain(columns)],
        [made((OWN, WIDTH), LOW)] * 4,
        after=after,
        work=cost(1.5e9, 5e6),
    )


def token_last_kernel(place, own, own_got, across, first_grad, token0, token1):
    total = own[...].astype(FLOAT) + own_got[...].astype(FLOAT) + across[8 * JOINT_SECOND :].astype(FLOAT) + first_grad[...]
    total = total.astype(LOW)
    token0[...] = total[0:BLOCK]
    token1[...] = total[BLOCK:]


def token_last(place, arrays, after=()):
    return call(
        token_last_kernel,
        "token_last",
        place,
        [plain(array) for array in arrays],
        [made((BLOCK, WIDTH), LOW)] * 2,
        after=after,
        work=cost(1e6, 2e6),
    )


def back_rows_kernel(place, done0, done1, back0, back1, outputs, token_grad):
    odd = place[0] % 2
    outputs[odd] = done0[...]
    outputs[1 - odd] = done1[...]
    token_grad[odd] = back0[...].astype(FLOAT)
    token_grad[1 - odd] = back1[...].astype(FLOAT)


def back_rows(place, done, back, after=()):
    return call(
        back_rows_kernel,
        "back_rows",
        place,
        [plain(array) for array in (*done, *back)],
        [made((2, BLOCK, WIDTH), LOW), made((2, BLOCK, WIDTH), FLOAT)],
        after=after,
        work=cost(1e6, 2e6),
    )


def joint_kernel(
    place, t0, t1, t2, t3, t4, t5, t6, t7, dq, dk, dv, far, far_got, px_send, px, qy_send, qy, tokens_t, units
):
    y, x = place[1], place[2]
    qy_send[pl.ds(8 * JOINT_SECOND, OWN), :] = added(far[...], far_got[...])
    for index, block in enumerate((t0, t1, t2, t3, t4, t5, t6, t7)):
        tokens_t[:, pl.ds(index * BLOCK, BLOCK)] = jnp.transpose(block[...].astype(FLOAT)).astype(LOW)
    biases = jnp.concatenate([column_sum(dq[...].astype(FLOAT)), column_sum(dv[...].astype(FLOAT))], axis=1)
    biases = jnp.concatenate([biases, jnp.zeros((7, WIDTH), FLOAT)], axis=0)
    for z in range(4):
        rows = pl.ds(z * 192, 192)
        query = dot(tokens_t[rows, 0:512], dq[...])
        key = dot(tokens_t[rows, :], dk[...])
        value = dot(tokens_t[rows, :], dv[...])
        for line in range(2):
            for side in range(2):
                at = line * 96 + side * 48
                units[line, side, 0:JOINT_FIRST] = jnp.concatenate(
                    [query[at : at + 48], key[at : at + 48]], axis=1
                ).astype(LOW)
                rest = jnp.concatenate([value[at : at + 24], value[at + 24 : at + 48]], axis=1)
                units[line, side, JOINT_FIRST:] = jnp.concatenate([rest, biases], axis=0).astype(LOW)
        for line in range(2):
            px[z, line] = units[line, x, 0:JOINT_FIRST]
            px_send[z, line] = units[line, 1 - x, 0:JOINT_FIRST]
        for side in range(2):
            qy[z, side] = units[y, side, JOINT_FIRST:]
            qy_send[pl.ds((z * 2 + side) * JOINT_SECOND, JOINT_SECOND), :] = units[1 - y, side, JOINT_FIRST:]


def joint_units(place, blocks, dq, dk, dv, far, far_got, after=()):
    first, second = made((4, 2, JOINT_FIRST, WIDTH), LOW), made((4, 2, JOINT_SECOND, WIDTH), LOW)
    return call(
        joint_kernel,
        "joint_units",
        place,
        [plain(array) for array in (*blocks, dq, dk, dv, far, far_got)],
        [first, first, made((8 * JOINT_SECOND + OWN, WIDTH), LOW), second],
        scratch=[pltpu.VMEM((WIDTH, 1024), LOW), pltpu.VMEM((2, 2, JOINT_ROWS, WIDTH), LOW)],
        after=after,
        work=cost(1.5e9, 6e6),
    )


def added(left, right):
    return (left.astype(FLOAT) + right.astype(FLOAT)).astype(LOW)


def down_pair_kernel(place, px, px_got, qy, qy_got, x_in, y_in, x_send, y_send, p, q):
    y, x = place[1], place[2]
    p[0] = added(px[0, y], px_got[0, y])
    y_send[...] = added(px[0, 1 - y], px_got[0, 1 - y])
    q[0] = added(qy[0, x], qy_got[0, x])
    x_send[...] = added(qy[0, 1 - x], qy_got[0, 1 - x])


def down_pair_stage(place, arrays, x_send, y_send, after=()):
    half = DOWN_ROWS // 2
    block = pl.BlockSpec((1, 2, half, WIDTH), lambda i, place: (i, 0, 0, 0))
    sent = (x_send.shape, LOW, pl.BlockSpec((half, WIDTH), lambda i, place: (i, 0)))
    kept = ((4, half, WIDTH), LOW, pl.BlockSpec((1, half, WIDTH), lambda i, place: (i, 0, 0)))
    anywhere = pl.BlockSpec(memory_space=pl.ANY)
    return call(
        down_pair_kernel,
        "down_pair_stage",
        place,
        [(array, block) for array in arrays] + [(x_send, anywhere), (y_send, anywhere)],
        [sent, sent, kept, kept],
        grid=(4,),
        after=after,
        work=cost(1e6, 1e7),
        aliases=((4, 0), (5, 1)),
    )


def second_kernel(
    place, x_got, y_got, px, qy, down_p, down_q, x_send, y_send, p, q, down_send, down_keep
):
    z_here, y, x = place[0], place[1], place[2]
    half = UP_ROWS // 2
    for z in range(4):
        for got, have, own, keep, send in ((x_got, px, y, p, y_send), (y_got, qy, x, q, x_send)):
            at = DOWN_SENT + z * UP_ROWS
            mine = pl.ds(pl.multiple_of(at + own * half, half), half)
            other = pl.ds(pl.multiple_of(at + (1 - own) * half, half), half)
            keep[z] = added(have[z, own], got[mine, :])
            send[pl.ds(z * half, half), :] = added(have[z, 1 - own], got[other, :])
    low = z_here % 2
    small = DOWN_ROWS // 2
    for target, parity in ((down_keep, low), (down_send, 1 - low)):
        for high in range(2):
            index = 2 * high + parity
            rows = pl.ds(pl.multiple_of(index * small, small), small)
            target[high, 0:small] = added(down_p[index], y_got[rows, :])
            target[high, small:] = added(down_q[index], x_got[rows, :])


def second_stage(place, arrays, after=()):
    kept = made((4, UP_ROWS // 2, WIDTH), LOW)
    down = made((2, DOWN_ROWS, WIDTH), LOW)
    return call(
        second_kernel,
        "second_stage",
        place,
        [plain(array) for array in arrays],
        [made((OWN, WIDTH), LOW), made((OWN, WIDTH), LOW), kept, kept, down, down],
        after=after,
        work=cost(1e6, 1e7),
    )


def joint_pair_kernel(place, px, px_got, qy, qy_got, x_send, y_send, p, q):
    y, x = place[1], place[2]
    for z in range(4):
        p[z] = added(px[z, y], px_got[z, y])
        y_send[z] = added(px[z, 1 - y], px_got[z, 1 - y])


        def from_y(side):
            return qy_got[pl.ds(pl.multiple_of((z * 2 + side) * JOINT_SECOND, 32), JOINT_SECOND), :]

        q[z] = added(qy[z, x], from_y(x))
        x_send[z] = added(qy[z, 1 - x], from_y(1 - x))


def joint_pair_stage(place, arrays, after=()):
    first, second = made((4, JOINT_FIRST, WIDTH), LOW), made((4, JOINT_SECOND, WIDTH), LOW)
    return call(
        joint_pair_kernel,
        "joint_pair_stage",
        place,
        [plain(array) for array in arrays],
        [second, first, first, second],
        after=after,
        work=cost(1e6, 1e7),
    )


def up_line_kernel(place, x_got, y_got, p, q, down_two, down_got, send, keep, down_send, down_keep):
    low, high_here = place[0] % 2, place[0] // 2
    half = UP_ROWS // 2
    for target, parity in ((keep, low), (send, 1 - low)):
        for high in range(2):
            index = 2 * high + parity
            rows = pl.ds(pl.multiple_of(index * half, half), half)
            target[high, 0:half] = added(p[index], y_got[rows, :])
            target[high, half:] = added(q[index], x_got[rows, :])
    down_keep[...] = added(down_two[high_here], down_got[high_here])
    down_send[...] = added(down_two[1 - high_here], down_got[1 - high_here])


def up_line_stage(place, arrays, after=()):
    return call(
        up_line_kernel,
        "up_line_stage",
        place,
        [plain(array) for array in arrays],
        [made((2, UP_ROWS, WIDTH), LOW)] * 2 + [made((DOWN_ROWS, WIDTH), LOW)] * 2,
        after=after,
        work=cost(1e6, 1e7),
    )


def joint_line_kernel(place, x_got, y_got, p, q, keep, one, two, three):
    low, high = place[0] % 2, place[0] // 2
    for target, index in (
        (keep, 2 * high + low), (one, 2 * high + 1 - low), (two, 2 * (1 - high) + low), (three, 2 * (1 - high) + 1 - low)
    ):
        target[0:JOINT_FIRST] = added(p[index], y_got[index])
        target[JOINT_FIRST:] = added(q[index], x_got[index])


def joint_line_stage(place, arrays, after=()):
    return call(
        joint_line_kernel,
        "joint_line_stage",
        place,
        [plain(array) for array in arrays],
        [made((JOINT_ROWS, WIDTH), LOW)] * 4,
        after=after,
        work=cost(1e6, 1e6),
    )


def end_stage_kernel(place, keep_two, got, send, keep):
    high = place[0] // 2
    keep[...] = added(keep_two[high], got[high])
    send[...] = added(keep_two[1 - high], got[1 - high])


def end_stage(place, keep_two, got, after=()):
    return call(
        end_stage_kernel,
        "end_stage",
        place,
        [plain(keep_two), plain(got)],
        [made(keep_two.shape[1:], LOW)] * 2,
        after=after,
        work=cost(1e6, 1e6),
    )


def joint_sum_kernel(place, first, second, third, fourth, out):
    total = (first[...].astype(FLOAT) + second[...].astype(FLOAT)) + (third[...].astype(FLOAT) + fourth[...].astype(FLOAT))
    out[...] = total.astype(LOW)


def joint_sum(place, arrays, after=()):
    results, mark = call(
        joint_sum_kernel,
        "joint_sum",
        place,
        [plain(array) for array in arrays],
        [made((JOINT_ROWS, WIDTH), LOW)],
        after=after,
        work=cost(1e6, 1e6),
    )
    return results[0], mark


def last_sum_kernel(place, *refs):
    count = len(refs) // 3
    for index in range(count):
        refs[2 * count + index][...] = added(refs[2 * index][...], refs[2 * index + 1][...])


def last_sum(place, pairs, after=()):
    return call(
        last_sum_kernel,
        "last_sum",
        place,
        [plain(array) for pair in pairs for array in pair],
        [made(pair[0].shape, LOW) for pair in pairs],
        after=after,
        work=cost(1e6, 1e6),
    )


def gathered(unit, mark=None):
    across = x_swap(unit)
    if mark is not None:
        across, mark = lax.optimization_barrier((across, mark))
    return unit, core_swap(unit), across, core_swap(across)


def quarters(place):
    x, c = place[2], place[3]
    return (x, c), (x, 1 - c), (1 - x, c), (1 - x, 1 - c)


def line_shift(place):
    seq = place[0] * 2 + place[1]
    return lax.rem(WIDTH - seq * 96, WIDTH)


def dense_out_kernel(
    place, d0, d1, d2, d3, u0, u1, u2, u3,
    down, up, out, gain2, shift2, down_bias, gain1, shift1, out_bias, up_bias, heads, tails,
):
    for down_unit, unit, (x, c) in zip((d0, d1, d2, d3), (u0, u1, u2, u3), quarters(place)):
        quarter = 2 * x + c
        down[pl.ds(pl.multiple_of(quarter * DOWN_ROWS, 32), DOWN_ROWS), :] = down_unit[...].astype(FLOAT)
        up[:, pl.ds(pl.multiple_of(quarter * WIDTH, LANES), WIDTH)] = unit[0:96, :].astype(FLOAT)
        rest = unit[96:128, :].astype(FLOAT)
        lanes = pl.ds(pl.multiple_of(c * HALF, LANES), HALF)
        out[pl.ds(pl.multiple_of(x * 48, 8), 24), lanes] = rest[0:24, 0:HALF]
        out[pl.ds(pl.multiple_of(x * 48 + 24, 8), 24), lanes] = rest[0:24, HALF:]

        @pl.when(x == 0)
        def _(rest=rest):
            heads[...] = rest[24:32]

        @pl.when(x == 1)
        def _(rest=rest):
            tails[...] = rest[24:32]

    seq = place[0] * 2 + place[1]
    shift = line_shift(place)
    head = pltpu.roll(heads[...], shift, 1)
    gain2[...] = head[0:1, 0:96]
    shift2[...] = head[1:2, 0:96]
    down_bias[...] = head[2:3, 0:96]
    tail = pltpu.roll(tails[...], shift, 1)
    gain1[...] = tail[0:1, 0:96]
    shift1[...] = tail[1:2, 0:96]
    out_bias[...] = tail[2:3, 0:96]
    wide = tails[pl.ds(4 + seq // 2, 1), :]
    up_bias[...] = jnp.where(seq % 2 == 0, wide[:, 0:HALF], wide[:, HALF:]).reshape(HALF)


def dense_outputs(place, units, after=()):
    results, mark = call(
        dense_out_kernel,
        "dense_outputs",
        place,
        [plain(unit) for unit in units],
        [made((4 * DOWN_ROWS, WIDTH), FLOAT), made((96, FF), FLOAT), made((96, WIDTH), FLOAT)]
        + [made((1, 96), FLOAT)] * 6
        + [made((HALF,), FLOAT)],
        scratch=[pltpu.VMEM((8, WIDTH), FLOAT)] * 2,
        after=after,
        work=cost(1e6, 3e6),
    )
    return (*results[:3], *(vector.reshape(-1) for vector in results[3:])), mark


def joint_out_kernel(place, u0, u1, u2, u3, joint, query_bias, value_bias, sums):
    for unit, (x, c) in zip((u0, u1, u2, u3), quarters(place)):

        def lanes(kind):
            return pl.ds(pl.multiple_of(kind * WIDTH + c * HALF, LANES), HALF)

        first = unit[0:JOINT_FIRST].astype(FLOAT)
        rest = unit[JOINT_FIRST:].astype(FLOAT)
        rows = pl.ds(pl.multiple_of(x * 48, 16), 48)
        joint[rows, lanes(0)] = first[:, 0:HALF]
        joint[rows, lanes(1)] = first[:, HALF:]
        joint[pl.ds(pl.multiple_of(x * 48, 8), 24), lanes(2)] = rest[0:24, 0:HALF]
        joint[pl.ds(pl.multiple_of(x * 48 + 24, 8), 24), lanes(2)] = rest[0:24, HALF:]

        @pl.when(x == 0)
        def _(rest=rest, c=c):
            half = pl.ds(pl.multiple_of(c * HALF, LANES), HALF)
            sums[0:1, half] = rest[24:25, 0:HALF]
            sums[1:2, half] = rest[24:25, HALF:]

    turned = pltpu.roll(sums[...], line_shift(place), 1)
    query_bias[...] = turned[0:1, 0:96]
    value_bias[...] = turned[1:2, 0:96]


def joint_outputs(place, units, after=()):
    results, mark = call(
        joint_out_kernel,
        "joint_outputs",
        place,
        [plain(unit) for unit in units],
        [made((96, 3 * WIDTH), FLOAT), made((1, 96), FLOAT), made((1, 96), FLOAT)],
        scratch=[pltpu.VMEM((8, WIDTH), FLOAT)],
        after=after,
        work=cost(1e6, 2e6),
    )
    return (results[0], results[1].reshape(-1), results[2].reshape(-1)), mark


def row_body(
    tokens,
    pair_lengths,
    joint_weight,
    query_bias,
    value_bias,
    out_weight,
    out_bias,
    first_gain,
    first_shift,
    up_weight,
    up_bias,
    down_weight,
    down_bias,
    second_gain,
    second_shift,
    cotangent,
):
    seq, rows = lax.axis_index("seq"), lax.axis_index("rows")
    z, y, x, c = seq // 2, seq % 2, rows // 2, rows % 2
    place = jnp.stack([z, y, x, c]).astype(jnp.int32)
    odd = z % 2
    weights = {
        "out": out_weight, "out_bias": out_bias, "gain1": first_gain, "shift1": first_shift,
        "up": up_weight, "up_bias": up_bias, "down": down_weight, "down_bias": down_bias,
        "gain2": second_gain, "shift2": second_shift,
    }

    def local_row(array, index):
        return lax.dynamic_index_in_dim(array, index, 0, keepdims=False)

    columns, query_row, value_row = own_columns(place, joint_weight, query_bias, value_bias)
    lengths = (pair_lengths, core_swap(pair_lengths))
    own = [row_swap(local_row(tokens, odd), 0), row_swap(local_row(tokens, 1 - odd), 1)]
    *own, columns, lengths = lax.optimization_barrier((*own, columns, lengths))
    across = [y_swap(block) for block in own]
    here = own + [core_swap(block) for block in own]
    (q, k_here, v_here, summed, stats), mark = first_attention(
        place, lengths, here, columns, query_row, value_row
    )
    padding = jnp.zeros((16, WIDTH), LOW)
    cotangents = [
        row_swap(jnp.concatenate([local_row(cotangent, index), padding], axis=0), second)
        for second, index in ((0, odd), (1, 1 - odd))
    ]
    across[0], across[1], mark = lax.optimization_barrier((across[0], across[1], mark))
    there = across + [core_swap(block) for block in across]
    blocks = here + there
    (att, k_there, v_there, log_total), mark = attention(
        place, lengths, there, columns, value_row, q, summed, stats, (mark,)
    )
    att, *cotangents = lax.optimization_barrier((att, *cotangents))
    att_got = core_swap(att)
    results, mark = forward(place, att, att_got, own, cotangents, weights, (mark,))
    (
        result0, result1, feed, second_grad, act, act_send, slope, unit1, inverse1, normed, normed_t, att_t, sums0
    ) = results
    act_got, feed_got, normed_got = core_swap(act_send), core_swap(feed), core_swap(normed)
    done = (row_swap(result0, 0), row_swap(result1, 1))
    (px_send, px, qy_send, qy), mark = down_units(place, act, act_got, feed, feed_got, (mark,))
    down_pair = (px, x_swap(px_send), qy, y_swap(qy_send))
    results, mark = backward(place, feed, slope, second_grad, unit1, inverse1, weights, (mark, normed_got))
    inner0, inner1, send0, send1, first_grad, branch_own, back_own, misc_send, sums1 = results
    got, misc = (core_swap(send0), core_swap(send1)), core_swap(misc_send)
    (x_send, y_send, px, qy), mark = up_units(
        place, normed_t, normed_got, (inner0, inner1), got, att_t, branch_own, misc, sums0, sums1, feed_got, (mark,)
    )
    (x_send, y_send, down_p, down_q), mark = down_pair_stage(place, down_pair, x_send, y_send, (mark,))
    x_got, y_got = x_swap(x_send), y_swap(y_send)
    (dq, dk, dv), mark = attention_back(
        place, lengths, q, (k_here, k_there), (v_here, v_there), log_total, att, back_own, misc, (mark,)
    )
    (token_own, own_send, token_far, far_send), mark = token_parts(place, dq, dk, dv, columns, (mark, *done))
    own_got, far_got = core_swap(own_send), core_swap(far_send)
    (px_send, joint_px, qy_send, joint_qy), mark = joint_units(
        place, blocks, dq, dk, dv, token_far, far_got, (mark,)
    )
    (x_send, y_send, p, q_, down_send, down_two), mark = second_stage(
        place, (x_got, y_got, px, qy, down_p, down_q), (mark, own_got)
    )
    x_got, y_got, down_got = x_swap(x_send), y_swap(y_send), z_swap(down_send, 1)
    px_send, qy_send, mark = lax.optimization_barrier((px_send, qy_send, mark))
    across = y_swap(qy_send)
    joint_pair = (joint_px, x_swap(px_send), joint_qy, across)
    (up_send, up_two, down_send, down_keep), mark = up_line_stage(
        place, (x_got, y_got, p, q_, down_two, down_got), (mark,)
    )
    up_got, down_got = z_swap(up_send, 1), z_swap(down_send, 2)
    (up_send, up_keep), mark = end_stage(place, up_two, up_got, (mark, down_got))
    up_got = z_swap(up_send, 2)
    (down_unit,), mark = last_sum(place, ((down_keep, down_got),), (mark,))
    down_across = x_swap(down_unit)
    (x_send, y_send, joint_p, joint_q), mark = joint_pair_stage(place, joint_pair, (mark,))
    joint_x_got, joint_y_got = x_swap(x_send), y_swap(y_send)
    down_own, up_got = lax.optimization_barrier((down_unit, up_got))
    down_all = (down_unit, core_swap(down_own), down_across, core_swap(down_across))
    (token0, token1), mark = token_last(place, (token_own, own_got, across, first_grad), (mark,))
    back = (row_swap(token0, 0), row_swap(token1, 1))
    (up_unit,), mark = last_sum(place, ((up_keep, up_got),), (mark,))
    up_all = gathered(up_unit)
    (keep, one, two, three), mark = joint_line_stage(
        place, (joint_x_got, joint_y_got, joint_p, joint_q), (mark, *down_all[1:])
    )
    joint_last = (keep, z_swap(two, 2), z_swap(three, 3), z_swap(one, 1))
    joint_unit, mark = joint_sum(place, joint_last, (mark,))
    joint_across = x_swap(joint_unit)
    joint_across, first_back = lax.optimization_barrier((joint_across, back[0]))
    joint_all = (joint_unit, core_swap(joint_unit), joint_across, core_swap(joint_across))
    (
        down_grad, up_grad, out_grad, second_gain_grad, second_shift_grad, down_bias_grad, first_gain_grad,
        first_shift_grad, out_bias_grad, up_bias_grad,
    ), mark = dense_outputs(place, (*down_all, *up_all), (mark,))
    (joint_grad, query_bias_grad, value_bias_grad), mark = joint_outputs(place, joint_all, (mark,))
    (outputs, token_grad), mark = back_rows(place, done, (first_back, back[1]), (mark,))
    return (
        outputs,
        token_grad,
        joint_grad,
        query_bias_grad,
        value_bias_grad,
        out_grad,
        out_bias_grad,
        first_gain_grad,
        first_shift_grad,
        up_grad,
        up_bias_grad,
        down_grad,
        down_bias_grad,
        second_gain_grad,
        second_shift_grad,
    )


def body(tokens, *others):
    if (lax.axis_size("seq"), lax.axis_size("rows")) == (8, 4) and tokens.shape == (2, BLOCK, WIDTH):
        return row_body(tokens, *others)
    return general_body(tokens, *others)


def solution(mesh):
    placed = (
        P("rows", "seq", None),
        P("rows", None),
        P(),
        P(),
        P(),
        P(),
        P(),
        P(),
        P(),
        P(),
        P(),
        P(),
        P(),
        P(),
        P(),
        P("rows", "seq", None),
    )
    return jax.shard_map(
        body,
        mesh=mesh,
        in_specs=placed,
        out_specs=(
            P("rows", "seq", None),
            P("rows", "seq", None),
            P("seq", None),
            P("seq"),
            P("seq"),
            P("seq", None),
            P("seq"),
            P("seq"),
            P("seq"),
            P("seq", None),
            P("seq"),
            P("seq", None),
            P("seq"),
            P("seq"),
            P("seq"),
        ),
        check_vma=False,
    )
```

```python
import functools
import math

import jax
import jax.numpy as jnp
from jax import lax
from jax.experimental import pallas as pl
from jax.experimental.pallas import tpu as pltpu
from jax.sharding import PartitionSpec as P

HEADS = 12
HEAD_DIM = 64


NEGATIVE = -1e30
EPSILON = 1e-12


def from_behind(value, axis, steps):
    count = lax.axis_size(axis)
    pairs = [(source, (source + steps) % count) for source in range(count)]
    return lax.ppermute(value, axis, pairs)


def layer_norm(value, gain, shift):
    mean = jnp.mean(value, axis=-1, keepdims=True)
    centred = value - mean
    spread = jnp.mean(centred * centred, axis=-1, keepdims=True)
    return centred * lax.rsqrt(spread + EPSILON) * gain + shift


def gelu_exact(value):
    return jax.nn.gelu(value, approximate=False)


def pair_index(positions, ends):
    return jnp.sum((positions[None, :, None] >= ends[:, None, :]).astype(jnp.int32), axis=2)


def split_heads(array):
    return array.reshape(array.shape[0], array.shape[1], HEADS, HEAD_DIM)


def online_block(state, query_heads, query_pairs, key_block, value_block, key_pairs):
    highest, total, summed = state
    scores = jnp.einsum(
        "rqhd,rkhd->rhqk", query_heads, split_heads(key_block), preferred_element_type=jnp.float32
    ) * HEAD_DIM ** (-0.5)
    allowed = query_pairs[:, None, :, None] == key_pairs[:, None, None, :]
    masked = jnp.where(allowed, scores, NEGATIVE)
    new_high = jnp.maximum(highest, jnp.max(masked, axis=3))
    weights = jnp.where(allowed, jnp.exp(masked - new_high[..., None]), 0.0)
    factor = jnp.exp(highest - new_high)
    total = total * factor + jnp.sum(weights, axis=3)
    summed = summed * jnp.swapaxes(factor, 1, 2)[..., None] + jnp.einsum(
        "rhqk,rkhd->rqhd",
        weights.astype(jnp.bfloat16),
        split_heads(value_block),
        preferred_element_type=jnp.float32,
    )
    return (new_high, total, summed)


def tile_terms(queries, out_grad, log_total, delta, query_pairs, keys, values, key_pairs):
    scale = HEAD_DIM ** (-0.5)
    query_heads = split_heads(queries)
    grad_heads = split_heads(out_grad)
    key_heads = split_heads(keys)
    value_heads = split_heads(values)
    scores = (
        jnp.einsum("rqhd,rkhd->rhqk", query_heads, key_heads, preferred_element_type=jnp.float32)
        * scale
    )
    allowed = query_pairs[:, None, :, None] == key_pairs[:, None, None, :]
    weights = jnp.where(
        allowed, jnp.exp(jnp.where(allowed, scores, NEGATIVE) - log_total[..., None]), 0.0
    )
    weight_grad = jnp.einsum(
        "rqhd,rkhd->rhqk", grad_heads, value_heads, preferred_element_type=jnp.float32
    )
    score_grad = (weights * (weight_grad - delta[..., None])).astype(jnp.bfloat16)
    query_term = (
        jnp.einsum("rhqk,rkhd->rqhd", score_grad, key_heads, preferred_element_type=jnp.float32)
        * scale
    )
    key_term = (
        jnp.einsum("rhqk,rqhd->rkhd", score_grad, query_heads, preferred_element_type=jnp.float32)
        * scale
    )
    value_term = jnp.einsum(
        "rhqk,rqhd->rkhd",
        weights.astype(jnp.bfloat16),
        grad_heads,
        preferred_element_type=jnp.float32,
    )
    return (
        query_term.reshape(queries.shape),
        key_term.reshape(keys.shape),
        value_term.reshape(values.shape),
    )


def general_body(
    tokens,
    pair_lengths,
    joint_weight,
    query_bias,
    value_bias,
    out_weight,
    out_bias,
    first_gain,
    first_shift,
    up_weight,
    up_bias,
    down_weight,
    down_bias,
    second_gain,
    second_shift,
    cotangent,
):
    rows_here, seq_here, width = tokens.shape
    count = lax.axis_size("seq")
    cycle_index = lax.axis_index("seq")
    ends = jnp.cumsum(pair_lengths, axis=1)
    offsets = jnp.arange(seq_here, dtype=jnp.int32)
    own_pairs = pair_index(cycle_index * seq_here + offsets, ends)
    block_shape = (rows_here, seq_here, width)
    flat = tokens.reshape(rows_here * seq_here, width)
    projected = jnp.dot(flat, joint_weight, preferred_element_type=jnp.float32)
    queries = (projected[:, :width] + query_bias).astype(jnp.bfloat16).reshape(block_shape)
    keys = projected[:, width : 2 * width].astype(jnp.bfloat16).reshape(block_shape)
    values = (projected[:, 2 * width :] + value_bias).astype(jnp.bfloat16).reshape(block_shape)
    query_heads = split_heads(queries)
    initial = (
        jnp.full((rows_here, HEADS, seq_here), NEGATIVE, jnp.float32),
        jnp.zeros((rows_here, HEADS, seq_here), jnp.float32),
        jnp.zeros((rows_here, seq_here, HEADS, HEAD_DIM), jnp.float32),
    )
    key_piece = lax.all_gather(keys, "seq", axis=1, tiled=True)
    value_piece = lax.all_gather(values, "seq", axis=1, tiled=True)
    length = key_piece.shape[1]
    block = math.gcd(length, seq_here)

    def one_block(index, inner_state):
        first = index * block
        key_block = lax.dynamic_slice_in_dim(key_piece, first, block, 1)
        value_block = lax.dynamic_slice_in_dim(value_piece, first, block, 1)
        key_pairs = pair_index(first + jnp.arange(block, dtype=jnp.int32), ends)
        return online_block(inner_state, query_heads, own_pairs, key_block, value_block, key_pairs)

    highest, total, summed = lax.fori_loop(0, length // block, one_block, initial)
    log_total = highest + jnp.log(total)
    attended = (
        (summed / jnp.swapaxes(total, 1, 2)[..., None]).astype(jnp.bfloat16).reshape(flat.shape)
    )
    branch = jnp.dot(attended, out_weight, preferred_element_type=jnp.float32) + out_bias
    first_sum = flat.astype(jnp.float32) + branch
    normed, first_back = jax.vjp(layer_norm, first_sum, first_gain, first_shift)
    normed_low = normed.astype(jnp.bfloat16)
    inner = jnp.dot(normed_low, up_weight, preferred_element_type=jnp.float32) + up_bias
    activated_full, gelu_back = jax.vjp(gelu_exact, inner)
    activated = activated_full.astype(jnp.bfloat16)
    feed = jnp.dot(activated, down_weight, preferred_element_type=jnp.float32) + down_bias
    second_sum = normed + feed
    result, second_back = jax.vjp(layer_norm, second_sum, second_gain, second_shift)
    outputs = result.astype(jnp.bfloat16).reshape(tokens.shape)
    second_grad, second_gain_grad, second_shift_grad = second_back(
        cotangent.astype(jnp.float32).reshape(flat.shape)
    )
    feed_grad = second_grad.astype(jnp.bfloat16)
    down_grad = jnp.einsum("ti,tj->ij", activated, feed_grad, preferred_element_type=jnp.float32)
    down_bias_grad = jnp.sum(feed_grad.astype(jnp.float32), axis=0)
    activated_grad = jnp.einsum(
        "tj,ij->ti", feed_grad, down_weight, preferred_element_type=jnp.float32
    )
    inner_grad = gelu_back(activated_grad)[0].astype(jnp.bfloat16)
    up_grad = jnp.einsum("ti,tj->ij", normed_low, inner_grad, preferred_element_type=jnp.float32)
    up_bias_grad = jnp.sum(inner_grad.astype(jnp.float32), axis=0)
    normed_grad = second_grad + jnp.einsum(
        "tj,ij->ti", inner_grad, up_weight, preferred_element_type=jnp.float32
    )
    first_grad, first_gain_grad, first_shift_grad = first_back(normed_grad)
    branch_grad = first_grad.astype(jnp.bfloat16)
    out_grad = jnp.einsum("ti,tj->ij", attended, branch_grad, preferred_element_type=jnp.float32)
    out_bias_grad = jnp.sum(branch_grad.astype(jnp.float32), axis=0)
    attended_grad = jnp.einsum(
        "tj,ij->ti", branch_grad, out_weight, preferred_element_type=jnp.float32
    ).astype(jnp.bfloat16)
    delta = jnp.sum(
        (attended_grad.astype(jnp.float32) * attended.astype(jnp.float32)).reshape(
            rows_here, seq_here, HEADS, HEAD_DIM
        ),
        axis=3,
    )
    delta = jnp.swapaxes(delta, 1, 2)
    attended_grad = attended_grad.reshape(block_shape)
    zeros_block = jnp.zeros(block_shape, jnp.float32)

    def send_key_sums(sums):
        return (
            from_behind(sums[0].astype(jnp.bfloat16), "seq", 1).astype(jnp.float32),
            from_behind(sums[1].astype(jnp.bfloat16), "seq", 1).astype(jnp.float32),
        )

    def key_work(turn, pair_block, sums, query_sum):
        anchor = (cycle_index - turn) % count
        key_pairs = pair_index(anchor * seq_here + offsets, ends)
        query_term, key_term, value_term = tile_terms(
            queries,
            attended_grad,
            log_total,
            delta,
            own_pairs,
            pair_block[0],
            pair_block[1],
            key_pairs,
        )
        return ((sums[0] + key_term, sums[1] + value_term), query_sum + query_term)

    def key_turn(turn, state):
        pair_block, sums, query_sum = state
        sums, query_sum = key_work(turn, pair_block, sums, query_sum)
        sums = send_key_sums(sums)
        pair_block = from_behind((pair_block[0], pair_block[1]), "seq", 1)
        return (pair_block, sums, query_sum)

    pair_block, sums, query_sum = lax.fori_loop(
        0, count - 1, key_turn, ((keys, values), (zeros_block, zeros_block), zeros_block)
    )
    sums, query_sum = key_work(count - 1, pair_block, sums, query_sum)
    key_sum, value_sum = send_key_sums(sums)
    query_low = query_sum.astype(jnp.bfloat16).reshape(flat.shape)
    key_low = key_sum.astype(jnp.bfloat16).reshape(flat.shape)
    value_low = value_sum.astype(jnp.bfloat16).reshape(flat.shape)
    joint_low = jnp.concatenate([query_low, key_low, value_low], axis=1)
    joint_grad = jnp.einsum("ti,tj->ij", flat, joint_low, preferred_element_type=jnp.float32)
    query_bias_grad = jnp.sum(query_low.astype(jnp.float32), axis=0)
    value_bias_grad = jnp.sum(value_low.astype(jnp.float32), axis=0)
    token_grad = first_grad + jnp.einsum(
        "tj,ij->ti", joint_low, joint_weight, preferred_element_type=jnp.float32
    )
    gradients = (
        joint_grad,
        query_bias_grad,
        value_bias_grad,
        out_grad,
        out_bias_grad,
        first_gain_grad,
        first_shift_grad,
        up_grad,
        up_bias_grad,
        down_grad,
        down_bias_grad,
        second_gain_grad,
        second_shift_grad,
    )
    shares = (
        lax.psum_scatter(
            gradients[0].astype(jnp.bfloat16), "seq", scatter_dimension=0, tiled=True
        ).astype(jnp.float32),
        lax.psum_scatter(
            gradients[1].astype(jnp.bfloat16), "seq", scatter_dimension=0, tiled=True
        ).astype(jnp.float32),
        lax.psum_scatter(
            gradients[2].astype(jnp.bfloat16), "seq", scatter_dimension=0, tiled=True
        ).astype(jnp.float32),
        lax.psum_scatter(
            gradients[3].astype(jnp.bfloat16), "seq", scatter_dimension=0, tiled=True
        ).astype(jnp.float32),
        lax.psum_scatter(
            gradients[4].astype(jnp.bfloat16), "seq", scatter_dimension=0, tiled=True
        ).astype(jnp.float32),
        lax.psum_scatter(
            gradients[5].astype(jnp.bfloat16), "seq", scatter_dimension=0, tiled=True
        ).astype(jnp.float32),
        lax.psum_scatter(
            gradients[6].astype(jnp.bfloat16), "seq", scatter_dimension=0, tiled=True
        ).astype(jnp.float32),
        lax.psum_scatter(
            gradients[7].astype(jnp.bfloat16), "seq", scatter_dimension=0, tiled=True
        ).astype(jnp.float32),
        lax.psum_scatter(
            gradients[8].astype(jnp.bfloat16), "seq", scatter_dimension=0, tiled=True
        ).astype(jnp.float32),
        lax.psum_scatter(
            gradients[9].astype(jnp.bfloat16), "seq", scatter_dimension=0, tiled=True
        ).astype(jnp.float32),
        lax.psum_scatter(
            gradients[10].astype(jnp.bfloat16), "seq", scatter_dimension=0, tiled=True
        ).astype(jnp.float32),
        lax.psum_scatter(
            gradients[11].astype(jnp.bfloat16), "seq", scatter_dimension=0, tiled=True
        ).astype(jnp.float32),
        lax.psum_scatter(
            gradients[12].astype(jnp.bfloat16), "seq", scatter_dimension=0, tiled=True
        ).astype(jnp.float32),
    )
    shares = (
        lax.psum(shares[0].astype(jnp.bfloat16), "rows").astype(jnp.float32),
        lax.psum(shares[1].astype(jnp.bfloat16), "rows").astype(jnp.float32),
        lax.psum(shares[2].astype(jnp.bfloat16), "rows").astype(jnp.float32),
        lax.psum(shares[3].astype(jnp.bfloat16), "rows").astype(jnp.float32),
        lax.psum(shares[4].astype(jnp.bfloat16), "rows").astype(jnp.float32),
        lax.psum(shares[5].astype(jnp.bfloat16), "rows").astype(jnp.float32),
        lax.psum(shares[6].astype(jnp.bfloat16), "rows").astype(jnp.float32),
        lax.psum(shares[7].astype(jnp.bfloat16), "rows").astype(jnp.float32),
        lax.psum(shares[8].astype(jnp.bfloat16), "rows").astype(jnp.float32),
        lax.psum(shares[9].astype(jnp.bfloat16), "rows").astype(jnp.float32),
        lax.psum(shares[10].astype(jnp.bfloat16), "rows").astype(jnp.float32),
        lax.psum(shares[11].astype(jnp.bfloat16), "rows").astype(jnp.float32),
        lax.psum(shares[12].astype(jnp.bfloat16), "rows").astype(jnp.float32),
    )
    return (outputs, token_grad.reshape(tokens.shape)) + tuple(shares)


WIDTH = HEADS * HEAD_DIM
HALF = WIDTH // 2
FF = 4 * WIDTH
BLOCK = 128
OWN = 2 * BLOCK
LANES = 128
PAIRS_OF_HEADS = HALF // LANES
JOINT_ROWS = 80
JOINT_FIRST = 48
JOINT_SECOND = JOINT_ROWS - JOINT_FIRST
UP_ROWS = 128
DOWN_ROWS = 96
EXT = OWN + 16
DOWN_SENT = 2 * DOWN_ROWS
FLOAT = jnp.float32
LOW = jnp.bfloat16
AXES = ("seq", "rows")


def kernel_params(megabytes):
    return pltpu.CompilerParams(vmem_limit_bytes=megabytes << 20)


def shaped(shape, kind):
    return jax.ShapeDtypeStruct(shape, kind)


def whole(shape):
    return pl.BlockSpec(shape, lambda *_: (0,) * len(shape))


def cost(flops, moved, exps=0):
    return pl.CostEstimate(flops=1024, bytes_accessed=1024, transcendentals=0)


def dot(left, right):
    return lax.dot_general(left, right, (((1,), (0,)), ((), ())), preferred_element_type=FLOAT)


def dot_nt(left, right):
    return lax.dot_general(left, right, (((1,), (1,)), ((), ())), preferred_element_type=FLOAT)


def call(kernel, name, place, inputs, outputs, scratch=(), grid=(1,), scalars=(), after=(), megabytes=28, work=None, aliases=()):
    prefetch = 1 + len(scalars)
    given, made = len(inputs), len(outputs)

    def ordered(*refs):
        first = prefetch + given
        mark = refs[first + len(after) + made]
        mark[...] = jnp.zeros_like(mark)
        kernel(*refs[:first], *refs[first + len(after) : first + len(after) + made], *refs[first + len(after) + made + 1 :])

    results = pl.pallas_call(
        ordered,
        grid_spec=pltpu.PrefetchScalarGridSpec(
            num_scalar_prefetch=prefetch,
            grid=grid,
            in_specs=[spec for _, spec in inputs] + [pl.BlockSpec(memory_space=pl.ANY)] * len(after),
            out_specs=[spec for _, _, spec in outputs] + [whole((8, LANES))],
            scratch_shapes=list(scratch),
        ),
        out_shape=[shaped(shape, kind) for shape, kind, _ in outputs] + [shaped((8, LANES), FLOAT)],
        compiler_params=kernel_params(megabytes),
        cost_estimate=work,
        input_output_aliases={prefetch + source: target for source, target in aliases},
        name=name,
    )(place, *scalars, *[array for array, _ in inputs], *after)
    return results[:-1], results[-1]


def plain(array):
    return array, whole(array.shape)


def made(shape, kind):
    return shape, kind, whole(shape)


def device_at(z, y, x, c):
    return ((z * 2 + y) * 2 + x) * 2 + c


def permute(value, target):
    pairs = []
    for z in range(4):
        for y in range(2):
            for x in range(2):
                for c in range(2):
                    pairs.append((device_at(z, y, x, c), device_at(*target(z, y, x, c))))
    return lax.ppermute(value, AXES, pairs)


def core_swap(value):
    return permute(value, lambda z, y, x, c: (z, y, x, 1 - c))


def x_swap(value):
    return permute(value, lambda z, y, x, c: (z, y, 1 - x, c))


def y_swap(value):
    return permute(value, lambda z, y, x, c: (z, 1 - y, x, c))


def z_swap(value, bits):
    return permute(value, lambda z, y, x, c: (z ^ bits, y, x, c))


def row_swap(value, second):
    return permute(value, lambda z, y, x, c: (2 * c + (z % 2 ^ second), y, x, z // 2))


def first_positions(place):
    z, y, c = place[0], place[1], place[3]
    bases = []
    for core, line in ((c, y), (1 - c, y), (c, 1 - y), (1 - c, 1 - y)):
        for second in (0, 1):
            parity = z % 2
            parity = 1 - parity if second else parity
            bases.append((2 * (2 * core + parity) + line) * BLOCK)
    return bases


def pair_ends(place, own_lengths, peer_lengths):
    z, c = place[0], place[3]
    here = (z // 2) == c
    line = z % 2
    ends, end = [], 0
    for pair in range(own_lengths.shape[1]):
        end = end + jnp.where(here, own_lengths[line, pair], peer_lengths[line, pair])
        ends.append(end)
    return ends


def pairs_along(base, ends, axis):
    shape = (8, BLOCK) if axis == 1 else (BLOCK, LANES)
    position = base + lax.broadcasted_iota(jnp.int32, shape, axis)
    ids = jnp.zeros(shape, jnp.int32)
    for end in ends:
        ids = ids + (position >= end).astype(jnp.int32)
    return ids


def head_mask(rows):
    return lax.broadcasted_iota(jnp.int32, (rows, LANES), 1) < HEAD_DIM


def columns_kernel(place, columns, query_bias, value_bias, out, query_row, value_row):
    out[0] = columns[...]
    query_row[...] = query_bias[...]
    value_row[...] = value_bias[...]


def own_columns(place, joint_weight, query_bias, value_bias):
    half_row = pl.BlockSpec((1, HALF), lambda i, place: (0, place[3]))
    results, _ = call(
        columns_kernel,
        "own_columns",
        place,
        [
            (joint_weight, pl.BlockSpec((WIDTH, HALF), lambda i, place: (0, 2 * i + place[3]))),
            (row_of(query_bias), half_row),
            (row_of(value_bias), half_row),
        ],
        [((3, WIDTH, HALF), LOW, pl.BlockSpec((1, WIDTH, HALF), lambda i, place: (i, 0, 0)))]
        + [made((1, HALF), FLOAT)] * 2,
        grid=(3,),
        work=cost(1e6, 4e6),
    )
    return results


def first_attention_kernel(
    place, own_lengths, peer_lengths, t0, t1, t2, t3, columns, qb, vb, q_out, k_out, v_out, summed, stats, bias
):
    bases = first_positions(place)
    ends = pair_ends(place, own_lengths, peer_lengths)
    tokens = jnp.concatenate([block[...] for block in (t0, t1, t2, t3)], axis=0)
    queries = dot(tokens, columns[0]) + qb[...]
    q_out[...] = (queries.astype(LOW).astype(FLOAT) * HEAD_DIM**-0.5).astype(LOW)
    k_out[...] = dot(tokens, columns[1]).astype(LOW)
    v_out[...] = (dot(tokens, columns[2]) + vb[...]).astype(LOW)
    fill_bias(bias, bases[:4], bases[:4], ends)
    stats[...] = jnp.zeros_like(stats)
    for pair in range(PAIRS_OF_HEADS):
        lanes = pl.ds(pair * LANES, LANES)
        scores = masked_scores(k_out[:, lanes], q_out[:, lanes], bias)
        highest = jnp.max(scores, axis=0, keepdims=True)
        weights = jnp.exp(scores - highest)
        summed[pair] = dot(turned(v_out[:, lanes]), weights.astype(LOW))
        stats[2 * pair : 2 * pair + 1, :] = highest
        stats[2 * pair + 1 : 2 * pair + 2, :] = column_sum(weights)


def turned(array):
    return jnp.transpose(array.astype(FLOAT)).astype(LOW)


def masked_scores(keys, queries, bias):
    mask = bias[...]
    chosen = jnp.concatenate(halves_of(queries), axis=0)
    return dot_nt(keys, chosen) + jnp.concatenate([mask, mask], axis=1)


def fill_bias(bias, query_bases, key_bases, ends):
    key_ids = [pairs_along(base, ends, 1)[0:1] for base in key_bases]
    for i, base in enumerate(query_bases):
        query_ids = pairs_along(base, ends, 0)
        for j in range(len(key_bases)):
            bias[pl.ds(i * BLOCK, BLOCK), pl.ds(j * BLOCK, BLOCK)] = jnp.where(query_ids == key_ids[j], 0.0, NEGATIVE)


def halves_of(array):
    left = head_mask(array.shape[0])
    zeros = jnp.zeros_like(array)
    return jnp.where(left, array, zeros), jnp.where(left, zeros, array)


def first_attention(place, lengths, blocks, columns, query_bias, value_bias, after=()):
    return call(
        first_attention_kernel,
        "first_attention",
        place,
        [plain(array) for array in (*blocks, columns, query_bias, value_bias)],
        [made((512, HALF), LOW)] * 3 + [made((PAIRS_OF_HEADS, LANES, 1024), FLOAT), made((8, 1024), FLOAT)],
        scratch=[pltpu.VMEM((512, 512), FLOAT)],
        scalars=lengths,
        after=after,
        work=cost(4e9, 8e6, 3e6),
    )


def attention_kernel(
    place, own_lengths, peer_lengths, t0, t1, t2, t3, columns, vb, q, summed, stats,
    att_out, k_out, v_out, log_out, bias,
):
    bases = first_positions(place)
    ends = pair_ends(place, own_lengths, peer_lengths)
    tokens = jnp.concatenate([block[...] for block in (t0, t1, t2, t3)], axis=0)
    k_out[...] = dot(tokens, columns[1]).astype(LOW)
    v_out[...] = (dot(tokens, columns[2]) + vb[...]).astype(LOW)
    fill_bias(bias, bases[4:], bases[:4], ends)
    log_out[...] = jnp.zeros_like(log_out)
    top = lax.broadcasted_iota(jnp.int32, (LANES, 512), 0) < HEAD_DIM
    for pair in range(PAIRS_OF_HEADS):
        lanes = pl.ds(pair * LANES, LANES)
        scores = masked_scores(k_out[:, lanes], q[:, lanes], bias)
        before = stats[2 * pair : 2 * pair + 1, :]
        highest = jnp.maximum(before, jnp.max(scores, axis=0, keepdims=True))
        weights = jnp.exp(scores - highest)
        shrink = jnp.exp(before - highest)
        sums = column_sum(weights) + shrink * stats[2 * pair + 1 : 2 * pair + 2, :]
        total = (dot(turned(v_out[:, lanes]), weights.astype(LOW)) + shrink * summed[pair]) / sums
        att_out[:, lanes] = jnp.transpose(jnp.where(top, total[:, 0:512], total[:, 512:])).astype(LOW)
        logs = highest + jnp.log(sums)
        log_out[2 * pair : 2 * pair + 1, :] = logs[:, 0:512]
        log_out[2 * pair + 1 : 2 * pair + 2, :] = logs[:, 512:]


def attention(place, lengths, blocks, columns, value_bias, q, summed, stats, after=()):
    return call(
        attention_kernel,
        "attention",
        place,
        [plain(array) for array in (*blocks, columns, value_bias, q, summed, stats)],
        [made((512, HALF), LOW)] * 3 + [made((8, 512), FLOAT)],
        scratch=[pltpu.VMEM((512, 512), FLOAT)],
        scalars=lengths,
        after=after,
        work=cost(4e9, 8e6, 3e6),
    )


def centred_norm(value):
    mean = jnp.mean(value, axis=-1, keepdims=True)
    centred = value - mean
    spread = jnp.mean(centred * centred, axis=-1, keepdims=True)
    inverse = lax.rsqrt(spread + EPSILON)
    return centred * inverse, inverse


def norm_back(grad, unit, inverse):
    mean = jnp.mean(grad, axis=-1, keepdims=True)
    along = jnp.mean(grad * unit, axis=-1, keepdims=True)
    return (grad - mean - unit * along) * inverse


def column_sum(value):
    return jnp.sum(value, axis=0, keepdims=True)


def forward_kernel(
    place, att, att_got, wo_own, wo_other, out_bias, x0, x1, gain1, shift1, up, up_bias, down,
    down_bias, gain2, shift2, cot0, cot1,
    result0, result1, feed_ext, second_grad, act_keep, act_send, slope, unit1, inverse1, normed_low, normed_t, att_t, sums,
    act_t,
):
    c = place[3]
    tokens = jnp.concatenate([x0[...], x1[...]], axis=0).astype(FLOAT)
    att_own, att_other = att[0:OWN], att_got[OWN:]
    branch = dot(att_own, wo_own[...]) + dot(att_other, wo_other[...]) + out_bias[...]
    unit, inverse = centred_norm(tokens + branch)
    unit1[...] = unit
    inverse1[...] = jnp.broadcast_to(inverse, (OWN, LANES))
    normed = unit * gain1[...] + shift1[...]
    low = normed.astype(LOW)
    normed_low[...] = low
    normed_t[...] = jnp.transpose(normed).astype(LOW)
    mine = pl.ds(pl.multiple_of(c * HALF, HALF), HALF)
    other = pl.ds(pl.multiple_of((1 - c) * HALF, HALF), HALF)
    att_t[mine, :] = jnp.transpose(att[...].astype(FLOAT)).astype(LOW)
    att_t[other, 0:OWN] = jnp.transpose(att_other.astype(FLOAT)).astype(LOW)
    att_t[other, OWN:] = jnp.transpose(att_got[0:OWN].astype(FLOAT)).astype(LOW)
    inner = dot(low, up[...]) + up_bias[...]
    below = 0.5 + 0.5 * lax.erf(inner * math.sqrt(0.5))
    density = jnp.exp(inner * inner * -0.5) * (1.0 / math.sqrt(2.0 * math.pi))
    activated = inner * below
    slope[...] = (below + inner * density).astype(LOW)
    act_t[...] = jnp.transpose(activated).astype(LOW).reshape(16, 2, DOWN_ROWS, OWN)
    act_keep[...] = act_t[:, c]
    act_send[...] = act_t[:, 1 - c]
    feed = dot(activated.astype(LOW), down[...])
    unit, inverse = centred_norm(normed + feed + down_bias[...])
    result = (unit * gain2[...] + shift2[...]).astype(LOW)
    result0[...] = result[0:BLOCK]
    result1[...] = result[BLOCK:]
    cotangent = jnp.concatenate([cot0[0:BLOCK], cot1[0:BLOCK]], axis=0).astype(FLOAT)
    grad = norm_back(cotangent * gain2[...], unit, inverse)
    second_grad[...] = grad
    low_grad = grad.astype(LOW)
    rows = jnp.concatenate(
        [
            column_sum(cotangent * unit),
            column_sum(cotangent),
            column_sum(low_grad.astype(FLOAT)),
            jnp.zeros((5, WIDTH), FLOAT),
        ],
        axis=0,
    )
    sums[...] = rows
    feed_ext[0:OWN] = low_grad
    feed_ext[OWN:] = jnp.concatenate([rows, jnp.zeros_like(rows)], axis=0).astype(LOW)


def row_of(vector):
    return vector.reshape(1, vector.shape[0])


def forward(place, att, att_got, tokens, cotangents, weights, after=()):
    chunk = FF

    def vector(name):
        return plain(row_of(weights[name]))

    units = ((16, DOWN_ROWS, OWN), LOW, pl.BlockSpec((16, DOWN_ROWS, OWN), lambda i, place: (i, 0, 0)))
    return call(
        forward_kernel,
        "forward",
        place,
        [
            plain(att),
            plain(att_got),
            (weights["out"], pl.BlockSpec((HALF, WIDTH), lambda i, place: (place[3], 0))),
            (weights["out"], pl.BlockSpec((HALF, WIDTH), lambda i, place: (1 - place[3], 0))),
            vector("out_bias"), plain(tokens[0]), plain(tokens[1]), vector("gain1"), vector("shift1"),
            (weights["up"], pl.BlockSpec((WIDTH, chunk), lambda i, place: (0, i))),
            (row_of(weights["up_bias"]), pl.BlockSpec((1, chunk), lambda i, place: (0, i))),
            (weights["down"], pl.BlockSpec((chunk, WIDTH), lambda i, place: (i, 0))),
            vector("down_bias"), vector("gain2"), vector("shift2"), plain(cotangents[0]), plain(cotangents[1]),
        ],
        [
            made((BLOCK, WIDTH), LOW), made((BLOCK, WIDTH), LOW), made((EXT, WIDTH), LOW),
            made((OWN, WIDTH), FLOAT), units, units,
            ((OWN, FF), LOW, pl.BlockSpec((OWN, chunk), lambda i, place: (0, i))),
            made((OWN, WIDTH), FLOAT), made((OWN, LANES), FLOAT), made((OWN, WIDTH), LOW),
            made((WIDTH, OWN), LOW), made((WIDTH, 512), LOW), made((8, WIDTH), FLOAT),
        ],
        scratch=[pltpu.VMEM((16, 2, DOWN_ROWS, OWN), LOW)],
        after=after,
        work=cost(2.7e9, 20e6, 2e6),
    )


def split_units(place, units, px_send, px, qy_send, qy):
    y, x = place[1], place[2]
    half = units.shape[2] // 2
    for line in range(2):
        px[0, line] = units[line, x, 0:half]
        px_send[0, line] = units[line, 1 - x, 0:half]
    for side in range(2):
        qy[0, side] = units[y, side, half:]
        qy_send[0, side] = units[1 - y, side, half:]


def unit_outputs(rows, width):
    shape = (4, 2, rows // 2, width)
    return [(shape, LOW, pl.BlockSpec((1,) + shape[1:], lambda i, place: (i, 0, 0, 0)))] * 4


def down_kernel(place, act, act_got, feed, feed_got, px_send, px, qy_send, qy, units):
    shape = (4 * DOWN_ROWS, OWN)
    total = dot(act[...].reshape(shape), feed[0:OWN]) + dot(act_got[...].reshape(shape), feed_got[0:OWN])
    units[...] = total.astype(LOW).reshape(units.shape)
    split_units(place, units, px_send, px, qy_send, qy)


def down_units(place, act, act_got, feed, feed_got, after=()):
    block = pl.BlockSpec((4, DOWN_ROWS, OWN), lambda i, place: (i, 0, 0))
    return call(
        down_kernel,
        "down_units",
        place,
        [(act, block), (act_got, block), plain(feed), plain(feed_got)],
        unit_outputs(DOWN_ROWS, WIDTH),
        scratch=[pltpu.VMEM((2, 2, DOWN_ROWS, WIDTH), LOW)],
        grid=(4,),
        after=after,
        work=cost(0.6e9, 3.5e6),
    )


def backward_kernel(
    place, feed_ext, slope, up, down, second_grad, unit1, inverse1, gain1, wo_own, wo_other,
    inner0, inner1, send0, send1, first_grad, branch_own, back_own, misc, sums,
    inner, branch,
):
    c = place[3]
    grad = (dot_nt(feed_ext[0:OWN], down[...]) * slope[...].astype(FLOAT)).astype(LOW)
    inner[...] = grad
    for target, index in ((inner0, c), (inner1, 2 + c), (send0, 1 - c), (send1, 3 - c)):
        target[...] = inner[:, pl.ds(pl.multiple_of(index * WIDTH, LANES), WIDTH)]
    inner_sum = column_sum(grad.astype(FLOAT))
    total = second_grad[...] + dot_nt(grad, up[...])
    unit = unit1[...]
    grad1 = norm_back(total * gain1[...], unit, inverse1[:, 0:1])
    first_grad[...] = grad1
    low = grad1.astype(LOW)
    branch[...] = low
    rows = jnp.concatenate(
        [
            column_sum(total * unit),
            column_sum(total),
            column_sum(low.astype(FLOAT)),
            jnp.zeros((1, WIDTH), FLOAT),
        ]
        + [inner_sum[:, index * WIDTH : (index + 1) * WIDTH] for index in range(4)],
        axis=0,
    )
    sums[...] = rows
    branch_own[...] = branch[:, pl.ds(pl.multiple_of(c * HALF, LANES), HALF)]
    back_own[...] = dot_nt(low, wo_own[...]).astype(LOW)
    misc[0:OWN, 0:HALF] = branch[:, pl.ds(pl.multiple_of((1 - c) * HALF, LANES), HALF)]
    misc[0:OWN, HALF:] = dot_nt(low, wo_other[...]).astype(LOW)
    misc[OWN:] = jnp.concatenate([rows, jnp.zeros_like(rows)], axis=0).astype(LOW)


def backward(place, feed_ext, slope, second_grad, unit1, inverse1, weights, after=()):
    chunk = FF
    return call(
        backward_kernel,
        "backward",
        place,
        [
            plain(feed_ext),
            (slope, pl.BlockSpec((OWN, chunk), lambda i, place: (0, i))),
            (weights["up"], pl.BlockSpec((WIDTH, chunk), lambda i, place: (0, i))),
            (weights["down"], pl.BlockSpec((chunk, WIDTH), lambda i, place: (i, 0))),
            plain(second_grad), plain(unit1), plain(inverse1), plain(row_of(weights["gain1"])),
            (weights["out"], pl.BlockSpec((HALF, WIDTH), lambda i, place: (place[3], 0))),
            (weights["out"], pl.BlockSpec((HALF, WIDTH), lambda i, place: (1 - place[3], 0))),
        ],
        [made((OWN, WIDTH), LOW)] * 4
        + [
            made((OWN, WIDTH), FLOAT), made((OWN, HALF), LOW), made((OWN, HALF), LOW), made((EXT, WIDTH), LOW),
            made((8, WIDTH), FLOAT),
        ],
        scratch=[pltpu.VMEM((OWN, FF), LOW), pltpu.VMEM((OWN, WIDTH), LOW)],
        after=after,
        work=cost(2.7e9, 16e6),
    )


def up_kernel(
    place, normed_t, normed_got, inner0, inner1, got0, got1, att_t, branch, misc, sums0, sums1, feed_got,
    x_send, y_send, px, qy, units, normed_got_t,
):
    z = pl.program_id(0)
    y, x = place[1], place[2]

    @pl.when(z == 0)
    def _():
        normed_got_t[...] = jnp.transpose(normed_got[...].astype(FLOAT)).astype(LOW)

    theirs = normed_got_t[pl.ds(pl.multiple_of(z * 192, 32), 192), :]
    outer = dot(att_t[:, 0:OWN], branch[...]) + dot(att_t[:, OWN:], misc[0:OWN, 0:HALF])
    for side, inner, got, sums, pair in ((0, inner0, got0, sums0, feed_got), (1, inner1, got1, sums1, misc)):
        grad = dot(normed_t[...], inner[...]) + dot(theirs, got[...])
        vectors = sums[...] + pair[OWN:].astype(FLOAT)[0:8]
        for line in range(2):
            first = line * 96 + side * 48
            rest = jnp.concatenate([outer[first : first + 24], outer[first + 24 : first + 48]], axis=1)
            units[line, side] = jnp.concatenate(
                [grad[line * 96 : line * 96 + 96], rest, vectors], axis=0
            ).astype(LOW)
    half = UP_ROWS // 2
    for index in range(2):
        rows = pl.ds(pl.multiple_of(DOWN_SENT + (z * 2 + index) * half, half), half)
        px[0, index] = units[index, x, 0:half]
        x_send[rows, :] = units[index, 1 - x, 0:half]
        qy[0, index] = units[y, index, half:]
        y_send[rows, :] = units[1 - y, index, half:]


def up_units(place, normed_t, normed_got, inner, got, att_t, branch, misc, sums0, sums1, feed_got, after=()):
    rows = pl.BlockSpec((192, OWN), lambda i, place: (i, 0))
    return call(
        up_kernel,
        "up_units",
        place,
        [
            (normed_t, rows), plain(normed_got), plain(inner[0]), plain(inner[1]), plain(got[0]), plain(got[1]),
            (att_t, pl.BlockSpec((192, 512), lambda i, place: (i, 0))),
            plain(branch), plain(misc), plain(sums0), plain(sums1), plain(feed_got),
        ],
        [made((DOWN_SENT + 4 * UP_ROWS, WIDTH), LOW)] * 2 + unit_outputs(UP_ROWS, WIDTH)[:2],
        scratch=[pltpu.VMEM((2, 2, UP_ROWS, WIDTH), LOW), pltpu.VMEM((WIDTH, OWN), LOW)],
        grid=(4,),
        after=after,
        work=cost(0.9e9, 5e6),
    )


def attention_back_kernel(
    place, own_lengths, peer_lengths, q, k0, k1, v0, v1, log_total, att, back0, misc,
    dq_out, dk_out, dv_out, bias,
):
    bases = first_positions(place)
    ends = pair_ends(place, own_lengths, peer_lengths)
    query_ids = [pairs_along(base, ends, 1)[0:1] for base in bases[:4]]
    for j in range(8):
        key_ids = pairs_along(bases[j], ends, 0)
        for i in range(4):
            bias[pl.ds(j * BLOCK, BLOCK), pl.ds(i * BLOCK, BLOCK)] = jnp.where(
                key_ids == query_ids[i], 0.0, NEGATIVE
            )

    def one_pair(pair, carry):
        lanes = pl.ds(pl.multiple_of(pair * LANES, LANES), LANES)
        keys = jnp.concatenate([k0[:, lanes], k1[:, lanes]], axis=0)
        values = jnp.concatenate([v0[:, lanes], v1[:, lanes]], axis=0)
        keys_t = turned(keys)
        key_grad = jnp.zeros((1024, LANES), FLOAT)
        value_grad = jnp.zeros((1024, LANES), FLOAT)
        far = pl.ds(pl.multiple_of(HALF + pair * LANES, LANES), LANES)
        for part, back in ((0, back0[:, lanes]), (1, misc[0:OWN, far])):
            rows = pl.ds(part * OWN, OWN)
            product = jnp.transpose(back.astype(FLOAT) * att[rows, lanes].astype(FLOAT))
            delta = jnp.concatenate([column_sum(product[0:HEAD_DIM]), column_sum(product[HEAD_DIM:])], axis=1)
            logs = jnp.concatenate(
                [log_total[pl.ds(2 * pair, 1), rows], log_total[pl.ds(2 * pair + 1, 1), rows]], axis=1
            )
            chosen = jnp.concatenate(halves_of(q[rows, lanes]), axis=0)
            grads = jnp.concatenate(halves_of(back), axis=0)
            mask = bias[:, rows]
            weights = jnp.exp(dot_nt(keys, chosen) + jnp.concatenate([mask, mask], axis=1) - logs)
            score_grad = (weights * (dot_nt(values, grads) - delta)).astype(LOW)
            value_grad = value_grad + dot(weights.astype(LOW), grads)
            key_grad = key_grad + dot(score_grad, chosen)
            both = dot(keys_t, score_grad)
            query_grad_t = jnp.concatenate([both[0:HEAD_DIM, 0:OWN], both[HEAD_DIM:, OWN:]], axis=0)
            dq_out[rows, lanes] = (jnp.transpose(query_grad_t) * HEAD_DIM**-0.5).astype(LOW)
        dk_out[:, lanes] = key_grad.astype(LOW)
        dv_out[:, lanes] = value_grad.astype(LOW)
        return carry

    lax.fori_loop(0, PAIRS_OF_HEADS, one_pair, 0)


def attention_back(place, lengths, q, keys, values, log_total, att, back_own, misc, after=()):
    return call(
        attention_back_kernel,
        "attention_back",
        place,
        [plain(array) for array in (q, *keys, *values, log_total, att, back_own, misc)],
        [made((512, HALF), LOW), made((1024, HALF), LOW), made((1024, HALF), LOW)],
        scratch=[pltpu.VMEM((1024, 512), FLOAT)],
        scalars=lengths,
        after=after,
        work=cost(7e9, 6e6, 3e6),
    )


def token_kernel(place, dq, dk, dv, columns, own, own_send, far, far_send):
    for part, target in enumerate((own, own_send, far, far_send)):
        rows = pl.ds(part * OWN, OWN)
        total = dot_nt(dk[rows, :], columns[1]) + dot_nt(dv[rows, :], columns[2])
        if part < 2:
            total = total + dot_nt(dq[rows, :], columns[0])
        target[...] = total.astype(LOW)


def token_parts(place, dq, dk, dv, columns, after=()):
    return call(
        token_kernel,
        "token_parts",
        place,
        [plain(dq), plain(dk), plain(dv), plain(columns)],
        [made((OWN, WIDTH), LOW)] * 4,
        after=after,
        work=cost(1.5e9, 5e6),
    )


def token_last_kernel(place, own, own_got, across, first_grad, token0, token1):
    total = own[...].astype(FLOAT) + own_got[...].astype(FLOAT) + across[8 * JOINT_SECOND :].astype(FLOAT) + first_grad[...]
    total = total.astype(LOW)
    token0[...] = total[0:BLOCK]
    token1[...] = total[BLOCK:]


def token_last(place, arrays, after=()):
    return call(
        token_last_kernel,
        "token_last",
        place,
        [plain(array) for array in arrays],
        [made((BLOCK, WIDTH), LOW)] * 2,
        after=after,
        work=cost(1e6, 2e6),
    )


def back_rows_kernel(place, done0, done1, back0, back1, outputs, token_grad):
    odd = place[0] % 2
    outputs[odd] = done0[...]
    outputs[1 - odd] = done1[...]
    token_grad[odd] = back0[...].astype(FLOAT)
    token_grad[1 - odd] = back1[...].astype(FLOAT)


def back_rows(place, done, back, after=()):
    return call(
        back_rows_kernel,
        "back_rows",
        place,
        [plain(array) for array in (*done, *back)],
        [made((2, BLOCK, WIDTH), LOW), made((2, BLOCK, WIDTH), FLOAT)],
        after=after,
        work=cost(1e6, 2e6),
    )


def joint_kernel(
    place, t0, t1, t2, t3, t4, t5, t6, t7, dq, dk, dv, far, far_got, px_send, px, qy_send, qy, tokens_t, units
):
    y, x = place[1], place[2]
    qy_send[pl.ds(8 * JOINT_SECOND, OWN), :] = added(far[...], far_got[...])
    for index, block in enumerate((t0, t1, t2, t3, t4, t5, t6, t7)):
        tokens_t[:, pl.ds(index * BLOCK, BLOCK)] = jnp.transpose(block[...].astype(FLOAT)).astype(LOW)
    biases = jnp.concatenate([column_sum(dq[...].astype(FLOAT)), column_sum(dv[...].astype(FLOAT))], axis=1)
    biases = jnp.concatenate([biases, jnp.zeros((7, WIDTH), FLOAT)], axis=0)
    for z in range(4):
        rows = pl.ds(z * 192, 192)
        query = dot(tokens_t[rows, 0:512], dq[...])
        key = dot(tokens_t[rows, :], dk[...])
        value = dot(tokens_t[rows, :], dv[...])
        for line in range(2):
            for side in range(2):
                at = line * 96 + side * 48
                units[line, side, 0:JOINT_FIRST] = jnp.concatenate(
                    [query[at : at + 48], key[at : at + 48]], axis=1
                ).astype(LOW)
                rest = jnp.concatenate([value[at : at + 24], value[at + 24 : at + 48]], axis=1)
                units[line, side, JOINT_FIRST:] = jnp.concatenate([rest, biases], axis=0).astype(LOW)
        for line in range(2):
            px[z, line] = units[line, x, 0:JOINT_FIRST]
            px_send[z, line] = units[line, 1 - x, 0:JOINT_FIRST]
        for side in range(2):
            qy[z, side] = units[y, side, JOINT_FIRST:]
            qy_send[pl.ds((z * 2 + side) * JOINT_SECOND, JOINT_SECOND), :] = units[1 - y, side, JOINT_FIRST:]


def joint_units(place, blocks, dq, dk, dv, far, far_got, after=()):
    first, second = made((4, 2, JOINT_FIRST, WIDTH), LOW), made((4, 2, JOINT_SECOND, WIDTH), LOW)
    return call(
        joint_kernel,
        "joint_units",
        place,
        [plain(array) for array in (*blocks, dq, dk, dv, far, far_got)],
        [first, first, made((8 * JOINT_SECOND + OWN, WIDTH), LOW), second],
        scratch=[pltpu.VMEM((WIDTH, 1024), LOW), pltpu.VMEM((2, 2, JOINT_ROWS, WIDTH), LOW)],
        after=after,
        work=cost(1.5e9, 6e6),
    )


def added(left, right):
    return (left.astype(FLOAT) + right.astype(FLOAT)).astype(LOW)


def down_pair_kernel(place, px, px_got, qy, qy_got, x_in, y_in, x_send, y_send, p, q):
    y, x = place[1], place[2]
    p[0] = added(px[0, y], px_got[0, y])
    y_send[...] = added(px[0, 1 - y], px_got[0, 1 - y])
    q[0] = added(qy[0, x], qy_got[0, x])
    x_send[...] = added(qy[0, 1 - x], qy_got[0, 1 - x])


def down_pair_stage(place, arrays, x_send, y_send, after=()):
    half = DOWN_ROWS // 2
    block = pl.BlockSpec((1, 2, half, WIDTH), lambda i, place: (i, 0, 0, 0))
    sent = (x_send.shape, LOW, pl.BlockSpec((half, WIDTH), lambda i, place: (i, 0)))
    kept = ((4, half, WIDTH), LOW, pl.BlockSpec((1, half, WIDTH), lambda i, place: (i, 0, 0)))
    anywhere = pl.BlockSpec(memory_space=pl.ANY)
    return call(
        down_pair_kernel,
        "down_pair_stage",
        place,
        [(array, block) for array in arrays] + [(x_send, anywhere), (y_send, anywhere)],
        [sent, sent, kept, kept],
        grid=(4,),
        after=after,
        work=cost(1e6, 1e7),
        aliases=((4, 0), (5, 1)),
    )


def second_kernel(
    place, x_got, y_got, px, qy, down_p, down_q, x_send, y_send, p, q, down_send, down_keep
):
    z_here, y, x = place[0], place[1], place[2]
    half = UP_ROWS // 2
    for z in range(4):
        for got, have, own, keep, send in ((x_got, px, y, p, y_send), (y_got, qy, x, q, x_send)):
            at = DOWN_SENT + z * UP_ROWS
            mine = pl.ds(pl.multiple_of(at + own * half, half), half)
            other = pl.ds(pl.multiple_of(at + (1 - own) * half, half), half)
            keep[z] = added(have[z, own], got[mine, :])
            send[pl.ds(z * half, half), :] = added(have[z, 1 - own], got[other, :])
    low = z_here % 2
    small = DOWN_ROWS // 2
    for target, parity in ((down_keep, low), (down_send, 1 - low)):
        for high in range(2):
            index = 2 * high + parity
            rows = pl.ds(pl.multiple_of(index * small, small), small)
            target[high, 0:small] = added(down_p[index], y_got[rows, :])
            target[high, small:] = added(down_q[index], x_got[rows, :])


def second_stage(place, arrays, after=()):
    kept = made((4, UP_ROWS // 2, WIDTH), LOW)
    down = made((2, DOWN_ROWS, WIDTH), LOW)
    return call(
        second_kernel,
        "second_stage",
        place,
        [plain(array) for array in arrays],
        [made((OWN, WIDTH), LOW), made((OWN, WIDTH), LOW), kept, kept, down, down],
        after=after,
        work=cost(1e6, 1e7),
    )


def joint_pair_kernel(place, px, px_got, qy, qy_got, x_send, y_send, p, q):
    y, x = place[1], place[2]
    for z in range(4):
        p[z] = added(px[z, y], px_got[z, y])
        y_send[z] = added(px[z, 1 - y], px_got[z, 1 - y])


        def from_y(side):
            return qy_got[pl.ds(pl.multiple_of((z * 2 + side) * JOINT_SECOND, 32), JOINT_SECOND), :]

        q[z] = added(qy[z, x], from_y(x))
        x_send[z] = added(qy[z, 1 - x], from_y(1 - x))


def joint_pair_stage(place, arrays, after=()):
    first, second = made((4, JOINT_FIRST, WIDTH), LOW), made((4, JOINT_SECOND, WIDTH), LOW)
    return call(
        joint_pair_kernel,
        "joint_pair_stage",
        place,
        [plain(array) for array in arrays],
        [second, first, first, second],
        after=after,
        work=cost(1e6, 1e7),
    )


def up_line_kernel(place, y_got, x_got, p, q, down_two, down_got, send, keep, down_send, down_keep):
    low, high_here = place[0] % 2, place[0] // 2
    half = UP_ROWS // 2
    for target, parity in ((keep, low), (send, 1 - low)):
        for high in range(2):
            index = 2 * high + parity
            rows = pl.ds(pl.multiple_of(index * half, half), half)
            target[high, 0:half] = added(p[index], y_got[rows, :])
            target[high, half:] = added(q[index], x_got[rows, :])
    down_keep[...] = added(down_two[high_here], down_got[high_here])
    down_send[...] = added(down_two[1 - high_here], down_got[1 - high_here])


def up_line_stage(place, arrays, after=()):
    return call(
        up_line_kernel,
        "up_line_stage",
        place,
        [plain(array) for array in arrays],
        [made((2, UP_ROWS, WIDTH), LOW)] * 2 + [made((DOWN_ROWS, WIDTH), LOW)] * 2,
        after=after,
        work=cost(1e6, 1e7),
    )


def joint_line_kernel(place, x_got, y_got, p, q, keep, one, two, three):
    low, high = place[0] % 2, place[0] // 2
    for target, index in (
        (keep, 2 * high + low), (one, 2 * high + 1 - low), (two, 2 * (1 - high) + low), (three, 2 * (1 - high) + 1 - low)
    ):
        target[0:JOINT_FIRST] = added(p[index], y_got[index])
        target[JOINT_FIRST:] = added(q[index], x_got[index])


def joint_line_stage(place, arrays, after=()):
    return call(
        joint_line_kernel,
        "joint_line_stage",
        place,
        [plain(array) for array in arrays],
        [made((JOINT_ROWS, WIDTH), LOW)] * 4,
        after=after,
        work=cost(1e6, 1e6),
    )


def end_stage_kernel(place, keep_two, got, send, keep):
    high = place[0] // 2
    keep[...] = added(keep_two[high], got[high])
    send[...] = added(keep_two[1 - high], got[1 - high])


def end_stage(place, keep_two, got, after=()):
    return call(
        end_stage_kernel,
        "end_stage",
        place,
        [plain(keep_two), plain(got)],
        [made(keep_two.shape[1:], LOW)] * 2,
        after=after,
        work=cost(1e6, 1e6),
    )


def joint_sum_kernel(place, first, second, third, fourth, out):
    total = (first[...].astype(FLOAT) + second[...].astype(FLOAT)) + (third[...].astype(FLOAT) + fourth[...].astype(FLOAT))
    out[...] = total.astype(LOW)


def joint_sum(place, arrays, after=()):
    results, mark = call(
        joint_sum_kernel,
        "joint_sum",
        place,
        [plain(array) for array in arrays],
        [made((JOINT_ROWS, WIDTH), LOW)],
        after=after,
        work=cost(1e6, 1e6),
    )
    return results[0], mark


def last_sum_kernel(place, *refs):
    count = len(refs) // 3
    for index in range(count):
        refs[2 * count + index][...] = added(refs[2 * index][...], refs[2 * index + 1][...])


def last_sum(place, pairs, after=()):
    return call(
        last_sum_kernel,
        "last_sum",
        place,
        [plain(array) for pair in pairs for array in pair],
        [made(pair[0].shape, LOW) for pair in pairs],
        after=after,
        work=cost(1e6, 1e6),
    )


def gathered(unit, mark=None):
    across = x_swap(unit)
    if mark is not None:
        across, mark = lax.optimization_barrier((across, mark))
    return unit, core_swap(unit), across, core_swap(across)


def quarters(place):
    x, c = place[2], place[3]
    return (x, c), (x, 1 - c), (1 - x, c), (1 - x, 1 - c)


def line_shift(place):
    seq = place[0] * 2 + place[1]
    return lax.rem(WIDTH - seq * 96, WIDTH)


def dense_out_kernel(
    place, d0, d1, d2, d3, u0, u1, u2, u3,
    down, up, out, gain2, shift2, down_bias, gain1, shift1, out_bias, up_bias, heads, tails,
):
    for down_unit, unit, (x, c) in zip((d0, d1, d2, d3), (u0, u1, u2, u3), quarters(place)):
        quarter = 2 * x + c
        down[pl.ds(pl.multiple_of(quarter * DOWN_ROWS, 32), DOWN_ROWS), :] = down_unit[...].astype(FLOAT)
        up[:, pl.ds(pl.multiple_of(quarter * WIDTH, LANES), WIDTH)] = unit[0:96, :].astype(FLOAT)
        rest = unit[96:128, :].astype(FLOAT)
        lanes = pl.ds(pl.multiple_of(c * HALF, LANES), HALF)
        out[pl.ds(pl.multiple_of(x * 48, 8), 24), lanes] = rest[0:24, 0:HALF]
        out[pl.ds(pl.multiple_of(x * 48 + 24, 8), 24), lanes] = rest[0:24, HALF:]

        @pl.when(x == 0)
        def _(rest=rest):
            heads[...] = rest[24:32]

        @pl.when(x == 1)
        def _(rest=rest):
            tails[...] = rest[24:32]

    seq = place[0] * 2 + place[1]
    shift = line_shift(place)
    head = pltpu.roll(heads[...], shift, 1)
    gain2[...] = head[0:1, 0:96]
    shift2[...] = head[1:2, 0:96]
    down_bias[...] = head[2:3, 0:96]
    tail = pltpu.roll(tails[...], shift, 1)
    gain1[...] = tail[0:1, 0:96]
    shift1[...] = tail[1:2, 0:96]
    out_bias[...] = tail[2:3, 0:96]
    wide = tails[pl.ds(4 + seq // 2, 1), :]
    up_bias[...] = jnp.where(seq % 2 == 0, wide[:, 0:HALF], wide[:, HALF:]).reshape(HALF)


def dense_outputs(place, units, after=()):
    results, mark = call(
        dense_out_kernel,
        "dense_outputs",
        place,
        [plain(unit) for unit in units],
        [made((4 * DOWN_ROWS, WIDTH), FLOAT), made((96, FF), FLOAT), made((96, WIDTH), FLOAT)]
        + [made((1, 96), FLOAT)] * 6
        + [made((HALF,), FLOAT)],
        scratch=[pltpu.VMEM((8, WIDTH), FLOAT)] * 2,
        after=after,
        work=cost(1e6, 3e6),
    )
    return (*results[:3], *(vector.reshape(-1) for vector in results[3:])), mark


def joint_out_kernel(place, u0, u1, u2, u3, joint, query_bias, value_bias, sums):
    for unit, (x, c) in zip((u0, u1, u2, u3), quarters(place)):

        def lanes(kind):
            return pl.ds(pl.multiple_of(kind * WIDTH + c * HALF, LANES), HALF)

        first = unit[0:JOINT_FIRST].astype(FLOAT)
        rest = unit[JOINT_FIRST:].astype(FLOAT)
        rows = pl.ds(pl.multiple_of(x * 48, 16), 48)
        joint[rows, lanes(0)] = first[:, 0:HALF]
        joint[rows, lanes(1)] = first[:, HALF:]
        joint[pl.ds(pl.multiple_of(x * 48, 8), 24), lanes(2)] = rest[0:24, 0:HALF]
        joint[pl.ds(pl.multiple_of(x * 48 + 24, 8), 24), lanes(2)] = rest[0:24, HALF:]

        @pl.when(x == 0)
        def _(rest=rest, c=c):
            half = pl.ds(pl.multiple_of(c * HALF, LANES), HALF)
            sums[0:1, half] = rest[24:25, 0:HALF]
            sums[1:2, half] = rest[24:25, HALF:]

    turned = pltpu.roll(sums[...], line_shift(place), 1)
    query_bias[...] = turned[0:1, 0:96]
    value_bias[...] = turned[1:2, 0:96]


def joint_outputs(place, units, after=()):
    results, mark = call(
        joint_out_kernel,
        "joint_outputs",
        place,
        [plain(unit) for unit in units],
        [made((96, 3 * WIDTH), FLOAT), made((1, 96), FLOAT), made((1, 96), FLOAT)],
        scratch=[pltpu.VMEM((8, WIDTH), FLOAT)],
        after=after,
        work=cost(1e6, 2e6),
    )
    return (results[0], results[1].reshape(-1), results[2].reshape(-1)), mark


def row_body(
    tokens,
    pair_lengths,
    joint_weight,
    query_bias,
    value_bias,
    out_weight,
    out_bias,
    first_gain,
    first_shift,
    up_weight,
    up_bias,
    down_weight,
    down_bias,
    second_gain,
    second_shift,
    cotangent,
):
    seq, rows = lax.axis_index("seq"), lax.axis_index("rows")
    z, y, x, c = seq // 2, seq % 2, rows // 2, rows % 2
    place = jnp.stack([z, y, x, c]).astype(jnp.int32)
    odd = z % 2
    weights = {
        "out": out_weight, "out_bias": out_bias, "gain1": first_gain, "shift1": first_shift,
        "up": up_weight, "up_bias": up_bias, "down": down_weight, "down_bias": down_bias,
        "gain2": second_gain, "shift2": second_shift,
    }

    def local_row(array, index):
        return lax.dynamic_index_in_dim(array, index, 0, keepdims=False)

    columns, query_row, value_row = own_columns(place, joint_weight, query_bias, value_bias)
    lengths = (pair_lengths, core_swap(pair_lengths))
    own = [row_swap(local_row(tokens, odd), 0), row_swap(local_row(tokens, 1 - odd), 1)]
    *own, columns, lengths = lax.optimization_barrier((*own, columns, lengths))
    across = [y_swap(block) for block in own]
    here = own + [core_swap(block) for block in own]
    (q, k_here, v_here, summed, stats), mark = first_attention(
        place, lengths, here, columns, query_row, value_row
    )
    padding = jnp.zeros((16, WIDTH), LOW)
    cotangents = [
        row_swap(jnp.concatenate([local_row(cotangent, index), padding], axis=0), second)
        for second, index in ((0, odd), (1, 1 - odd))
    ]
    across[0], across[1], mark = lax.optimization_barrier((across[0], across[1], mark))
    there = across + [core_swap(block) for block in across]
    blocks = here + there
    (att, k_there, v_there, log_total), mark = attention(
        place, lengths, there, columns, value_row, q, summed, stats, (mark,)
    )
    att, *cotangents = lax.optimization_barrier((att, *cotangents))
    att_got = core_swap(att)
    results, mark = forward(place, att, att_got, own, cotangents, weights, (mark,))
    (
        result0, result1, feed, second_grad, act, act_send, slope, unit1, inverse1, normed, normed_t, att_t, sums0
    ) = results
    act_got, feed_got, normed_got = core_swap(act_send), core_swap(feed), core_swap(normed)
    done = (row_swap(result0, 0), row_swap(result1, 1))
    (px_send, px, qy_send, qy), mark = down_units(place, act, act_got, feed, feed_got, (mark,))
    down_pair = (px, x_swap(px_send), qy, y_swap(qy_send))
    results, mark = backward(place, feed, slope, second_grad, unit1, inverse1, weights, (mark, normed_got))
    inner0, inner1, send0, send1, first_grad, branch_own, back_own, misc_send, sums1 = results
    got, misc = (core_swap(send0), core_swap(send1)), core_swap(misc_send)
    (x_send, y_send, px, qy), mark = up_units(
        place, normed_t, normed_got, (inner0, inner1), got, att_t, branch_own, misc, sums0, sums1, feed_got, (mark,)
    )
    (x_send, y_send, down_p, down_q), mark = down_pair_stage(place, down_pair, x_send, y_send, (mark,))
    x_got, y_got = x_swap(x_send), y_swap(y_send)
    (dq, dk, dv), mark = attention_back(
        place, lengths, q, (k_here, k_there), (v_here, v_there), log_total, att, back_own, misc, (mark,)
    )
    (token_own, own_send, token_far, far_send), mark = token_parts(place, dq, dk, dv, columns, (mark, *done))
    own_got, far_got = core_swap(own_send), core_swap(far_send)
    (px_send, joint_px, qy_send, joint_qy), mark = joint_units(
        place, blocks, dq, dk, dv, token_far, far_got, (mark,)
    )
    (x_send, y_send, p, q_, down_send, down_two), mark = second_stage(
        place, (x_got, y_got, px, qy, down_p, down_q), (mark, own_got)
    )
    x_got, y_got, down_got = x_swap(x_send), y_swap(y_send), z_swap(down_send, 1)
    px_send, qy_send, mark = lax.optimization_barrier((px_send, qy_send, mark))
    across = y_swap(qy_send)
    joint_pair = (joint_px, x_swap(px_send), joint_qy, across)
    (up_send, up_two, down_send, down_keep), mark = up_line_stage(
        place, (y_got, x_got, p, q_, down_two, down_got), (mark,)
    )
    up_got, down_got = z_swap(up_send, 1), z_swap(down_send, 2)
    (up_send, up_keep), mark = end_stage(place, up_two, up_got, (mark, down_got))
    up_got = z_swap(up_send, 2)
    (down_unit,), mark = last_sum(place, ((down_keep, down_got),), (mark,))
    down_across = x_swap(down_unit)
    (x_send, y_send, joint_p, joint_q), mark = joint_pair_stage(place, joint_pair, (mark,))
    joint_x_got, joint_y_got = x_swap(x_send), y_swap(y_send)
    down_own, up_got = lax.optimization_barrier((down_unit, up_got))
    down_all = (down_unit, core_swap(down_own), down_across, core_swap(down_across))
    (token0, token1), mark = token_last(place, (token_own, own_got, across, first_grad), (mark,))
    back = (row_swap(token0, 0), row_swap(token1, 1))
    (up_unit,), mark = last_sum(place, ((up_keep, up_got),), (mark,))
    up_all = gathered(up_unit)
    (keep, one, two, three), mark = joint_line_stage(
        place, (joint_x_got, joint_y_got, joint_p, joint_q), (mark, *down_all[1:])
    )
    joint_last = (keep, z_swap(two, 2), z_swap(three, 3), z_swap(one, 1))
    joint_unit, mark = joint_sum(place, joint_last, (mark,))
    joint_across = x_swap(joint_unit)
    joint_across, first_back = lax.optimization_barrier((joint_across, back[0]))
    joint_all = (joint_unit, core_swap(joint_unit), joint_across, core_swap(joint_across))
    (
        down_grad, up_grad, out_grad, second_gain_grad, second_shift_grad, down_bias_grad, first_gain_grad,
        first_shift_grad, out_bias_grad, up_bias_grad,
    ), mark = dense_outputs(place, (*down_all, *up_all), (mark,))
    (joint_grad, query_bias_grad, value_bias_grad), mark = joint_outputs(place, joint_all, (mark,))
    (outputs, token_grad), mark = back_rows(place, done, (first_back, back[1]), (mark,))
    return (
        outputs,
        token_grad,
        joint_grad,
        query_bias_grad,
        value_bias_grad,
        out_grad,
        out_bias_grad,
        first_gain_grad,
        first_shift_grad,
        up_grad,
        up_bias_grad,
        down_grad,
        down_bias_grad,
        second_gain_grad,
        second_shift_grad,
    )


def body(tokens, *others):
    if (lax.axis_size("seq"), lax.axis_size("rows")) == (8, 4) and tokens.shape == (2, BLOCK, WIDTH):
        return row_body(tokens, *others)
    return general_body(tokens, *others)


def solution(mesh):
    placed = (
        P("rows", "seq", None),
        P("rows", None),
        P(),
        P(),
        P(),
        P(),
        P(),
        P(),
        P(),
        P(),
        P(),
        P(),
        P(),
        P(),
        P(),
        P("rows", "seq", None),
    )
    return jax.shard_map(
        body,
        mesh=mesh,
        in_specs=placed,
        out_specs=(
            P("rows", "seq", None),
            P("rows", "seq", None),
            P("seq", None),
            P("seq"),
            P("seq"),
            P("seq", None),
            P("seq"),
            P("seq"),
            P("seq"),
            P("seq", None),
            P("seq"),
            P("seq", None),
            P("seq"),
            P("seq"),
            P("seq"),
        ),
        check_vma=False,
    )
```
